32 devices in a mesh: row: 8 (over z, x), col: 4 (over y, core).
Axes of the slice: x: 2, y: 2, z: 4, core: 2. Of those that a mesh axis runs over, the one named last changes fastest.
Arguments:
- populations: float32 [256, 27, 4096], P(('row', 'col')), may hold values from 0 to 3, as said below
- destination: int32 [256], P(('row', 'col')), may hold values from 0 to 255, as said below
- refinement: int32 [256], P(('row', 'col')), may hold values from 0 to 4
Outputs:
- final_populations: float32 [256, 27, 4096], P(('row', 'col'))
The draws below stay inside these ranges and needn't reach their ends.
Inputs may be any that keep to these rules, and one draw needn't show every extreme that they name: `destination`: A permutation of all slots. A slot's device is slot // 8, with row index device // 4 and column index device % 4. Of one device's blocks, 0 or 2 are bound for each row index, one row possibly taking a smaller remainder; the blocks of one column bound for one row number exactly 8, and of those, 0 or 4 are bound for each column index, one possibly taking a smaller remainder. Both bounds are reached. `populations`: Positive.
All inputs are finite; a program needn't handle non-finite values.
Results may differ from the reference program's by a relative error of at most 0.0001.
Values sent between devices are 32-bit elements; how exact they have to be, the bound alone decides.
No kernel may reach another device: no remote copies, remote signals or barrier semaphores. Data moves between devices by JAX's collectives and lax.ppermute only.
A program may use at most 192 MiB of HBM per device.

```python
import jax
import jax.numpy as jnp
from jax import lax

EDGE = 16
BLK_DEV = 8
STEPS = 1
CELLS = 4096
NBLK = 256
N_ROW = 8
N_COL = 4


def shuffled(key, count, copies):
    keys = jax.random.split(key, copies)
    return jax.vmap(lambda single: jax.random.permutation(single, count))(keys)


def draw_destination(key, part):
    row_count = N_ROW
    col_count = N_COL
    blocks = BLK_DEV
    cap_row = 2 * ((blocks + row_count - 1) // row_count)
    cap_col = 2 * ((blocks + col_count - 1) // col_count)
    keys = jax.random.split(jax.random.fold_in(key, 11), 6)
    order_one = shuffled(keys[0], row_count, col_count)
    shift_one = shuffled(keys[1], row_count, col_count)
    place_one = shuffled(keys[2], blocks, row_count * col_count).reshape(row_count, col_count, blocks)
    order_two = shuffled(keys[3], col_count, row_count)
    shift_two = shuffled(keys[4], col_count, row_count)
    place_two = shuffled(keys[5], blocks, row_count * col_count).reshape(row_count, col_count, blocks)
    rank_one = jnp.argsort(order_one, axis=1).astype(jnp.int32)
    rank_two = jnp.argsort(order_two, axis=1).astype(jnp.int32)
    rows = jnp.arange(row_count, dtype=jnp.int32)[:, None, None]
    cols = jnp.arange(col_count, dtype=jnp.int32)[None, :, None]
    listed = jnp.arange(blocks, dtype=jnp.int32)[None, None, :]
    step_one = shift_one[cols, listed // cap_row]
    middle_row = order_one[cols, (rank_one[cols, rows] + step_one) % row_count]
    position_two = place_two[middle_row, cols, listed]
    step_two = shift_two[middle_row, position_two // cap_col]
    final_col = order_two[middle_row, (rank_two[middle_row, cols] + step_two) % col_count]
    final_slot = (middle_row * col_count + final_col) * blocks + position_two
    old_slot = (rows * col_count + cols) * blocks + place_one
    total = row_count * col_count * blocks
    result = jnp.zeros((total,), jnp.int32).at[old_slot.reshape(-1)].set(final_slot.reshape(-1).astype(jnp.int32))
    return result


def draw_populations(key, part):
    component = jnp.arange(27)

    def axis_weight(index):
        return jnp.where(index == 1, 2.0 / 3.0, 1.0 / 6.0)
    weight = axis_weight(component // 9) * axis_weight(component // 3 % 3) * axis_weight(component % 3)
    base = (weight * 4.0)[None, :, None]
    noise = jax.random.uniform(jax.random.fold_in(key, 5), (NBLK, 27, CELLS), jnp.float32, 0.1, 1.9)
    return (base * noise).astype(jnp.float32)


def plant(drawn, own_key, low, top_value):
    index_at = [jax.random.randint(jax.random.fold_in(own_key, axis), (), 0, length) for axis, length in enumerate(drawn.shape)]
    main_axis = drawn.shape.index(max(drawn.shape))
    next_to = index_at[:main_axis] + [(index_at[main_axis] + 1) % drawn.shape[main_axis]] + index_at[main_axis + 1:]
    return drawn.at[tuple(index_at)].set(low).at[tuple(next_to)].set(top_value)


def setup_inputs(seed: int = 0) -> dict:
    arg_keys = jax.random.split(jax.random.key(seed), 4)
    populations = draw_populations(jax.random.fold_in(arg_keys[3], 71), 0)
    destination = draw_destination(jax.random.fold_in(arg_keys[3], 71), 0)
    refinement = plant(jax.random.randint(arg_keys[2], (NBLK,), 0, 5), jax.random.fold_in(arg_keys[2], 1), 0, 4).astype(jnp.int32)
    return {"populations": populations, "destination": destination, "refinement": refinement}


VISCOSITY = 0.01


def relax_rate(levels):
    return 1.0 / (3.0 * VISCOSITY * jnp.exp2(levels.astype(jnp.float32)) + 0.5)


def axis_forward(values, velocity, axis):
    moved = jnp.moveaxis(values, axis, 0)
    minus_part, rest_part, plus_part = moved[0], moved[1], moved[2]
    offset_minus = -1.0 - velocity
    offset_rest = -velocity
    offset_plus = 1.0 - velocity
    zeroth = minus_part + rest_part + plus_part
    first = offset_minus * minus_part + offset_rest * rest_part + offset_plus * plus_part
    second = (offset_minus * offset_minus * minus_part + offset_rest * offset_rest * rest_part
              + offset_plus * offset_plus * plus_part)
    return jnp.moveaxis(jnp.stack([zeroth, first, second]), 0, axis)


def axis_backward(moments, velocity, axis):
    moved = jnp.moveaxis(moments, axis, 0)
    zeroth, first, second = moved[0], moved[1], moved[2]
    raw_one = first + velocity * zeroth
    raw_two = second + 2.0 * velocity * first + velocity * velocity * zeroth
    minus_part = 0.5 * (raw_two - raw_one)
    rest_part = zeroth - raw_two
    plus_part = 0.5 * (raw_one + raw_two)
    return jnp.moveaxis(jnp.stack([minus_part, rest_part, plus_part]), 0, axis)


def collide(flat, rate):
    grid = flat.reshape((3, 3, 3) + flat.shape[1:])
    density = jnp.sum(flat, axis=0)
    velocity_x = (jnp.sum(grid[2], axis=(0, 1)) - jnp.sum(grid[0], axis=(0, 1))) / density
    velocity_y = (jnp.sum(grid[:, 2], axis=(0, 1)) - jnp.sum(grid[:, 0], axis=(0, 1))) / density
    velocity_z = (jnp.sum(grid[:, :, 2], axis=(0, 1)) - jnp.sum(grid[:, :, 0], axis=(0, 1))) / density
    central = axis_forward(grid, velocity_x, 0)
    central = axis_forward(central, velocity_y, 1)
    central = axis_forward(central, velocity_z, 2)
    keep = 1.0 - rate
    post_xy = keep * central[1, 1, 0]
    post_xz = keep * central[1, 0, 1]
    post_yz = keep * central[0, 1, 1]
    dev_one = keep * (central[2, 0, 0] - central[0, 2, 0])
    dev_two = keep * (central[2, 0, 0] - central[0, 0, 2])
    post_xx = (density + dev_one + dev_two) / 3.0
    post_yy = post_xx - dev_one
    post_zz = post_xx - dev_two
    inverse = 1.0 / density
    entries = {
        (0, 0, 0): density,
        (2, 0, 0): post_xx, (0, 2, 0): post_yy, (0, 0, 2): post_zz,
        (1, 1, 0): post_xy, (1, 0, 1): post_xz, (0, 1, 1): post_yz,
        (2, 2, 0): (post_xx * post_yy + 2.0 * post_xy * post_xy) * inverse,
        (2, 0, 2): (post_xx * post_zz + 2.0 * post_xz * post_xz) * inverse,
        (0, 2, 2): (post_yy * post_zz + 2.0 * post_yz * post_yz) * inverse,
        (2, 1, 1): (post_xx * post_yz + 2.0 * post_xy * post_xz) * inverse,
        (1, 2, 1): (post_yy * post_xz + 2.0 * post_xy * post_yz) * inverse,
        (1, 1, 2): (post_zz * post_xy + 2.0 * post_xz * post_yz) * inverse,
        (2, 2, 2): (post_xx * post_yy * post_zz
                    + 2.0 * (post_xx * post_yz * post_yz + post_yy * post_xz * post_xz + post_zz * post_xy * post_xy)
                    + 8.0 * post_xy * post_xz * post_yz) * inverse * inverse,
    }
    zeros_field = jnp.zeros_like(density)
    stacked = jnp.stack([entries.get((power_x, power_y, power_z), zeros_field)
                         for power_x in range(3) for power_y in range(3) for power_z in range(3)])
    moments = stacked.reshape(grid.shape)
    back = axis_backward(moments, velocity_z, 2)
    back = axis_backward(back, velocity_y, 1)
    back = axis_backward(back, velocity_x, 0)
    return back.reshape(flat.shape)


def to_lattice(blocks):
    shaped = blocks.reshape(N_ROW, N_COL, BLK_DEV, 27, EDGE, EDGE, EDGE)
    ordered = jnp.transpose(shaped, (3, 0, 4, 1, 5, 2, 6))
    return ordered.reshape(27, N_ROW * EDGE, N_COL * EDGE, BLK_DEV * EDGE)


def from_lattice(lattice):
    shaped = lattice.reshape(27, N_ROW, EDGE, N_COL, EDGE, BLK_DEV, EDGE)
    ordered = jnp.transpose(shaped, (1, 3, 5, 0, 2, 4, 6))
    return ordered.reshape(NBLK, 27, CELLS)


def stream_lattice(post):
    read = []
    for component in range(27):
        shift_x = component // 9 - 1
        shift_y = (component // 3) % 3 - 1
        shift_z = component % 3 - 1
        mirror = post[26 - component]
        shifted = jnp.roll(post[component], (shift_x, shift_y), axis=(0, 1))
        if shift_z == 1:
            shifted = jnp.concatenate([mirror[..., :1], shifted[..., :-1]], axis=-1)
        elif shift_z == -1:
            shifted = jnp.concatenate([shifted[..., 1:], mirror[..., -1:]], axis=-1)
        read.append(shifted)
    return jnp.stack(read)


def reference(populations, destination, refinement):
    arrived = jnp.zeros_like(populations).at[destination].set(populations)
    levels = jnp.zeros_like(refinement).at[destination].set(refinement)
    rates = relax_rate(levels)
    current = arrived
    for iteration in range(STEPS):
        post = lax.map(lambda operands: collide(operands[0], operands[1]), (current, rates))
        current = from_lattice(stream_lattice(to_lattice(post)))
    return current
```

```python
import functools

import jax
import jax.numpy as jnp
import numpy as np
from jax import lax
from jax.experimental import pallas as pl
from jax.experimental.pallas import tpu as pltpu
from jax.sharding import PartitionSpec as P

EDGE = 16
VISCOSITY = 0.01
LANES = 128
SUB = 8
NQ = 27
QPAD = 32
NFIELD = 9
GROUPS = 4
VMEM_LIMIT = 50 * 1024 * 1024


def velocity(q):
    return (q // 9 - 1, (q // 3) % 3 - 1, q % 3 - 1)


def moment_matrix(blocks):
    powers = [
        (0, 0, 0), (1, 0, 0), (0, 1, 0), (0, 0, 1), (2, 0, 0),
        (0, 2, 0), (0, 0, 2), (1, 1, 0), (1, 0, 1), (0, 1, 1),
    ]
    out = np.zeros((len(powers), blocks, blocks, QPAD), np.float32)
    for m, (a, b, c) in enumerate(powers):
        for q in range(NQ):
            cx, cy, cz = velocity(q)
            for t in range(blocks):
                out[m, t, t, q] = float(cx**a * cy**b * cz**c)
    return out.reshape(len(powers) * blocks, blocks * QPAD)


def pre_kernel(cap, per_row, dest_ref, level_ref, w_ref, x_ref, out_ref, mom_ref, swap_ref):
    blocks = x_ref.shape[0]
    cells = x_ref.shape[2]
    chunks = cells // LANES
    x = x_ref[...]
    comp = lax.broadcasted_iota(jnp.int32, x.shape, 1)
    x = jnp.where(comp < NQ, x, 0.0).reshape(blocks * QPAD, cells)
    w = w_ref[...].astype(jnp.bfloat16)
    high = x.astype(jnp.bfloat16)
    rest = x - high.astype(jnp.float32)
    mid = rest.astype(jnp.bfloat16)
    low = (rest - mid.astype(jnp.float32)).astype(jnp.bfloat16)
    dot = functools.partial(jnp.dot, preferred_element_type=jnp.float32)
    mom_ref[...] = dot(w, low) + dot(w, mid) + dot(w, high)

    which = lax.broadcasted_iota(jnp.int32, (SUB, LANES), 0)
    scale = jnp.zeros((SUB, LANES), jnp.int32)
    for t in range(blocks):
        scale = jnp.where(which == t, jnp.left_shift(1, level_ref[t]), scale)
    rate = 1.0 / (3.0 * VISCOSITY * scale.astype(jnp.float32) + 0.5)
    keep = 1.0 - rate

    for c in range(chunks):
        rho, jx, jy, jz, mxx, myy, mzz, mxy, mxz, myz = [
            mom_ref[m * SUB : (m + 1) * SUB, c * LANES : (c + 1) * LANES] for m in range(10)
        ]
        inverse = 1.0 / rho
        ux, uy, uz = jx * inverse, jy * inverse, jz * inverse
        kxx = mxx - jx * ux
        fields = (
            rho, ux, uy, uz,
            keep * (mxy - jx * uy),
            keep * (mxz - jx * uz),
            keep * (myz - jy * uz),
            keep * (kxx - (myy - jy * uy)),
            keep * (kxx - (mzz - jz * uz)),
        )
        for n, field in enumerate(fields):
            base = (n * chunks + c) * SUB
            swap_ref[base : base + SUB, :] = field

    rows = [dest_ref[t] // per_row for t in range(blocks)]
    for t in range(blocks):
        slot = rows[t] * cap
        for other in range(t):
            slot = slot + jnp.where(rows[other] == rows[t], 1, 0)
        for n in range(NFIELD):
            out_ref[slot, 0, n] = swap_ref[pl.ds(n * chunks * SUB + t, SUB, stride=SUB), :]


def pre(populations, destination, refinement, row_count, cap, per_row):
    blocks = populations.shape[0]
    cells = populations.shape[2] // GROUPS
    weights = jnp.asarray(moment_matrix(blocks))
    slots = row_count * cap
    return pl.pallas_call(
        functools.partial(pre_kernel, cap, per_row),
        grid_spec=pltpu.PrefetchScalarGridSpec(
            num_scalar_prefetch=2,
            grid=(GROUPS,),
            in_specs=[
                pl.BlockSpec(weights.shape, lambda g, *_: (0, 0)),
                pl.BlockSpec((blocks, QPAD, cells), lambda g, *_: (0, 0, g)),
            ],
            out_specs=pl.BlockSpec((slots, 1, NFIELD, SUB, LANES), lambda g, *_: (0, g, 0, 0, 0)),
            scratch_shapes=[
                pltpu.VMEM((10 * SUB, cells), jnp.float32),
                pltpu.VMEM((NFIELD * cells // LANES * SUB, LANES), jnp.float32),
            ],
        ),
        out_shape=jax.ShapeDtypeStruct((slots, GROUPS, NFIELD, SUB, LANES), jnp.float32),
        compiler_params=pltpu.CompilerParams(vmem_limit_bytes=VMEM_LIMIT),
        cost_estimate=pl.CostEstimate(flops=10**8, bytes_accessed=6 * 10**6, transcendentals=0),
    )(destination, refinement, weights, populations)


def repack_kernel(source_ref, target_ref, in_ref, out_ref, sems):
    count = source_ref.shape[0]
    copies = [
        pltpu.make_async_copy(in_ref.at[source_ref[j]], out_ref.at[target_ref[j]], sems.at[j])
        for j in range(count)
    ]
    for copy in copies:
        copy.start()
    for copy in copies:
        copy.wait()


def repack(source, target, landed, slots):
    count = source.shape[0]
    return pl.pallas_call(
        repack_kernel,
        in_specs=[
            pl.BlockSpec(memory_space=pltpu.SMEM),
            pl.BlockSpec(memory_space=pltpu.SMEM),
            pl.BlockSpec(memory_space=pl.ANY),
        ],
        out_specs=pl.BlockSpec(memory_space=pl.ANY),
        scratch_shapes=[pltpu.SemaphoreType.DMA((count,))],
        out_shape=jax.ShapeDtypeStruct((slots,) + landed.shape[1:], jnp.float32),
        cost_estimate=pl.CostEstimate(flops=0, bytes_accessed=3 * 10**6, transcendentals=0),
    )(source, target, landed)


def backward(zeroth, first, second, u):
    raw_one, raw_two = first, second
    if zeroth is not None:
        moved = u * zeroth
        raw_one = moved if raw_one is None else raw_one + moved
        square = u * moved
        raw_two = square if raw_two is None else raw_two + square
    if first is not None:
        cross = (u + u) * first
        raw_two = cross if raw_two is None else raw_two + cross
    rest = -raw_two if zeroth is None else zeroth - raw_two
    return 0.5 * (raw_two - raw_one), rest, 0.5 * (raw_one + raw_two)


def post_populations(rho, ux, uy, uz, pxy, pxz, pyz, dev_one, dev_two):
    inverse = 1.0 / rho
    pxx = (rho + dev_one + dev_two) * (1.0 / 3.0)
    pyy = pxx - dev_one
    pzz = pxx - dev_two
    sxy, sxz, syz = pxy * inverse, pxz * inverse, pyz * inverse
    sxx, syy = pxx * inverse, pyy * inverse
    szz = pzz * inverse
    central = {
        (0, 0, 0): rho, (2, 0, 0): pxx, (0, 2, 0): pyy, (0, 0, 2): pzz,
        (1, 1, 0): pxy, (1, 0, 1): pxz, (0, 1, 1): pyz,
        (2, 2, 0): pxx * syy + 2.0 * pxy * sxy,
        (2, 0, 2): pxx * szz + 2.0 * pxz * sxz,
        (0, 2, 2): pyy * szz + 2.0 * pyz * syz,
        (2, 1, 1): pxx * syz + 2.0 * pxy * sxz,
        (1, 2, 1): pyy * sxz + 2.0 * pxy * syz,
        (1, 1, 2): pzz * sxy + 2.0 * pxz * syz,
        (2, 2, 2): pxx * syy * szz
        + 2.0 * (pxx * syz * syz + pyy * sxz * sxz + pzz * sxy * sxy)
        + 8.0 * pxy * sxz * syz,
    }
    along_z = {}
    for a in range(3):
        for b in range(3):
            parts = backward(*(central.get((a, b, c)) for c in range(3)), uz)
            for k in range(3):
                along_z[a, b, k] = parts[k]
    along_y = {}
    for a in range(3):
        for k in range(3):
            parts = backward(*(along_z[a, b, k] for b in range(3)), uy)
            for j in range(3):
                along_y[a, j, k] = parts[j]
    result = [None] * NQ
    for j in range(3):
        for k in range(3):
            parts = backward(*(along_y[a, j, k] for a in range(3)), ux)
            for i in range(3):
                result[i * 9 + j * 3 + k] = parts[i]
    return result


def post_kernel(picked_ref, *refs):
    ins, (post_ref, xlo_ref, xhi_ref, ylo_ref, yhi_ref, mm_ref, mp_ref, pm_ref, pp_ref, swap_ref) = (
        refs[:SUB], refs[SUB:],
    )
    g = pl.program_id(0)
    for t in range(SUB):
        for n in range(NFIELD):
            swap_ref[pl.ds(n * SUB * SUB + t, SUB, stride=SUB), :] = ins[t][0, 0, n]
    lane = lax.broadcasted_iota(jnp.int32, (SUB, LANES), 1)
    for c in range(SUB):
        fields = [swap_ref[(n * SUB + c) * SUB : (n * SUB + c + 1) * SUB, :] for n in range(NFIELD)]
        result = post_populations(*fields)
        for q in range(NQ):
            post_ref[q, c] = result[q]
        x_in, half = c // 2, c % 2
        spot = (g % 2) * 4 + x_in
        inside = (lane // EDGE) == spot
        face_ref, first, shift = ((ylo_ref, 0, 0), (yhi_ref, 6, EDGE))[half]
        turn = spot * EDGE + shift
        for i in range(3):
            for k in range(3):
                value = pltpu.roll(result[i * 9 + first + k], turn % LANES, axis=1)
                face_ref[i * 3 + k, 0] = jnp.where(inside, value, face_ref[i * 3 + k, 0])

        if x_in == 0:

            @pl.when(g == 0)
            def _():
                for q in range(9):
                    xlo_ref[q, half] = result[q]
                for k in range(3):
                    if half == 0:
                        mm_ref[k] = result[k]
                    else:
                        mp_ref[k] = result[6 + k]

        if x_in == 3:

            @pl.when(g == GROUPS - 1)
            def _():
                for q in range(9):
                    xhi_ref[q, half] = result[18 + q]
                for k in range(3):
                    if half == 0:
                        pm_ref[k] = result[18 + k]
                    else:
                        pp_ref[k] = result[24 + k]


def post(picked, landed):
    shape = jax.ShapeDtypeStruct
    face = (9, 2, SUB, LANES)
    corner = (3, SUB, LANES)

    def pick(t):
        return pl.BlockSpec(
            (1, 1, NFIELD, SUB, LANES), lambda g, picked_ref: (picked_ref[t], g, 0, 0, 0)
        )

    whole_face = pl.BlockSpec(face, lambda g, *_: (0, 0, 0, 0))
    half_face = pl.BlockSpec((9, 1, SUB, LANES), lambda g, *_: (0, g // 2, 0, 0))
    whole_corner = pl.BlockSpec(corner, lambda g, *_: (0, 0, 0))
    return pl.pallas_call(
        post_kernel,
        grid_spec=pltpu.PrefetchScalarGridSpec(
            num_scalar_prefetch=1,
            grid=(GROUPS,),
            in_specs=[pick(t) for t in range(SUB)],
            out_specs=[
                pl.BlockSpec((NQ, SUB, SUB, LANES), lambda g, *_: (0, g, 0, 0)),
                whole_face, whole_face, half_face, half_face,
                whole_corner, whole_corner, whole_corner, whole_corner,
            ],
            scratch_shapes=[pltpu.VMEM((NFIELD * SUB * SUB, LANES), jnp.float32)],
        ),
        out_shape=[shape((NQ, GROUPS * SUB, SUB, LANES), jnp.float32)]
        + [shape(face, jnp.float32)] * 4
        + [shape(corner, jnp.float32)] * 4,
        compiler_params=pltpu.CompilerParams(vmem_limit_bytes=VMEM_LIMIT),
        cost_estimate=pl.CostEstimate(flops=10**7, bytes_accessed=5 * 10**6, transcendentals=0),
    )(picked, *([landed] * SUB))


def stream_kernel(
    main_ref, prev_ref, next_ref, xlo_ref, xhi_ref, ylo_ref, yhi_ref,
    mm_ref, mp_ref, pm_ref, pp_ref, out_ref, below_ref, above_ref, swap_ref,
):
    g = pl.program_id(0)
    width = EDGE // GROUPS

    @pl.when(g == 0)
    def _():
        for k in range(9):
            for x in range(EDGE):
                packed = ylo_ref[k, x // 8]
                below_ref[k, x + 1] = pltpu.roll(packed, (LANES - EDGE - EDGE * (x % 8)) % LANES, axis=1)
                packed = yhi_ref[k, x // 8]
                above_ref[k, x + 1] = pltpu.roll(packed, (LANES - EDGE * (x % 8)) % LANES, axis=1)
        for k in range(3):
            below_ref[6 + k, 0] = pp_ref[k]
            below_ref[k, EDGE + 1] = mp_ref[k]
            above_ref[6 + k, 0] = pm_ref[k]
            above_ref[k, EDGE + 1] = mm_ref[k]

    lane = lax.broadcasted_iota(jnp.int32, (SUB, LANES), 1)
    block = lax.broadcasted_iota(jnp.int32, (SUB, LANES), 0)
    along = lane % EDGE
    first_z, last_z = along == 0, along == EDGE - 1
    floor = first_z & (block == 0)
    ceiling = last_z & (block == SUB - 1)
    low_y, high_y = lane < EDGE, lane >= LANES - EDGE

    for x in range(width):

        def source(q, half):
            cx = velocity(q)[0]
            at = x - cx
            if at < 0:
                return jnp.where(g == 0, xlo_ref[q - 18, half], prev_ref[q - 18, half])
            if at >= width:
                return jnp.where(g == GROUPS - 1, xhi_ref[q, half], next_ref[q, half])
            return main_ref[q, at * 2 + half]

        for half in range(2):
            c = x * 2 + half
            for q in range(NQ):
                cx, cy, cz = velocity(q)
                a = source(q, half)
                side = g * width + x - cx + 1
                k = (cx + 1) * 3 + cz + 1
                if cy == 1:
                    a = jnp.where(high_y, below_ref[k, side] if half == 0 else source(q, 0), a)
                elif cy == -1:
                    a = jnp.where(low_y, above_ref[k, side] if half == 1 else source(q, 1), a)
                shift = EDGE * cy + cz
                value = a if shift == 0 else pltpu.roll(a, shift % LANES, axis=1)
                if cz == 1:
                    fill = pltpu.roll(pltpu.roll(a, 1, axis=0), (shift - EDGE) % LANES, axis=1)
                    value = jnp.where(first_z, fill, value)
                    value = jnp.where(floor, main_ref[26 - q, c], value)
                elif cz == -1:
                    fill = pltpu.roll(pltpu.roll(a, SUB - 1, axis=0), (shift + EDGE) % LANES, axis=1)
                    value = jnp.where(last_z, fill, value)
                    value = jnp.where(ceiling, main_ref[26 - q, c], value)
                base = (c * QPAD + q) * SUB
                swap_ref[base : base + SUB, :] = value
            for t in range(SUB):
                moved = swap_ref[pl.ds(c * QPAD * SUB + t, QPAD, stride=SUB), :]
                out_ref[t, :, c * LANES : (c + 1) * LANES] = moved[:NQ]


def stream(lattice, halos):
    cells = GROUPS * SUB * LANES
    face = (9, 2, SUB, LANES)
    whole_face = pl.BlockSpec(face, lambda g: (0, 0, 0, 0))
    whole_corner = pl.BlockSpec((3, SUB, LANES), lambda g: (0, 0, 0))
    width = EDGE // GROUPS
    return pl.pallas_call(
        stream_kernel,
        grid=(GROUPS,),
        in_specs=[
            pl.BlockSpec((NQ, SUB, SUB, LANES), lambda g: (0, g, 0, 0)),
            pl.BlockSpec(face, lambda g: (2, jnp.maximum(width * g - 1, 0), 0, 0)),
            pl.BlockSpec(face, lambda g: (0, jnp.minimum(width * g + width, EDGE - 1), 0, 0)),
        ]
        + [whole_face] * 4
        + [whole_corner] * 4,
        out_specs=pl.BlockSpec((SUB, NQ, SUB * LANES), lambda g: (0, 0, g)),
        out_shape=jax.ShapeDtypeStruct((SUB, NQ, cells), jnp.float32),
        scratch_shapes=[
            pltpu.VMEM((9, EDGE + 2, SUB, LANES), jnp.float32),
            pltpu.VMEM((9, EDGE + 2, SUB, LANES), jnp.float32),
            pltpu.VMEM((SUB * QPAD * SUB, LANES), jnp.float32),
        ],
        compiler_params=pltpu.CompilerParams(vmem_limit_bytes=VMEM_LIMIT),
        cost_estimate=pl.CostEstimate(flops=10**7, bytes_accessed=8 * 10**6, transcendentals=0),
    )(lattice, lattice, lattice, *halos)


def exchange(xlo, xhi, ylo, yhi, mm, mp, pm, pp, row_count, col_count):
    def send(value, dr, dc):
        pairs = []
        for r in range(row_count):
            for c in range(col_count):
                to = ((r + dr) % row_count) * col_count + (c + dc) % col_count
                pairs.append((r * col_count + c, to))
        return lax.ppermute(value, ("row", "col"), pairs)

    return (
        send(xhi, 1, 0), send(xlo, -1, 0), send(yhi, 0, 1), send(ylo, 0, -1),
        send(mm, -1, -1), send(mp, -1, 1), send(pm, 1, -1), send(pp, 1, 1),
    )


def routes(everywhere, blocks, row_count, col_count, cap_row, cap_col):
    row = lax.axis_index("row")
    col = lax.axis_index("col")
    per_row = blocks * col_count
    count = row_count * blocks
    table = everywhere.reshape(row_count, col_count, blocks)
    to_row = table // per_row
    earlier = jnp.asarray(np.tril(np.ones((blocks, blocks), np.bool_), -1))
    rank = jnp.sum((to_row[..., :, None] == to_row[..., None, :]) & earlier, axis=-1)
    landed_at = jnp.arange(row_count)[:, None, None] * cap_row + rank
    table = jnp.transpose(table, (1, 0, 2)).reshape(col_count, count)
    landed_at = jnp.transpose(landed_at, (1, 0, 2)).reshape(col_count, count)
    here = table // per_row == row
    to_col = table // blocks % col_count
    before = jnp.asarray(np.tril(np.ones((count, count), np.bool_), -1))

    mine = lax.dynamic_index_in_dim(here, col, 0, False)
    my_col = lax.dynamic_index_in_dim(to_col, col, 0, False)
    my_landed = lax.dynamic_index_in_dim(landed_at, col, 0, False)
    order = jnp.sum(before & mine[None, :], axis=1)
    place = jnp.sum(before & mine[None, :] & (my_col[:, None] == my_col[None, :]), axis=1)
    hit = mine[None, :] & (order[None, :] == jnp.arange(blocks)[:, None])
    source = jnp.sum(jnp.where(hit, my_landed[None, :], 0), axis=1)
    target = jnp.sum(jnp.where(hit, (my_col * cap_col + place)[None, :], 0), axis=1)

    final = here & (to_col == col)
    place = jnp.sum(before[None] & final[:, None, :], axis=2)
    place = place + jnp.arange(col_count)[:, None] * cap_col
    hit = final[None] & ((table % blocks)[None] == jnp.arange(blocks)[:, None, None])
    picked = jnp.sum(jnp.where(hit, place[None], 0), axis=(1, 2))
    return source.astype(jnp.int32), target.astype(jnp.int32), picked.astype(jnp.int32)


def on_device(populations, destination, refinement):
    blocks = populations.shape[0]
    row_count = lax.axis_size("row")
    col_count = lax.axis_size("col")
    cap_row = 2 * ((blocks + row_count - 1) // row_count)
    cap_col = 2 * ((blocks + col_count - 1) // col_count)
    everywhere = lax.all_gather(destination, ("row", "col"), tiled=True)
    outgoing = pre(populations, destination, refinement, row_count, cap_row, blocks * col_count)
    source, target, picked = routes(everywhere, blocks, row_count, col_count, cap_row, cap_col)
    landed = lax.all_to_all(outgoing, "row", split_axis=0, concat_axis=0, tiled=True)
    outgoing = repack(source, target, landed, col_count * cap_col)
    landed = lax.all_to_all(outgoing, "col", split_axis=0, concat_axis=0, tiled=True)
    lattice, *sides = post(picked, landed)
    halos = exchange(*sides, row_count, col_count)
    return stream(lattice, halos)


def solution(mesh):
    return jax.shard_map(
        on_device,
        mesh=mesh,
        in_specs=(P(("row", "col"), None, None), P(("row", "col")), P(("row", "col"))),
        out_specs=P(("row", "col"), None, None),
        check_vma=False,
    )
```

```python
import functools

import jax
import jax.numpy as jnp
from jax import lax
from jax.experimental import pallas as pl
from jax.experimental.pallas import tpu as pltpu
from jax.sharding import PartitionSpec as P

EDGE = 16
VISCOSITY = 0.01
LANES = 128
SUB = 8
NQ = 27
NFIELD = 9
GROUPS = 4
WIDTH = EDGE // GROUPS
CHUNKS = ((0, 3), (1, 2))
VMEM_LIMIT = 50 * 1024 * 1024


def velocity(q):
    return (q // 9 - 1, (q // 3) % 3 - 1, q % 3 - 1)


def quarter(part, g):
    first, second = CHUNKS[part]
    return first + (second - first) * g


def raw_moments(f):
    whole, slope, outer = {}, {}, {}
    for i in range(3):
        for j in range(3):
            low, rest, high = (f[i * 9 + j * 3 + k] for k in range(3))
            outer[i, j] = low + high
            whole[i, j] = outer[i, j] + rest
            slope[i, j] = high - low
    column = [whole[i, 0] + whole[i, 1] + whole[i, 2] for i in range(3)]
    tilt = [slope[i, 0] + slope[i, 1] + slope[i, 2] for i in range(3)]
    low_y = whole[0, 0] + whole[1, 0] + whole[2, 0]
    high_y = whole[0, 2] + whole[1, 2] + whole[2, 2]
    ends = column[0] + column[2]
    mzz = sum(outer[i, j] for i in range(3) for j in range(3))
    mxy = (whole[2, 2] - whole[2, 0]) - (whole[0, 2] - whole[0, 0])
    myz = (slope[0, 2] + slope[1, 2] + slope[2, 2]) - (slope[0, 0] + slope[1, 0] + slope[2, 0])
    return (
        ends + column[1],
        column[2] - column[0],
        high_y - low_y,
        tilt[0] + tilt[1] + tilt[2],
        ends,
        low_y + high_y,
        mzz,
        mxy,
        tilt[2] - tilt[0],
        myz,
    )


def pre_kernel(cap, per_row, tagged, dest_ref, level_ref, x_ref, out_ref, swap_ref):
    g = pl.program_id(0)
    blocks = x_ref.shape[1]
    chunks = x_ref.shape[2] // LANES
    which = lax.broadcasted_iota(jnp.int32, (SUB, LANES), 0)
    scale = jnp.zeros((SUB, LANES), jnp.int32)
    for t in range(blocks):
        scale = jnp.where(which == t, jnp.left_shift(1, level_ref[t]), scale)
    rate = 1.0 / (3.0 * VISCOSITY * scale.astype(jnp.float32) + 0.5)
    keep = 1.0 - rate

    for c in range(chunks):
        rho, jx, jy, jz, mxx, myy, mzz, mxy, mxz, myz = raw_moments(
            [x_ref[q, :, c * LANES : (c + 1) * LANES] for q in range(NQ)]
        )
        inverse = 1.0 / rho
        ux, uy, uz = jx * inverse, jy * inverse, jz * inverse
        kxx = mxx - jx * ux
        fields = (
            rho, ux, uy, uz,
            keep * (mxy - jx * uy),
            keep * (mxz - jx * uz),
            keep * (myz - jy * uz),
            keep * (kxx - (myy - jy * uy)),
            keep * (kxx - (mzz - jz * uz)),
        )
        for n, field in enumerate(fields):
            base = (n * chunks + c) * SUB
            swap_ref[base : base + SUB, :] = field

    tag = out_ref.shape[1] - 1
    if tagged:

        @pl.when(g == 0)
        def _():
            for slot in range(out_ref.shape[0]):
                out_ref[slot, tag] = jnp.full((SUB, LANES), -1.0, jnp.float32)

    rows = [dest_ref[t] // per_row for t in range(blocks)]
    for t in range(blocks):
        slot = rows[t] * cap
        for other in range(t):
            slot = slot + jnp.where(rows[other] == rows[t], 1, 0)
        for n in range(NFIELD):
            moved = swap_ref[pl.ds(n * chunks * SUB + t, SUB, stride=SUB), :]
            out_ref[slot, g * NFIELD + n] = moved
        if tagged:

            @pl.when(g == 0)
            def _():
                out_ref[slot, tag] = jnp.full((SUB, LANES), dest_ref[t], jnp.int32).astype(jnp.float32)


def pre(populations, destination, refinement, part, row_count, cap, per_row):
    blocks = populations.shape[1]
    cells = populations.shape[2] // GROUPS
    steps = len(CHUNKS[part])
    tagged = part == 0
    shape = (row_count * cap, steps * NFIELD + tagged, SUB, LANES)
    return pl.pallas_call(
        functools.partial(pre_kernel, cap, per_row, tagged),
        grid_spec=pltpu.PrefetchScalarGridSpec(
            num_scalar_prefetch=2,
            grid=(steps,),
            in_specs=[pl.BlockSpec((NQ, blocks, cells), lambda g, *_: (0, 0, quarter(part, g)))],
            out_specs=pl.BlockSpec(shape, lambda g, *_: (0, 0, 0, 0)),
            scratch_shapes=[pltpu.VMEM((NFIELD * cells // LANES * SUB, LANES), jnp.float32)],
        ),
        out_shape=jax.ShapeDtypeStruct(shape, jnp.float32),
        compiler_params=pltpu.CompilerParams(vmem_limit_bytes=VMEM_LIMIT),
        cost_estimate=pl.CostEstimate(flops=10**7, bytes_accessed=4 * 10**6, transcendentals=0),
        name="pre_%d" % part,
    )(destination, refinement, populations)


def repack_kernel(cap, blocks, col_count, tagged, tags_ref, in_ref, out_ref, count_ref):
    tag = out_ref.shape[1] - 1
    if tagged:
        for slot in range(out_ref.shape[0]):
            out_ref[slot, tag] = jnp.full((SUB, LANES), -1.0, jnp.float32)
    for c in range(col_count):
        count_ref[c] = c * cap
    for slot in range(in_ref.shape[0]):

        @pl.when(tags_ref[slot] >= 0)
        def _():
            c = tags_ref[slot] // blocks % col_count
            target = count_ref[c]
            count_ref[c] = target + 1
            out_ref[target] = in_ref[slot]


def repack(tags, landed, part, blocks, col_count, cap):
    shape = (col_count * cap,) + landed.shape[1:]
    return pl.pallas_call(
        functools.partial(repack_kernel, cap, blocks, col_count, part == 0),
        in_specs=[pl.BlockSpec(memory_space=pltpu.SMEM), pl.BlockSpec(memory_space=pltpu.VMEM)],
        out_specs=pl.BlockSpec(memory_space=pltpu.VMEM),
        scratch_shapes=[pltpu.SMEM((col_count,), jnp.int32)],
        out_shape=jax.ShapeDtypeStruct(shape, jnp.float32),
        compiler_params=pltpu.CompilerParams(vmem_limit_bytes=VMEM_LIMIT),
        cost_estimate=pl.CostEstimate(flops=0, bytes_accessed=3 * 10**6, transcendentals=0),
        name="repack_%d" % part,
    )(tags, landed)


def backward(zeroth, first, second, u):
    raw_one, raw_two = first, second
    if zeroth is not None:
        moved = u * zeroth
        raw_one = moved if raw_one is None else raw_one + moved
        square = u * moved
        raw_two = square if raw_two is None else raw_two + square
    if first is not None:
        cross = (u + u) * first
        raw_two = cross if raw_two is None else raw_two + cross
    rest = -raw_two if zeroth is None else zeroth - raw_two
    return 0.5 * (raw_two - raw_one), rest, 0.5 * (raw_one + raw_two)


def post_populations(rho, ux, uy, uz, pxy, pxz, pyz, dev_one, dev_two):
    inverse = 1.0 / rho
    pxx = (rho + dev_one + dev_two) * (1.0 / 3.0)
    pyy = pxx - dev_one
    pzz = pxx - dev_two
    sxy, sxz, syz = pxy * inverse, pxz * inverse, pyz * inverse
    syy, szz = pyy * inverse, pzz * inverse
    central = {
        (0, 0, 0): rho, (2, 0, 0): pxx, (0, 2, 0): pyy, (0, 0, 2): pzz,
        (1, 1, 0): pxy, (1, 0, 1): pxz, (0, 1, 1): pyz,
        (2, 2, 0): pxx * syy + 2.0 * pxy * sxy,
        (2, 0, 2): pxx * szz + 2.0 * pxz * sxz,
        (0, 2, 2): pyy * szz + 2.0 * pyz * syz,
        (2, 1, 1): pxx * syz + 2.0 * pxy * sxz,
        (1, 2, 1): pyy * sxz + 2.0 * pxy * syz,
        (1, 1, 2): pzz * sxy + 2.0 * pxz * syz,
        (2, 2, 2): pxx * syy * szz
        + 2.0 * (pxx * syz * syz + pyy * sxz * sxz + pzz * sxy * sxy)
        + 8.0 * pxy * sxz * syz,
    }
    along_z = {}
    for a in range(3):
        for b in range(3):
            parts = backward(*(central.get((a, b, c)) for c in range(3)), uz)
            for k in range(3):
                along_z[a, b, k] = parts[k]
    along_y = {}
    for a in range(3):
        for k in range(3):
            parts = backward(*(along_z[a, b, k] for b in range(3)), uy)
            for j in range(3):
                along_y[a, j, k] = parts[j]
    result = [None] * NQ
    for j in range(3):
        for k in range(3):
            parts = backward(*(along_y[a, j, k] for a in range(3)), ux)
            for i in range(3):
                result[i * 9 + j * 3 + k] = parts[i]
    return result


def post_kernel(outer, tags_ref, *refs):
    if outer:
        in_ref, post_ref, ylo_ref, yhi_ref, xlo_ref, xhi_ref, swap_ref, picked_ref = refs
    else:
        in_ref, _, post_ref, ylo_ref, yhi_ref, swap_ref, picked_ref = refs
    g = pl.program_id(0)
    for t in range(SUB):
        picked_ref[t] = 0
    for slot in range(in_ref.shape[0]):

        @pl.when(tags_ref[slot] >= 0)
        def _():
            picked_ref[tags_ref[slot] % SUB] = slot

    for t in range(SUB):
        slot = picked_ref[t]
        for n in range(NFIELD):
            swap_ref[pl.ds(n * SUB * SUB + t, SUB, stride=SUB), :] = in_ref[slot, g * NFIELD + n]
    lane = lax.broadcasted_iota(jnp.int32, (SUB, LANES), 1)
    for c in range(SUB):
        fields = [swap_ref[(n * SUB + c) * SUB : (n * SUB + c + 1) * SUB, :] for n in range(NFIELD)]
        result = post_populations(*fields)
        for q in range(NQ):
            post_ref[q, c] = result[q]
        x, half = c // 2, c % 2
        spot = g * WIDTH + x
        inside = (lane // EDGE) == spot
        face_ref, first, shift = ((ylo_ref, 0, 0), (yhi_ref, 6, EDGE))[half]
        for i in range(3):
            for k in range(3):
                value = pltpu.roll(result[i * 9 + first + k], (spot * EDGE + shift) % LANES, axis=1)
                face_ref[i * 3 + k] = jnp.where(inside, value, face_ref[i * 3 + k])

        if outer and x == 0:

            @pl.when(g == 0)
            def _():
                for q in range(9):
                    xlo_ref[q, half] = result[q]

        if outer and x == WIDTH - 1:

            @pl.when(g == 1)
            def _():
                for q in range(9):
                    xhi_ref[q, half] = result[18 + q]


def post(tags, landed, part, before):
    shape = jax.ShapeDtypeStruct
    outer = part == 0
    side_y = (9, SUB, LANES)
    side_x = (9, 2, SUB, LANES)
    whole = (NQ, GROUPS * SUB, SUB, LANES)
    spec_y = pl.BlockSpec(side_y, lambda g, *_: (0, 0, 0))
    spec_x = pl.BlockSpec(side_x, lambda g, *_: (0, 0, 0, 0))
    in_specs = [pl.BlockSpec(landed.shape, lambda g, *_: (0, 0, 0, 0))]
    if not outer:
        in_specs.append(pl.BlockSpec(memory_space=pl.ANY))
    return pl.pallas_call(
        functools.partial(post_kernel, outer),
        grid_spec=pltpu.PrefetchScalarGridSpec(
            num_scalar_prefetch=1,
            grid=(len(CHUNKS[part]),),
            in_specs=in_specs,
            out_specs=[
                pl.BlockSpec((NQ, SUB, SUB, LANES), lambda g, *_: (0, quarter(part, g), 0, 0)),
                spec_y, spec_y,
            ]
            + ([spec_x, spec_x] if outer else []),
            scratch_shapes=[
                pltpu.VMEM((NFIELD * SUB * SUB, LANES), jnp.float32),
                pltpu.SMEM((SUB,), jnp.int32),
            ],
        ),
        out_shape=[shape(whole, jnp.float32)]
        + [shape(side_y, jnp.float32)] * 2
        + ([shape(side_x, jnp.float32)] * 2 if outer else []),
        input_output_aliases={} if outer else {2: 0},
        compiler_params=pltpu.CompilerParams(vmem_limit_bytes=VMEM_LIMIT),
        cost_estimate=pl.CostEstimate(flops=10**7, bytes_accessed=3 * 10**6, transcendentals=0),
        name="post_%d" % part,
    )(tags, landed, *(() if outer else (before,)))


def stream_kernel(
    main_ref, prev_ref, next_ref, xlo_ref, xhi_ref, below_0, above_0, below_1, above_1,
    out_ref, below_ref, above_ref,
):
    g = pl.program_id(0)

    @pl.when(g == 0)
    def _():
        for x in range(EDGE):
            inner = WIDTH <= x < EDGE - WIDTH
            spot = x - WIDTH if inner else (x if x < WIDTH else x - 2 * WIDTH)
            for k in range(9):
                packed = (below_1 if inner else below_0)[k]
                below_ref[k, x + 1] = pltpu.roll(packed, (LANES - EDGE - EDGE * spot) % LANES, axis=1)
                packed = (above_1 if inner else above_0)[k]
                above_ref[k, x + 1] = pltpu.roll(packed, (LANES - EDGE * spot) % LANES, axis=1)
        for k in range(3):
            below_ref[6 + k, 0] = xlo_ref[18 + k]
            above_ref[6 + k, 0] = pltpu.roll(xlo_ref[21 + k], EDGE, axis=1)
            below_ref[k, EDGE + 1] = pltpu.roll(xhi_ref[18 + k], LANES - EDGE, axis=1)
            above_ref[k, EDGE + 1] = xhi_ref[21 + k]

    lane = lax.broadcasted_iota(jnp.int32, (SUB, LANES), 1)
    block = lax.broadcasted_iota(jnp.int32, (SUB, LANES), 0)
    along = lane % EDGE
    first_z, last_z = along == 0, along == EDGE - 1
    floor = first_z & (block == 0)
    ceiling = last_z & (block == SUB - 1)
    low_y, high_y = lane < EDGE, lane >= LANES - EDGE

    for x in range(WIDTH):

        def source(q, half):
            at = x - velocity(q)[0]
            if at < 0:
                return jnp.where(g == 0, xlo_ref[(q - 18) * 2 + half], prev_ref[q - 18, half])
            if at >= WIDTH:
                return jnp.where(g == GROUPS - 1, xhi_ref[q * 2 + half], next_ref[q, half])
            return main_ref[q, at * 2 + half]

        for half in range(2):
            c = x * 2 + half
            for q in range(NQ):
                cx, cy, cz = velocity(q)
                a = source(q, half)
                side = g * WIDTH + x - cx + 1
                k = (cx + 1) * 3 + cz + 1
                if cy == 1:
                    a = jnp.where(high_y, below_ref[k, side] if half == 0 else source(q, 0), a)
                elif cy == -1:
                    a = jnp.where(low_y, above_ref[k, side] if half == 1 else source(q, 1), a)
                shift = EDGE * cy + cz
                value = a if shift == 0 else pltpu.roll(a, shift % LANES, axis=1)
                if cz == 1:
                    fill = pltpu.roll(pltpu.roll(a, 1, axis=0), (shift - EDGE) % LANES, axis=1)
                    value = jnp.where(first_z, fill, value)
                    value = jnp.where(floor, main_ref[26 - q, c], value)
                elif cz == -1:
                    fill = pltpu.roll(pltpu.roll(a, SUB - 1, axis=0), (shift + EDGE) % LANES, axis=1)
                    value = jnp.where(last_z, fill, value)
                    value = jnp.where(ceiling, main_ref[26 - q, c], value)
                out_ref[q, :, c * LANES : (c + 1) * LANES] = value


def stream(lattice, xlo, xhi, sides):
    cells = GROUPS * SUB * LANES
    face = (9, 2, SUB, LANES)
    spec_x = pl.BlockSpec(xlo.shape, lambda g: (0, 0, 0))
    spec_y = pl.BlockSpec((9, SUB, LANES), lambda g: (0, 0, 0))
    return pl.pallas_call(
        stream_kernel,
        grid=(GROUPS,),
        in_specs=[
            pl.BlockSpec((NQ, SUB, SUB, LANES), lambda g: (0, g, 0, 0)),
            pl.BlockSpec(face, lambda g: (2, jnp.maximum(WIDTH * g - 1, 0), 0, 0)),
            pl.BlockSpec(face, lambda g: (0, jnp.minimum(WIDTH * g + WIDTH, EDGE - 1), 0, 0)),
            spec_x, spec_x, spec_y, spec_y, spec_y, spec_y,
        ],
        out_specs=pl.BlockSpec((NQ, SUB, SUB * LANES), lambda g: (0, 0, g)),
        out_shape=jax.ShapeDtypeStruct((NQ, SUB, cells), jnp.float32),
        scratch_shapes=[
            pltpu.VMEM((9, EDGE + 2, SUB, LANES), jnp.float32),
            pltpu.VMEM((9, EDGE + 2, SUB, LANES), jnp.float32),
        ],
        compiler_params=pltpu.CompilerParams(vmem_limit_bytes=VMEM_LIMIT),
        cost_estimate=pl.CostEstimate(flops=10**7, bytes_accessed=8 * 10**6, transcendentals=0),
        name="stream",
    )(lattice, lattice, lattice, xlo, xhi, *sides)


def shifted(value, axis, step):
    count = lax.axis_size(axis)
    return lax.ppermute(value, axis, [(i, (i + step) % count) for i in range(count)])


def tags_of(landed):
    return landed[:, -1, 0, 0].astype(jnp.int32)


def on_device(populations, destination, refinement):
    blocks = populations.shape[0]
    row_count = lax.axis_size("row")
    col_count = lax.axis_size("col")
    cap_row = 2 * ((blocks + row_count - 1) // row_count)
    cap_col = 2 * ((blocks + col_count - 1) // col_count)
    swap = functools.partial(lax.all_to_all, split_axis=0, concat_axis=0, tiled=True)
    ordered = jnp.transpose(populations, (1, 0, 2))
    parts = range(len(CHUNKS))
    sent = [
        pre(ordered, destination, refinement, part, row_count, cap_row, blocks * col_count)
        for part in parts
    ]
    in_row = [swap(value, "row") for value in sent]
    tags = tags_of(in_row[0])
    packed = [repack(tags, in_row[part], part, blocks, col_count, cap_col) for part in parts]
    home = [swap(value, "col") for value in packed]
    tags = tags_of(home[0])
    lattice, ylo, yhi, xlo, xhi = post(tags, home[0], 0, None)
    below, above = shifted(yhi, "col", 1), shifted(ylo, "col", -1)
    up = jnp.concatenate([xhi.reshape(18, SUB, LANES), below[6:], above[6:]])
    down = jnp.concatenate([xlo.reshape(18, SUB, LANES), below[:3], above[:3]])
    xlo, xhi = shifted(up, "row", 1), shifted(down, "row", -1)
    lattice, ylo, yhi = post(tags, home[1], 1, lattice)
    sides = (below, above, shifted(yhi, "col", 1), shifted(ylo, "col", -1))
    return jnp.transpose(stream(lattice, xlo, xhi, sides), (1, 0, 2))


def solution(mesh):
    return jax.shard_map(
        on_device,
        mesh=mesh,
        in_specs=(P(("row", "col"), None, None), P(("row", "col")), P(("row", "col"))),
        out_specs=P(("row", "col"), None, None),
        check_vma=False,
    )
```

```python
import functools

import jax
import jax.numpy as jnp
from jax import lax
from jax.experimental import pallas as pl
from jax.experimental.pallas import tpu as pltpu
from jax.sharding import PartitionSpec as P

EDGE = 16
VISCOSITY = 0.01
LANES = 128
SUB = 8
NQ = 27
NFIELD = 9
GROUPS = 4
WIDTH = EDGE // GROUPS
CHUNKS = ((0, 3), (1, 2))
SIDE_TILES = 3
VMEM_LIMIT = 50 * 1024 * 1024


def velocity(q):
    return (q // 9 - 1, (q // 3) % 3 - 1, q % 3 - 1)


def tiles_of(part):
    return len(CHUNKS[part]) * NFIELD + (0 if part else SIDE_TILES)


def raw_moments(f):
    whole, slope, outer = {}, {}, {}
    for i in range(3):
        for j in range(3):
            low, rest, high = (f[i * 9 + j * 3 + k] for k in range(3))
            outer[i, j] = low + high
            whole[i, j] = outer[i, j] + rest
            slope[i, j] = high - low
    column = [whole[i, 0] + whole[i, 1] + whole[i, 2] for i in range(3)]
    tilt = [slope[i, 0] + slope[i, 1] + slope[i, 2] for i in range(3)]
    low_y = whole[0, 0] + whole[1, 0] + whole[2, 0]
    high_y = whole[0, 2] + whole[1, 2] + whole[2, 2]
    ends = column[0] + column[2]
    mzz = sum(outer[i, j] for i in range(3) for j in range(3))
    mxy = (whole[2, 2] - whole[2, 0]) - (whole[0, 2] - whole[0, 0])
    myz = (slope[0, 2] + slope[1, 2] + slope[2, 2]) - (slope[0, 0] + slope[1, 0] + slope[2, 0])
    return (
        ends + column[1],
        column[2] - column[0],
        high_y - low_y,
        tilt[0] + tilt[1] + tilt[2],
        ends,
        low_y + high_y,
        mzz,
        mxy,
        tilt[2] - tilt[0],
        myz,
    )


def collided(f, keep):
    rho, jx, jy, jz, mxx, myy, mzz, mxy, mxz, myz = raw_moments(f)
    inverse = 1.0 / rho
    ux, uy, uz = jx * inverse, jy * inverse, jz * inverse
    kxx = mxx - jx * ux
    return (
        rho, ux, uy, uz,
        keep * (mxy - jx * uy),
        keep * (mxz - jx * uz),
        keep * (myz - jy * uz),
        keep * (kxx - (myy - jy * uy)),
        keep * (kxx - (mzz - jz * uz)),
    )


def pre_kernel(cap, per_row, part, dest_ref, level_ref, x_ref, out_ref, swap_ref, *more):
    g = pl.program_id(0)
    steps = len(CHUNKS[part])
    blocks = x_ref.shape[1]
    chunks = x_ref.shape[2] // LANES
    which = lax.broadcasted_iota(jnp.int32, (SUB, LANES), 0)
    spot = lax.broadcasted_iota(jnp.int32, (SUB, LANES), 1) // EDGE
    scale = jnp.zeros((SUB, LANES), jnp.int32)
    for t in range(blocks):
        scale = jnp.where(which == t, jnp.left_shift(1, level_ref[t]), scale)
    rate = 1.0 / (3.0 * VISCOSITY * scale.astype(jnp.float32) + 0.5)
    keep = 1.0 - rate
    rows = [dest_ref[t] // per_row for t in range(blocks)]
    slots = []
    for t in range(blocks):
        slot = rows[t] * cap
        for other in range(t):
            slot = slot + jnp.where(rows[other] == rows[t], 1, 0)
        slots.append(slot)

    def full():
        for c in range(chunks):
            fields = collided([x_ref[q, :, c * LANES : (c + 1) * LANES] for q in range(NQ)], keep)
            for n, field in enumerate(fields):
                base = (n * chunks + c) * SUB
                swap_ref[base : base + SUB, :] = field
        for t in range(blocks):
            for n in range(NFIELD):
                moved = swap_ref[pl.ds(n * chunks * SUB + t, SUB, stride=SUB), :]
                out_ref[slots[t], g * NFIELD + n] = moved

    if part == 1:
        full()
        return
    pl.when(g < steps)(full)
    packed_ref, side_ref = more

    def pack(step):
        first_x = CHUNKS[1][step] * WIDTH
        for q in range(NQ):
            for half in range(2):
                value = packed_ref[half * NQ + q] if step else None
                for x in range(WIDTH):
                    c = x * 2 + half
                    at = (first_x + x) % SUB
                    moved = x_ref[q, :, c * LANES : (c + 1) * LANES]
                    turn = (at + half) * EDGE % LANES
                    if turn:
                        moved = pltpu.roll(moved, turn, axis=1)
                    value = moved if value is None else jnp.where(spot == at, moved, value)
                packed_ref[half * NQ + q] = value

    for step in range(len(CHUNKS[1])):
        pl.when(g == steps + step)(functools.partial(pack, step))

    @pl.when(g == pl.num_programs(0) - 1)
    def _():
        tag = jnp.zeros((SUB, LANES), jnp.int32)
        for t in range(blocks):
            tag = jnp.where(which == t, dest_ref[t], tag)
        tag = tag.astype(jnp.float32)
        for half in range(2):
            fields = collided([packed_ref[half * NQ + q] for q in range(NQ)], keep)
            for n, field in enumerate(fields):
                base = (half * NFIELD + n) * SUB
                side_ref[base : base + SUB, :] = field
        for row in range(2 * NFIELD, SIDE_TILES * SUB):
            side_ref[row * SUB : (row + 1) * SUB, :] = tag
        first = steps * NFIELD
        for slot in range(out_ref.shape[0]):
            out_ref[slot, first + SIDE_TILES - 1] = jnp.full((SUB, LANES), -1.0, jnp.float32)
        for t in range(blocks):
            for tile in range(SIDE_TILES):
                moved = side_ref[pl.ds(tile * SUB * SUB + t, SUB, stride=SUB), :]
                out_ref[slots[t], first + tile] = moved


def pre(populations, destination, refinement, part, row_count, cap, per_row):
    blocks = populations.shape[1]
    cells = populations.shape[2] // GROUPS
    order = CHUNKS[1] if part else CHUNKS[0] + CHUNKS[1]
    shape = (row_count * cap, tiles_of(part), SUB, LANES)

    def place(g, *_):
        index = order[-1]
        for step in range(len(order) - 1):
            index = jnp.where(g == step, order[step], index)
        return (0, 0, index)

    scratch = [pltpu.VMEM((NFIELD * cells // LANES * SUB, LANES), jnp.float32)]
    if part == 0:
        scratch += [
            pltpu.VMEM((2 * NQ, SUB, LANES), jnp.float32),
            pltpu.VMEM((SIDE_TILES * SUB * SUB, LANES), jnp.float32),
        ]
    return pl.pallas_call(
        functools.partial(pre_kernel, cap, per_row, part),
        grid_spec=pltpu.PrefetchScalarGridSpec(
            num_scalar_prefetch=2,
            grid=(len(order),),
            in_specs=[pl.BlockSpec((NQ, blocks, cells), place)],
            out_specs=pl.BlockSpec(shape, lambda g, *_: (0, 0, 0, 0)),
            scratch_shapes=scratch,
        ),
        out_shape=jax.ShapeDtypeStruct(shape, jnp.float32),
        compiler_params=pltpu.CompilerParams(vmem_limit_bytes=VMEM_LIMIT),
        cost_estimate=pl.CostEstimate(flops=10**7, bytes_accessed=4 * 10**6, transcendentals=0),
        name="pre_%d" % part,
    )(destination, refinement, populations)


def repack_kernel(cap, col_count, tagged, away_ref, in_ref, *refs):
    outs, (source_ref, count_ref) = refs[:col_count], refs[col_count:]
    for d in range(col_count):
        count_ref[d] = 0
        for k in range(cap):
            source_ref[d * cap + k] = -1
    for slot in range(in_ref.shape[0]):

        @pl.when(away_ref[slot] >= 0)
        def _():
            d = away_ref[slot]
            k = count_ref[d]
            count_ref[d] = k + 1
            source_ref[d * cap + k] = slot

    for d in range(col_count):
        for k in range(cap):
            slot = source_ref[d * cap + k]

            @pl.when(slot >= 0)
            def _():
                outs[d][k] = in_ref[slot]

            if tagged:

                @pl.when(slot < 0)
                def _():
                    outs[d][k, in_ref.shape[1] - 1] = jnp.full((SUB, LANES), -1.0, jnp.float32)


def repack(away, landed, part, col_count, cap):
    out = jax.ShapeDtypeStruct((cap,) + landed.shape[1:], jnp.float32)
    return pl.pallas_call(
        functools.partial(repack_kernel, cap, col_count, part == 0),
        in_specs=[pl.BlockSpec(memory_space=pltpu.SMEM), pl.BlockSpec(memory_space=pltpu.VMEM)],
        out_specs=[pl.BlockSpec(memory_space=pltpu.VMEM)] * col_count,
        scratch_shapes=[
            pltpu.SMEM((col_count * cap,), jnp.int32),
            pltpu.SMEM((col_count,), jnp.int32),
        ],
        out_shape=[out] * col_count,
        compiler_params=pltpu.CompilerParams(vmem_limit_bytes=VMEM_LIMIT),
        cost_estimate=pl.CostEstimate(flops=0, bytes_accessed=3 * 10**6, transcendentals=0),
        name="repack_%d" % part,
    )(away, landed)


def backward(zeroth, first, second, u):
    raw_one, raw_two = first, second
    if zeroth is not None:
        moved = u * zeroth
        raw_one = moved if raw_one is None else raw_one + moved
        square = u * moved
        raw_two = square if raw_two is None else raw_two + square
    if first is not None:
        cross = (u + u) * first
        raw_two = cross if raw_two is None else raw_two + cross
    rest = -raw_two if zeroth is None else zeroth - raw_two
    return 0.5 * (raw_two - raw_one), rest, 0.5 * (raw_one + raw_two)


def post_populations(rho, ux, uy, uz, pxy, pxz, pyz, dev_one, dev_two):
    inverse = 1.0 / rho
    pxx = (rho + dev_one + dev_two) * (1.0 / 3.0)
    pyy = pxx - dev_one
    pzz = pxx - dev_two
    sxy, sxz, syz = pxy * inverse, pxz * inverse, pyz * inverse
    syy, szz = pyy * inverse, pzz * inverse
    central = {
        (0, 0, 0): rho, (2, 0, 0): pxx, (0, 2, 0): pyy, (0, 0, 2): pzz,
        (1, 1, 0): pxy, (1, 0, 1): pxz, (0, 1, 1): pyz,
        (2, 2, 0): pxx * syy + 2.0 * pxy * sxy,
        (2, 0, 2): pxx * szz + 2.0 * pxz * sxz,
        (0, 2, 2): pyy * szz + 2.0 * pyz * syz,
        (2, 1, 1): pxx * syz + 2.0 * pxy * sxz,
        (1, 2, 1): pyy * sxz + 2.0 * pxy * syz,
        (1, 1, 2): pzz * sxy + 2.0 * pxz * syz,
        (2, 2, 2): pxx * syy * szz
        + 2.0 * (pxx * syz * syz + pyy * sxz * sxz + pzz * sxy * sxy)
        + 8.0 * pxy * sxz * syz,
    }
    along_z = {}
    for a in range(3):
        for b in range(3):
            parts = backward(*(central.get((a, b, c)) for c in range(3)), uz)
            for k in range(3):
                along_z[a, b, k] = parts[k]
    along_y = {}
    for a in range(3):
        for k in range(3):
            parts = backward(*(along_z[a, b, k] for b in range(3)), uy)
            for j in range(3):
                along_y[a, j, k] = parts[j]
    result = [None] * NQ
    for j in range(3):
        for k in range(3):
            parts = backward(*(along_y[a, j, k] for a in range(3)), ux)
            for i in range(3):
                result[i * 9 + j * 3 + k] = parts[i]
    return result


def unload(tags_ref, ins, block_ref):
    cap = ins[0].shape[0]
    for d, in_ref in enumerate(ins):
        for k in range(cap):
            tag = tags_ref[d * cap + k]

            @pl.when(tag >= 0)
            def _():
                block_ref[tag % SUB] = in_ref[k]


def side_spot(lane, x):
    return (lane // EDGE) == x % SUB


def post_kernel(count, tags_ref, *refs):
    ins = refs[:count]
    post_ref, ylo_ref, yhi_ref, xlo_ref, xhi_ref, block_ref, swap_ref, side_ref = refs[count:]
    g = pl.program_id(0)
    steps = len(CHUNKS[0])
    lane = lax.broadcasted_iota(jnp.int32, (SUB, LANES), 1)

    @pl.when(g == 0)
    def _():
        unload(tags_ref, ins, block_ref)
        for t in range(SUB):
            for tile in range(SIDE_TILES):
                side_ref[pl.ds(tile * SUB * SUB + t, SUB, stride=SUB), :] = block_ref[
                    t, steps * NFIELD + tile
                ]
        for half in range(2):
            fields = [
                side_ref[(half * NFIELD + n) * SUB : (half * NFIELD + n + 1) * SUB, :]
                for n in range(NFIELD)
            ]
            result = post_populations(*fields)
            for i in range(3):
                for k in range(3):
                    value = result[i * 9 + 6 * half + k]
                    for tile in range(2):
                        (yhi_ref if half else ylo_ref)[i * 3 + k, tile] = value

    for t in range(SUB):
        for n in range(NFIELD):
            swap_ref[pl.ds(n * SUB * SUB + t, SUB, stride=SUB), :] = block_ref[t, g * NFIELD + n]
    group = CHUNKS[0][0]
    for step in range(1, steps):
        group = jnp.where(g == step, CHUNKS[0][step], group)
    for c in range(SUB):
        fields = [swap_ref[(n * SUB + c) * SUB : (n * SUB + c + 1) * SUB, :] for n in range(NFIELD)]
        result = post_populations(*fields)
        for q in range(NQ):
            post_ref[q, c] = result[q]
        x_in, half = c // 2, c % 2
        x = group * WIDTH + x_in
        inside = side_spot(lane, x)
        face_ref, first, shift = ((ylo_ref, 0, 0), (yhi_ref, 6, EDGE))[half]
        turn = ((x % SUB) * EDGE + shift) % LANES
        for i in range(3):
            for k in range(3):
                value = pltpu.roll(result[i * 9 + first + k], turn, axis=1)
                at = (i * 3 + k, x // SUB)
                face_ref[at] = jnp.where(inside, value, face_ref[at])

        if x_in == 0:

            @pl.when(group == 0)
            def _():
                for q in range(9):
                    xlo_ref[q, half] = result[q]

        if x_in == WIDTH - 1:

            @pl.when(group == GROUPS - 1)
            def _():
                for q in range(9):
                    xhi_ref[q, half] = result[18 + q]


def post(tags, homes):
    shape = jax.ShapeDtypeStruct
    face = (9, 2, SUB, LANES)
    steps = len(CHUNKS[0])
    spec = pl.BlockSpec(face, lambda g, *_: (0, 0, 0, 0))
    return pl.pallas_call(
        functools.partial(post_kernel, len(homes)),
        grid_spec=pltpu.PrefetchScalarGridSpec(
            num_scalar_prefetch=1,
            grid=(steps,),
            in_specs=[pl.BlockSpec(homes[0].shape, lambda g, *_: (0, 0, 0, 0))] * len(homes),
            out_specs=[pl.BlockSpec((NQ, SUB, SUB, LANES), lambda g, *_: (0, g, 0, 0))] + [spec] * 4,
            scratch_shapes=[
                pltpu.VMEM((SUB, tiles_of(0), SUB, LANES), jnp.float32),
                pltpu.VMEM((NFIELD * SUB * SUB, LANES), jnp.float32),
                pltpu.VMEM((SIDE_TILES * SUB * SUB, LANES), jnp.float32),
            ],
        ),
        out_shape=[shape((NQ, steps * SUB, SUB, LANES), jnp.float32)]
        + [shape(face, jnp.float32)] * 4,
        compiler_params=pltpu.CompilerParams(vmem_limit_bytes=VMEM_LIMIT),
        cost_estimate=pl.CostEstimate(flops=10**7, bytes_accessed=3 * 10**6, transcendentals=0),
        name="post",
    )(tags, *homes)


def finish_kernel(count, tags_ref, *refs):
    ins = refs[:count]
    (
        early_ref, xlo_ref, xhi_ref, below_in, above_in,
        out_ref, main_ref, below_ref, above_ref, block_ref, swap_ref, sems,
    ) = refs[count:]
    g = pl.program_id(0)

    @pl.when(g == 0)
    def _():
        copies = [
            pltpu.make_async_copy(
                early_ref.at[:, pl.ds(step * SUB, SUB)],
                main_ref.at[:, pl.ds(group * SUB, SUB)],
                sems.at[step],
            )
            for step, group in enumerate(CHUNKS[0])
        ]
        for copy in copies:
            copy.start()
        unload(tags_ref, ins, block_ref)
        for step, group in enumerate(CHUNKS[1]):
            for t in range(SUB):
                for n in range(NFIELD):
                    swap_ref[pl.ds(n * SUB * SUB + t, SUB, stride=SUB), :] = block_ref[
                        t, step * NFIELD + n
                    ]
            for c in range(SUB):
                fields = [
                    swap_ref[(n * SUB + c) * SUB : (n * SUB + c + 1) * SUB, :] for n in range(NFIELD)
                ]
                for q, value in enumerate(post_populations(*fields)):
                    main_ref[q, group * SUB + c] = value
        for x in range(EDGE):
            at = x % SUB
            for k in range(9):
                packed = below_in[k, x // SUB]
                below_ref[k, x + 1] = pltpu.roll(packed, (LANES - EDGE - EDGE * at) % LANES, axis=1)
                packed = above_in[k, x // SUB]
                above_ref[k, x + 1] = pltpu.roll(packed, (LANES - EDGE * at) % LANES, axis=1)
        for k in range(3):
            below_ref[6 + k, 0] = xlo_ref[18 + k]
            above_ref[6 + k, 0] = pltpu.roll(xlo_ref[21 + k], EDGE, axis=1)
            below_ref[k, EDGE + 1] = pltpu.roll(xhi_ref[18 + k], LANES - EDGE, axis=1)
            above_ref[k, EDGE + 1] = xhi_ref[21 + k]
        for copy in copies:
            copy.wait()

    lane = lax.broadcasted_iota(jnp.int32, (SUB, LANES), 1)
    block = lax.broadcasted_iota(jnp.int32, (SUB, LANES), 0)
    along = lane % EDGE
    first_z, last_z = along == 0, along == EDGE - 1
    floor = first_z & (block == 0)
    ceiling = last_z & (block == SUB - 1)
    low_y, high_y = lane < EDGE, lane >= LANES - EDGE

    for x in range(WIDTH):

        def source(q, half):
            at = x - velocity(q)[0]
            row = (g * WIDTH + at) * 2 + half
            if at < 0:
                inside = main_ref[q, jnp.maximum(row, 0)]
                return jnp.where(g == 0, xlo_ref[(q - 18) * 2 + half], inside)
            if at >= WIDTH:
                inside = main_ref[q, jnp.minimum(row, GROUPS * SUB - 1)]
                return jnp.where(g == GROUPS - 1, xhi_ref[q * 2 + half], inside)
            return main_ref[q, row]

        for half in range(2):
            c = x * 2 + half
            for q in range(NQ):
                cx, cy, cz = velocity(q)
                a = source(q, half)
                side = g * WIDTH + x - cx + 1
                k = (cx + 1) * 3 + cz + 1
                if cy == 1:
                    a = jnp.where(high_y, below_ref[k, side] if half == 0 else source(q, 0), a)
                elif cy == -1:
                    a = jnp.where(low_y, above_ref[k, side] if half == 1 else source(q, 1), a)
                shift = EDGE * cy + cz
                value = a if shift == 0 else pltpu.roll(a, shift % LANES, axis=1)
                if cz == 1:
                    fill = pltpu.roll(pltpu.roll(a, 1, axis=0), (shift - EDGE) % LANES, axis=1)
                    value = jnp.where(first_z, fill, value)
                    value = jnp.where(floor, main_ref[26 - q, g * SUB + c], value)
                elif cz == -1:
                    fill = pltpu.roll(pltpu.roll(a, SUB - 1, axis=0), (shift + EDGE) % LANES, axis=1)
                    value = jnp.where(last_z, fill, value)
                    value = jnp.where(ceiling, main_ref[26 - q, g * SUB + c], value)
                out_ref[q, :, c * LANES : (c + 1) * LANES] = value


def finish(tags, homes, early, xlo, xhi, below, above):
    def whole(value):
        rank = len(value.shape)
        return pl.BlockSpec(value.shape, lambda g, *_: (0,) * rank)

    return pl.pallas_call(
        functools.partial(finish_kernel, len(homes)),
        grid_spec=pltpu.PrefetchScalarGridSpec(
            num_scalar_prefetch=1,
            grid=(GROUPS,),
            in_specs=[whole(value) for value in homes]
            + [pl.BlockSpec(memory_space=pl.ANY)]
            + [whole(value) for value in (xlo, xhi, below, above)],
            out_specs=pl.BlockSpec((NQ, SUB, SUB * LANES), lambda g, *_: (0, 0, g)),
            scratch_shapes=[
                pltpu.VMEM((NQ, GROUPS * SUB, SUB, LANES), jnp.float32),
                pltpu.VMEM((9, EDGE + 2, SUB, LANES), jnp.float32),
                pltpu.VMEM((9, EDGE + 2, SUB, LANES), jnp.float32),
                pltpu.VMEM((SUB, tiles_of(1), SUB, LANES), jnp.float32),
                pltpu.VMEM((NFIELD * SUB * SUB, LANES), jnp.float32),
                pltpu.SemaphoreType.DMA((len(CHUNKS[0]),)),
            ],
        ),
        out_shape=jax.ShapeDtypeStruct((NQ, SUB, GROUPS * SUB * LANES), jnp.float32),
        compiler_params=pltpu.CompilerParams(vmem_limit_bytes=VMEM_LIMIT),
        cost_estimate=pl.CostEstimate(flops=10**7, bytes_accessed=8 * 10**6, transcendentals=0),
        name="finish",
    )(tags, *homes, early, xlo, xhi, below, above)


def shifted(value, axis, step):
    count = lax.axis_size(axis)
    return lax.ppermute(value, axis, [(i, (i + step) % count) for i in range(count)])


def tags_of(landed):
    return landed[:, -1, 2 * NFIELD - (SIDE_TILES - 1) * SUB, 0].astype(jnp.int32)


def on_device(populations, destination, refinement):
    blocks = populations.shape[0]
    row_count = lax.axis_size("row")
    col_count = lax.axis_size("col")
    cap_row = 2 * ((blocks + row_count - 1) // row_count)
    cap_col = 2 * ((blocks + col_count - 1) // col_count)
    ordered = jnp.transpose(populations, (1, 0, 2))
    in_row = [
        lax.all_to_all(
            pre(ordered, destination, refinement, part, row_count, cap_row, blocks * col_count),
            "row", split_axis=0, concat_axis=0, tiled=True,
        )
        for part in range(2)
    ]
    tags = tags_of(in_row[0])
    away = jnp.where(tags >= 0, (tags // blocks - lax.axis_index("col")) % col_count, -1)

    def to_columns(part):
        packed = repack(away, in_row[part], part, col_count, cap_col)
        return [packed[d] if d == 0 else shifted(packed[d], "col", d) for d in range(col_count)]

    homes = to_columns(0)
    tags = jnp.concatenate([tags_of(value) for value in homes])
    early, ylo, yhi, xlo, xhi = post(tags, homes)
    below, above = shifted(yhi, "col", 1), shifted(ylo, "col", -1)
    up = jnp.concatenate([xhi.reshape(18, SUB, LANES), below[6:, 1], above[6:, 1]])
    down = jnp.concatenate([xlo.reshape(18, SUB, LANES), below[:3, 0], above[:3, 0]])
    xlo, xhi = shifted(up, "row", 1), shifted(down, "row", -1)
    homes = to_columns(1)
    return jnp.transpose(finish(tags, homes, early, xlo, xhi, below, above), (1, 0, 2))


def solution(mesh):
    return jax.shard_map(
        on_device,
        mesh=mesh,
        in_specs=(P(("row", "col"), None, None), P(("row", "col")), P(("row", "col"))),
        out_specs=P(("row", "col"), None, None),
        check_vma=False,
    )
```

```python
import functools

import jax
import jax.numpy as jnp
from jax import lax
from jax.experimental import pallas as pl
from jax.experimental.pallas import tpu as pltpu
from jax.sharding import PartitionSpec as P

EDGE = 16
VISCOSITY = 0.01
LANES = 128
SUB = 8
NQ = 27
NFIELD = 9
GROUPS = 4
WIDTH = EDGE // GROUPS
CHUNKS = ((0, 3), (1, 2))
SIDE_TILES = 3
VMEM_LIMIT = 20 * 1024 * 1024


def velocity(q):
    return (q // 9 - 1, (q // 3) % 3 - 1, q % 3 - 1)


def tiles_of(part):
    return len(CHUNKS[part]) * NFIELD + (0 if part else SIDE_TILES)


def raw_moments(f):
    whole, slope, outer = {}, {}, {}
    for i in range(3):
        for j in range(3):
            low, rest, high = (f[i * 9 + j * 3 + k] for k in range(3))
            outer[i, j] = low + high
            whole[i, j] = outer[i, j] + rest
            slope[i, j] = high - low
    column = [whole[i, 0] + whole[i, 1] + whole[i, 2] for i in range(3)]
    tilt = [slope[i, 0] + slope[i, 1] + slope[i, 2] for i in range(3)]
    low_y = whole[0, 0] + whole[1, 0] + whole[2, 0]
    high_y = whole[0, 2] + whole[1, 2] + whole[2, 2]
    ends = column[0] + column[2]
    mzz = sum(outer[i, j] for i in range(3) for j in range(3))
    mxy = (whole[2, 2] - whole[2, 0]) - (whole[0, 2] - whole[0, 0])
    myz = (slope[0, 2] + slope[1, 2] + slope[2, 2]) - (slope[0, 0] + slope[1, 0] + slope[2, 0])
    return (
        ends + column[1],
        column[2] - column[0],
        high_y - low_y,
        tilt[0] + tilt[1] + tilt[2],
        ends,
        low_y + high_y,
        mzz,
        mxy,
        tilt[2] - tilt[0],
        myz,
    )


def collided(f, keep):
    rho, jx, jy, jz, mxx, myy, mzz, mxy, mxz, myz = raw_moments(f)
    inverse = 1.0 / rho
    ux, uy, uz = jx * inverse, jy * inverse, jz * inverse
    kxx = mxx - jx * ux
    return (
        rho, ux, uy, uz,
        keep * (mxy - jx * uy),
        keep * (mxz - jx * uz),
        keep * (myz - jy * uz),
        keep * (kxx - (myy - jy * uy)),
        keep * (kxx - (mzz - jz * uz)),
    )


def pre_kernel(cap, per_row, part, dest_ref, level_ref, x_ref, out_ref, swap_ref, *more):
    g = pl.program_id(0)
    steps = len(CHUNKS[part])
    blocks = x_ref.shape[1]
    chunks = x_ref.shape[2] // LANES
    which = lax.broadcasted_iota(jnp.int32, (SUB, LANES), 0)
    spot = lax.broadcasted_iota(jnp.int32, (SUB, LANES), 1) // EDGE
    scale = jnp.zeros((SUB, LANES), jnp.int32)
    for t in range(blocks):
        scale = jnp.where(which == t, jnp.left_shift(1, level_ref[t]), scale)
    rate = 1.0 / (3.0 * VISCOSITY * scale.astype(jnp.float32) + 0.5)
    keep = 1.0 - rate
    rows = [dest_ref[t] // per_row for t in range(blocks)]
    slots = []
    for t in range(blocks):
        slot = rows[t] * cap
        for other in range(t):
            slot = slot + jnp.where(rows[other] == rows[t], 1, 0)
        slots.append(slot)

    def full():
        for c in range(chunks):
            fields = collided([x_ref[q, :, c * LANES : (c + 1) * LANES] for q in range(NQ)], keep)
            for n, field in enumerate(fields):
                base = (n * chunks + c) * SUB
                swap_ref[base : base + SUB, :] = field
        for t in range(blocks):
            for n in range(NFIELD):
                moved = swap_ref[pl.ds(n * chunks * SUB + t, SUB, stride=SUB), :]
                out_ref[slots[t], g * NFIELD + n] = moved

    if part == 1:
        full()
        return
    pl.when(g < steps)(full)
    packed_ref, side_ref = more

    def pack(step):
        first_x = CHUNKS[1][step] * WIDTH
        for q in range(NQ):
            for half in range(2):
                value = packed_ref[half * NQ + q] if step else None
                for x in range(WIDTH):
                    c = x * 2 + half
                    at = (first_x + x) % SUB
                    moved = x_ref[q, :, c * LANES : (c + 1) * LANES]
                    turn = (at + half) * EDGE % LANES
                    if turn:
                        moved = pltpu.roll(moved, turn, axis=1)
                    value = moved if value is None else jnp.where(spot == at, moved, value)
                packed_ref[half * NQ + q] = value

    for step in range(len(CHUNKS[1])):
        pl.when(g == steps + step)(functools.partial(pack, step))

    @pl.when(g == pl.num_programs(0) - 1)
    def _():
        tag = jnp.zeros((SUB, LANES), jnp.int32)
        for t in range(blocks):
            tag = jnp.where(which == t, dest_ref[t], tag)
        tag = tag.astype(jnp.float32)
        for half in range(2):
            fields = collided([packed_ref[half * NQ + q] for q in range(NQ)], keep)
            for n, field in enumerate(fields):
                base = (half * NFIELD + n) * SUB
                side_ref[base : base + SUB, :] = field
        for row in range(2 * NFIELD, SIDE_TILES * SUB):
            side_ref[row * SUB : (row + 1) * SUB, :] = tag
        first = steps * NFIELD
        for slot in range(out_ref.shape[0]):
            out_ref[slot, first + SIDE_TILES - 1] = jnp.full((SUB, LANES), -1.0, jnp.float32)
        for t in range(blocks):
            for tile in range(SIDE_TILES):
                moved = side_ref[pl.ds(tile * SUB * SUB + t, SUB, stride=SUB), :]
                out_ref[slots[t], first + tile] = moved


def pre(populations, destination, refinement, part, row_count, cap, per_row):
    blocks = populations.shape[1]
    cells = populations.shape[2] // GROUPS
    order = CHUNKS[1] if part else CHUNKS[0] + CHUNKS[1]
    shape = (row_count * cap, tiles_of(part), SUB, LANES)

    def place(g, *_):
        index = order[-1]
        for step in range(len(order) - 1):
            index = jnp.where(g == step, order[step], index)
        return (0, 0, index)

    scratch = [pltpu.VMEM((NFIELD * cells // LANES * SUB, LANES), jnp.float32)]
    if part == 0:
        scratch += [
            pltpu.VMEM((2 * NQ, SUB, LANES), jnp.float32),
            pltpu.VMEM((SIDE_TILES * SUB * SUB, LANES), jnp.float32),
        ]
    return pl.pallas_call(
        functools.partial(pre_kernel, cap, per_row, part),
        grid_spec=pltpu.PrefetchScalarGridSpec(
            num_scalar_prefetch=2,
            grid=(len(order),),
            in_specs=[pl.BlockSpec((NQ, blocks, cells), place)],
            out_specs=pl.BlockSpec(shape, lambda g, *_: (0, 0, 0, 0)),
            scratch_shapes=scratch,
        ),
        out_shape=jax.ShapeDtypeStruct(shape, jnp.float32),
        compiler_params=pltpu.CompilerParams(vmem_limit_bytes=VMEM_LIMIT),
        cost_estimate=pl.CostEstimate(flops=10**7, bytes_accessed=4 * 10**6, transcendentals=0),
        name="pre_%d" % part,
    )(destination, refinement, populations)


def repack_kernel(cap, col_count, tagged, away_ref, in_ref, *refs):
    outs, (source_ref, count_ref) = refs[:col_count], refs[col_count:]
    for d in range(col_count):
        count_ref[d] = 0
        for k in range(cap):
            source_ref[d * cap + k] = -1
    for slot in range(in_ref.shape[0]):

        @pl.when(away_ref[slot] >= 0)
        def _():
            d = away_ref[slot]
            k = count_ref[d]
            count_ref[d] = k + 1
            source_ref[d * cap + k] = slot

    for d in range(col_count):
        for k in range(cap):
            slot = source_ref[d * cap + k]

            @pl.when(slot >= 0)
            def _():
                outs[d][k] = in_ref[slot]

            if tagged:

                @pl.when(slot < 0)
                def _():
                    outs[d][k, in_ref.shape[1] - 1] = jnp.full((SUB, LANES), -1.0, jnp.float32)


def repack(away, landed, part, col_count, cap):
    out = jax.ShapeDtypeStruct((cap,) + landed.shape[1:], jnp.float32)
    return pl.pallas_call(
        functools.partial(repack_kernel, cap, col_count, part == 0),
        in_specs=[pl.BlockSpec(memory_space=pltpu.SMEM), pl.BlockSpec(memory_space=pltpu.VMEM)],
        out_specs=[pl.BlockSpec(memory_space=pltpu.VMEM)] * col_count,
        scratch_shapes=[
            pltpu.SMEM((col_count * cap,), jnp.int32),
            pltpu.SMEM((col_count,), jnp.int32),
        ],
        out_shape=[out] * col_count,
        compiler_params=pltpu.CompilerParams(vmem_limit_bytes=VMEM_LIMIT),
        cost_estimate=pl.CostEstimate(flops=0, bytes_accessed=3 * 10**6, transcendentals=0),
        name="repack_%d" % part,
    )(away, landed)


def backward(zeroth, first, second, u):
    raw_one, raw_two = first, second
    if zeroth is not None:
        moved = u * zeroth
        raw_one = moved if raw_one is None else raw_one + moved
        square = u * moved
        raw_two = square if raw_two is None else raw_two + square
    if first is not None:
        cross = (u + u) * first
        raw_two = cross if raw_two is None else raw_two + cross
    rest = -raw_two if zeroth is None else zeroth - raw_two
    return 0.5 * (raw_two - raw_one), rest, 0.5 * (raw_one + raw_two)


def post_populations(rho, ux, uy, uz, pxy, pxz, pyz, dev_one, dev_two):
    inverse = 1.0 / rho
    pxx = (rho + dev_one + dev_two) * (1.0 / 3.0)
    pyy = pxx - dev_one
    pzz = pxx - dev_two
    sxy, sxz, syz = pxy * inverse, pxz * inverse, pyz * inverse
    syy, szz = pyy * inverse, pzz * inverse
    central = {
        (0, 0, 0): rho, (2, 0, 0): pxx, (0, 2, 0): pyy, (0, 0, 2): pzz,
        (1, 1, 0): pxy, (1, 0, 1): pxz, (0, 1, 1): pyz,
        (2, 2, 0): pxx * syy + 2.0 * pxy * sxy,
        (2, 0, 2): pxx * szz + 2.0 * pxz * sxz,
        (0, 2, 2): pyy * szz + 2.0 * pyz * syz,
        (2, 1, 1): pxx * syz + 2.0 * pxy * sxz,
        (1, 2, 1): pyy * sxz + 2.0 * pxy * syz,
        (1, 1, 2): pzz * sxy + 2.0 * pxz * syz,
        (2, 2, 2): pxx * syy * szz
        + 2.0 * (pxx * syz * syz + pyy * sxz * sxz + pzz * sxy * sxy)
        + 8.0 * pxy * sxz * syz,
    }
    along_z = {}
    for a in range(3):
        for b in range(3):
            parts = backward(*(central.get((a, b, c)) for c in range(3)), uz)
            for k in range(3):
                along_z[a, b, k] = parts[k]
    along_y = {}
    for a in range(3):
        for k in range(3):
            parts = backward(*(along_z[a, b, k] for b in range(3)), uy)
            for j in range(3):
                along_y[a, j, k] = parts[j]
    result = [None] * NQ
    for j in range(3):
        for k in range(3):
            parts = backward(*(along_y[a, j, k] for a in range(3)), ux)
            for i in range(3):
                result[i * 9 + j * 3 + k] = parts[i]
    return result


def unload(tags_ref, ins, block_ref):
    cap = ins[0].shape[0]
    for d, in_ref in enumerate(ins):
        for k in range(cap):
            tag = tags_ref[d * cap + k]

            @pl.when(tag >= 0)
            def _():
                block_ref[tag % SUB] = in_ref[k]


def side_spot(lane, x):
    return (lane // EDGE) == x % SUB


def post_kernel(count, tags_ref, *refs):
    ins = refs[:count]
    post_ref, ylo_ref, yhi_ref, xlo_ref, xhi_ref, block_ref, swap_ref, side_ref = refs[count:]
    g = pl.program_id(0)
    steps = len(CHUNKS[0])
    lane = lax.broadcasted_iota(jnp.int32, (SUB, LANES), 1)

    @pl.when(g == 0)
    def _():
        unload(tags_ref, ins, block_ref)
        for t in range(SUB):
            for tile in range(SIDE_TILES):
                side_ref[pl.ds(tile * SUB * SUB + t, SUB, stride=SUB), :] = block_ref[
                    t, steps * NFIELD + tile
                ]
        for half in range(2):
            fields = [
                side_ref[(half * NFIELD + n) * SUB : (half * NFIELD + n + 1) * SUB, :]
                for n in range(NFIELD)
            ]
            result = post_populations(*fields)
            for i in range(3):
                for k in range(3):
                    value = result[i * 9 + 6 * half + k]
                    for tile in range(2):
                        (yhi_ref if half else ylo_ref)[i * 3 + k, tile] = value

    for t in range(SUB):
        for n in range(NFIELD):
            swap_ref[pl.ds(n * SUB * SUB + t, SUB, stride=SUB), :] = block_ref[t, g * NFIELD + n]
    group = CHUNKS[0][0]
    for step in range(1, steps):
        group = jnp.where(g == step, CHUNKS[0][step], group)
    for c in range(SUB):
        fields = [swap_ref[(n * SUB + c) * SUB : (n * SUB + c + 1) * SUB, :] for n in range(NFIELD)]
        result = post_populations(*fields)
        for q in range(NQ):
            post_ref[q, c] = result[q]
        x_in, half = c // 2, c % 2
        x = group * WIDTH + x_in
        inside = side_spot(lane, x)
        face_ref, first, shift = ((ylo_ref, 0, 0), (yhi_ref, 6, EDGE))[half]
        turn = ((x % SUB) * EDGE + shift) % LANES
        for i in range(3):
            for k in range(3):
                value = pltpu.roll(result[i * 9 + first + k], turn, axis=1)
                at = (i * 3 + k, x // SUB)
                face_ref[at] = jnp.where(inside, value, face_ref[at])

        if x_in == 0:

            @pl.when(group == 0)
            def _():
                for q in range(9):
                    xlo_ref[q, half] = result[q]

        if x_in == WIDTH - 1:

            @pl.when(group == GROUPS - 1)
            def _():
                for q in range(9):
                    xhi_ref[q, half] = result[18 + q]


def post(tags, homes):
    shape = jax.ShapeDtypeStruct
    face = (9, 2, SUB, LANES)
    steps = len(CHUNKS[0])
    spec = pl.BlockSpec(face, lambda g, *_: (0, 0, 0, 0))
    return pl.pallas_call(
        functools.partial(post_kernel, len(homes)),
        grid_spec=pltpu.PrefetchScalarGridSpec(
            num_scalar_prefetch=1,
            grid=(steps,),
            in_specs=[pl.BlockSpec(homes[0].shape, lambda g, *_: (0, 0, 0, 0))] * len(homes),
            out_specs=[pl.BlockSpec((NQ, SUB, SUB, LANES), lambda g, *_: (0, g, 0, 0))] + [spec] * 4,
            scratch_shapes=[
                pltpu.VMEM((SUB, tiles_of(0), SUB, LANES), jnp.float32),
                pltpu.VMEM((NFIELD * SUB * SUB, LANES), jnp.float32),
                pltpu.VMEM((SIDE_TILES * SUB * SUB, LANES), jnp.float32),
            ],
        ),
        out_shape=[shape((NQ, steps * SUB, SUB, LANES), jnp.float32)]
        + [shape(face, jnp.float32)] * 4,
        compiler_params=pltpu.CompilerParams(vmem_limit_bytes=VMEM_LIMIT),
        cost_estimate=pl.CostEstimate(flops=10**7, bytes_accessed=3 * 10**6, transcendentals=0),
        name="post",
    )(tags, *homes)


def finish_kernel(count, tags_ref, *refs):
    ins = refs[:count]
    (
        early_ref, xlo_ref, xhi_ref, below_in, above_in,
        out_ref, main_ref, below_ref, above_ref, block_ref, swap_ref, sems,
    ) = refs[count:]
    g = pl.program_id(0)

    @pl.when(g == 0)
    def _():
        copies = [
            pltpu.make_async_copy(
                early_ref.at[:, pl.ds(step * SUB, SUB)],
                main_ref.at[:, pl.ds(group * SUB, SUB)],
                sems.at[step],
            )
            for step, group in enumerate(CHUNKS[0])
        ]
        for copy in copies:
            copy.start()
        unload(tags_ref, ins, block_ref)
        for step, group in enumerate(CHUNKS[1]):
            for t in range(SUB):
                for n in range(NFIELD):
                    swap_ref[pl.ds(n * SUB * SUB + t, SUB, stride=SUB), :] = block_ref[
                        t, step * NFIELD + n
                    ]
            for c in range(SUB):
                fields = [
                    swap_ref[(n * SUB + c) * SUB : (n * SUB + c + 1) * SUB, :] for n in range(NFIELD)
                ]
                for q, value in enumerate(post_populations(*fields)):
                    main_ref[q, group * SUB + c] = value
        for x in range(EDGE):
            at = x % SUB
            for k in range(9):
                packed = below_in[k, x // SUB]
                below_ref[k, x + 1] = pltpu.roll(packed, (LANES - EDGE - EDGE * at) % LANES, axis=1)
                packed = above_in[k, x // SUB]
                above_ref[k, x + 1] = pltpu.roll(packed, (LANES - EDGE * at) % LANES, axis=1)
        for k in range(3):
            below_ref[6 + k, 0] = xlo_ref[18 + k]
            above_ref[6 + k, 0] = pltpu.roll(xlo_ref[21 + k], EDGE, axis=1)
            below_ref[k, EDGE + 1] = pltpu.roll(xhi_ref[18 + k], LANES - EDGE, axis=1)
            above_ref[k, EDGE + 1] = xhi_ref[21 + k]
        for copy in copies:
            copy.wait()

    lane = lax.broadcasted_iota(jnp.int32, (SUB, LANES), 1)
    block = lax.broadcasted_iota(jnp.int32, (SUB, LANES), 0)
    along = lane % EDGE
    first_z, last_z = along == 0, along == EDGE - 1
    floor = first_z & (block == 0)
    ceiling = last_z & (block == SUB - 1)
    low_y, high_y = lane < EDGE, lane >= LANES - EDGE

    for x in range(WIDTH):

        def source(q, half):
            at = x - velocity(q)[0]
            row = (g * WIDTH + at) * 2 + half
            if at < 0:
                inside = main_ref[q, jnp.maximum(row, 0)]
                return jnp.where(g == 0, xlo_ref[(q - 18) * 2 + half], inside)
            if at >= WIDTH:
                inside = main_ref[q, jnp.minimum(row, GROUPS * SUB - 1)]
                return jnp.where(g == GROUPS - 1, xhi_ref[q * 2 + half], inside)
            return main_ref[q, row]

        for half in range(2):
            c = x * 2 + half
            for q in range(NQ):
                cx, cy, cz = velocity(q)
                a = source(q, half)
                side = g * WIDTH + x - cx + 1
                k = (cx + 1) * 3 + cz + 1
                if cy == 1:
                    a = jnp.where(high_y, below_ref[k, side] if half == 0 else source(q, 0), a)
                elif cy == -1:
                    a = jnp.where(low_y, above_ref[k, side] if half == 1 else source(q, 1), a)
                shift = EDGE * cy + cz
                value = a if shift == 0 else pltpu.roll(a, shift % LANES, axis=1)
                if cz == 1:
                    fill = pltpu.roll(pltpu.roll(a, 1, axis=0), (shift - EDGE) % LANES, axis=1)
                    value = jnp.where(first_z, fill, value)
                    value = jnp.where(floor, main_ref[26 - q, g * SUB + c], value)
                elif cz == -1:
                    fill = pltpu.roll(pltpu.roll(a, SUB - 1, axis=0), (shift + EDGE) % LANES, axis=1)
                    value = jnp.where(last_z, fill, value)
                    value = jnp.where(ceiling, main_ref[26 - q, g * SUB + c], value)
                out_ref[q, :, c * LANES : (c + 1) * LANES] = value


def finish(tags, homes, early, xlo, xhi, below, above):
    def whole(value):
        rank = len(value.shape)
        return pl.BlockSpec(value.shape, lambda g, *_: (0,) * rank)

    return pl.pallas_call(
        functools.partial(finish_kernel, len(homes)),
        grid_spec=pltpu.PrefetchScalarGridSpec(
            num_scalar_prefetch=1,
            grid=(GROUPS,),
            in_specs=[whole(value) for value in homes]
            + [pl.BlockSpec(memory_space=pl.ANY)]
            + [whole(value) for value in (xlo, xhi, below, above)],
            out_specs=pl.BlockSpec((NQ, SUB, SUB * LANES), lambda g, *_: (0, 0, g)),
            scratch_shapes=[
                pltpu.VMEM((NQ, GROUPS * SUB, SUB, LANES), jnp.float32),
                pltpu.VMEM((9, EDGE + 2, SUB, LANES), jnp.float32),
                pltpu.VMEM((9, EDGE + 2, SUB, LANES), jnp.float32),
                pltpu.VMEM((SUB, tiles_of(1), SUB, LANES), jnp.float32),
                pltpu.VMEM((NFIELD * SUB * SUB, LANES), jnp.float32),
                pltpu.SemaphoreType.DMA((len(CHUNKS[0]),)),
            ],
        ),
        out_shape=jax.ShapeDtypeStruct((NQ, SUB, GROUPS * SUB * LANES), jnp.float32),
        compiler_params=pltpu.CompilerParams(vmem_limit_bytes=VMEM_LIMIT),
        cost_estimate=pl.CostEstimate(flops=10**7, bytes_accessed=8 * 10**6, transcendentals=0),
        name="finish",
    )(tags, *homes, early, xlo, xhi, below, above)


def shifted(value, axis, step):
    count = lax.axis_size(axis)
    return lax.ppermute(value, axis, [(i, (i + step) % count) for i in range(count)])


def tags_of(landed):
    return landed[:, -1, 2 * NFIELD - (SIDE_TILES - 1) * SUB, 0].astype(jnp.int32)


def on_device(populations, destination, refinement):
    blocks = populations.shape[0]
    row_count = lax.axis_size("row")
    col_count = lax.axis_size("col")
    cap_row = 2 * ((blocks + row_count - 1) // row_count)
    cap_col = 2 * ((blocks + col_count - 1) // col_count)
    ordered = jnp.transpose(populations, (1, 0, 2))
    in_row = [
        lax.all_to_all(
            pre(ordered, destination, refinement, part, row_count, cap_row, blocks * col_count),
            "row", split_axis=0, concat_axis=0, tiled=True,
        )
        for part in range(2)
    ]
    tags = tags_of(in_row[0])
    away = jnp.where(tags >= 0, (tags // blocks - lax.axis_index("col")) % col_count, -1)

    def to_columns(part):
        packed = repack(away, in_row[part], part, col_count, cap_col)
        return [packed[d] if d == 0 else shifted(packed[d], "col", d) for d in range(col_count)]

    homes = to_columns(0)
    tags = jnp.concatenate([tags_of(value) for value in homes])
    early, ylo, yhi, xlo, xhi = post(tags, homes)
    below, above = shifted(yhi, "col", 1), shifted(ylo, "col", -1)
    up = jnp.concatenate([xhi.reshape(18, SUB, LANES), below[6:, 1], above[6:, 1]])
    down = jnp.concatenate([xlo.reshape(18, SUB, LANES), below[:3, 0], above[:3, 0]])
    xlo, xhi = shifted(up, "row", 1), shifted(down, "row", -1)
    in_row[1], below, above = lax.optimization_barrier((in_row[1], below, above))
    homes = to_columns(1)
    return jnp.transpose(finish(tags, homes, early, xlo, xhi, below, above), (1, 0, 2))


def solution(mesh):
    return jax.shard_map(
        on_device,
        mesh=mesh,
        in_specs=(P(("row", "col"), None, None), P(("row", "col")), P(("row", "col"))),
        out_specs=P(("row", "col"), None, None),
        check_vma=False,
    )
```

```python
import functools

import jax
import jax.numpy as jnp
from jax import lax
from jax.experimental import pallas as pl
from jax.experimental.pallas import tpu as pltpu
from jax.sharding import PartitionSpec as P

EDGE = 16
VISCOSITY = 0.01
LANES = 128
SUB = 8
NQ = 27
NFIELD = 9
GROUPS = 4
WIDTH = EDGE // GROUPS
CHUNKS = ((0, 3), (1, 2))
SIDE_TILES = 3
START_AFTER = 1
TAG_ROW = 2 * NFIELD - (SIDE_TILES - 1) * SUB
VMEM_LIMIT = 20 * 1024 * 1024
PRE_VMEM_LIMIT = 60 * 1024 * 1024


def velocity(q):
    return (q // 9 - 1, (q // 3) % 3 - 1, q % 3 - 1)


def tiles_of(part):
    return len(CHUNKS[part]) * NFIELD + (0 if part else SIDE_TILES)


def step_to(target, here, count):
    if count & (count - 1) == 0:
        return target ^ here
    return lax.rem(target - here + count, count)


def origin_of(step, here, count):
    if count & (count - 1) == 0:
        return here ^ step
    return lax.rem(here - step + count, count)


def issue_order(count):
    near = list(range(1, count // 2))
    far = list(range(count - 1, count // 2 - 1, -1))
    return near[:2] + far + near[2:] + [0]


def exchanged(value, axis, step):
    count = lax.axis_size(axis)
    if count & (count - 1) == 0:
        pairs = [(i, i ^ step) for i in range(count)]
    else:
        pairs = [(i, (i + step) % count) for i in range(count)]
    return lax.ppermute(value, axis, pairs)


def raw_moments(f):
    whole, slope, outer = {}, {}, {}
    for i in range(3):
        for j in range(3):
            low, rest, high = (f[i * 9 + j * 3 + k] for k in range(3))
            outer[i, j] = low + high
            whole[i, j] = outer[i, j] + rest
            slope[i, j] = high - low
    column = [whole[i, 0] + whole[i, 1] + whole[i, 2] for i in range(3)]
    tilt = [slope[i, 0] + slope[i, 1] + slope[i, 2] for i in range(3)]
    low_y = whole[0, 0] + whole[1, 0] + whole[2, 0]
    high_y = whole[0, 2] + whole[1, 2] + whole[2, 2]
    ends = column[0] + column[2]
    mzz = sum(outer[i, j] for i in range(3) for j in range(3))
    mxy = (whole[2, 2] - whole[2, 0]) - (whole[0, 2] - whole[0, 0])
    myz = (slope[0, 2] + slope[1, 2] + slope[2, 2]) - (slope[0, 0] + slope[1, 0] + slope[2, 0])
    return (
        ends + column[1],
        column[2] - column[0],
        high_y - low_y,
        tilt[0] + tilt[1] + tilt[2],
        ends,
        low_y + high_y,
        mzz,
        mxy,
        tilt[2] - tilt[0],
        myz,
    )


def collided(f, keep):
    rho, jx, jy, jz, mxx, myy, mzz, mxy, mxz, myz = raw_moments(f)
    inverse = 1.0 / rho
    ux, uy, uz = jx * inverse, jy * inverse, jz * inverse
    kxx = mxx - jx * ux
    return (
        rho, ux, uy, uz,
        keep * (mxy - jx * uy),
        keep * (mxz - jx * uz),
        keep * (myz - jy * uz),
        keep * (kxx - (myy - jy * uy)),
        keep * (kxx - (mzz - jz * uz)),
    )


def pre_kernel(cap, row_count, per_row, part, dest_hbm, level_hbm, x_hbm, *refs):
    outs = refs[:-8]
    x_ref, swap_ref, packed_ref, side_ref, dest_ref, level_ref, source_ref, sems = refs[-8:]
    order = CHUNKS[1] if part else CHUNKS[0] + CHUNKS[1]
    steps = len(CHUNKS[part])
    blocks = x_ref.shape[2]
    cells = x_ref.shape[3]
    chunks = cells // LANES
    small = [
        pltpu.make_async_copy(dest_hbm, dest_ref, sems.at[0]),
        pltpu.make_async_copy(level_hbm, level_ref, sems.at[1]),
    ]
    large = [
        pltpu.make_async_copy(
            x_hbm.at[:, :, pl.ds(group * cells, cells)], x_ref.at[step], sems.at[2 + step]
        )
        for step, group in enumerate(order)
    ]
    for copy in small + large:
        copy.start()
    for copy in small:
        copy.wait()

    which = lax.broadcasted_iota(jnp.int32, (SUB, LANES), 0)
    spot = lax.broadcasted_iota(jnp.int32, (SUB, LANES), 1) // EDGE
    scale = jnp.zeros((SUB, LANES), jnp.int32)
    tag = jnp.zeros((SUB, LANES), jnp.int32)
    for t in range(blocks):
        scale = jnp.where(which == t, jnp.left_shift(1, level_ref[t]), scale)
        tag = jnp.where(which == t, dest_ref[t], tag)
    rate = 1.0 / (3.0 * VISCOSITY * scale.astype(jnp.float32) + 0.5)
    keep = 1.0 - rate

    here = lax.axis_index("row")
    for e in range(row_count * cap):
        source_ref[e] = -1
    rows = [dest_ref[t] // per_row for t in range(blocks)]
    for t in range(blocks):
        e = (rows[t] if part else step_to(rows[t], here, row_count)) * cap
        for other in range(t):
            e = e + jnp.where(rows[other] == rows[t], 1, 0)
        source_ref[e] = t

    def spread(ref, first, count):
        for e in range(row_count * cap):
            t = source_ref[e]

            @pl.when(t >= 0)
            def _():
                for n in range(count):
                    moved = ref[pl.ds(n * SUB * SUB + t, SUB, stride=SUB), :]
                    if part:
                        outs[0][e, first + n] = moved
                    else:
                        outs[e // cap][e % cap, first + n] = moved

    for step, group in enumerate(order):
        large[step].wait()
        if step < steps:
            for c in range(chunks):
                fields = collided(
                    [x_ref[step, q, :, c * LANES : (c + 1) * LANES] for q in range(NQ)], keep
                )
                for n, field in enumerate(fields):
                    base = (n * chunks + c) * SUB
                    swap_ref[base : base + SUB, :] = field
            spread(swap_ref, step * NFIELD, NFIELD)
            continue
        for q in range(NQ):
            for half in range(2):
                value = packed_ref[half * NQ + q] if step > steps else None
                for x in range(WIDTH):
                    c = x * 2 + half
                    at = (group * WIDTH + x) % SUB
                    moved = x_ref[step, q, :, c * LANES : (c + 1) * LANES]
                    turn = (at + half) * EDGE % LANES
                    if turn:
                        moved = pltpu.roll(moved, turn, axis=1)
                    value = moved if value is None else jnp.where(spot == at, moved, value)
                packed_ref[half * NQ + q] = value

    if part == 0:
        for half in range(2):
            fields = collided([packed_ref[half * NQ + q] for q in range(NQ)], keep)
            for n, field in enumerate(fields):
                base = (half * NFIELD + n) * SUB
                side_ref[base : base + SUB, :] = field
        for row in range(2 * NFIELD, SIDE_TILES * SUB):
            side_ref[row * SUB : (row + 1) * SUB, :] = tag.astype(jnp.float32)
        for out in outs:
            for k in range(cap):
                out[k, tiles_of(0) - 1] = jnp.full((SUB, LANES), -1.0, jnp.float32)
        spread(side_ref, steps * NFIELD, SIDE_TILES)


def pre(populations, destination, refinement, part, row_count, cap, per_row):
    blocks = populations.shape[1]
    cells = populations.shape[2] // GROUPS
    loaded = len(CHUNKS[part]) + (0 if part else len(CHUNKS[1]))
    arrays = 1 if part else row_count
    slots = row_count * cap // arrays
    out = jax.ShapeDtypeStruct((slots, tiles_of(part), SUB, LANES), jnp.float32)
    return pl.pallas_call(
        functools.partial(pre_kernel, cap, row_count, per_row, part),
        in_specs=[pl.BlockSpec(memory_space=pltpu.HBM)] * 3,
        out_specs=[pl.BlockSpec(memory_space=pltpu.VMEM)] * arrays,
        out_shape=[out] * arrays,
        scratch_shapes=[
            pltpu.VMEM((loaded, NQ, blocks, cells), jnp.float32),
            pltpu.VMEM((NFIELD * cells // LANES * SUB, LANES), jnp.float32),
            pltpu.VMEM((2 * NQ, SUB, LANES), jnp.float32),
            pltpu.VMEM((SIDE_TILES * SUB * SUB, LANES), jnp.float32),
            pltpu.SMEM((blocks,), jnp.int32),
            pltpu.SMEM((blocks,), jnp.int32),
            pltpu.SMEM((row_count * cap,), jnp.int32),
            pltpu.SemaphoreType.DMA((2 + loaded,)),
        ],
        compiler_params=pltpu.CompilerParams(vmem_limit_bytes=PRE_VMEM_LIMIT),
        cost_estimate=pl.CostEstimate(flops=10**7, bytes_accessed=4 * 10**6, transcendentals=0),
        name="pre_%d" % part,
    )(destination, refinement, populations)


def read_tags(ins, tag_ref, sems):
    cap, tiles = ins[0].shape[:2]
    copies = [
        pltpu.make_async_copy(in_ref.at[k, tiles - 1], tag_ref.at[d * cap + k], sems.at[d * cap + k])
        for d, in_ref in enumerate(ins)
        for k in range(cap)
    ]
    for copy in copies:
        copy.start()
    for copy in copies:
        copy.wait()
    return lambda e: tag_ref[e, TAG_ROW, 0].astype(jnp.int32)


def tag_scratch(slots):
    return [pltpu.SMEM((slots, SUB, LANES), jnp.float32), pltpu.SemaphoreType.DMA((slots,))]


def repack_kernel(cap, cap_in, row_count, col_count, blocks, part, *refs):
    refs = list(refs)
    if part == 0:
        tag_ref, sems, block_ref, count_ref = refs[-4:]
        ins, outs, plan_ref = refs[: -5 - col_count], refs[-5 - col_count : -5], refs[-5]
    else:
        plan_ref, block_ref = refs[0], refs[-1]
        ins, outs = refs[1 : -1 - col_count], refs[-1 - col_count : -1]
    tiles = ins[0].shape[1]
    slots_in = row_count * cap_in
    order = issue_order(row_count)
    if part == 0:
        tag_at = read_tags(ins, tag_ref, sems)
        here = lax.axis_index("col")
        for d in range(col_count + 1):
            count_ref[d] = 0
        for e in range(col_count * cap):
            plan_ref[slots_in + e] = -1
        for e in range(slots_in):
            tag = tag_at(e)
            plan_ref[e] = -1

            @pl.when(tag >= 0)
            def _():
                d = step_to(lax.rem(tag // blocks, col_count), here, col_count)
                k = count_ref[d]
                count_ref[d] = k + 1
                j = count_ref[col_count]
                count_ref[col_count] = j + 1
                plan_ref[e] = j
                plan_ref[slots_in + d * cap + k] = j

    row = lax.axis_index("row")
    for e in range(slots_in):
        j = plan_ref[e]

        @pl.when(j >= 0)
        def _():
            if part:
                origin = origin_of(order[e // cap_in], row, row_count)
                block_ref[j] = ins[0][origin * cap_in + e % cap_in]
            else:
                block_ref[j] = ins[e // cap_in][e % cap_in]

    for e in range(col_count * cap):
        j = plan_ref[slots_in + e]
        out = outs[e // cap]

        @pl.when(j >= 0)
        def _():
            out[e % cap] = block_ref[j]

        if part == 0:

            @pl.when(j < 0)
            def _():
                out[e % cap, tiles - 1] = jnp.full((SUB, LANES), -1.0, jnp.float32)


def repack(landed, plan, part, row_count, col_count, cap, cap_in, blocks):
    slots_in = row_count * cap_in
    tiles = landed[0].shape[1:]
    whole = pl.BlockSpec(memory_space=pltpu.VMEM)
    scalars = pl.BlockSpec(memory_space=pltpu.SMEM)
    length = slots_in + col_count * cap
    scratch = [pltpu.VMEM((blocks,) + tiles, jnp.float32)]
    if part == 0:
        scratch = tag_scratch(slots_in) + scratch + [pltpu.SMEM((col_count + 1,), jnp.int32)]
    *packed, last = pl.pallas_call(
        functools.partial(repack_kernel, cap, cap_in, row_count, col_count, blocks, part),
        in_specs=([scalars] if part else []) + [whole] * len(landed),
        out_specs=[whole] * col_count + ([] if part else [scalars]),
        scratch_shapes=scratch,
        out_shape=[jax.ShapeDtypeStruct((cap,) + tiles, jnp.float32)] * col_count
        + ([] if part else [jax.ShapeDtypeStruct((length,), jnp.int32)]),
        compiler_params=pltpu.CompilerParams(vmem_limit_bytes=VMEM_LIMIT),
        cost_estimate=pl.CostEstimate(flops=0, bytes_accessed=3 * 10**6, transcendentals=0),
        name="repack_%d" % part,
    )(*([plan] if part else []), *landed)
    return (packed + [last], plan) if part else (packed, last)


def backward(zeroth, first, second, u):
    raw_one, raw_two = first, second
    if zeroth is not None:
        moved = u * zeroth
        raw_one = moved if raw_one is None else raw_one + moved
        square = u * moved
        raw_two = square if raw_two is None else raw_two + square
    if first is not None:
        cross = (u + u) * first
        raw_two = cross if raw_two is None else raw_two + cross
    rest = -raw_two if zeroth is None else zeroth - raw_two
    return 0.5 * (raw_two - raw_one), rest, 0.5 * (raw_one + raw_two)


def post_populations(rho, ux, uy, uz, pxy, pxz, pyz, dev_one, dev_two):
    inverse = 1.0 / rho
    pxx = (rho + dev_one + dev_two) * (1.0 / 3.0)
    pyy = pxx - dev_one
    pzz = pxx - dev_two
    sxy, sxz, syz = pxy * inverse, pxz * inverse, pyz * inverse
    syy, szz = pyy * inverse, pzz * inverse
    central = {
        (0, 0, 0): rho, (2, 0, 0): pxx, (0, 2, 0): pyy, (0, 0, 2): pzz,
        (1, 1, 0): pxy, (1, 0, 1): pxz, (0, 1, 1): pyz,
        (2, 2, 0): pxx * syy + 2.0 * pxy * sxy,
        (2, 0, 2): pxx * szz + 2.0 * pxz * sxz,
        (0, 2, 2): pyy * szz + 2.0 * pyz * syz,
        (2, 1, 1): pxx * syz + 2.0 * pxy * sxz,
        (1, 2, 1): pyy * sxz + 2.0 * pxy * syz,
        (1, 1, 2): pzz * sxy + 2.0 * pxz * syz,
        (2, 2, 2): pxx * syy * szz
        + 2.0 * (pxx * syz * syz + pyy * sxz * sxz + pzz * sxy * sxy)
        + 8.0 * pxy * sxz * syz,
    }
    along_z = {}
    for a in range(3):
        for b in range(3):
            parts = backward(*(central.get((a, b, c)) for c in range(3)), uz)
            for k in range(3):
                along_z[a, b, k] = parts[k]
    along_y = {}
    for a in range(3):
        for k in range(3):
            parts = backward(*(along_z[a, b, k] for b in range(3)), uy)
            for j in range(3):
                along_y[a, j, k] = parts[j]
    result = [None] * NQ
    for j in range(3):
        for k in range(3):
            parts = backward(*(along_y[a, j, k] for a in range(3)), ux)
            for i in range(3):
                result[i * 9 + j * 3 + k] = parts[i]
    return result


def unload(plan_ref, ins, block_ref):
    cap = ins[0].shape[0]
    for e in range(len(ins) * cap):
        t = plan_ref[e]

        @pl.when(t >= 0)
        def _():
            block_ref[t] = ins[e // cap][e % cap]


def side_spot(lane, x):
    return (lane // EDGE) == x % SUB


def post_kernel(count, *refs):
    ins = refs[:count]
    (
        post_ref, ylo_ref, yhi_ref, xlo_ref, xhi_ref, plan_ref,
        block_ref, swap_ref, side_ref, tag_ref, sems,
    ) = refs[count:]
    g = pl.program_id(0)
    steps = len(CHUNKS[0])
    lane = lax.broadcasted_iota(jnp.int32, (SUB, LANES), 1)

    @pl.when(g == 0)
    def _():
        tag_at = read_tags(ins, tag_ref, sems)
        for e in range(count * ins[0].shape[0]):
            tag = tag_at(e)
            plan_ref[e] = jnp.where(tag >= 0, lax.rem(tag, SUB), -1)
        unload(plan_ref, ins, block_ref)
        for t in range(SUB):
            for tile in range(SIDE_TILES):
                side_ref[pl.ds(tile * SUB * SUB + t, SUB, stride=SUB), :] = block_ref[
                    t, steps * NFIELD + tile
                ]
        for half in range(2):
            fields = [
                side_ref[(half * NFIELD + n) * SUB : (half * NFIELD + n + 1) * SUB, :]
                for n in range(NFIELD)
            ]
            result = post_populations(*fields)
            for i in range(3):
                for k in range(3):
                    value = result[i * 9 + 6 * half + k]
                    for tile in range(2):
                        (yhi_ref if half else ylo_ref)[i * 3 + k, tile] = value

    for t in range(SUB):
        for n in range(NFIELD):
            swap_ref[pl.ds(n * SUB * SUB + t, SUB, stride=SUB), :] = block_ref[t, g * NFIELD + n]
    group = CHUNKS[0][0]
    for step in range(1, steps):
        group = jnp.where(g == step, CHUNKS[0][step], group)
    for c in range(SUB):
        fields = [swap_ref[(n * SUB + c) * SUB : (n * SUB + c + 1) * SUB, :] for n in range(NFIELD)]
        result = post_populations(*fields)
        for q in range(NQ):
            post_ref[q, c] = result[q]
        x_in, half = c // 2, c % 2
        x = group * WIDTH + x_in
        inside = side_spot(lane, x)
        face_ref, first, shift = ((ylo_ref, 0, 0), (yhi_ref, 6, EDGE))[half]
        turn = ((x % SUB) * EDGE + shift) % LANES
        for i in range(3):
            for k in range(3):
                value = pltpu.roll(result[i * 9 + first + k], turn, axis=1)
                at = (i * 3 + k, x // SUB)
                face_ref[at] = jnp.where(inside, value, face_ref[at])

        if x_in == 0:

            @pl.when(group == 0)
            def _():
                for q in range(9):
                    xlo_ref[q, half] = result[q]

        if x_in == WIDTH - 1:

            @pl.when(group == GROUPS - 1)
            def _():
                for q in range(9):
                    xhi_ref[q, half] = result[18 + q]


def post(homes):
    shape = jax.ShapeDtypeStruct
    face = (9, 2, SUB, LANES)
    steps = len(CHUNKS[0])
    slots = len(homes) * homes[0].shape[0]
    spec = pl.BlockSpec(face, lambda g: (0, 0, 0, 0))
    return pl.pallas_call(
        functools.partial(post_kernel, len(homes)),
        grid=(steps,),
        in_specs=[pl.BlockSpec(homes[0].shape, lambda g: (0, 0, 0, 0))] * len(homes),
        out_specs=[pl.BlockSpec((NQ, SUB, SUB, LANES), lambda g: (0, g, 0, 0))]
        + [spec] * 4
        + [pl.BlockSpec(memory_space=pltpu.SMEM)],
        scratch_shapes=[
            pltpu.VMEM((SUB, tiles_of(0), SUB, LANES), jnp.float32),
            pltpu.VMEM((NFIELD * SUB * SUB, LANES), jnp.float32),
            pltpu.VMEM((SIDE_TILES * SUB * SUB, LANES), jnp.float32),
        ]
        + tag_scratch(slots),
        out_shape=[shape((NQ, steps * SUB, SUB, LANES), jnp.float32)]
        + [shape(face, jnp.float32)] * 4
        + [shape((slots,), jnp.int32)],
        compiler_params=pltpu.CompilerParams(vmem_limit_bytes=VMEM_LIMIT),
        cost_estimate=pl.CostEstimate(flops=10**7, bytes_accessed=3 * 10**6, transcendentals=0),
        name="post",
    )(*homes)


def finish_kernel(count, plan_ref, *refs):
    ins = refs[:count]
    (
        early_ref, xlo_ref, xhi_ref, below_in, above_in,
        out_ref, main_ref, below_ref, above_ref, block_ref, swap_ref, sems,
    ) = refs[count:]
    g = pl.program_id(0)

    @pl.when(g == 0)
    def _():
        copies = [
            pltpu.make_async_copy(
                early_ref.at[:, pl.ds(step * SUB, SUB)],
                main_ref.at[:, pl.ds(group * SUB, SUB)],
                sems.at[step],
            )
            for step, group in enumerate(CHUNKS[0])
        ]
        for copy in copies:
            copy.start()
        unload(plan_ref, ins, block_ref)
        for step, group in enumerate(CHUNKS[1]):
            for t in range(SUB):
                for n in range(NFIELD):
                    swap_ref[pl.ds(n * SUB * SUB + t, SUB, stride=SUB), :] = block_ref[
                        t, step * NFIELD + n
                    ]
            for c in range(SUB):
                fields = [
                    swap_ref[(n * SUB + c) * SUB : (n * SUB + c + 1) * SUB, :] for n in range(NFIELD)
                ]
                for q, value in enumerate(post_populations(*fields)):
                    main_ref[q, group * SUB + c] = value
        for x in range(EDGE):
            at = x % SUB
            for k in range(9):
                packed = below_in[k, x // SUB]
                below_ref[k, x + 1] = pltpu.roll(packed, (LANES - EDGE - EDGE * at) % LANES, axis=1)
                packed = above_in[k, x // SUB]
                above_ref[k, x + 1] = pltpu.roll(packed, (LANES - EDGE * at) % LANES, axis=1)
        for k in range(3):
            below_ref[6 + k, 0] = xlo_ref[18 + k]
            above_ref[6 + k, 0] = pltpu.roll(xlo_ref[21 + k], EDGE, axis=1)
            below_ref[k, EDGE + 1] = pltpu.roll(xhi_ref[18 + k], LANES - EDGE, axis=1)
            above_ref[k, EDGE + 1] = xhi_ref[21 + k]
        for copy in copies:
            copy.wait()

    lane = lax.broadcasted_iota(jnp.int32, (SUB, LANES), 1)
    block = lax.broadcasted_iota(jnp.int32, (SUB, LANES), 0)
    along = lane % EDGE
    first_z, last_z = along == 0, along == EDGE - 1
    floor = first_z & (block == 0)
    ceiling = last_z & (block == SUB - 1)
    low_y, high_y = lane < EDGE, lane >= LANES - EDGE

    for x in range(WIDTH):

        def source(q, half):
            at = x - velocity(q)[0]
            row = (g * WIDTH + at) * 2 + half
            if at < 0:
                inside = main_ref[q, jnp.maximum(row, 0)]
                return jnp.where(g == 0, xlo_ref[(q - 18) * 2 + half], inside)
            if at >= WIDTH:
                inside = main_ref[q, jnp.minimum(row, GROUPS * SUB - 1)]
                return jnp.where(g == GROUPS - 1, xhi_ref[q * 2 + half], inside)
            return main_ref[q, row]

        for half in range(2):
            c = x * 2 + half
            for q in range(NQ):
                cx, cy, cz = velocity(q)
                a = source(q, half)
                side = g * WIDTH + x - cx + 1
                k = (cx + 1) * 3 + cz + 1
                if cy == 1:
                    a = jnp.where(high_y, below_ref[k, side] if half == 0 else source(q, 0), a)
                elif cy == -1:
                    a = jnp.where(low_y, above_ref[k, side] if half == 1 else source(q, 1), a)
                shift = EDGE * cy + cz
                value = a if shift == 0 else pltpu.roll(a, shift % LANES, axis=1)
                if cz == 1:
                    fill = pltpu.roll(pltpu.roll(a, 1, axis=0), (shift - EDGE) % LANES, axis=1)
                    value = jnp.where(first_z, fill, value)
                    value = jnp.where(floor, main_ref[26 - q, g * SUB + c], value)
                elif cz == -1:
                    fill = pltpu.roll(pltpu.roll(a, SUB - 1, axis=0), (shift + EDGE) % LANES, axis=1)
                    value = jnp.where(last_z, fill, value)
                    value = jnp.where(ceiling, main_ref[26 - q, g * SUB + c], value)
                out_ref[q, :, c * LANES : (c + 1) * LANES] = value


def finish(plan, homes, early, xlo, xhi, below, above):
    def whole(value):
        rank = len(value.shape)
        return pl.BlockSpec(value.shape, lambda g, *_: (0,) * rank)

    return pl.pallas_call(
        functools.partial(finish_kernel, len(homes)),
        grid_spec=pltpu.PrefetchScalarGridSpec(
            num_scalar_prefetch=1,
            grid=(GROUPS,),
            in_specs=[whole(value) for value in homes]
            + [pl.BlockSpec(memory_space=pl.ANY)]
            + [whole(value) for value in (xlo, xhi, below, above)],
            out_specs=pl.BlockSpec((NQ, SUB, SUB * LANES), lambda g, *_: (0, 0, g)),
            scratch_shapes=[
                pltpu.VMEM((NQ, GROUPS * SUB, SUB, LANES), jnp.float32),
                pltpu.VMEM((9, EDGE + 2, SUB, LANES), jnp.float32),
                pltpu.VMEM((9, EDGE + 2, SUB, LANES), jnp.float32),
                pltpu.VMEM((SUB, tiles_of(1), SUB, LANES), jnp.float32),
                pltpu.VMEM((NFIELD * SUB * SUB, LANES), jnp.float32),
                pltpu.SemaphoreType.DMA((len(CHUNKS[0]),)),
            ],
        ),
        out_shape=jax.ShapeDtypeStruct((NQ, SUB, GROUPS * SUB * LANES), jnp.float32),
        compiler_params=pltpu.CompilerParams(vmem_limit_bytes=VMEM_LIMIT),
        cost_estimate=pl.CostEstimate(flops=10**7, bytes_accessed=8 * 10**6, transcendentals=0),
        name="finish",
    )(plan, *homes, early, xlo, xhi, below, above)


def shifted(value, axis, step):
    count = lax.axis_size(axis)
    return lax.ppermute(value, axis, [(i, (i + step) % count) for i in range(count)])


def on_device(populations, destination, refinement):
    blocks = populations.shape[0]
    row_count = lax.axis_size("row")
    col_count = lax.axis_size("col")
    cap_row = 2 * ((blocks + row_count - 1) // row_count)
    cap_col = 2 * ((blocks + col_count - 1) // col_count)
    ordered = jnp.transpose(populations, (1, 0, 2))

    def travel(packed, axis):
        return [exchanged(packed[d], axis, d) if d else packed[0] for d in issue_order(len(packed))]

    early_row = travel(
        pre(ordered, destination, refinement, 0, row_count, cap_row, blocks * col_count), "row"
    )
    waited = START_AFTER
    destination, early_row[waited] = lax.optimization_barrier((destination, early_row[waited]))
    (late,) = pre(ordered, destination, refinement, 1, row_count, cap_row, blocks * col_count)
    late_row = lax.all_to_all(late, "row", split_axis=0, concat_axis=0, tiled=True)
    packed, plan = repack(early_row, None, 0, row_count, col_count, cap_col, cap_row, blocks)
    early, ylo, yhi, xlo, xhi, picked = post(travel(packed, "col"))
    below, above = shifted(yhi, "col", 1), shifted(ylo, "col", -1)
    up = jnp.concatenate([xhi.reshape(18, SUB, LANES), below[6:, 1], above[6:, 1]])
    down = jnp.concatenate([xlo.reshape(18, SUB, LANES), below[:3, 0], above[:3, 0]])
    xlo, xhi = shifted(up, "row", 1), shifted(down, "row", -1)
    late_row, below, above = lax.optimization_barrier((late_row, below, above))
    packed, _ = repack([late_row], plan, 1, row_count, col_count, cap_col, cap_row, blocks)
    homes = travel(packed, "col")
    return jnp.transpose(finish(picked, homes, early, xlo, xhi, below, above), (1, 0, 2))


def solution(mesh):
    return jax.shard_map(
        on_device,
        mesh=mesh,
        in_specs=(P(("row", "col"), None, None), P(("row", "col")), P(("row", "col"))),
        out_specs=P(("row", "col"), None, None),
        check_vma=False,
    )
```

```python
import functools

import jax
import jax.numpy as jnp
from jax import lax
from jax.experimental import pallas as pl
from jax.experimental.pallas import tpu as pltpu
from jax.sharding import PartitionSpec as P

EDGE = 16
VISCOSITY = 0.01
LANES = 128
SUB = 8
NQ = 27
NFIELD = 9
GROUPS = 4
WIDTH = EDGE // GROUPS
CHUNKS = ((0, 3), (1, 2))
SIDE_TILES = 3
LATE_TILES = -(-2 * NFIELD * (SUB - 1) // SUB)
VMEM_LIMIT = 20 * 1024 * 1024
PRE_VMEM_LIMIT = 60 * 1024 * 1024


def velocity(q):
    return (q // 9 - 1, (q // 3) % 3 - 1, q % 3 - 1)


def tiles_of(part):
    return LATE_TILES if part else len(CHUNKS[0]) * NFIELD + SIDE_TILES


def free_place(c):
    return (c % 2) * (SUB - 1)


def step_to(target, here, count):
    if count & (count - 1) == 0:
        return target ^ here
    return lax.rem(target - here + count, count)


def exchanged(value, axis, step):
    count = lax.axis_size(axis)
    if count & (count - 1) == 0:
        pairs = [(i, i ^ step) for i in range(count)]
    else:
        pairs = [(i, (i + step) % count) for i in range(count)]
    return lax.ppermute(value, axis, pairs)


def raw_moments(f):
    whole, slope, outer = {}, {}, {}
    for i in range(3):
        for j in range(3):
            low, rest, high = (f[i * 9 + j * 3 + k] for k in range(3))
            outer[i, j] = low + high
            whole[i, j] = outer[i, j] + rest
            slope[i, j] = high - low
    column = [whole[i, 0] + whole[i, 1] + whole[i, 2] for i in range(3)]
    tilt = [slope[i, 0] + slope[i, 1] + slope[i, 2] for i in range(3)]
    low_y = whole[0, 0] + whole[1, 0] + whole[2, 0]
    high_y = whole[0, 2] + whole[1, 2] + whole[2, 2]
    ends = column[0] + column[2]
    mzz = sum(outer[i, j] for i in range(3) for j in range(3))
    mxy = (whole[2, 2] - whole[2, 0]) - (whole[0, 2] - whole[0, 0])
    myz = (slope[0, 2] + slope[1, 2] + slope[2, 2]) - (slope[0, 0] + slope[1, 0] + slope[2, 0])
    return (
        ends + column[1],
        column[2] - column[0],
        high_y - low_y,
        tilt[0] + tilt[1] + tilt[2],
        ends,
        low_y + high_y,
        mzz,
        mxy,
        tilt[2] - tilt[0],
        myz,
    )


def collided(f, keep):
    rho, jx, jy, jz, mxx, myy, mzz, mxy, mxz, myz = raw_moments(f)
    inverse = 1.0 / rho
    ux, uy, uz = jx * inverse, jy * inverse, jz * inverse
    kxx = mxx - jx * ux
    return (
        rho, ux, uy, uz,
        keep * (mxy - jx * uy),
        keep * (mxz - jx * uz),
        keep * (myz - jy * uz),
        keep * (kxx - (myy - jy * uy)),
        keep * (kxx - (mzz - jz * uz)),
    )


def pre_kernel(cap, row_count, per_row, part, dest_hbm, level_hbm, x_hbm, out_ref, *refs):
    x_ref, swap_ref, packed_ref, side_ref, dest_ref, level_ref, sems = refs
    order = CHUNKS[1] if part else CHUNKS[0] + CHUNKS[1]
    steps = len(CHUNKS[part])
    blocks = x_ref.shape[2]
    cells = x_ref.shape[3]
    chunks = cells // LANES
    small = [
        pltpu.make_async_copy(dest_hbm, dest_ref, sems.at[0]),
        pltpu.make_async_copy(level_hbm, level_ref, sems.at[1]),
    ]
    large = [
        pltpu.make_async_copy(
            x_hbm.at[:, :, pl.ds(group * cells, cells)], x_ref.at[step], sems.at[2 + step]
        )
        for step, group in enumerate(order)
    ]
    for copy in small + large:
        copy.start()
    for copy in small:
        copy.wait()

    which = lax.broadcasted_iota(jnp.int32, (SUB, LANES), 0)
    spot = lax.broadcasted_iota(jnp.int32, (SUB, LANES), 1) // EDGE
    scale = jnp.zeros((SUB, LANES), jnp.int32)
    tag = jnp.zeros((SUB, LANES), jnp.int32)
    for t in range(blocks):
        scale = jnp.where(which == t, jnp.left_shift(1, level_ref[t]), scale)
        tag = jnp.where(which == t, dest_ref[t], tag)
    rate = 1.0 / (3.0 * VISCOSITY * scale.astype(jnp.float32) + 0.5)
    keep = 1.0 - rate

    rows = [dest_ref[t] // per_row for t in range(blocks)]
    slots = []
    for t in range(blocks):
        slot = rows[t] * cap
        for other in range(t):
            slot = slot + jnp.where(rows[other] == rows[t], 1, 0)
        slots.append(slot)

    def spread(ref, first, count):
        for t in range(blocks):
            for n in range(count):
                moved = ref[pl.ds(n * SUB * SUB + t, SUB, stride=SUB), :]
                out_ref[slots[t], first + n] = moved

    def fields_at(step, c):
        return collided([x_ref[step, q, :, c * LANES : (c + 1) * LANES] for q in range(NQ)], keep)

    for step, group in enumerate(order):
        large[step].wait()
        if part:
            last = fields_at(step, chunks - 1)
            for c in range(chunks - 1):
                place = free_place(c)
                turn = (place - c) * EDGE % LANES
                for n, field in enumerate(fields_at(step, c)):
                    other = pltpu.roll(last[n], turn, axis=1) if turn else last[n]
                    base = ((step * NFIELD + n) * (chunks - 1) + c) * SUB
                    swap_ref[base : base + SUB, :] = jnp.where(spot == place, other, field)
            continue
        if step < steps:
            for c in range(chunks):
                for n, field in enumerate(fields_at(step, c)):
                    base = (n * chunks + c) * SUB
                    swap_ref[base : base + SUB, :] = field
            spread(swap_ref, SIDE_TILES + step * NFIELD, NFIELD)
            continue
        for q in range(NQ):
            for half in range(2):
                value = packed_ref[half * NQ + q] if step > steps else None
                for x in range(WIDTH):
                    c = x * 2 + half
                    at = (group * WIDTH + x) % SUB
                    moved = x_ref[step, q, :, c * LANES : (c + 1) * LANES]
                    turn = (at + half) * EDGE % LANES
                    if turn:
                        moved = pltpu.roll(moved, turn, axis=1)
                    value = moved if value is None else jnp.where(spot == at, moved, value)
                packed_ref[half * NQ + q] = value

    if part:
        for row in range(steps * NFIELD * (chunks - 1), LATE_TILES * SUB):
            swap_ref[row * SUB : (row + 1) * SUB, :] = tag.astype(jnp.float32)
        spread(swap_ref, 0, LATE_TILES)
        return
    for row in range(SIDE_TILES * SUB):
        if not 1 <= row <= 2 * NFIELD:
            side_ref[row * SUB : (row + 1) * SUB, :] = tag.astype(jnp.float32)
    for half in range(2):
        fields = collided([packed_ref[half * NQ + q] for q in range(NQ)], keep)
        for n, field in enumerate(fields):
            base = (1 + half * NFIELD + n) * SUB
            side_ref[base : base + SUB, :] = field
    for slot in range(row_count * cap):
        out_ref[slot, 0] = jnp.full((SUB, LANES), -1.0, jnp.float32)
    spread(side_ref, 0, SIDE_TILES)


def pre(populations, destination, refinement, part, row_count, cap, per_row):
    blocks = populations.shape[1]
    cells = populations.shape[2] // GROUPS
    loaded = len(CHUNKS[part]) + (0 if part else len(CHUNKS[1]))
    rows = LATE_TILES * SUB if part else NFIELD * cells // LANES
    return pl.pallas_call(
        functools.partial(pre_kernel, cap, row_count, per_row, part),
        in_specs=[pl.BlockSpec(memory_space=pltpu.HBM)] * 3,
        out_specs=pl.BlockSpec(memory_space=pltpu.VMEM),
        out_shape=jax.ShapeDtypeStruct((row_count * cap, tiles_of(part), SUB, LANES), jnp.float32),
        scratch_shapes=[
            pltpu.VMEM((loaded, NQ, blocks, cells), jnp.float32),
            pltpu.VMEM((rows * SUB, LANES), jnp.float32),
            pltpu.VMEM((2 * NQ, SUB, LANES), jnp.float32),
            pltpu.VMEM((SIDE_TILES * SUB * SUB, LANES), jnp.float32),
            pltpu.SMEM((blocks,), jnp.int32),
            pltpu.SMEM((blocks,), jnp.int32),
            pltpu.SemaphoreType.DMA((2 + loaded,)),
        ],
        compiler_params=pltpu.CompilerParams(vmem_limit_bytes=PRE_VMEM_LIMIT),
        cost_estimate=pl.CostEstimate(flops=10**7, bytes_accessed=4 * 10**6, transcendentals=0),
        name="pre_%d" % part,
    )(destination, refinement, populations)


def read_tags(ins, tag_ref, sems):
    cap = ins[0].shape[0]
    copies = [
        pltpu.make_async_copy(in_ref.at[:, 0, pl.ds(0, 1)], tag_ref.at[pl.ds(d * cap, cap)], sems.at[d])
        for d, in_ref in enumerate(ins)
    ]
    for copy in copies:
        copy.start()
    for copy in copies:
        copy.wait()
    return lambda e: tag_ref[e, 0, 0].astype(jnp.int32)


def tag_scratch(arrays, slots):
    return [pltpu.SMEM((slots, 1, LANES), jnp.float32), pltpu.SemaphoreType.DMA((arrays,))]


def repack_kernel(cap, col_count, blocks, part, *refs):
    if part:
        plan_ref, in_ref, *outs = refs
    else:
        in_ref, *outs, plan_ref, tag_ref, sems, count_ref = refs
        tag_at = read_tags([in_ref], tag_ref, sems)
        here = lax.axis_index("col")
        for d in range(col_count):
            count_ref[d] = 0
        for e in range(col_count * cap):
            plan_ref[e] = -1
        for e in range(in_ref.shape[0]):
            tag = tag_at(e)

            @pl.when(tag >= 0)
            def _():
                d = step_to(lax.rem(tag // blocks, col_count), here, col_count)
                k = count_ref[d]
                count_ref[d] = k + 1
                plan_ref[d * cap + k] = e

    for d, out in enumerate(outs):
        for k in range(cap):
            e = plan_ref[d * cap + k]

            @pl.when(e >= 0)
            def _():
                out[k] = in_ref[e]

            if part == 0:

                @pl.when(e < 0)
                def _():
                    out[k, 0] = jnp.full((SUB, LANES), -1.0, jnp.float32)


def repack(landed, plan, part, col_count, cap, blocks):
    whole = pl.BlockSpec(memory_space=pltpu.VMEM)
    scalars = pl.BlockSpec(memory_space=pltpu.SMEM)
    scratch = []
    if part == 0:
        scratch = tag_scratch(1, landed.shape[0]) + [pltpu.SMEM((col_count,), jnp.int32)]
    packed = pl.pallas_call(
        functools.partial(repack_kernel, cap, col_count, blocks, part),
        in_specs=([scalars] if part else []) + [whole],
        out_specs=[whole] * col_count + ([] if part else [scalars]),
        scratch_shapes=scratch,
        out_shape=[jax.ShapeDtypeStruct((cap,) + landed.shape[1:], jnp.float32)] * col_count
        + ([] if part else [jax.ShapeDtypeStruct((col_count * cap,), jnp.int32)]),
        compiler_params=pltpu.CompilerParams(vmem_limit_bytes=VMEM_LIMIT),
        cost_estimate=pl.CostEstimate(flops=0, bytes_accessed=3 * 10**6, transcendentals=0),
        name="repack_%d" % part,
    )(*([plan] if part else []), landed)
    return packed if part else (packed[:-1], packed[-1])


def backward(zeroth, first, second, u):
    raw_one, raw_two = first, second
    if zeroth is not None:
        moved = u * zeroth
        raw_one = moved if raw_one is None else raw_one + moved
        square = u * moved
        raw_two = square if raw_two is None else raw_two + square
    if first is not None:
        cross = (u + u) * first
        raw_two = cross if raw_two is None else raw_two + cross
    rest = -raw_two if zeroth is None else zeroth - raw_two
    return 0.5 * (raw_two - raw_one), rest, 0.5 * (raw_one + raw_two)


def post_populations(rho, ux, uy, uz, pxy, pxz, pyz, dev_one, dev_two):
    inverse = 1.0 / rho
    pxx = (rho + dev_one + dev_two) * (1.0 / 3.0)
    pyy = pxx - dev_one
    pzz = pxx - dev_two
    sxy, sxz, syz = pxy * inverse, pxz * inverse, pyz * inverse
    syy, szz = pyy * inverse, pzz * inverse
    central = {
        (0, 0, 0): rho, (2, 0, 0): pxx, (0, 2, 0): pyy, (0, 0, 2): pzz,
        (1, 1, 0): pxy, (1, 0, 1): pxz, (0, 1, 1): pyz,
        (2, 2, 0): pxx * syy + 2.0 * pxy * sxy,
        (2, 0, 2): pxx * szz + 2.0 * pxz * sxz,
        (0, 2, 2): pyy * szz + 2.0 * pyz * syz,
        (2, 1, 1): pxx * syz + 2.0 * pxy * sxz,
        (1, 2, 1): pyy * sxz + 2.0 * pxy * syz,
        (1, 1, 2): pzz * sxy + 2.0 * pxz * syz,
        (2, 2, 2): pxx * syy * szz
        + 2.0 * (pxx * syz * syz + pyy * sxz * sxz + pzz * sxy * sxy)
        + 8.0 * pxy * sxz * syz,
    }
    along_z = {}
    for a in range(3):
        for b in range(3):
            parts = backward(*(central.get((a, b, c)) for c in range(3)), uz)
            for k in range(3):
                along_z[a, b, k] = parts[k]
    along_y = {}
    for a in range(3):
        for k in range(3):
            parts = backward(*(along_z[a, b, k] for b in range(3)), uy)
            for j in range(3):
                along_y[a, j, k] = parts[j]
    result = [None] * NQ
    for j in range(3):
        for k in range(3):
            parts = backward(*(along_y[a, j, k] for a in range(3)), ux)
            for i in range(3):
                result[i * 9 + j * 3 + k] = parts[i]
    return result


def unload(plan_ref, ins, block_ref):
    cap = ins[0].shape[0]
    for e in range(len(ins) * cap):
        t = plan_ref[e]

        @pl.when(t >= 0)
        def _():
            block_ref[t] = ins[e // cap][e % cap]


def side_spot(lane, x):
    return (lane // EDGE) == x % SUB


def post_kernel(count, *refs):
    ins = refs[:count]
    (
        post_ref, ylo_ref, yhi_ref, xlo_ref, xhi_ref, plan_ref, side_ref,
        block_ref, swap_ref, tag_ref, sems,
    ) = refs[count:]
    g = pl.program_id(0)
    steps = len(CHUNKS[0])
    lane = lax.broadcasted_iota(jnp.int32, (SUB, LANES), 1)

    @pl.when(g == 0)
    def _():
        tag_at = read_tags(ins, tag_ref, sems)
        for e in range(count * ins[0].shape[0]):
            tag = tag_at(e)
            plan_ref[e] = jnp.where(tag >= 0, lax.rem(tag, SUB), -1)
        unload(plan_ref, ins, block_ref)
        for t in range(SUB):
            for tile in range(SIDE_TILES):
                swap_ref[pl.ds(tile * SUB * SUB + t, SUB, stride=SUB), :] = block_ref[t, tile]
        for half in range(2):
            fields = []
            for n in range(NFIELD):
                base = (1 + half * NFIELD + n) * SUB
                field = swap_ref[base : base + SUB, :]
                side_ref[half, n] = field
                fields.append(field)
            result = post_populations(*fields)
            for i in range(3):
                for k in range(3):
                    value = result[i * 9 + 6 * half + k]
                    for tile in range(2):
                        (yhi_ref if half else ylo_ref)[i * 3 + k, tile] = value

    for t in range(SUB):
        for n in range(NFIELD):
            swap_ref[pl.ds(n * SUB * SUB + t, SUB, stride=SUB), :] = block_ref[
                t, SIDE_TILES + g * NFIELD + n
            ]
    group = CHUNKS[0][0]
    for step in range(1, steps):
        group = jnp.where(g == step, CHUNKS[0][step], group)
    for c in range(SUB):
        fields = [swap_ref[(n * SUB + c) * SUB : (n * SUB + c + 1) * SUB, :] for n in range(NFIELD)]
        result = post_populations(*fields)
        for q in range(NQ):
            post_ref[q, c] = result[q]
        x_in, half = c // 2, c % 2
        x = group * WIDTH + x_in
        inside = side_spot(lane, x)
        face_ref, first, shift = ((ylo_ref, 0, 0), (yhi_ref, 6, EDGE))[half]
        turn = ((x % SUB) * EDGE + shift) % LANES
        for i in range(3):
            for k in range(3):
                value = pltpu.roll(result[i * 9 + first + k], turn, axis=1)
                at = (i * 3 + k, x // SUB)
                face_ref[at] = jnp.where(inside, value, face_ref[at])

        if x_in == 0:

            @pl.when(group == 0)
            def _():
                for q in range(9):
                    xlo_ref[q, half] = result[q]

        if x_in == WIDTH - 1:

            @pl.when(group == GROUPS - 1)
            def _():
                for q in range(9):
                    xhi_ref[q, half] = result[18 + q]


def post(homes):
    shape = jax.ShapeDtypeStruct
    face = (9, 2, SUB, LANES)
    steps = len(CHUNKS[0])
    slots = len(homes) * homes[0].shape[0]
    spec = pl.BlockSpec(face, lambda g: (0, 0, 0, 0))
    return pl.pallas_call(
        functools.partial(post_kernel, len(homes)),
        grid=(steps,),
        in_specs=[pl.BlockSpec(homes[0].shape, lambda g: (0, 0, 0, 0))] * len(homes),
        out_specs=[pl.BlockSpec((NQ, SUB, SUB, LANES), lambda g: (0, g, 0, 0))]
        + [spec] * 4
        + [
            pl.BlockSpec(memory_space=pltpu.SMEM),
            pl.BlockSpec((2, NFIELD, SUB, LANES), lambda g: (0, 0, 0, 0)),
        ],
        scratch_shapes=[
            pltpu.VMEM((SUB, tiles_of(0), SUB, LANES), jnp.float32),
            pltpu.VMEM((NFIELD * SUB * SUB, LANES), jnp.float32),
        ]
        + tag_scratch(len(homes), slots),
        out_shape=[shape((NQ, steps * SUB, SUB, LANES), jnp.float32)]
        + [shape(face, jnp.float32)] * 4
        + [shape((slots,), jnp.int32), shape((2, NFIELD, SUB, LANES), jnp.float32)],
        compiler_params=pltpu.CompilerParams(vmem_limit_bytes=VMEM_LIMIT),
        cost_estimate=pl.CostEstimate(flops=10**7, bytes_accessed=3 * 10**6, transcendentals=0),
        name="post",
    )(*homes)


def finish_kernel(count, plan_ref, *refs):
    ins = refs[:count]
    (
        early_ref, side_ref, xlo_ref, xhi_ref, below_in, above_in,
        out_ref, main_ref, below_ref, above_ref, block_ref, swap_ref, sems,
    ) = refs[count:]
    g = pl.program_id(0)

    @pl.when(g == 0)
    def _():
        copies = [
            pltpu.make_async_copy(
                early_ref.at[:, pl.ds(step * SUB, SUB)],
                main_ref.at[:, pl.ds(group * SUB, SUB)],
                sems.at[step],
            )
            for step, group in enumerate(CHUNKS[0])
        ]
        for copy in copies:
            copy.start()
        unload(plan_ref, ins, block_ref)
        for t in range(SUB):
            for tile in range(LATE_TILES):
                swap_ref[pl.ds(tile * SUB * SUB + t, SUB, stride=SUB), :] = block_ref[t, tile]
        spot = lax.broadcasted_iota(jnp.int32, (SUB, LANES), 1) // EDGE

        def turned(value, places):
            turn = places * EDGE % LANES
            return pltpu.roll(value, turn, axis=1) if turn else value

        for step, group in enumerate(CHUNKS[1]):
            last = [None] * NFIELD
            for c in range(SUB):
                at = (group * WIDTH + c // 2) % SUB
                place = free_place(c)
                fields = []
                for n in range(NFIELD):
                    if c < SUB - 1:
                        base = ((step * NFIELD + n) * (SUB - 1) + c) * SUB
                        row = swap_ref[base : base + SUB, :]
                        part = turned(row, c - place)
                        last[n] = part if c == 0 else jnp.where(spot == c, part, last[n])
                    else:
                        row = last[n]
                    side = turned(side_ref[c % 2, n], place - at)
                    fields.append(jnp.where(spot == place, side, row))
                for q, value in enumerate(post_populations(*fields)):
                    main_ref[q, group * SUB + c] = value
        for x in range(EDGE):
            at = x % SUB
            for k in range(9):
                packed = below_in[k, x // SUB]
                below_ref[k, x + 1] = pltpu.roll(packed, (LANES - EDGE - EDGE * at) % LANES, axis=1)
                packed = above_in[k, x // SUB]
                above_ref[k, x + 1] = pltpu.roll(packed, (LANES - EDGE * at) % LANES, axis=1)
        for k in range(3):
            below_ref[6 + k, 0] = xlo_ref[18 + k]
            above_ref[6 + k, 0] = pltpu.roll(xlo_ref[21 + k], EDGE, axis=1)
            below_ref[k, EDGE + 1] = pltpu.roll(xhi_ref[18 + k], LANES - EDGE, axis=1)
            above_ref[k, EDGE + 1] = xhi_ref[21 + k]
        for copy in copies:
            copy.wait()

    lane = lax.broadcasted_iota(jnp.int32, (SUB, LANES), 1)
    block = lax.broadcasted_iota(jnp.int32, (SUB, LANES), 0)
    along = lane % EDGE
    first_z, last_z = along == 0, along == EDGE - 1
    floor = first_z & (block == 0)
    ceiling = last_z & (block == SUB - 1)
    low_y, high_y = lane < EDGE, lane >= LANES - EDGE

    for x in range(WIDTH):

        def source(q, half):
            at = x - velocity(q)[0]
            row = (g * WIDTH + at) * 2 + half
            if at < 0:
                inside = main_ref[q, jnp.maximum(row, 0)]
                return jnp.where(g == 0, xlo_ref[(q - 18) * 2 + half], inside)
            if at >= WIDTH:
                inside = main_ref[q, jnp.minimum(row, GROUPS * SUB - 1)]
                return jnp.where(g == GROUPS - 1, xhi_ref[q * 2 + half], inside)
            return main_ref[q, row]

        for half in range(2):
            c = x * 2 + half
            for q in range(NQ):
                cx, cy, cz = velocity(q)
                a = source(q, half)
                side = g * WIDTH + x - cx + 1
                k = (cx + 1) * 3 + cz + 1
                if cy == 1:
                    a = jnp.where(high_y, below_ref[k, side] if half == 0 else source(q, 0), a)
                elif cy == -1:
                    a = jnp.where(low_y, above_ref[k, side] if half == 1 else source(q, 1), a)
                shift = EDGE * cy + cz
                value = a if shift == 0 else pltpu.roll(a, shift % LANES, axis=1)
                if cz == 1:
                    fill = pltpu.roll(pltpu.roll(a, 1, axis=0), (shift - EDGE) % LANES, axis=1)
                    value = jnp.where(first_z, fill, value)
                    value = jnp.where(floor, main_ref[26 - q, g * SUB + c], value)
                elif cz == -1:
                    fill = pltpu.roll(pltpu.roll(a, SUB - 1, axis=0), (shift + EDGE) % LANES, axis=1)
                    value = jnp.where(last_z, fill, value)
                    value = jnp.where(ceiling, main_ref[26 - q, g * SUB + c], value)
                out_ref[q, :, c * LANES : (c + 1) * LANES] = value


def finish(plan, homes, early, sides, xlo, xhi, below, above):
    def whole(value):
        rank = len(value.shape)
        return pl.BlockSpec(value.shape, lambda g, *_: (0,) * rank)

    return pl.pallas_call(
        functools.partial(finish_kernel, len(homes)),
        grid_spec=pltpu.PrefetchScalarGridSpec(
            num_scalar_prefetch=1,
            grid=(GROUPS,),
            in_specs=[whole(value) for value in homes]
            + [pl.BlockSpec(memory_space=pl.ANY)]
            + [whole(value) for value in (sides, xlo, xhi, below, above)],
            out_specs=pl.BlockSpec((NQ, SUB, SUB * LANES), lambda g, *_: (0, 0, g)),
            scratch_shapes=[
                pltpu.VMEM((NQ, GROUPS * SUB, SUB, LANES), jnp.float32),
                pltpu.VMEM((9, EDGE + 2, SUB, LANES), jnp.float32),
                pltpu.VMEM((9, EDGE + 2, SUB, LANES), jnp.float32),
                pltpu.VMEM((SUB, LATE_TILES, SUB, LANES), jnp.float32),
                pltpu.VMEM((LATE_TILES * SUB * SUB, LANES), jnp.float32),
                pltpu.SemaphoreType.DMA((len(CHUNKS[0]),)),
            ],
        ),
        out_shape=jax.ShapeDtypeStruct((NQ, SUB, GROUPS * SUB * LANES), jnp.float32),
        compiler_params=pltpu.CompilerParams(vmem_limit_bytes=VMEM_LIMIT),
        cost_estimate=pl.CostEstimate(flops=10**7, bytes_accessed=8 * 10**6, transcendentals=0),
        name="finish",
    )(plan, *homes, early, sides, xlo, xhi, below, above)


def shifted(value, axis, step):
    count = lax.axis_size(axis)
    return lax.ppermute(value, axis, [(i, (i + step) % count) for i in range(count)])


def on_device(populations, destination, refinement):
    blocks = populations.shape[0]
    row_count = lax.axis_size("row")
    col_count = lax.axis_size("col")
    cap_row = 2 * ((blocks + row_count - 1) // row_count)
    cap_col = 2 * ((blocks + col_count - 1) // col_count)
    ordered = jnp.transpose(populations, (1, 0, 2))

    in_row = [
        lax.all_to_all(
            pre(ordered, destination, refinement, part, row_count, cap_row, blocks * col_count),
            "row", split_axis=0, concat_axis=0, tiled=True,
        )
        for part in range(2)
    ]

    def to_columns(packed):
        return [exchanged(packed[d], "col", d) for d in range(col_count - 1, 0, -1)] + [packed[0]]

    packed, plan = repack(in_row[0], None, 0, col_count, cap_col, blocks)
    early, ylo, yhi, xlo, xhi, picked, sides = post(to_columns(packed))
    below, above = shifted(yhi, "col", 1), shifted(ylo, "col", -1)
    up = jnp.concatenate([xhi.reshape(18, SUB, LANES), below[6:, 1], above[6:, 1]])
    down = jnp.concatenate([xlo.reshape(18, SUB, LANES), below[:3, 0], above[:3, 0]])
    xlo, xhi = shifted(up, "row", 1), shifted(down, "row", -1)
    in_row[1], below, above = lax.optimization_barrier((in_row[1], below, above))
    homes = to_columns(repack(in_row[1], plan, 1, col_count, cap_col, blocks))
    return jnp.transpose(finish(picked, homes, early, sides, xlo, xhi, below, above), (1, 0, 2))


def solution(mesh):
    return jax.shard_map(
        on_device,
        mesh=mesh,
        in_specs=(P(("row", "col"), None, None), P(("row", "col")), P(("row", "col"))),
        out_specs=P(("row", "col"), None, None),
        check_vma=False,
    )
```

```python
import functools

import jax
import jax.numpy as jnp
from jax import lax
from jax.experimental import pallas as pl
from jax.experimental.pallas import tpu as pltpu
from jax.sharding import PartitionSpec as P

EDGE = 16
VISCOSITY = 0.01
LANES = 128
SUB = 8
NQ = 27
NFIELD = 9
GROUPS = 4
WIDTH = EDGE // GROUPS
CHUNKS = ((0, 3), (1,), (2,))
INNER = (1, 2)
SIDE_TILES = 3
LATE_TILES = -(-NFIELD * (SUB - 1) // SUB)
VMEM_LIMIT = 20 * 1024 * 1024
LARGE_VMEM_LIMIT = 60 * 1024 * 1024


def velocity(q):
    return (q // 9 - 1, (q // 3) % 3 - 1, q % 3 - 1)


def tiles_of(part):
    return LATE_TILES if part else len(CHUNKS[0]) * NFIELD + SIDE_TILES


def free_place(c):
    return (c % 2) * (SUB - 1)


def step_to(target, here, count):
    if count & (count - 1) == 0:
        return target ^ here
    return lax.rem(target - here + count, count)


def exchanged(value, axis, step):
    count = lax.axis_size(axis)
    if count & (count - 1) == 0:
        pairs = [(i, i ^ step) for i in range(count)]
    else:
        pairs = [(i, (i + step) % count) for i in range(count)]
    return lax.ppermute(value, axis, pairs)


def raw_moments(f):
    whole, slope, outer = {}, {}, {}
    for i in range(3):
        for j in range(3):
            low, rest, high = (f[i * 9 + j * 3 + k] for k in range(3))
            outer[i, j] = low + high
            whole[i, j] = outer[i, j] + rest
            slope[i, j] = high - low
    column = [whole[i, 0] + whole[i, 1] + whole[i, 2] for i in range(3)]
    tilt = [slope[i, 0] + slope[i, 1] + slope[i, 2] for i in range(3)]
    low_y = whole[0, 0] + whole[1, 0] + whole[2, 0]
    high_y = whole[0, 2] + whole[1, 2] + whole[2, 2]
    ends = column[0] + column[2]
    mzz = sum(outer[i, j] for i in range(3) for j in range(3))
    mxy = (whole[2, 2] - whole[2, 0]) - (whole[0, 2] - whole[0, 0])
    myz = (slope[0, 2] + slope[1, 2] + slope[2, 2]) - (slope[0, 0] + slope[1, 0] + slope[2, 0])
    return (
        ends + column[1],
        column[2] - column[0],
        high_y - low_y,
        tilt[0] + tilt[1] + tilt[2],
        ends,
        low_y + high_y,
        mzz,
        mxy,
        tilt[2] - tilt[0],
        myz,
    )


def collided(f, keep):
    rho, jx, jy, jz, mxx, myy, mzz, mxy, mxz, myz = raw_moments(f)
    inverse = 1.0 / rho
    ux, uy, uz = jx * inverse, jy * inverse, jz * inverse
    kxx = mxx - jx * ux
    return (
        rho, ux, uy, uz,
        keep * (mxy - jx * uy),
        keep * (mxz - jx * uz),
        keep * (myz - jy * uz),
        keep * (kxx - (myy - jy * uy)),
        keep * (kxx - (mzz - jz * uz)),
    )


def pre_kernel(cap, row_count, per_row, part, dest_hbm, level_hbm, x_hbm, out_ref, *refs):
    x_ref, swap_ref, packed_ref, side_ref, dest_ref, level_ref, sems = refs
    order = CHUNKS[part] if part else CHUNKS[0] + INNER
    steps = len(CHUNKS[part])
    blocks = x_ref.shape[2]
    cells = x_ref.shape[3]
    chunks = cells // LANES
    small = [
        pltpu.make_async_copy(dest_hbm, dest_ref, sems.at[0]),
        pltpu.make_async_copy(level_hbm, level_ref, sems.at[1]),
    ]
    large = [
        pltpu.make_async_copy(
            x_hbm.at[:, :, pl.ds(group * cells, cells)], x_ref.at[step], sems.at[2 + step]
        )
        for step, group in enumerate(order)
    ]
    for copy in small + large:
        copy.start()
    for copy in small:
        copy.wait()

    which = lax.broadcasted_iota(jnp.int32, (SUB, LANES), 0)
    spot = lax.broadcasted_iota(jnp.int32, (SUB, LANES), 1) // EDGE
    scale = jnp.zeros((SUB, LANES), jnp.int32)
    tag = jnp.zeros((SUB, LANES), jnp.int32)
    for t in range(blocks):
        scale = jnp.where(which == t, jnp.left_shift(1, level_ref[t]), scale)
        tag = jnp.where(which == t, dest_ref[t], tag)
    rate = 1.0 / (3.0 * VISCOSITY * scale.astype(jnp.float32) + 0.5)
    keep = 1.0 - rate

    rows = [dest_ref[t] // per_row for t in range(blocks)]
    slots = []
    for t in range(blocks):
        slot = rows[t] * cap
        for other in range(t):
            slot = slot + jnp.where(rows[other] == rows[t], 1, 0)
        slots.append(slot)

    def spread(ref, first, count):
        for t in range(blocks):
            for n in range(count):
                moved = ref[pl.ds(n * SUB * SUB + t, SUB, stride=SUB), :]
                out_ref[slots[t], first + n] = moved

    def fields_at(step, c):
        return collided([x_ref[step, q, :, c * LANES : (c + 1) * LANES] for q in range(NQ)], keep)

    for step, group in enumerate(order):
        large[step].wait()
        if part:
            last = fields_at(step, chunks - 1)
            for c in range(chunks - 1):
                place = free_place(c)
                turn = (place - c) * EDGE % LANES
                for n, field in enumerate(fields_at(step, c)):
                    other = pltpu.roll(last[n], turn, axis=1) if turn else last[n]
                    base = ((step * NFIELD + n) * (chunks - 1) + c) * SUB
                    swap_ref[base : base + SUB, :] = jnp.where(spot == place, other, field)
            continue
        if step < steps:
            for c in range(chunks):
                for n, field in enumerate(fields_at(step, c)):
                    base = (n * chunks + c) * SUB
                    swap_ref[base : base + SUB, :] = field
            spread(swap_ref, SIDE_TILES + step * NFIELD, NFIELD)
            continue
        for q in range(NQ):
            for half in range(2):
                value = packed_ref[half * NQ + q] if step > steps else None
                for x in range(WIDTH):
                    c = x * 2 + half
                    at = (group * WIDTH + x) % SUB
                    moved = x_ref[step, q, :, c * LANES : (c + 1) * LANES]
                    turn = (at + half) * EDGE % LANES
                    if turn:
                        moved = pltpu.roll(moved, turn, axis=1)
                    value = moved if value is None else jnp.where(spot == at, moved, value)
                packed_ref[half * NQ + q] = value

    if part:
        for row in range(steps * NFIELD * (chunks - 1), LATE_TILES * SUB):
            swap_ref[row * SUB : (row + 1) * SUB, :] = tag.astype(jnp.float32)
        spread(swap_ref, 0, LATE_TILES)
        return
    for row in range(SIDE_TILES * SUB):
        if not 1 <= row <= 2 * NFIELD:
            side_ref[row * SUB : (row + 1) * SUB, :] = tag.astype(jnp.float32)
    for half in range(2):
        fields = collided([packed_ref[half * NQ + q] for q in range(NQ)], keep)
        for n, field in enumerate(fields):
            base = (1 + half * NFIELD + n) * SUB
            side_ref[base : base + SUB, :] = field
    for slot in range(row_count * cap):
        out_ref[slot, 0] = jnp.full((SUB, LANES), -1.0, jnp.float32)
    spread(side_ref, 0, SIDE_TILES)


def pre(populations, destination, refinement, part, row_count, cap, per_row):
    blocks = populations.shape[1]
    cells = populations.shape[2] // GROUPS
    loaded = len(CHUNKS[part]) + (0 if part else len(INNER))
    rows = LATE_TILES * SUB if part else NFIELD * cells // LANES
    return pl.pallas_call(
        functools.partial(pre_kernel, cap, row_count, per_row, part),
        in_specs=[pl.BlockSpec(memory_space=pltpu.HBM)] * 3,
        out_specs=pl.BlockSpec(memory_space=pltpu.VMEM),
        out_shape=jax.ShapeDtypeStruct((row_count * cap, tiles_of(part), SUB, LANES), jnp.float32),
        scratch_shapes=[
            pltpu.VMEM((loaded, NQ, blocks, cells), jnp.float32),
            pltpu.VMEM((rows * SUB, LANES), jnp.float32),
            pltpu.VMEM((2 * NQ, SUB, LANES), jnp.float32),
            pltpu.VMEM((SIDE_TILES * SUB * SUB, LANES), jnp.float32),
            pltpu.SMEM((blocks,), jnp.int32),
            pltpu.SMEM((blocks,), jnp.int32),
            pltpu.SemaphoreType.DMA((2 + loaded,)),
        ],
        compiler_params=pltpu.CompilerParams(vmem_limit_bytes=LARGE_VMEM_LIMIT),
        cost_estimate=pl.CostEstimate(flops=10**7, bytes_accessed=4 * 10**6, transcendentals=0),
        name="pre_%d" % part,
    )(destination, refinement, populations)


def read_tags(ins, tag_ref, sems):
    cap = ins[0].shape[0]
    copies = [
        pltpu.make_async_copy(in_ref.at[:, 0, pl.ds(0, 1)], tag_ref.at[pl.ds(d * cap, cap)], sems.at[d])
        for d, in_ref in enumerate(ins)
    ]
    for copy in copies:
        copy.start()
    for copy in copies:
        copy.wait()
    return lambda e: tag_ref[e, 0, 0].astype(jnp.int32)


def tag_scratch(arrays, slots):
    return [pltpu.SMEM((slots, 1, LANES), jnp.float32), pltpu.SemaphoreType.DMA((arrays,))]


def repack_kernel(cap, col_count, blocks, part, *refs):
    if part:
        plan_ref, in_ref, *outs = refs
    else:
        in_ref, *outs, plan_ref, tag_ref, sems, count_ref = refs
        tag_at = read_tags([in_ref], tag_ref, sems)
        here = lax.axis_index("col")
        for d in range(col_count):
            count_ref[d] = 0
        for e in range(col_count * cap):
            plan_ref[e] = -1
        for e in range(in_ref.shape[0]):
            tag = tag_at(e)

            @pl.when(tag >= 0)
            def _():
                d = step_to(lax.rem(tag // blocks, col_count), here, col_count)
                k = count_ref[d]
                count_ref[d] = k + 1
                plan_ref[d * cap + k] = e

    for d, out in enumerate(outs):
        for k in range(cap):
            e = plan_ref[d * cap + k]

            @pl.when(e >= 0)
            def _():
                out[k] = in_ref[e]

            if part == 0:

                @pl.when(e < 0)
                def _():
                    out[k, 0] = jnp.full((SUB, LANES), -1.0, jnp.float32)


def repack(landed, plan, part, col_count, cap, blocks):
    whole = pl.BlockSpec(memory_space=pltpu.VMEM)
    scalars = pl.BlockSpec(memory_space=pltpu.SMEM)
    scratch = []
    if part == 0:
        scratch = tag_scratch(1, landed.shape[0]) + [pltpu.SMEM((col_count,), jnp.int32)]
    packed = pl.pallas_call(
        functools.partial(repack_kernel, cap, col_count, blocks, part),
        in_specs=([scalars] if part else []) + [whole],
        out_specs=[whole] * col_count + ([] if part else [scalars]),
        scratch_shapes=scratch,
        out_shape=[jax.ShapeDtypeStruct((cap,) + landed.shape[1:], jnp.float32)] * col_count
        + ([] if part else [jax.ShapeDtypeStruct((col_count * cap,), jnp.int32)]),
        compiler_params=pltpu.CompilerParams(vmem_limit_bytes=VMEM_LIMIT),
        cost_estimate=pl.CostEstimate(flops=0, bytes_accessed=3 * 10**6, transcendentals=0),
        name="repack_%d" % part,
    )(*([plan] if part else []), landed)
    return packed if part else (packed[:-1], packed[-1])


def backward(zeroth, first, second, u):
    raw_one, raw_two = first, second
    if zeroth is not None:
        moved = u * zeroth
        raw_one = moved if raw_one is None else raw_one + moved
        square = u * moved
        raw_two = square if raw_two is None else raw_two + square
    if first is not None:
        cross = (u + u) * first
        raw_two = cross if raw_two is None else raw_two + cross
    rest = -raw_two if zeroth is None else zeroth - raw_two
    return 0.5 * (raw_two - raw_one), rest, 0.5 * (raw_one + raw_two)


def post_populations(rho, ux, uy, uz, pxy, pxz, pyz, dev_one, dev_two):
    inverse = 1.0 / rho
    pxx = (rho + dev_one + dev_two) * (1.0 / 3.0)
    pyy = pxx - dev_one
    pzz = pxx - dev_two
    sxy, sxz, syz = pxy * inverse, pxz * inverse, pyz * inverse
    syy, szz = pyy * inverse, pzz * inverse
    central = {
        (0, 0, 0): rho, (2, 0, 0): pxx, (0, 2, 0): pyy, (0, 0, 2): pzz,
        (1, 1, 0): pxy, (1, 0, 1): pxz, (0, 1, 1): pyz,
        (2, 2, 0): pxx * syy + 2.0 * pxy * sxy,
        (2, 0, 2): pxx * szz + 2.0 * pxz * sxz,
        (0, 2, 2): pyy * szz + 2.0 * pyz * syz,
        (2, 1, 1): pxx * syz + 2.0 * pxy * sxz,
        (1, 2, 1): pyy * sxz + 2.0 * pxy * syz,
        (1, 1, 2): pzz * sxy + 2.0 * pxz * syz,
        (2, 2, 2): pxx * syy * szz
        + 2.0 * (pxx * syz * syz + pyy * sxz * sxz + pzz * sxy * sxy)
        + 8.0 * pxy * sxz * syz,
    }
    along_z = {}
    for a in range(3):
        for b in range(3):
            parts = backward(*(central.get((a, b, c)) for c in range(3)), uz)
            for k in range(3):
                along_z[a, b, k] = parts[k]
    along_y = {}
    for a in range(3):
        for k in range(3):
            parts = backward(*(along_z[a, b, k] for b in range(3)), uy)
            for j in range(3):
                along_y[a, j, k] = parts[j]
    result = [None] * NQ
    for j in range(3):
        for k in range(3):
            parts = backward(*(along_y[a, j, k] for a in range(3)), ux)
            for i in range(3):
                result[i * 9 + j * 3 + k] = parts[i]
    return result


def unload(plan_ref, ins, fields_ref):
    cap, tiles = ins[0].shape[:2]
    for e in range(len(ins) * cap):
        t = plan_ref[e]

        @pl.when(t >= 0)
        def _():
            for tile in range(tiles):
                fields_ref[pl.ds(tile * SUB * SUB + t, SUB, stride=SUB), :] = ins[e // cap][e % cap, tile]


def row_of(ref, row):
    return ref[row * SUB : (row + 1) * SUB, :]


def turned(value, places):
    turn = places * EDGE % LANES
    return pltpu.roll(value, turn, axis=1) if turn else value


def places_y():
    return lax.broadcasted_iota(jnp.int32, (SUB, LANES), 1) // EDGE


def outer_fields(fields_ref, step, c):
    first = (SIDE_TILES + step * NFIELD) * SUB
    return [row_of(fields_ref, first + n * SUB + c) for n in range(NFIELD)]


def side_fields(fields_ref, half):
    return [row_of(fields_ref, 1 + half * NFIELD + n) for n in range(NFIELD)]


def fill_outer(fields_ref, main_ref):
    for step, group in enumerate(CHUNKS[0]):
        for c in range(SUB):
            for q, value in enumerate(post_populations(*outer_fields(fields_ref, step, c))):
                main_ref[q, 2 + group * SUB + c] = value


def fill_inner(fields_ref, late_ref, group, main_ref):
    spot = places_y()
    last = [None] * NFIELD
    for c in range(SUB):
        at = (group * WIDTH + c // 2) % SUB
        place = free_place(c)
        side = side_fields(fields_ref, c % 2)
        fields = []
        for n in range(NFIELD):
            if c < SUB - 1:
                row = row_of(late_ref, n * (SUB - 1) + c)
                part = turned(row, c - place)
                last[n] = part if c == 0 else jnp.where(spot == c, part, last[n])
            else:
                row = last[n]
            fields.append(jnp.where(spot == place, turned(side[n], place - at), row))
        for q, value in enumerate(post_populations(*fields)):
            main_ref[q, 2 + group * SUB + c] = value


def fill_sides(below_in, above_in, below_ref, above_ref, first, last):
    for x in range(first, last):
        at = x % SUB
        for k in range(9):
            below_ref[k, x + 1] = turned(below_in[k, x // SUB], SUB - 1 - at)
            above_ref[k, x + 1] = turned(above_in[k, x // SUB], -at)


def stream_pair(first_x, out_ref, main_ref, below_ref, above_ref):
    lane = lax.broadcasted_iota(jnp.int32, (SUB, LANES), 1)
    block = lax.broadcasted_iota(jnp.int32, (SUB, LANES), 0)
    along = lane % EDGE
    first_z, last_z = along == 0, along == EDGE - 1
    floor = first_z & (block == 0)
    ceiling = last_z & (block == SUB - 1)
    low_y, high_y = lane < EDGE, lane >= LANES - EDGE
    for i in range(2):
        for half in range(2):
            c = i * 2 + half
            for q in range(NQ):
                cx, cy, cz = velocity(q)
                x = first_x + i - cx + 1
                a = main_ref[q, x * 2 + half]
                k = (cx + 1) * 3 + cz + 1
                if cy == 1:
                    a = jnp.where(high_y, main_ref[q, x * 2] if half else below_ref[k, x], a)
                elif cy == -1:
                    a = jnp.where(low_y, above_ref[k, x] if half else main_ref[q, x * 2 + 1], a)
                shift = EDGE * cy + cz
                value = a if shift == 0 else pltpu.roll(a, shift % LANES, axis=1)
                if cz:
                    bounced = main_ref[26 - q, (first_x + i + 1) * 2 + half]
                    turn = (1 if cz == 1 else SUB - 1)
                    fill = pltpu.roll(pltpu.roll(a, turn, axis=0), (shift - cz * EDGE) % LANES, axis=1)
                    value = jnp.where(first_z if cz == 1 else last_z, fill, value)
                    value = jnp.where(floor if cz == 1 else ceiling, bounced, value)
                out_ref[q, :, c * LANES : (c + 1) * LANES] = value


def faces_kernel(count, *refs):
    ins = refs[:count]
    ylo_ref, yhi_ref, xlo_ref, xhi_ref, plan_ref, fields_ref, tag_ref, sems = refs[count:]
    tag_at = read_tags(ins, tag_ref, sems)
    for e in range(count * ins[0].shape[0]):
        tag = tag_at(e)
        plan_ref[e] = jnp.where(tag >= 0, lax.rem(tag, SUB), -1)
    unload(plan_ref, ins, fields_ref)
    spot = places_y()
    for half in range(2):
        packed = [side_fields(fields_ref, half)] * 2
        place = half * (SUB - 1)
        for step, group in enumerate(CHUNKS[0]):
            tile = group * WIDTH // SUB
            for x in range(group * WIDTH, (group + 1) * WIDTH):
                c = (x - group * WIDTH) * 2 + half
                packed[tile] = [
                    jnp.where(spot == x % SUB, turned(value, x % SUB - place), old)
                    for value, old in zip(outer_fields(fields_ref, step, c), packed[tile])
                ]
        for tile in range(2):
            result = post_populations(*packed[tile])
            for i in range(3):
                for k in range(3):
                    (yhi_ref if half else ylo_ref)[i * 3 + k, tile] = result[i * 9 + half * 6 + k]
        low = post_populations(*outer_fields(fields_ref, CHUNKS[0].index(0), half))
        high = post_populations(*outer_fields(fields_ref, CHUNKS[0].index(GROUPS - 1), SUB - 2 + half))
        for q in range(9):
            xlo_ref[q, half] = low[q]
            xhi_ref[q, half] = high[18 + q]


def faces(homes):
    shape = jax.ShapeDtypeStruct
    face = shape((9, 2, SUB, LANES), jnp.float32)
    slots = len(homes) * homes[0].shape[0]
    whole = pl.BlockSpec(memory_space=pltpu.VMEM)
    return pl.pallas_call(
        functools.partial(faces_kernel, len(homes)),
        in_specs=[whole] * len(homes),
        out_specs=[whole] * 4 + [pl.BlockSpec(memory_space=pltpu.SMEM), whole],
        scratch_shapes=tag_scratch(len(homes), slots),
        out_shape=[face] * 4
        + [shape((slots,), jnp.int32), shape((tiles_of(0) * SUB * SUB, LANES), jnp.float32)],
        compiler_params=pltpu.CompilerParams(vmem_limit_bytes=VMEM_LIMIT),
        cost_estimate=pl.CostEstimate(flops=10**7, bytes_accessed=3 * 10**6, transcendentals=0),
        name="faces",
    )(*homes)


PAIRS = ((0, 1, 2, 7), (3, 4, 5, 6))
KEPT = ((5, 8), (12, 15))


def advance_kernel(count, plan_ref, *refs):
    ins = refs[:count]
    (
        fields_ref, xlo_ref, xhi_ref, below_in, above_in, out_ref, kept_ref,
        main_ref, below_ref, above_ref, late_ref,
    ) = refs[count:]
    g = pl.program_id(0)

    @pl.when(g == 0)
    def _():
        unload(plan_ref, ins, late_ref)
        fill_outer(fields_ref, main_ref)
        fill_inner(fields_ref, late_ref, CHUNKS[1][0], main_ref)
        fill_sides(below_in, above_in, below_ref, above_ref, 0, 7)
        fill_sides(below_in, above_in, below_ref, above_ref, 13, EDGE)
        for k in range(3):
            below_ref[6 + k, 0] = xlo_ref[18 + k]
            above_ref[6 + k, 0] = turned(xlo_ref[21 + k], 1)
            below_ref[k, EDGE + 1] = turned(xhi_ref[18 + k], -1)
            above_ref[k, EDGE + 1] = xhi_ref[21 + k]
        for q in range(9):
            for half in range(2):
                main_ref[18 + q, half] = xlo_ref[q * 2 + half]
                main_ref[q, 2 * EDGE + 2 + half] = xhi_ref[q * 2 + half]
        to = 0
        for first, last in KEPT:
            for row in range(2 * first + 2, 2 * last + 2):
                for q in range(NQ):
                    kept_ref[q, to] = main_ref[q, row]
                to += 1

    first_x = 2 * jnp.where(g == len(PAIRS[0]) - 1, PAIRS[0][-1], g)
    stream_pair(first_x, out_ref, main_ref, below_ref, above_ref)


def finish_kernel(count, plan_ref, *refs):
    ins = refs[:count]
    (
        fields_ref, kept_ref, below_in, above_in, _, out_ref,
        main_ref, below_ref, above_ref, late_ref, sems,
    ) = refs[count:]
    g = pl.program_id(0)

    @pl.when(g == 0)
    def _():
        copies = []
        to = 0
        for first, last in KEPT:
            rows = 2 * (last - first)
            copies.append(
                pltpu.make_async_copy(
                    kept_ref.at[:, pl.ds(to, rows)],
                    main_ref.at[:, pl.ds(2 * first + 2, rows)],
                    sems.at[len(copies)],
                )
            )
            to += rows
        for copy in copies:
            copy.start()
        unload(plan_ref, ins, late_ref)
        fill_inner(fields_ref, late_ref, CHUNKS[2][0], main_ref)
        fill_sides(below_in, above_in, below_ref, above_ref, 5, 15)
        for copy in copies:
            copy.wait()

    stream_pair(2 * (PAIRS[1][0] + g), out_ref, main_ref, below_ref, above_ref)


def whole_of(value):
    rank = len(value.shape)
    return pl.BlockSpec(value.shape, lambda g, *_: (0,) * rank)


def scratch_of_lattice():
    side = pltpu.VMEM((9, EDGE + 2, SUB, LANES), jnp.float32)
    return [
        pltpu.VMEM((NQ, 2 * EDGE + 4, SUB, LANES), jnp.float32), side, side,
        pltpu.VMEM((LATE_TILES * SUB * SUB, LANES), jnp.float32),
    ]


def advance(plan, homes, fields, xlo, xhi, below, above):
    pairs = PAIRS[0]
    inputs = [*homes, fields, xlo, xhi, below, above]
    kept = jax.ShapeDtypeStruct(
        (NQ, 2 * sum(last - first for first, last in KEPT), SUB, LANES), jnp.float32
    )
    return pl.pallas_call(
        functools.partial(advance_kernel, len(homes)),
        grid_spec=pltpu.PrefetchScalarGridSpec(
            num_scalar_prefetch=1,
            grid=(len(pairs),),
            in_specs=[whole_of(value) for value in inputs],
            out_specs=[
                pl.BlockSpec(
                    (NQ, SUB, 4 * LANES),
                    lambda g, *_: (0, 0, jnp.where(g == len(pairs) - 1, pairs[-1], g)),
                ),
                whole_of(kept),
            ],
            scratch_shapes=scratch_of_lattice(),
        ),
        out_shape=[jax.ShapeDtypeStruct((NQ, SUB, GROUPS * SUB * LANES), jnp.float32), kept],
        compiler_params=pltpu.CompilerParams(vmem_limit_bytes=LARGE_VMEM_LIMIT),
        cost_estimate=pl.CostEstimate(flops=10**7, bytes_accessed=5 * 10**6, transcendentals=0),
        name="advance",
    )(plan, *inputs)


def finish(plan, homes, fields, kept, below, above, out):
    pairs = PAIRS[1]
    anywhere = pl.BlockSpec(memory_space=pl.ANY)
    return pl.pallas_call(
        functools.partial(finish_kernel, len(homes)),
        grid_spec=pltpu.PrefetchScalarGridSpec(
            num_scalar_prefetch=1,
            grid=(len(pairs),),
            in_specs=[whole_of(value) for value in (*homes, fields)]
            + [anywhere, whole_of(below), whole_of(above), anywhere],
            out_specs=pl.BlockSpec((NQ, SUB, 4 * LANES), lambda g, *_: (0, 0, pairs[0] + g)),
            scratch_shapes=scratch_of_lattice() + [pltpu.SemaphoreType.DMA((len(KEPT),))],
        ),
        out_shape=jax.ShapeDtypeStruct(out.shape, jnp.float32),
        input_output_aliases={len(homes) + 5: 0},
        compiler_params=pltpu.CompilerParams(vmem_limit_bytes=VMEM_LIMIT),
        cost_estimate=pl.CostEstimate(flops=10**7, bytes_accessed=5 * 10**6, transcendentals=0),
        name="finish",
    )(plan, *homes, fields, kept, below, above, out)


def shifted(value, axis, step):
    count = lax.axis_size(axis)
    return lax.ppermute(value, axis, [(i, (i + step) % count) for i in range(count)])


def on_device(populations, destination, refinement):
    blocks = populations.shape[0]
    row_count = lax.axis_size("row")
    col_count = lax.axis_size("col")
    cap_row = 2 * ((blocks + row_count - 1) // row_count)
    cap_col = 2 * ((blocks + col_count - 1) // col_count)
    ordered = jnp.transpose(populations, (1, 0, 2))

    in_row = [
        lax.all_to_all(
            pre(ordered, destination, refinement, part, row_count, cap_row, blocks * col_count),
            "row", split_axis=0, concat_axis=0, tiled=True,
        )
        for part in range(len(CHUNKS))
    ]

    def to_columns(packed):
        return [exchanged(packed[d], "col", d) for d in range(col_count - 1, 0, -1)] + [packed[0]]

    packed, plan = repack(in_row[0], None, 0, col_count, cap_col, blocks)
    ylo, yhi, xlo, xhi, picked, fields = faces(to_columns(packed))
    below, above = shifted(yhi, "col", 1), shifted(ylo, "col", -1)
    up = jnp.concatenate([xhi.reshape(18, SUB, LANES), below[6:, 1], above[6:, 1]])
    down = jnp.concatenate([xlo.reshape(18, SUB, LANES), below[:3, 0], above[:3, 0]])
    xlo, xhi = shifted(up, "row", 1), shifted(down, "row", -1)
    middle = to_columns(repack(in_row[1], plan, 1, col_count, cap_col, blocks))
    packed = repack(in_row[2], plan, 2, col_count, cap_col, blocks)
    picked, packed = lax.optimization_barrier((picked, list(packed)))
    last = to_columns(packed)
    out, kept = advance(picked, middle, fields, xlo, xhi, below, above)
    return jnp.transpose(finish(picked, last, fields, kept, below, above, out), (1, 0, 2))


def solution(mesh):
    return jax.shard_map(
        on_device,
        mesh=mesh,
        in_specs=(P(("row", "col"), None, None), P(("row", "col")), P(("row", "col"))),
        out_specs=P(("row", "col"), None, None),
        check_vma=False,
    )
```

```python
import functools

import jax
import jax.numpy as jnp
from jax import lax
from jax.experimental import pallas as pl
from jax.experimental.pallas import tpu as pltpu
from jax.sharding import PartitionSpec as P

EDGE = 16
VISCOSITY = 0.01
LANES = 128
SUB = 8
NQ = 27
NFIELD = 9
GROUPS = 4
WIDTH = EDGE // GROUPS
CHUNKS = ((0, 3), (1,), (2,))
INNER = (1, 2)
SIDE_TILES = 3
LATE_TILES = -(-NFIELD * (SUB - 1) // SUB)
VMEM_LIMIT = 20 * 1024 * 1024
LARGE_VMEM_LIMIT = 60 * 1024 * 1024


def velocity(q):
    return (q // 9 - 1, (q // 3) % 3 - 1, q % 3 - 1)


def tiles_of(part):
    return LATE_TILES if part else len(CHUNKS[0]) * NFIELD + SIDE_TILES


def free_place(c):
    return (c % 2) * (SUB - 1)


def step_to(target, here, count):
    if count & (count - 1) == 0:
        return target ^ here
    return lax.rem(target - here + count, count)


def exchanged(value, axis, step):
    count = lax.axis_size(axis)
    if count & (count - 1) == 0:
        pairs = [(i, i ^ step) for i in range(count)]
    else:
        pairs = [(i, (i + step) % count) for i in range(count)]
    return lax.ppermute(value, axis, pairs)


def raw_moments(f):
    whole, slope, outer = {}, {}, {}
    for i in range(3):
        for j in range(3):
            low, rest, high = (f[i * 9 + j * 3 + k] for k in range(3))
            outer[i, j] = low + high
            whole[i, j] = outer[i, j] + rest
            slope[i, j] = high - low
    column = [whole[i, 0] + whole[i, 1] + whole[i, 2] for i in range(3)]
    tilt = [slope[i, 0] + slope[i, 1] + slope[i, 2] for i in range(3)]
    low_y = whole[0, 0] + whole[1, 0] + whole[2, 0]
    high_y = whole[0, 2] + whole[1, 2] + whole[2, 2]
    ends = column[0] + column[2]
    mzz = sum(outer[i, j] for i in range(3) for j in range(3))
    mxy = (whole[2, 2] - whole[2, 0]) - (whole[0, 2] - whole[0, 0])
    myz = (slope[0, 2] + slope[1, 2] + slope[2, 2]) - (slope[0, 0] + slope[1, 0] + slope[2, 0])
    return (
        ends + column[1],
        column[2] - column[0],
        high_y - low_y,
        tilt[0] + tilt[1] + tilt[2],
        ends,
        low_y + high_y,
        mzz,
        mxy,
        tilt[2] - tilt[0],
        myz,
    )


def collided(f, keep):
    rho, jx, jy, jz, mxx, myy, mzz, mxy, mxz, myz = raw_moments(f)
    inverse = 1.0 / rho
    ux, uy, uz = jx * inverse, jy * inverse, jz * inverse
    kxx = mxx - jx * ux
    return (
        rho, ux, uy, uz,
        keep * (mxy - jx * uy),
        keep * (mxz - jx * uz),
        keep * (myz - jy * uz),
        keep * (kxx - (myy - jy * uy)),
        keep * (kxx - (mzz - jz * uz)),
    )


def pre_kernel(cap, row_count, per_row, part, dest_hbm, level_hbm, x_hbm, out_ref, *refs):
    x_ref, swap_ref, packed_ref, side_ref, dest_ref, level_ref, sems = refs
    order = CHUNKS[part] if part else CHUNKS[0] + INNER
    steps = len(CHUNKS[part])
    blocks = x_ref.shape[2]
    cells = x_ref.shape[3]
    chunks = cells // LANES
    small = [
        pltpu.make_async_copy(dest_hbm, dest_ref, sems.at[0]),
        pltpu.make_async_copy(level_hbm, level_ref, sems.at[1]),
    ]
    large = [
        pltpu.make_async_copy(
            x_hbm.at[:, :, pl.ds(group * cells, cells)], x_ref.at[step], sems.at[2 + step]
        )
        for step, group in enumerate(order)
    ]
    for copy in small + large:
        copy.start()
    for copy in small:
        copy.wait()

    which = lax.broadcasted_iota(jnp.int32, (SUB, LANES), 0)
    spot = lax.broadcasted_iota(jnp.int32, (SUB, LANES), 1) // EDGE
    scale = jnp.zeros((SUB, LANES), jnp.int32)
    tag = jnp.zeros((SUB, LANES), jnp.int32)
    for t in range(blocks):
        scale = jnp.where(which == t, jnp.left_shift(1, level_ref[t]), scale)
        tag = jnp.where(which == t, dest_ref[t], tag)
    rate = 1.0 / (3.0 * VISCOSITY * scale.astype(jnp.float32) + 0.5)
    keep = 1.0 - rate

    rows = [dest_ref[t] // per_row for t in range(blocks)]
    slots = []
    for t in range(blocks):
        slot = rows[t] * cap
        for other in range(t):
            slot = slot + jnp.where(rows[other] == rows[t], 1, 0)
        slots.append(slot)

    def spread(ref, first, count):
        for t in range(blocks):
            for n in range(count):
                moved = ref[pl.ds(n * SUB * SUB + t, SUB, stride=SUB), :]
                out_ref[slots[t], first + n] = moved

    def fields_at(step, c):
        return collided([x_ref[step, q, :, c * LANES : (c + 1) * LANES] for q in range(NQ)], keep)

    for step, group in enumerate(order):
        large[step].wait()
        if part:
            last = fields_at(step, chunks - 1)
            for c in range(chunks - 1):
                place = free_place(c)
                turn = (place - c) * EDGE % LANES
                for n, field in enumerate(fields_at(step, c)):
                    other = pltpu.roll(last[n], turn, axis=1) if turn else last[n]
                    base = ((step * NFIELD + n) * (chunks - 1) + c) * SUB
                    swap_ref[base : base + SUB, :] = jnp.where(spot == place, other, field)
            continue
        if step < steps:
            for c in range(chunks):
                for n, field in enumerate(fields_at(step, c)):
                    base = (n * chunks + c) * SUB
                    swap_ref[base : base + SUB, :] = field
            spread(swap_ref, SIDE_TILES + step * NFIELD, NFIELD)
            continue
        for q in range(NQ):
            for half in range(2):
                value = packed_ref[half * NQ + q] if step > steps else None
                for x in range(WIDTH):
                    c = x * 2 + half
                    at = (group * WIDTH + x) % SUB
                    moved = x_ref[step, q, :, c * LANES : (c + 1) * LANES]
                    turn = (at + half) * EDGE % LANES
                    if turn:
                        moved = pltpu.roll(moved, turn, axis=1)
                    value = moved if value is None else jnp.where(spot == at, moved, value)
                packed_ref[half * NQ + q] = value

    if part:
        for row in range(steps * NFIELD * (chunks - 1), LATE_TILES * SUB):
            swap_ref[row * SUB : (row + 1) * SUB, :] = tag.astype(jnp.float32)
        spread(swap_ref, 0, LATE_TILES)
        return
    for row in range(SIDE_TILES * SUB):
        if not 1 <= row <= 2 * NFIELD:
            side_ref[row * SUB : (row + 1) * SUB, :] = tag.astype(jnp.float32)
    for half in range(2):
        fields = collided([packed_ref[half * NQ + q] for q in range(NQ)], keep)
        for n, field in enumerate(fields):
            base = (1 + half * NFIELD + n) * SUB
            side_ref[base : base + SUB, :] = field
    for slot in range(row_count * cap):
        out_ref[slot, 0] = jnp.full((SUB, LANES), -1.0, jnp.float32)
    spread(side_ref, 0, SIDE_TILES)


def pre(populations, destination, refinement, part, row_count, cap, per_row):
    blocks = populations.shape[1]
    cells = populations.shape[2] // GROUPS
    loaded = len(CHUNKS[part]) + (0 if part else len(INNER))
    rows = LATE_TILES * SUB if part else NFIELD * cells // LANES
    return pl.pallas_call(
        functools.partial(pre_kernel, cap, row_count, per_row, part),
        in_specs=[pl.BlockSpec(memory_space=pltpu.HBM)] * 3,
        out_specs=pl.BlockSpec(memory_space=pltpu.VMEM),
        out_shape=jax.ShapeDtypeStruct((row_count * cap, tiles_of(part), SUB, LANES), jnp.float32),
        scratch_shapes=[
            pltpu.VMEM((loaded, NQ, blocks, cells), jnp.float32),
            pltpu.VMEM((rows * SUB, LANES), jnp.float32),
            pltpu.VMEM((2 * NQ, SUB, LANES), jnp.float32),
            pltpu.VMEM((SIDE_TILES * SUB * SUB, LANES), jnp.float32),
            pltpu.SMEM((blocks,), jnp.int32),
            pltpu.SMEM((blocks,), jnp.int32),
            pltpu.SemaphoreType.DMA((2 + loaded,)),
        ],
        compiler_params=pltpu.CompilerParams(vmem_limit_bytes=LARGE_VMEM_LIMIT),
        cost_estimate=pl.CostEstimate(flops=10**7, bytes_accessed=4 * 10**6, transcendentals=0),
        name="pre_%d" % part,
    )(destination, refinement, populations)


def read_tags(ins, tag_ref, sems):
    cap = ins[0].shape[0]
    copies = [
        pltpu.make_async_copy(in_ref.at[:, 0, pl.ds(0, 1)], tag_ref.at[pl.ds(d * cap, cap)], sems.at[d])
        for d, in_ref in enumerate(ins)
    ]
    for copy in copies:
        copy.start()
    for copy in copies:
        copy.wait()
    return lambda e: tag_ref[e, 0, 0].astype(jnp.int32)


def tag_scratch(arrays, slots):
    return [pltpu.SMEM((slots, 1, LANES), jnp.float32), pltpu.SemaphoreType.DMA((arrays,))]


def repack_kernel(cap, col_count, blocks, part, *refs):
    if part:
        plan_ref, in_ref, *outs = refs
    else:
        in_ref, *outs, plan_ref, tag_ref, sems, count_ref = refs
        tag_at = read_tags([in_ref], tag_ref, sems)
        here = lax.axis_index("col")
        for d in range(col_count):
            count_ref[d] = 0
        for e in range(col_count * cap):
            plan_ref[e] = -1
        for e in range(in_ref.shape[0]):
            tag = tag_at(e)

            @pl.when(tag >= 0)
            def _():
                d = step_to(lax.rem(tag // blocks, col_count), here, col_count)
                k = count_ref[d]
                count_ref[d] = k + 1
                plan_ref[d * cap + k] = e

    for d, out in enumerate(outs):
        for k in range(cap):
            e = plan_ref[d * cap + k]

            @pl.when(e >= 0)
            def _():
                out[k] = in_ref[e]

            if part == 0:

                @pl.when(e < 0)
                def _():
                    out[k, 0] = jnp.full((SUB, LANES), -1.0, jnp.float32)


def repack(landed, plan, part, col_count, cap, blocks):
    whole = pl.BlockSpec(memory_space=pltpu.VMEM)
    scalars = pl.BlockSpec(memory_space=pltpu.SMEM)
    scratch = []
    if part == 0:
        scratch = tag_scratch(1, landed.shape[0]) + [pltpu.SMEM((col_count,), jnp.int32)]
    packed = pl.pallas_call(
        functools.partial(repack_kernel, cap, col_count, blocks, part),
        in_specs=([scalars] if part else []) + [whole],
        out_specs=[whole] * col_count + ([] if part else [scalars]),
        scratch_shapes=scratch,
        out_shape=[jax.ShapeDtypeStruct((cap,) + landed.shape[1:], jnp.float32)] * col_count
        + ([] if part else [jax.ShapeDtypeStruct((col_count * cap,), jnp.int32)]),
        compiler_params=pltpu.CompilerParams(vmem_limit_bytes=VMEM_LIMIT),
        cost_estimate=pl.CostEstimate(flops=0, bytes_accessed=3 * 10**6, transcendentals=0),
        name="repack_%d" % part,
    )(*([plan] if part else []), landed)
    return packed if part else (packed[:-1], packed[-1])


def backward(zeroth, first, second, u):
    raw_one, raw_two = first, second
    if zeroth is not None:
        moved = u * zeroth
        raw_one = moved if raw_one is None else raw_one + moved
        square = u * moved
        raw_two = square if raw_two is None else raw_two + square
    if first is not None:
        cross = (u + u) * first
        raw_two = cross if raw_two is None else raw_two + cross
    rest = -raw_two if zeroth is None else zeroth - raw_two
    return 0.5 * (raw_two - raw_one), rest, 0.5 * (raw_one + raw_two)


def post_populations(rho, ux, uy, uz, pxy, pxz, pyz, dev_one, dev_two):
    inverse = 1.0 / rho
    pxx = (rho + dev_one + dev_two) * (1.0 / 3.0)
    pyy = pxx - dev_one
    pzz = pxx - dev_two
    sxy, sxz, syz = pxy * inverse, pxz * inverse, pyz * inverse
    syy, szz = pyy * inverse, pzz * inverse
    central = {
        (0, 0, 0): rho, (2, 0, 0): pxx, (0, 2, 0): pyy, (0, 0, 2): pzz,
        (1, 1, 0): pxy, (1, 0, 1): pxz, (0, 1, 1): pyz,
        (2, 2, 0): pxx * syy + 2.0 * pxy * sxy,
        (2, 0, 2): pxx * szz + 2.0 * pxz * sxz,
        (0, 2, 2): pyy * szz + 2.0 * pyz * syz,
        (2, 1, 1): pxx * syz + 2.0 * pxy * sxz,
        (1, 2, 1): pyy * sxz + 2.0 * pxy * syz,
        (1, 1, 2): pzz * sxy + 2.0 * pxz * syz,
        (2, 2, 2): pxx * syy * szz
        + 2.0 * (pxx * syz * syz + pyy * sxz * sxz + pzz * sxy * sxy)
        + 8.0 * pxy * sxz * syz,
    }
    along_z = {}
    for a in range(3):
        for b in range(3):
            parts = backward(*(central.get((a, b, c)) for c in range(3)), uz)
            for k in range(3):
                along_z[a, b, k] = parts[k]
    along_y = {}
    for a in range(3):
        for k in range(3):
            parts = backward(*(along_z[a, b, k] for b in range(3)), uy)
            for j in range(3):
                along_y[a, j, k] = parts[j]
    result = [None] * NQ
    for j in range(3):
        for k in range(3):
            parts = backward(*(along_y[a, j, k] for a in range(3)), ux)
            for i in range(3):
                result[i * 9 + j * 3 + k] = parts[i]
    return result


def unload(plan_ref, ins, fields_ref):
    cap, tiles = ins[0].shape[:2]
    for e in range(len(ins) * cap):
        t = plan_ref[e]

        @pl.when(t >= 0)
        def _():
            for tile in range(tiles):
                fields_ref[pl.ds(tile * SUB * SUB + t, SUB, stride=SUB), :] = ins[e // cap][e % cap, tile]


def row_of(ref, row):
    return ref[row * SUB : (row + 1) * SUB, :]


def turned(value, places):
    turn = places * EDGE % LANES
    return pltpu.roll(value, turn, axis=1) if turn else value


def places_y():
    return lax.broadcasted_iota(jnp.int32, (SUB, LANES), 1) // EDGE


def outer_fields(fields_ref, step, c):
    first = (SIDE_TILES + step * NFIELD) * SUB
    return [row_of(fields_ref, first + n * SUB + c) for n in range(NFIELD)]


def side_fields(fields_ref, half):
    return [row_of(fields_ref, 1 + half * NFIELD + n) for n in range(NFIELD)]


def fill_outer(fields_ref, main_ref):
    for step, group in enumerate(CHUNKS[0]):
        for c in range(SUB):
            for q, value in enumerate(post_populations(*outer_fields(fields_ref, step, c))):
                main_ref[q, 2 + group * SUB + c] = value


def fill_inner(fields_ref, late_ref, group, main_ref):
    spot = places_y()
    last = [None] * NFIELD
    for c in range(SUB):
        at = (group * WIDTH + c // 2) % SUB
        place = free_place(c)
        side = side_fields(fields_ref, c % 2)
        fields = []
        for n in range(NFIELD):
            if c < SUB - 1:
                row = row_of(late_ref, n * (SUB - 1) + c)
                part = turned(row, c - place)
                last[n] = part if c == 0 else jnp.where(spot == c, part, last[n])
            else:
                row = last[n]
            fields.append(jnp.where(spot == place, turned(side[n], place - at), row))
        for q, value in enumerate(post_populations(*fields)):
            main_ref[q, 2 + group * SUB + c] = value


def fill_sides(below_in, above_in, below_ref, above_ref, first, last):
    for x in range(first, last):
        at = x % SUB
        for k in range(9):
            below_ref[k, x + 1] = turned(below_in[k, x // SUB], SUB - 1 - at)
            above_ref[k, x + 1] = turned(above_in[k, x // SUB], -at)


def stream_pair(first_x, out_ref, main_ref, below_ref, above_ref):
    lane = lax.broadcasted_iota(jnp.int32, (SUB, LANES), 1)
    block = lax.broadcasted_iota(jnp.int32, (SUB, LANES), 0)
    along = lane % EDGE
    first_z, last_z = along == 0, along == EDGE - 1
    floor = first_z & (block == 0)
    ceiling = last_z & (block == SUB - 1)
    low_y, high_y = lane < EDGE, lane >= LANES - EDGE
    for i in range(2):
        for half in range(2):
            c = i * 2 + half
            for q in range(NQ):
                cx, cy, cz = velocity(q)
                x = first_x + i - cx + 1
                a = main_ref[q, x * 2 + half]
                k = (cx + 1) * 3 + cz + 1
                if cy == 1:
                    a = jnp.where(high_y, main_ref[q, x * 2] if half else below_ref[k, x], a)
                elif cy == -1:
                    a = jnp.where(low_y, above_ref[k, x] if half else main_ref[q, x * 2 + 1], a)
                shift = EDGE * cy + cz
                value = a if shift == 0 else pltpu.roll(a, shift % LANES, axis=1)
                if cz:
                    bounced = main_ref[26 - q, (first_x + i + 1) * 2 + half]
                    turn = (1 if cz == 1 else SUB - 1)
                    fill = pltpu.roll(pltpu.roll(a, turn, axis=0), (shift - cz * EDGE) % LANES, axis=1)
                    value = jnp.where(first_z if cz == 1 else last_z, fill, value)
                    value = jnp.where(floor if cz == 1 else ceiling, bounced, value)
                out_ref[q, :, c * LANES : (c + 1) * LANES] = value


def faces_kernel(count, *refs):
    ins = refs[:count]
    ylo_ref, yhi_ref, xlo_ref, xhi_ref, plan_ref, fields_ref, tag_ref, sems = refs[count:]
    tag_at = read_tags(ins, tag_ref, sems)
    for e in range(count * ins[0].shape[0]):
        tag = tag_at(e)
        plan_ref[e] = jnp.where(tag >= 0, lax.rem(tag, SUB), -1)
    unload(plan_ref, ins, fields_ref)
    spot = places_y()
    for half in range(2):
        packed = [side_fields(fields_ref, half)] * 2
        place = half * (SUB - 1)
        for step, group in enumerate(CHUNKS[0]):
            tile = group * WIDTH // SUB
            for x in range(group * WIDTH, (group + 1) * WIDTH):
                c = (x - group * WIDTH) * 2 + half
                packed[tile] = [
                    jnp.where(spot == x % SUB, turned(value, x % SUB - place), old)
                    for value, old in zip(outer_fields(fields_ref, step, c), packed[tile])
                ]
        for tile in range(2):
            result = post_populations(*packed[tile])
            for i in range(3):
                for k in range(3):
                    (yhi_ref if half else ylo_ref)[i * 3 + k, tile] = result[i * 9 + half * 6 + k]
        low = post_populations(*outer_fields(fields_ref, CHUNKS[0].index(0), half))
        high = post_populations(*outer_fields(fields_ref, CHUNKS[0].index(GROUPS - 1), SUB - 2 + half))
        for q in range(9):
            xlo_ref[q, half] = low[q]
            xhi_ref[q, half] = high[18 + q]


def faces(homes):
    shape = jax.ShapeDtypeStruct
    face = shape((9, 2, SUB, LANES), jnp.float32)
    slots = len(homes) * homes[0].shape[0]
    whole = pl.BlockSpec(memory_space=pltpu.VMEM)
    return pl.pallas_call(
        functools.partial(faces_kernel, len(homes)),
        in_specs=[whole] * len(homes),
        out_specs=[whole] * 4 + [pl.BlockSpec(memory_space=pltpu.SMEM), whole],
        scratch_shapes=tag_scratch(len(homes), slots),
        out_shape=[face] * 4
        + [shape((slots,), jnp.int32), shape((tiles_of(0) * SUB * SUB, LANES), jnp.float32)],
        compiler_params=pltpu.CompilerParams(vmem_limit_bytes=VMEM_LIMIT),
        cost_estimate=pl.CostEstimate(flops=10**7, bytes_accessed=3 * 10**6, transcendentals=0),
        name="faces",
    )(*homes)


PAIRS = ((0, 1, 2, 7), (3, 4, 5, 6))
KEPT = ((5, 8), (12, 15))


def advance_kernel(count, plan_ref, *refs):
    ins = refs[:count]
    (
        fields_ref, xlo_ref, xhi_ref, below_in, above_in, out_ref, kept_ref,
        main_ref, below_ref, above_ref, late_ref,
    ) = refs[count:]
    g = pl.program_id(0)

    @pl.when(g == 0)
    def _():
        unload(plan_ref, ins, late_ref)
        fill_outer(fields_ref, main_ref)
        fill_inner(fields_ref, late_ref, CHUNKS[1][0], main_ref)
        fill_sides(below_in, above_in, below_ref, above_ref, 0, 7)
        fill_sides(below_in, above_in, below_ref, above_ref, 13, EDGE)
        for k in range(3):
            below_ref[6 + k, 0] = xlo_ref[18 + k]
            above_ref[6 + k, 0] = turned(xlo_ref[21 + k], 1)
            below_ref[k, EDGE + 1] = turned(xhi_ref[18 + k], -1)
            above_ref[k, EDGE + 1] = xhi_ref[21 + k]
        for q in range(9):
            for half in range(2):
                main_ref[18 + q, half] = xlo_ref[q * 2 + half]
                main_ref[q, 2 * EDGE + 2 + half] = xhi_ref[q * 2 + half]
        to = 0
        for first, last in KEPT:
            for row in range(2 * first + 2, 2 * last + 2):
                for q in range(NQ):
                    kept_ref[q, to] = main_ref[q, row]
                to += 1

    first_x = 2 * jnp.where(g == len(PAIRS[0]) - 1, PAIRS[0][-1], g)
    stream_pair(first_x, out_ref, main_ref, below_ref, above_ref)


def finish_kernel(count, plan_ref, *refs):
    ins = refs[:count]
    (
        fields_ref, kept_ref, below_in, above_in, _, out_ref,
        main_ref, below_ref, above_ref, late_ref, sems,
    ) = refs[count:]
    g = pl.program_id(0)

    @pl.when(g == 0)
    def _():
        copies = []
        to = 0
        for first, last in KEPT:
            rows = 2 * (last - first)
            copies.append(
                pltpu.make_async_copy(
                    kept_ref.at[:, pl.ds(to, rows)],
                    main_ref.at[:, pl.ds(2 * first + 2, rows)],
                    sems.at[len(copies)],
                )
            )
            to += rows
        for copy in copies:
            copy.start()
        unload(plan_ref, ins, late_ref)
        fill_inner(fields_ref, late_ref, CHUNKS[2][0], main_ref)
        fill_sides(below_in, above_in, below_ref, above_ref, 5, 15)
        for copy in copies:
            copy.wait()

    stream_pair(2 * (PAIRS[1][0] + g), out_ref, main_ref, below_ref, above_ref)


def whole_of(value):
    rank = len(value.shape)
    return pl.BlockSpec(value.shape, lambda g, *_: (0,) * rank)


def scratch_of_lattice():
    side = pltpu.VMEM((9, EDGE + 2, SUB, LANES), jnp.float32)
    return [
        pltpu.VMEM((NQ, 2 * EDGE + 4, SUB, LANES), jnp.float32), side, side,
        pltpu.VMEM((LATE_TILES * SUB * SUB, LANES), jnp.float32),
    ]


def advance(plan, homes, fields, xlo, xhi, below, above):
    pairs = PAIRS[0]
    inputs = [*homes, fields, xlo, xhi, below, above]
    kept = jax.ShapeDtypeStruct(
        (NQ, 2 * sum(last - first for first, last in KEPT), SUB, LANES), jnp.float32
    )
    return pl.pallas_call(
        functools.partial(advance_kernel, len(homes)),
        grid_spec=pltpu.PrefetchScalarGridSpec(
            num_scalar_prefetch=1,
            grid=(len(pairs),),
            in_specs=[whole_of(value) for value in inputs],
            out_specs=[
                pl.BlockSpec(
                    (NQ, SUB, 4 * LANES),
                    lambda g, *_: (0, 0, jnp.where(g == len(pairs) - 1, pairs[-1], g)),
                ),
                whole_of(kept),
            ],
            scratch_shapes=scratch_of_lattice(),
        ),
        out_shape=[jax.ShapeDtypeStruct((NQ, SUB, GROUPS * SUB * LANES), jnp.float32), kept],
        compiler_params=pltpu.CompilerParams(vmem_limit_bytes=VMEM_LIMIT),
        cost_estimate=pl.CostEstimate(flops=10**7, bytes_accessed=5 * 10**6, transcendentals=0),
        name="advance",
    )(plan, *inputs)


def finish(plan, homes, fields, kept, below, above, out):
    pairs = PAIRS[1]
    anywhere = pl.BlockSpec(memory_space=pl.ANY)
    return pl.pallas_call(
        functools.partial(finish_kernel, len(homes)),
        grid_spec=pltpu.PrefetchScalarGridSpec(
            num_scalar_prefetch=1,
            grid=(len(pairs),),
            in_specs=[whole_of(value) for value in (*homes, fields)]
            + [anywhere, whole_of(below), whole_of(above), anywhere],
            out_specs=pl.BlockSpec((NQ, SUB, 4 * LANES), lambda g, *_: (0, 0, pairs[0] + g)),
            scratch_shapes=scratch_of_lattice() + [pltpu.SemaphoreType.DMA((len(KEPT),))],
        ),
        out_shape=jax.ShapeDtypeStruct(out.shape, jnp.float32),
        input_output_aliases={len(homes) + 5: 0},
        compiler_params=pltpu.CompilerParams(vmem_limit_bytes=VMEM_LIMIT),
        cost_estimate=pl.CostEstimate(flops=10**7, bytes_accessed=5 * 10**6, transcendentals=0),
        name="finish",
    )(plan, *homes, fields, kept, below, above, out)


def shifted(value, axis, step):
    count = lax.axis_size(axis)
    return lax.ppermute(value, axis, [(i, (i + step) % count) for i in range(count)])


def on_device(populations, destination, refinement):
    blocks = populations.shape[0]
    row_count = lax.axis_size("row")
    col_count = lax.axis_size("col")
    cap_row = 2 * ((blocks + row_count - 1) // row_count)
    cap_col = 2 * ((blocks + col_count - 1) // col_count)
    ordered = jnp.transpose(populations, (1, 0, 2))

    in_row = []
    for part in range(len(CHUNKS)):
        sent = pre(ordered, destination, refinement, part, row_count, cap_row, blocks * col_count)
        if part:
            sent, in_row[-1] = lax.optimization_barrier((sent, in_row[-1]))
        else:
            sent, destination = lax.optimization_barrier((sent, destination))
        in_row.append(lax.all_to_all(sent, "row", split_axis=0, concat_axis=0, tiled=True))

    def to_columns(packed):
        return [exchanged(packed[d], "col", d) for d in range(col_count - 1, 0, -1)] + [packed[0]]

    packed, plan = repack(in_row[0], None, 0, col_count, cap_col, blocks)
    ylo, yhi, xlo, xhi, picked, fields = faces(to_columns(packed))
    below, above = shifted(yhi, "col", 1), shifted(ylo, "col", -1)
    middle = to_columns(repack(in_row[1], plan, 1, col_count, cap_col, blocks))
    in_row[2], below, above = lax.optimization_barrier((in_row[2], below, above))
    up = jnp.concatenate([xhi.reshape(18, SUB, LANES), below[6:, 1], above[6:, 1]])
    down = jnp.concatenate([xlo.reshape(18, SUB, LANES), below[:3, 0], above[:3, 0]])
    xlo, xhi = shifted(up, "row", 1), shifted(down, "row", -1)
    packed = repack(in_row[2], plan, 2, col_count, cap_col, blocks)
    picked, packed = lax.optimization_barrier((picked, list(packed)))
    last = to_columns(packed)
    out, kept = advance(picked, middle, fields, xlo, xhi, below, above)
    return jnp.transpose(finish(picked, last, fields, kept, below, above, out), (1, 0, 2))


def solution(mesh):
    return jax.shard_map(
        on_device,
        mesh=mesh,
        in_specs=(P(("row", "col"), None, None), P(("row", "col")), P(("row", "col"))),
        out_specs=P(("row", "col"), None, None),
        check_vma=False,
    )
```

```python
import functools

import jax
import jax.numpy as jnp
from jax import lax
from jax.experimental import pallas as pl
from jax.experimental.pallas import tpu as pltpu
from jax.sharding import PartitionSpec as P

EDGE = 16
VISCOSITY = 0.01
LANES = 128
SUB = 8
NQ = 27
NFIELD = 9
GROUPS = 4
WIDTH = EDGE // GROUPS
CHUNKS = ((0, 3), (1,), (2,))
INNER = (1, 2)
SIDE_TILES = 3
LATE_TILES = -(-NFIELD * (SUB - 1) // SUB)
VMEM_LIMIT = 20 * 1024 * 1024
LARGE_VMEM_LIMIT = 60 * 1024 * 1024


def velocity(q):
    return (q // 9 - 1, (q // 3) % 3 - 1, q % 3 - 1)


def tiles_of(part):
    return LATE_TILES if part else len(CHUNKS[0]) * NFIELD + SIDE_TILES


def free_place(c):
    return (c % 2) * (SUB - 1)


def step_to(target, here, count):
    if count & (count - 1) == 0:
        return target ^ here
    return lax.rem(target - here + count, count)


def exchanged(value, axis, step):
    count = lax.axis_size(axis)
    if count & (count - 1) == 0:
        pairs = [(i, i ^ step) for i in range(count)]
    else:
        pairs = [(i, (i + step) % count) for i in range(count)]
    return lax.ppermute(value, axis, pairs)


def raw_moments(f):
    whole, slope, outer = {}, {}, {}
    for i in range(3):
        for j in range(3):
            low, rest, high = (f[i * 9 + j * 3 + k] for k in range(3))
            outer[i, j] = low + high
            whole[i, j] = outer[i, j] + rest
            slope[i, j] = high - low
    column = [whole[i, 0] + whole[i, 1] + whole[i, 2] for i in range(3)]
    tilt = [slope[i, 0] + slope[i, 1] + slope[i, 2] for i in range(3)]
    low_y = whole[0, 0] + whole[1, 0] + whole[2, 0]
    high_y = whole[0, 2] + whole[1, 2] + whole[2, 2]
    ends = column[0] + column[2]
    mzz = sum(outer[i, j] for i in range(3) for j in range(3))
    mxy = (whole[2, 2] - whole[2, 0]) - (whole[0, 2] - whole[0, 0])
    myz = (slope[0, 2] + slope[1, 2] + slope[2, 2]) - (slope[0, 0] + slope[1, 0] + slope[2, 0])
    return (
        ends + column[1],
        column[2] - column[0],
        high_y - low_y,
        tilt[0] + tilt[1] + tilt[2],
        ends,
        low_y + high_y,
        mzz,
        mxy,
        tilt[2] - tilt[0],
        myz,
    )


def collided(f, keep):
    rho, jx, jy, jz, mxx, myy, mzz, mxy, mxz, myz = raw_moments(f)
    inverse = 1.0 / rho
    ux, uy, uz = jx * inverse, jy * inverse, jz * inverse
    kxx = mxx - jx * ux
    return (
        rho, ux, uy, uz,
        keep * (mxy - jx * uy),
        keep * (mxz - jx * uz),
        keep * (myz - jy * uz),
        keep * (kxx - (myy - jy * uy)),
        keep * (kxx - (mzz - jz * uz)),
    )


def pre_kernel(cap, row_count, per_row, part, dest_hbm, level_hbm, x_hbm, out_ref, *refs):
    x_ref, swap_ref, packed_ref, side_ref, dest_ref, level_ref, sems = refs
    order = CHUNKS[part] if part else CHUNKS[0] + INNER
    steps = len(CHUNKS[part])
    blocks = x_ref.shape[2]
    cells = x_ref.shape[3]
    chunks = cells // LANES
    small = [
        pltpu.make_async_copy(dest_hbm, dest_ref, sems.at[0]),
        pltpu.make_async_copy(level_hbm, level_ref, sems.at[1]),
    ]
    large = [
        pltpu.make_async_copy(
            x_hbm.at[:, :, pl.ds(group * cells, cells)], x_ref.at[step], sems.at[2 + step]
        )
        for step, group in enumerate(order)
    ]
    for copy in small + large:
        copy.start()
    for copy in small:
        copy.wait()

    which = lax.broadcasted_iota(jnp.int32, (SUB, LANES), 0)
    spot = lax.broadcasted_iota(jnp.int32, (SUB, LANES), 1) // EDGE
    scale = jnp.zeros((SUB, LANES), jnp.int32)
    tag = jnp.zeros((SUB, LANES), jnp.int32)
    for t in range(blocks):
        scale = jnp.where(which == t, jnp.left_shift(1, level_ref[t]), scale)
        tag = jnp.where(which == t, dest_ref[t], tag)
    rate = 1.0 / (3.0 * VISCOSITY * scale.astype(jnp.float32) + 0.5)
    keep = 1.0 - rate

    rows = [dest_ref[t] // per_row for t in range(blocks)]
    slots = []
    for t in range(blocks):
        slot = rows[t] * cap
        for other in range(t):
            slot = slot + jnp.where(rows[other] == rows[t], 1, 0)
        slots.append(slot)

    def spread(ref, first, count):
        for t in range(blocks):
            for n in range(count):
                moved = ref[pl.ds(n * SUB * SUB + t, SUB, stride=SUB), :]
                out_ref[slots[t], first + n] = moved

    def fields_at(step, c):
        return collided([x_ref[step, q, :, c * LANES : (c + 1) * LANES] for q in range(NQ)], keep)

    for step, group in enumerate(order):
        large[step].wait()
        if part:
            last = fields_at(step, chunks - 1)
            for c in range(chunks - 1):
                place = free_place(c)
                turn = (place - c) * EDGE % LANES
                for n, field in enumerate(fields_at(step, c)):
                    other = pltpu.roll(last[n], turn, axis=1) if turn else last[n]
                    base = ((step * NFIELD + n) * (chunks - 1) + c) * SUB
                    swap_ref[base : base + SUB, :] = jnp.where(spot == place, other, field)
            continue
        if step < steps:
            for c in range(chunks):
                for n, field in enumerate(fields_at(step, c)):
                    base = (n * chunks + c) * SUB
                    swap_ref[base : base + SUB, :] = field
            spread(swap_ref, SIDE_TILES + step * NFIELD, NFIELD)
            continue
        for q in range(NQ):
            for half in range(2):
                value = packed_ref[half * NQ + q] if step > steps else None
                for x in range(WIDTH):
                    c = x * 2 + half
                    at = (group * WIDTH + x) % SUB
                    moved = x_ref[step, q, :, c * LANES : (c + 1) * LANES]
                    turn = (at + half) * EDGE % LANES
                    if turn:
                        moved = pltpu.roll(moved, turn, axis=1)
                    value = moved if value is None else jnp.where(spot == at, moved, value)
                packed_ref[half * NQ + q] = value

    if part:
        for row in range(steps * NFIELD * (chunks - 1), LATE_TILES * SUB):
            swap_ref[row * SUB : (row + 1) * SUB, :] = tag.astype(jnp.float32)
        spread(swap_ref, 0, LATE_TILES)
        return
    for row in range(SIDE_TILES * SUB):
        if not 1 <= row <= 2 * NFIELD:
            side_ref[row * SUB : (row + 1) * SUB, :] = tag.astype(jnp.float32)
    for half in range(2):
        fields = collided([packed_ref[half * NQ + q] for q in range(NQ)], keep)
        for n, field in enumerate(fields):
            base = (1 + half * NFIELD + n) * SUB
            side_ref[base : base + SUB, :] = field
    for slot in range(row_count * cap):
        out_ref[slot, 0] = jnp.full((SUB, LANES), -1.0, jnp.float32)
    spread(side_ref, 0, SIDE_TILES)


def pre(populations, destination, refinement, part, row_count, cap, per_row):
    blocks = populations.shape[1]
    cells = populations.shape[2] // GROUPS
    loaded = len(CHUNKS[part]) + (0 if part else len(INNER))
    rows = LATE_TILES * SUB if part else NFIELD * cells // LANES
    return pl.pallas_call(
        functools.partial(pre_kernel, cap, row_count, per_row, part),
        in_specs=[pl.BlockSpec(memory_space=pltpu.HBM)] * 3,
        out_specs=pl.BlockSpec(memory_space=pltpu.VMEM),
        out_shape=jax.ShapeDtypeStruct((row_count * cap, tiles_of(part), SUB, LANES), jnp.float32),
        scratch_shapes=[
            pltpu.VMEM((loaded, NQ, blocks, cells), jnp.float32),
            pltpu.VMEM((rows * SUB, LANES), jnp.float32),
            pltpu.VMEM((2 * NQ, SUB, LANES), jnp.float32),
            pltpu.VMEM((SIDE_TILES * SUB * SUB, LANES), jnp.float32),
            pltpu.SMEM((blocks,), jnp.int32),
            pltpu.SMEM((blocks,), jnp.int32),
            pltpu.SemaphoreType.DMA((2 + loaded,)),
        ],
        compiler_params=pltpu.CompilerParams(vmem_limit_bytes=LARGE_VMEM_LIMIT),
        cost_estimate=pl.CostEstimate(flops=10**7, bytes_accessed=4 * 10**6, transcendentals=0),
        name="pre_%d" % part,
    )(destination, refinement, populations)


def read_tags(ins, tag_ref, sems):
    cap = ins[0].shape[0]
    copies = [
        pltpu.make_async_copy(in_ref.at[:, 0, pl.ds(0, 1)], tag_ref.at[pl.ds(d * cap, cap)], sems.at[d])
        for d, in_ref in enumerate(ins)
    ]
    for copy in copies:
        copy.start()
    for copy in copies:
        copy.wait()
    return lambda e: tag_ref[e, 0, 0].astype(jnp.int32)


def tag_scratch(arrays, slots):
    return [pltpu.SMEM((slots, 1, LANES), jnp.float32), pltpu.SemaphoreType.DMA((arrays,))]


def repack_kernel(cap, col_count, blocks, part, *refs):
    if part:
        plan_ref, in_ref, *outs = refs
    else:
        in_ref, *outs, plan_ref, tag_ref, sems, count_ref = refs
        tag_at = read_tags([in_ref], tag_ref, sems)
        here = lax.axis_index("col")
        for d in range(col_count):
            count_ref[d] = 0
        for e in range(col_count * cap):
            plan_ref[e] = -1
        for e in range(in_ref.shape[0]):
            tag = tag_at(e)

            @pl.when(tag >= 0)
            def _():
                d = step_to(lax.rem(tag // blocks, col_count), here, col_count)
                k = count_ref[d]
                count_ref[d] = k + 1
                plan_ref[d * cap + k] = e

    for d, out in enumerate(outs):
        for k in range(cap):
            e = plan_ref[d * cap + k]

            @pl.when(e >= 0)
            def _():
                out[k] = in_ref[e]

            if part == 0:

                @pl.when(e < 0)
                def _():
                    out[k, 0] = jnp.full((SUB, LANES), -1.0, jnp.float32)


def repack(landed, plan, part, col_count, cap, blocks):
    whole = pl.BlockSpec(memory_space=pltpu.VMEM)
    scalars = pl.BlockSpec(memory_space=pltpu.SMEM)
    scratch = []
    if part == 0:
        scratch = tag_scratch(1, landed.shape[0]) + [pltpu.SMEM((col_count,), jnp.int32)]
    packed = pl.pallas_call(
        functools.partial(repack_kernel, cap, col_count, blocks, part),
        in_specs=([scalars] if part else []) + [whole],
        out_specs=[whole] * col_count + ([] if part else [scalars]),
        scratch_shapes=scratch,
        out_shape=[jax.ShapeDtypeStruct((cap,) + landed.shape[1:], jnp.float32)] * col_count
        + ([] if part else [jax.ShapeDtypeStruct((col_count * cap,), jnp.int32)]),
        compiler_params=pltpu.CompilerParams(vmem_limit_bytes=VMEM_LIMIT),
        cost_estimate=pl.CostEstimate(flops=0, bytes_accessed=3 * 10**6, transcendentals=0),
        name="repack_%d" % part,
    )(*([plan] if part else []), landed)
    return packed if part else (packed[:-1], packed[-1])


def backward(zeroth, first, second, u):
    raw_one, raw_two = first, second
    if zeroth is not None:
        moved = u * zeroth
        raw_one = moved if raw_one is None else raw_one + moved
        square = u * moved
        raw_two = square if raw_two is None else raw_two + square
    if first is not None:
        cross = (u + u) * first
        raw_two = cross if raw_two is None else raw_two + cross
    rest = -raw_two if zeroth is None else zeroth - raw_two
    return 0.5 * (raw_two - raw_one), rest, 0.5 * (raw_one + raw_two)


def post_populations(rho, ux, uy, uz, pxy, pxz, pyz, dev_one, dev_two):
    inverse = 1.0 / rho
    pxx = (rho + dev_one + dev_two) * (1.0 / 3.0)
    pyy = pxx - dev_one
    pzz = pxx - dev_two
    sxy, sxz, syz = pxy * inverse, pxz * inverse, pyz * inverse
    syy, szz = pyy * inverse, pzz * inverse
    central = {
        (0, 0, 0): rho, (2, 0, 0): pxx, (0, 2, 0): pyy, (0, 0, 2): pzz,
        (1, 1, 0): pxy, (1, 0, 1): pxz, (0, 1, 1): pyz,
        (2, 2, 0): pxx * syy + 2.0 * pxy * sxy,
        (2, 0, 2): pxx * szz + 2.0 * pxz * sxz,
        (0, 2, 2): pyy * szz + 2.0 * pyz * syz,
        (2, 1, 1): pxx * syz + 2.0 * pxy * sxz,
        (1, 2, 1): pyy * sxz + 2.0 * pxy * syz,
        (1, 1, 2): pzz * sxy + 2.0 * pxz * syz,
        (2, 2, 2): pxx * syy * szz
        + 2.0 * (pxx * syz * syz + pyy * sxz * sxz + pzz * sxy * sxy)
        + 8.0 * pxy * sxz * syz,
    }
    along_z = {}
    for a in range(3):
        for b in range(3):
            parts = backward(*(central.get((a, b, c)) for c in range(3)), uz)
            for k in range(3):
                along_z[a, b, k] = parts[k]
    along_y = {}
    for a in range(3):
        for k in range(3):
            parts = backward(*(along_z[a, b, k] for b in range(3)), uy)
            for j in range(3):
                along_y[a, j, k] = parts[j]
    result = [None] * NQ
    for j in range(3):
        for k in range(3):
            parts = backward(*(along_y[a, j, k] for a in range(3)), ux)
            for i in range(3):
                result[i * 9 + j * 3 + k] = parts[i]
    return result


def unload(plan_ref, ins, fields_ref):
    cap, tiles = ins[0].shape[:2]
    for e in range(len(ins) * cap):
        t = plan_ref[e]

        @pl.when(t >= 0)
        def _():
            for tile in range(tiles):
                fields_ref[pl.ds(tile * SUB * SUB + t, SUB, stride=SUB), :] = ins[e // cap][e % cap, tile]


def row_of(ref, row):
    return ref[row * SUB : (row + 1) * SUB, :]


def turned(value, places):
    turn = places * EDGE % LANES
    return pltpu.roll(value, turn, axis=1) if turn else value


def places_y():
    return lax.broadcasted_iota(jnp.int32, (SUB, LANES), 1) // EDGE


def outer_fields(fields_ref, step, c):
    first = (SIDE_TILES + step * NFIELD) * SUB
    return [row_of(fields_ref, first + n * SUB + c) for n in range(NFIELD)]


def side_fields(fields_ref, half):
    return [row_of(fields_ref, 1 + half * NFIELD + n) for n in range(NFIELD)]


def fill_outer(fields_ref, main_ref):
    for step, group in enumerate(CHUNKS[0]):
        for c in range(SUB):
            for q, value in enumerate(post_populations(*outer_fields(fields_ref, step, c))):
                main_ref[q, 2 + group * SUB + c] = value


def fill_inner(fields_ref, late_ref, group, main_ref):
    spot = places_y()
    last = [None] * NFIELD
    for c in range(SUB):
        at = (group * WIDTH + c // 2) % SUB
        place = free_place(c)
        side = side_fields(fields_ref, c % 2)
        fields = []
        for n in range(NFIELD):
            if c < SUB - 1:
                row = row_of(late_ref, n * (SUB - 1) + c)
                part = turned(row, c - place)
                last[n] = part if c == 0 else jnp.where(spot == c, part, last[n])
            else:
                row = last[n]
            fields.append(jnp.where(spot == place, turned(side[n], place - at), row))
        for q, value in enumerate(post_populations(*fields)):
            main_ref[q, 2 + group * SUB + c] = value


def fill_sides(below_in, above_in, below_ref, above_ref, first, last):
    for x in range(first, last):
        at = x % SUB
        for k in range(9):
            below_ref[k, x + 1] = turned(below_in[k, x // SUB], SUB - 1 - at)
            above_ref[k, x + 1] = turned(above_in[k, x // SUB], -at)


def stream_pair(first_x, out_ref, main_ref, below_ref, above_ref):
    lane = lax.broadcasted_iota(jnp.int32, (SUB, LANES), 1)
    block = lax.broadcasted_iota(jnp.int32, (SUB, LANES), 0)
    along = lane % EDGE
    first_z, last_z = along == 0, along == EDGE - 1
    floor = first_z & (block == 0)
    ceiling = last_z & (block == SUB - 1)
    low_y, high_y = lane < EDGE, lane >= LANES - EDGE
    for i in range(2):
        for half in range(2):
            c = i * 2 + half
            for q in range(NQ):
                cx, cy, cz = velocity(q)
                x = first_x + i - cx + 1
                a = main_ref[q, x * 2 + half]
                k = (cx + 1) * 3 + cz + 1
                if cy == 1:
                    a = jnp.where(high_y, main_ref[q, x * 2] if half else below_ref[k, x], a)
                elif cy == -1:
                    a = jnp.where(low_y, above_ref[k, x] if half else main_ref[q, x * 2 + 1], a)
                shift = EDGE * cy + cz
                value = a if shift == 0 else pltpu.roll(a, shift % LANES, axis=1)
                if cz:
                    bounced = main_ref[26 - q, (first_x + i + 1) * 2 + half]
                    turn = (1 if cz == 1 else SUB - 1)
                    fill = pltpu.roll(pltpu.roll(a, turn, axis=0), (shift - cz * EDGE) % LANES, axis=1)
                    value = jnp.where(first_z if cz == 1 else last_z, fill, value)
                    value = jnp.where(floor if cz == 1 else ceiling, bounced, value)
                out_ref[q, :, c * LANES : (c + 1) * LANES] = value


def faces_kernel(count, *refs):
    ins = refs[:count]
    ylo_ref, yhi_ref, xlo_ref, xhi_ref, plan_ref, fields_ref, tag_ref, sems = refs[count:]
    tag_at = read_tags(ins, tag_ref, sems)
    for e in range(count * ins[0].shape[0]):
        tag = tag_at(e)
        plan_ref[e] = jnp.where(tag >= 0, lax.rem(tag, SUB), -1)
    unload(plan_ref, ins, fields_ref)
    spot = places_y()
    for half in range(2):
        packed = [side_fields(fields_ref, half)] * 2
        place = half * (SUB - 1)
        for step, group in enumerate(CHUNKS[0]):
            tile = group * WIDTH // SUB
            for x in range(group * WIDTH, (group + 1) * WIDTH):
                c = (x - group * WIDTH) * 2 + half
                packed[tile] = [
                    jnp.where(spot == x % SUB, turned(value, x % SUB - place), old)
                    for value, old in zip(outer_fields(fields_ref, step, c), packed[tile])
                ]
        for tile in range(2):
            result = post_populations(*packed[tile])
            for i in range(3):
                for k in range(3):
                    (yhi_ref if half else ylo_ref)[i * 3 + k, tile] = result[i * 9 + half * 6 + k]
        low = post_populations(*outer_fields(fields_ref, CHUNKS[0].index(0), half))
        high = post_populations(*outer_fields(fields_ref, CHUNKS[0].index(GROUPS - 1), SUB - 2 + half))
        for q in range(9):
            xlo_ref[q, half] = low[q]
            xhi_ref[q, half] = high[18 + q]


def faces(homes):
    shape = jax.ShapeDtypeStruct
    face = shape((9, 2, SUB, LANES), jnp.float32)
    slots = len(homes) * homes[0].shape[0]
    whole = pl.BlockSpec(memory_space=pltpu.VMEM)
    return pl.pallas_call(
        functools.partial(faces_kernel, len(homes)),
        in_specs=[whole] * len(homes),
        out_specs=[whole] * 4 + [pl.BlockSpec(memory_space=pltpu.SMEM), whole],
        scratch_shapes=tag_scratch(len(homes), slots),
        out_shape=[face] * 4
        + [shape((slots,), jnp.int32), shape((tiles_of(0) * SUB * SUB, LANES), jnp.float32)],
        compiler_params=pltpu.CompilerParams(vmem_limit_bytes=VMEM_LIMIT),
        cost_estimate=pl.CostEstimate(flops=10**7, bytes_accessed=3 * 10**6, transcendentals=0),
        name="faces",
    )(*homes)


PAIRS = ((0, 1, 2, 7), (3, 4, 5, 6))
KEPT = ((5, 8), (12, 15))


def advance_kernel(count, plan_ref, *refs):
    ins = refs[:count]
    (
        fields_ref, xlo_ref, xhi_ref, below_in, above_in, out_ref, kept_ref,
        main_ref, below_ref, above_ref, late_ref,
    ) = refs[count:]
    g = pl.program_id(0)

    @pl.when(g == 0)
    def _():
        unload(plan_ref, ins, late_ref)
        fill_outer(fields_ref, main_ref)
        fill_inner(fields_ref, late_ref, CHUNKS[1][0], main_ref)
        fill_sides(below_in, above_in, below_ref, above_ref, 0, 7)
        fill_sides(below_in, above_in, below_ref, above_ref, 13, EDGE)
        for k in range(3):
            below_ref[6 + k, 0] = xlo_ref[18 + k]
            above_ref[6 + k, 0] = turned(xlo_ref[21 + k], 1)
            below_ref[k, EDGE + 1] = turned(xhi_ref[18 + k], -1)
            above_ref[k, EDGE + 1] = xhi_ref[21 + k]
        for q in range(9):
            for half in range(2):
                main_ref[18 + q, half] = xlo_ref[q * 2 + half]
                main_ref[q, 2 * EDGE + 2 + half] = xhi_ref[q * 2 + half]
        to = 0
        for first, last in KEPT:
            for row in range(2 * first + 2, 2 * last + 2):
                for q in range(NQ):
                    kept_ref[q, to] = main_ref[q, row]
                to += 1

    first_x = 2 * jnp.where(g == len(PAIRS[0]) - 1, PAIRS[0][-1], g)
    stream_pair(first_x, out_ref, main_ref, below_ref, above_ref)


def finish_kernel(count, plan_ref, *refs):
    ins = refs[:count]
    (
        fields_ref, kept_ref, below_in, above_in, _, out_ref,
        main_ref, below_ref, above_ref, late_ref, sems,
    ) = refs[count:]
    g = pl.program_id(0)

    @pl.when(g == 0)
    def _():
        copies = []
        to = 0
        for first, last in KEPT:
            rows = 2 * (last - first)
            copies.append(
                pltpu.make_async_copy(
                    kept_ref.at[:, pl.ds(to, rows)],
                    main_ref.at[:, pl.ds(2 * first + 2, rows)],
                    sems.at[len(copies)],
                )
            )
            to += rows
        for copy in copies:
            copy.start()
        unload(plan_ref, ins, late_ref)
        fill_inner(fields_ref, late_ref, CHUNKS[2][0], main_ref)
        fill_sides(below_in, above_in, below_ref, above_ref, 5, 15)
        for copy in copies:
            copy.wait()

    stream_pair(2 * (PAIRS[1][0] + g), out_ref, main_ref, below_ref, above_ref)


def whole_of(value):
    rank = len(value.shape)
    return pl.BlockSpec(value.shape, lambda g, *_: (0,) * rank)


def scratch_of_lattice():
    side = pltpu.VMEM((9, EDGE + 2, SUB, LANES), jnp.float32)
    return [
        pltpu.VMEM((NQ, 2 * EDGE + 4, SUB, LANES), jnp.float32), side, side,
        pltpu.VMEM((LATE_TILES * SUB * SUB, LANES), jnp.float32),
    ]


def advance(plan, homes, fields, xlo, xhi, below, above):
    pairs = PAIRS[0]
    inputs = [*homes, fields, xlo, xhi, below, above]
    kept = jax.ShapeDtypeStruct(
        (NQ, 2 * sum(last - first for first, last in KEPT), SUB, LANES), jnp.float32
    )
    return pl.pallas_call(
        functools.partial(advance_kernel, len(homes)),
        grid_spec=pltpu.PrefetchScalarGridSpec(
            num_scalar_prefetch=1,
            grid=(len(pairs),),
            in_specs=[whole_of(value) for value in inputs],
            out_specs=[
                pl.BlockSpec(
                    (NQ, SUB, 4 * LANES),
                    lambda g, *_: (0, 0, jnp.where(g == len(pairs) - 1, pairs[-1], g)),
                ),
                whole_of(kept),
            ],
            scratch_shapes=scratch_of_lattice(),
        ),
        out_shape=[jax.ShapeDtypeStruct((NQ, SUB, GROUPS * SUB * LANES), jnp.float32), kept],
        compiler_params=pltpu.CompilerParams(vmem_limit_bytes=VMEM_LIMIT),
        cost_estimate=pl.CostEstimate(flops=10**7, bytes_accessed=5 * 10**6, transcendentals=0),
        name="advance",
    )(plan, *inputs)


def finish(plan, homes, fields, kept, below, above, out):
    pairs = PAIRS[1]
    anywhere = pl.BlockSpec(memory_space=pl.ANY)
    return pl.pallas_call(
        functools.partial(finish_kernel, len(homes)),
        grid_spec=pltpu.PrefetchScalarGridSpec(
            num_scalar_prefetch=1,
            grid=(len(pairs),),
            in_specs=[whole_of(value) for value in (*homes, fields)]
            + [anywhere, whole_of(below), whole_of(above), anywhere],
            out_specs=pl.BlockSpec((NQ, SUB, 4 * LANES), lambda g, *_: (0, 0, pairs[0] + g)),
            scratch_shapes=scratch_of_lattice() + [pltpu.SemaphoreType.DMA((len(KEPT),))],
        ),
        out_shape=jax.ShapeDtypeStruct(out.shape, jnp.float32),
        input_output_aliases={len(homes) + 5: 0},
        compiler_params=pltpu.CompilerParams(vmem_limit_bytes=VMEM_LIMIT),
        cost_estimate=pl.CostEstimate(flops=10**7, bytes_accessed=5 * 10**6, transcendentals=0),
        name="finish",
    )(plan, *homes, fields, kept, below, above, out)


def shifted(value, axis, step):
    count = lax.axis_size(axis)
    return lax.ppermute(value, axis, [(i, (i + step) % count) for i in range(count)])


def after(value, *earlier):
    return lax.optimization_barrier((value, *earlier))[0]


def on_device(populations, destination, refinement):
    blocks = populations.shape[0]
    row_count = lax.axis_size("row")
    col_count = lax.axis_size("col")
    cap_row = 2 * ((blocks + row_count - 1) // row_count)
    cap_col = 2 * ((blocks + col_count - 1) // col_count)
    ordered = jnp.transpose(populations, (1, 0, 2))

    def prepared(part, *earlier):
        first = after(destination, *earlier)
        return pre(ordered, first, refinement, part, row_count, cap_row, blocks * col_count)

    def to_rows(sent):
        return lax.all_to_all(sent, "row", split_axis=0, concat_axis=0, tiled=True)

    def to_columns(packed):
        return [exchanged(packed[d], "col", d) for d in range(col_count - 1, 0, -1)] + [packed[0]]

    sent = prepared(0)
    in_row = [to_rows(sent)]
    in_row.append(to_rows(after(prepared(1, sent), in_row[0])))
    packed, plan = repack(in_row[0], None, 0, col_count, cap_col, blocks)
    in_row.append(to_rows(prepared(2, packed[0])))
    ylo, yhi, xlo, xhi, picked, fields = faces(to_columns(packed))
    below, above = shifted(yhi, "col", 1), shifted(ylo, "col", -1)
    middle = to_columns(repack(in_row[1], plan, 1, col_count, cap_col, blocks))
    in_row[2], below, above = lax.optimization_barrier((in_row[2], below, above))
    up = jnp.concatenate([xhi.reshape(18, SUB, LANES), below[6:, 1], above[6:, 1]])
    down = jnp.concatenate([xlo.reshape(18, SUB, LANES), below[:3, 0], above[:3, 0]])
    xlo, xhi = shifted(up, "row", 1), shifted(down, "row", -1)
    packed = repack(in_row[2], plan, 2, col_count, cap_col, blocks)
    picked, packed = lax.optimization_barrier((picked, list(packed)))
    last = to_columns(packed)
    out, kept = advance(picked, middle, fields, xlo, xhi, below, above)
    return jnp.transpose(finish(picked, last, fields, kept, below, above, out), (1, 0, 2))


def solution(mesh):
    return jax.shard_map(
        on_device,
        mesh=mesh,
        in_specs=(P(("row", "col"), None, None), P(("row", "col")), P(("row", "col"))),
        out_specs=P(("row", "col"), None, None),
        check_vma=False,
    )
```

```python
import functools

import jax
import jax.numpy as jnp
from jax import lax
from jax.experimental import pallas as pl
from jax.experimental.pallas import tpu as pltpu
from jax.sharding import PartitionSpec as P

EDGE = 16
VISCOSITY = 0.01
LANES = 128
SUB = 8
NQ = 27
NFIELD = 9
GROUPS = 4
WIDTH = EDGE // GROUPS
CHUNKS = ((0, 3), (1, 2))
INNER = CHUNKS[1]
SIDE_TILES = 3
LATE_TILES = -(-NFIELD * (SUB - 1) // SUB)
VMEM_LIMIT = 20 * 1024 * 1024
LARGE_VMEM_LIMIT = 60 * 1024 * 1024


def velocity(q):
    return (q // 9 - 1, (q // 3) % 3 - 1, q % 3 - 1)


def tiles_of(part):
    return len(INNER) * LATE_TILES if part else len(CHUNKS[0]) * NFIELD + SIDE_TILES


def free_place(c):
    return (c % 2) * (SUB - 1)


def step_to(target, here, count):
    if count & (count - 1) == 0:
        return target ^ here
    return lax.rem(target - here + count, count)


def exchanged(value, axis, step):
    count = lax.axis_size(axis)
    if count & (count - 1) == 0:
        pairs = [(i, i ^ step) for i in range(count)]
    else:
        pairs = [(i, (i + step) % count) for i in range(count)]
    return lax.ppermute(value, axis, pairs)


def raw_moments(f):
    whole, slope, outer = {}, {}, {}
    for i in range(3):
        for j in range(3):
            low, rest, high = (f[i * 9 + j * 3 + k] for k in range(3))
            outer[i, j] = low + high
            whole[i, j] = outer[i, j] + rest
            slope[i, j] = high - low
    column = [whole[i, 0] + whole[i, 1] + whole[i, 2] for i in range(3)]
    tilt = [slope[i, 0] + slope[i, 1] + slope[i, 2] for i in range(3)]
    low_y = whole[0, 0] + whole[1, 0] + whole[2, 0]
    high_y = whole[0, 2] + whole[1, 2] + whole[2, 2]
    ends = column[0] + column[2]
    mzz = sum(outer[i, j] for i in range(3) for j in range(3))
    mxy = (whole[2, 2] - whole[2, 0]) - (whole[0, 2] - whole[0, 0])
    myz = (slope[0, 2] + slope[1, 2] + slope[2, 2]) - (slope[0, 0] + slope[1, 0] + slope[2, 0])
    return (
        ends + column[1],
        column[2] - column[0],
        high_y - low_y,
        tilt[0] + tilt[1] + tilt[2],
        ends,
        low_y + high_y,
        mzz,
        mxy,
        tilt[2] - tilt[0],
        myz,
    )


def collided(f, keep):
    rho, jx, jy, jz, mxx, myy, mzz, mxy, mxz, myz = raw_moments(f)
    inverse = 1.0 / rho
    ux, uy, uz = jx * inverse, jy * inverse, jz * inverse
    kxx = mxx - jx * ux
    return (
        rho, ux, uy, uz,
        keep * (mxy - jx * uy),
        keep * (mxz - jx * uz),
        keep * (myz - jy * uz),
        keep * (kxx - (myy - jy * uy)),
        keep * (kxx - (mzz - jz * uz)),
    )


def pre_kernel(cap, row_count, per_row, part, dest_hbm, level_hbm, x_hbm, out_ref, *refs):
    x_ref, swap_ref, packed_ref, side_ref, dest_ref, level_ref, sems = refs
    order = CHUNKS[part] if part else CHUNKS[0] + INNER
    steps = len(CHUNKS[part])
    blocks = x_ref.shape[2]
    cells = x_ref.shape[3]
    chunks = cells // LANES
    small = [
        pltpu.make_async_copy(dest_hbm, dest_ref, sems.at[0]),
        pltpu.make_async_copy(level_hbm, level_ref, sems.at[1]),
    ]
    large = [
        pltpu.make_async_copy(
            x_hbm.at[:, :, pl.ds(group * cells, cells)], x_ref.at[step], sems.at[2 + step]
        )
        for step, group in enumerate(order)
    ]
    for copy in small + large:
        copy.start()
    for copy in small:
        copy.wait()

    which = lax.broadcasted_iota(jnp.int32, (SUB, LANES), 0)
    spot = lax.broadcasted_iota(jnp.int32, (SUB, LANES), 1) // EDGE
    scale = jnp.zeros((SUB, LANES), jnp.int32)
    tag = jnp.zeros((SUB, LANES), jnp.int32)
    for t in range(blocks):
        scale = jnp.where(which == t, jnp.left_shift(1, level_ref[t]), scale)
        tag = jnp.where(which == t, dest_ref[t], tag)
    rate = 1.0 / (3.0 * VISCOSITY * scale.astype(jnp.float32) + 0.5)
    keep = 1.0 - rate

    rows = [dest_ref[t] // per_row for t in range(blocks)]
    slots = []
    for t in range(blocks):
        slot = rows[t] * cap
        for other in range(t):
            slot = slot + jnp.where(rows[other] == rows[t], 1, 0)
        slots.append(slot)

    def spread(ref, first, count):
        for t in range(blocks):
            for n in range(count):
                moved = ref[pl.ds(n * SUB * SUB + t, SUB, stride=SUB), :]
                out_ref[slots[t], first + n] = moved

    def fields_at(step, c):
        return collided([x_ref[step, q, :, c * LANES : (c + 1) * LANES] for q in range(NQ)], keep)

    for step, group in enumerate(order):
        large[step].wait()
        if part:
            last = fields_at(step, chunks - 1)
            for c in range(chunks - 1):
                place = free_place(c)
                turn = (place - c) * EDGE % LANES
                for n, field in enumerate(fields_at(step, c)):
                    other = pltpu.roll(last[n], turn, axis=1) if turn else last[n]
                    base = (step * LATE_TILES * SUB + n * (chunks - 1) + c) * SUB
                    swap_ref[base : base + SUB, :] = jnp.where(spot == place, other, field)
            continue
        if step < steps:
            for c in range(chunks):
                for n, field in enumerate(fields_at(step, c)):
                    base = (n * chunks + c) * SUB
                    swap_ref[base : base + SUB, :] = field
            spread(swap_ref, SIDE_TILES + step * NFIELD, NFIELD)
            continue
        for q in range(NQ):
            for half in range(2):
                value = packed_ref[half * NQ + q] if step > steps else None
                for x in range(WIDTH):
                    c = x * 2 + half
                    at = (group * WIDTH + x) % SUB
                    moved = x_ref[step, q, :, c * LANES : (c + 1) * LANES]
                    turn = (at + half) * EDGE % LANES
                    if turn:
                        moved = pltpu.roll(moved, turn, axis=1)
                    value = moved if value is None else jnp.where(spot == at, moved, value)
                packed_ref[half * NQ + q] = value

    if part:
        for step in range(steps):
            for row in range(NFIELD * (chunks - 1), LATE_TILES * SUB):
                base = (step * LATE_TILES * SUB + row) * SUB
                swap_ref[base : base + SUB, :] = tag.astype(jnp.float32)
        spread(swap_ref, 0, steps * LATE_TILES)
        return
    for row in range(SIDE_TILES * SUB):
        if not 1 <= row <= 2 * NFIELD:
            side_ref[row * SUB : (row + 1) * SUB, :] = tag.astype(jnp.float32)
    for half in range(2):
        fields = collided([packed_ref[half * NQ + q] for q in range(NQ)], keep)
        for n, field in enumerate(fields):
            base = (1 + half * NFIELD + n) * SUB
            side_ref[base : base + SUB, :] = field
    for slot in range(row_count * cap):
        out_ref[slot, 0] = jnp.full((SUB, LANES), -1.0, jnp.float32)
    spread(side_ref, 0, SIDE_TILES)


def pre(populations, destination, refinement, part, row_count, cap, per_row):
    blocks = populations.shape[1]
    cells = populations.shape[2] // GROUPS
    loaded = len(CHUNKS[part]) + (0 if part else len(INNER))
    rows = tiles_of(1) * SUB if part else NFIELD * cells // LANES
    return pl.pallas_call(
        functools.partial(pre_kernel, cap, row_count, per_row, part),
        in_specs=[pl.BlockSpec(memory_space=pltpu.HBM)] * 3,
        out_specs=pl.BlockSpec(memory_space=pltpu.VMEM),
        out_shape=jax.ShapeDtypeStruct((row_count * cap, tiles_of(part), SUB, LANES), jnp.float32),
        scratch_shapes=[
            pltpu.VMEM((loaded, NQ, blocks, cells), jnp.float32),
            pltpu.VMEM((rows * SUB, LANES), jnp.float32),
            pltpu.VMEM((2 * NQ, SUB, LANES), jnp.float32),
            pltpu.VMEM((SIDE_TILES * SUB * SUB, LANES), jnp.float32),
            pltpu.SMEM((blocks,), jnp.int32),
            pltpu.SMEM((blocks,), jnp.int32),
            pltpu.SemaphoreType.DMA((2 + loaded,)),
        ],
        compiler_params=pltpu.CompilerParams(vmem_limit_bytes=LARGE_VMEM_LIMIT),
        cost_estimate=pl.CostEstimate(flops=10**7, bytes_accessed=4 * 10**6, transcendentals=0),
        name="pre_%d" % part,
    )(destination, refinement, populations)


def read_tags(ins, tag_ref, sems):
    cap = ins[0].shape[0]
    copies = [
        pltpu.make_async_copy(in_ref.at[:, 0, pl.ds(0, 1)], tag_ref.at[pl.ds(d * cap, cap)], sems.at[d])
        for d, in_ref in enumerate(ins)
    ]
    for copy in copies:
        copy.start()
    for copy in copies:
        copy.wait()
    return lambda e: tag_ref[e, 0, 0].astype(jnp.int32)


def tag_scratch(arrays, slots):
    return [pltpu.SMEM((slots, 1, LANES), jnp.float32), pltpu.SemaphoreType.DMA((arrays,))]


def repack_kernel(cap, col_count, blocks, part, *refs):
    if part:
        plan_ref, in_ref, *outs = refs
    else:
        in_ref, *outs, plan_ref, tag_ref, sems, count_ref = refs
        tag_at = read_tags([in_ref], tag_ref, sems)
        here = lax.axis_index("col")
        for d in range(col_count):
            count_ref[d] = 0
        for e in range(col_count * cap):
            plan_ref[e] = -1
        for e in range(in_ref.shape[0]):
            tag = tag_at(e)

            @pl.when(tag >= 0)
            def _():
                d = step_to(lax.rem(tag // blocks, col_count), here, col_count)
                k = count_ref[d]
                count_ref[d] = k + 1
                plan_ref[d * cap + k] = e

    tiles = outs[0].shape[1]
    for place, out in enumerate(outs):
        quarter, d = divmod(place, col_count)
        for k in range(cap):
            e = plan_ref[d * cap + k]

            @pl.when(e >= 0)
            def _():
                out[k] = in_ref[e, quarter * tiles : (quarter + 1) * tiles]

            if part == 0:

                @pl.when(e < 0)
                def _():
                    out[k, 0] = jnp.full((SUB, LANES), -1.0, jnp.float32)


def repack(landed, plan, part, col_count, cap, blocks):
    whole = pl.BlockSpec(memory_space=pltpu.VMEM)
    scalars = pl.BlockSpec(memory_space=pltpu.SMEM)
    scratch = []
    if part == 0:
        scratch = tag_scratch(1, landed.shape[0]) + [pltpu.SMEM((col_count,), jnp.int32)]
    quarters = len(INNER) if part else 1
    shape = (cap, landed.shape[1] // quarters) + landed.shape[2:]
    packed = pl.pallas_call(
        functools.partial(repack_kernel, cap, col_count, blocks, part),
        in_specs=([scalars] if part else []) + [whole],
        out_specs=[whole] * (quarters * col_count) + ([] if part else [scalars]),
        scratch_shapes=scratch,
        out_shape=[jax.ShapeDtypeStruct(shape, jnp.float32)] * (quarters * col_count)
        + ([] if part else [jax.ShapeDtypeStruct((col_count * cap,), jnp.int32)]),
        compiler_params=pltpu.CompilerParams(vmem_limit_bytes=VMEM_LIMIT),
        cost_estimate=pl.CostEstimate(flops=0, bytes_accessed=3 * 10**6, transcendentals=0),
        name="repack_%d" % part,
    )(*([plan] if part else []), landed)
    return packed if part else (packed[:-1], packed[-1])


def backward(zeroth, first, second, u):
    raw_one, raw_two = first, second
    if zeroth is not None:
        moved = u * zeroth
        raw_one = moved if raw_one is None else raw_one + moved
        square = u * moved
        raw_two = square if raw_two is None else raw_two + square
    if first is not None:
        cross = (u + u) * first
        raw_two = cross if raw_two is None else raw_two + cross
    rest = -raw_two if zeroth is None else zeroth - raw_two
    return 0.5 * (raw_two - raw_one), rest, 0.5 * (raw_one + raw_two)


def post_populations(rho, ux, uy, uz, pxy, pxz, pyz, dev_one, dev_two):
    inverse = 1.0 / rho
    pxx = (rho + dev_one + dev_two) * (1.0 / 3.0)
    pyy = pxx - dev_one
    pzz = pxx - dev_two
    sxy, sxz, syz = pxy * inverse, pxz * inverse, pyz * inverse
    syy, szz = pyy * inverse, pzz * inverse
    central = {
        (0, 0, 0): rho, (2, 0, 0): pxx, (0, 2, 0): pyy, (0, 0, 2): pzz,
        (1, 1, 0): pxy, (1, 0, 1): pxz, (0, 1, 1): pyz,
        (2, 2, 0): pxx * syy + 2.0 * pxy * sxy,
        (2, 0, 2): pxx * szz + 2.0 * pxz * sxz,
        (0, 2, 2): pyy * szz + 2.0 * pyz * syz,
        (2, 1, 1): pxx * syz + 2.0 * pxy * sxz,
        (1, 2, 1): pyy * sxz + 2.0 * pxy * syz,
        (1, 1, 2): pzz * sxy + 2.0 * pxz * syz,
        (2, 2, 2): pxx * syy * szz
        + 2.0 * (pxx * syz * syz + pyy * sxz * sxz + pzz * sxy * sxy)
        + 8.0 * pxy * sxz * syz,
    }
    along_z = {}
    for a in range(3):
        for b in range(3):
            parts = backward(*(central.get((a, b, c)) for c in range(3)), uz)
            for k in range(3):
                along_z[a, b, k] = parts[k]
    along_y = {}
    for a in range(3):
        for k in range(3):
            parts = backward(*(along_z[a, b, k] for b in range(3)), uy)
            for j in range(3):
                along_y[a, j, k] = parts[j]
    result = [None] * NQ
    for j in range(3):
        for k in range(3):
            parts = backward(*(along_y[a, j, k] for a in range(3)), ux)
            for i in range(3):
                result[i * 9 + j * 3 + k] = parts[i]
    return result


def unload(plan_ref, ins, fields_ref):
    cap, tiles = ins[0].shape[:2]
    for e in range(len(ins) * cap):
        t = plan_ref[e]

        @pl.when(t >= 0)
        def _():
            for tile in range(tiles):
                fields_ref[pl.ds(tile * SUB * SUB + t, SUB, stride=SUB), :] = ins[e // cap][e % cap, tile]


def row_of(ref, row):
    return ref[row * SUB : (row + 1) * SUB, :]


def turned(value, places):
    turn = places * EDGE % LANES
    return pltpu.roll(value, turn, axis=1) if turn else value


def places_y():
    return lax.broadcasted_iota(jnp.int32, (SUB, LANES), 1) // EDGE


def outer_fields(fields_ref, step, c):
    first = (SIDE_TILES + step * NFIELD) * SUB
    return [row_of(fields_ref, first + n * SUB + c) for n in range(NFIELD)]


def side_fields(fields_ref, half):
    return [row_of(fields_ref, 1 + half * NFIELD + n) for n in range(NFIELD)]


def fill_outer(fields_ref, main_ref):
    for step, group in enumerate(CHUNKS[0]):
        for c in range(SUB):
            for q, value in enumerate(post_populations(*outer_fields(fields_ref, step, c))):
                main_ref[q, 2 + group * SUB + c] = value


def fill_inner(fields_ref, late_ref, group, main_ref):
    spot = places_y()
    last = [None] * NFIELD
    for c in range(SUB):
        at = (group * WIDTH + c // 2) % SUB
        place = free_place(c)
        side = side_fields(fields_ref, c % 2)
        fields = []
        for n in range(NFIELD):
            if c < SUB - 1:
                row = row_of(late_ref, n * (SUB - 1) + c)
                part = turned(row, c - place)
                last[n] = part if c == 0 else jnp.where(spot == c, part, last[n])
            else:
                row = last[n]
            fields.append(jnp.where(spot == place, turned(side[n], place - at), row))
        for q, value in enumerate(post_populations(*fields)):
            main_ref[q, 2 + group * SUB + c] = value


def fill_sides(below_in, above_in, below_ref, above_ref, first, last):
    for x in range(first, last):
        at = x % SUB
        for k in range(9):
            below_ref[k, x + 1] = turned(below_in[k, x // SUB], SUB - 1 - at)
            above_ref[k, x + 1] = turned(above_in[k, x // SUB], -at)


def stream_pair(first_x, out_ref, main_ref, below_ref, above_ref):
    lane = lax.broadcasted_iota(jnp.int32, (SUB, LANES), 1)
    block = lax.broadcasted_iota(jnp.int32, (SUB, LANES), 0)
    along = lane % EDGE
    first_z, last_z = along == 0, along == EDGE - 1
    floor = first_z & (block == 0)
    ceiling = last_z & (block == SUB - 1)
    low_y, high_y = lane < EDGE, lane >= LANES - EDGE
    for i in range(2):
        for half in range(2):
            c = i * 2 + half
            for q in range(NQ):
                cx, cy, cz = velocity(q)
                x = first_x + i - cx + 1
                a = main_ref[q, x * 2 + half]
                k = (cx + 1) * 3 + cz + 1
                if cy == 1:
                    a = jnp.where(high_y, main_ref[q, x * 2] if half else below_ref[k, x], a)
                elif cy == -1:
                    a = jnp.where(low_y, above_ref[k, x] if half else main_ref[q, x * 2 + 1], a)
                shift = EDGE * cy + cz
                value = a if shift == 0 else pltpu.roll(a, shift % LANES, axis=1)
                if cz:
                    bounced = main_ref[26 - q, (first_x + i + 1) * 2 + half]
                    turn = (1 if cz == 1 else SUB - 1)
                    fill = pltpu.roll(pltpu.roll(a, turn, axis=0), (shift - cz * EDGE) % LANES, axis=1)
                    value = jnp.where(first_z if cz == 1 else last_z, fill, value)
                    value = jnp.where(floor if cz == 1 else ceiling, bounced, value)
                out_ref[q, :, c * LANES : (c + 1) * LANES] = value


def faces_kernel(count, *refs):
    ins = refs[:count]
    ylo_ref, yhi_ref, xlo_ref, xhi_ref, plan_ref, fields_ref, tag_ref, sems = refs[count:]
    tag_at = read_tags(ins, tag_ref, sems)
    for e in range(count * ins[0].shape[0]):
        tag = tag_at(e)
        plan_ref[e] = jnp.where(tag >= 0, lax.rem(tag, SUB), -1)
    unload(plan_ref, ins, fields_ref)
    spot = places_y()
    for half in range(2):
        packed = [side_fields(fields_ref, half)] * 2
        place = half * (SUB - 1)
        for step, group in enumerate(CHUNKS[0]):
            tile = group * WIDTH // SUB
            for x in range(group * WIDTH, (group + 1) * WIDTH):
                c = (x - group * WIDTH) * 2 + half
                packed[tile] = [
                    jnp.where(spot == x % SUB, turned(value, x % SUB - place), old)
                    for value, old in zip(outer_fields(fields_ref, step, c), packed[tile])
                ]
        for tile in range(2):
            result = post_populations(*packed[tile])
            for i in range(3):
                for k in range(3):
                    (yhi_ref if half else ylo_ref)[i * 3 + k, tile] = result[i * 9 + half * 6 + k]
        low = post_populations(*outer_fields(fields_ref, CHUNKS[0].index(0), half))
        high = post_populations(*outer_fields(fields_ref, CHUNKS[0].index(GROUPS - 1), SUB - 2 + half))
        for q in range(9):
            xlo_ref[q, half] = low[q]
            xhi_ref[q, half] = high[18 + q]


def faces(homes):
    shape = jax.ShapeDtypeStruct
    face = shape((9, 2, SUB, LANES), jnp.float32)
    slots = len(homes) * homes[0].shape[0]
    whole = pl.BlockSpec(memory_space=pltpu.VMEM)
    return pl.pallas_call(
        functools.partial(faces_kernel, len(homes)),
        in_specs=[whole] * len(homes),
        out_specs=[whole] * 4 + [pl.BlockSpec(memory_space=pltpu.SMEM), whole],
        scratch_shapes=tag_scratch(len(homes), slots),
        out_shape=[face] * 4
        + [shape((slots,), jnp.int32), shape((tiles_of(0) * SUB * SUB, LANES), jnp.float32)],
        compiler_params=pltpu.CompilerParams(vmem_limit_bytes=VMEM_LIMIT),
        cost_estimate=pl.CostEstimate(flops=10**7, bytes_accessed=3 * 10**6, transcendentals=0),
        name="faces",
    )(*homes)


PAIRS = ((0, 1, 2, 7), (3, 4, 5, 6))
KEPT = ((5, 8), (12, 15))


def advance_kernel(count, plan_ref, *refs):
    ins = refs[:count]
    (
        fields_ref, xlo_ref, xhi_ref, below_in, above_in, out_ref, kept_ref,
        main_ref, below_ref, above_ref, late_ref,
    ) = refs[count:]
    g = pl.program_id(0)

    @pl.when(g == 0)
    def _():
        unload(plan_ref, ins, late_ref)
        fill_outer(fields_ref, main_ref)
        fill_inner(fields_ref, late_ref, INNER[0], main_ref)
        fill_sides(below_in, above_in, below_ref, above_ref, 0, 7)
        fill_sides(below_in, above_in, below_ref, above_ref, 13, EDGE)
        for k in range(3):
            below_ref[6 + k, 0] = xlo_ref[18 + k]
            above_ref[6 + k, 0] = turned(xlo_ref[21 + k], 1)
            below_ref[k, EDGE + 1] = turned(xhi_ref[18 + k], -1)
            above_ref[k, EDGE + 1] = xhi_ref[21 + k]
        for q in range(9):
            for half in range(2):
                main_ref[18 + q, half] = xlo_ref[q * 2 + half]
                main_ref[q, 2 * EDGE + 2 + half] = xhi_ref[q * 2 + half]
        to = 0
        for first, last in KEPT:
            for row in range(2 * first + 2, 2 * last + 2):
                for q in range(NQ):
                    kept_ref[q, to] = main_ref[q, row]
                to += 1

    first_x = 2 * jnp.where(g == len(PAIRS[0]) - 1, PAIRS[0][-1], g)
    stream_pair(first_x, out_ref, main_ref, below_ref, above_ref)


def finish_kernel(count, plan_ref, *refs):
    ins = refs[:count]
    (
        fields_ref, kept_ref, below_in, above_in, _, out_ref,
        main_ref, below_ref, above_ref, late_ref, sems,
    ) = refs[count:]
    g = pl.program_id(0)

    @pl.when(g == 0)
    def _():
        copies = []
        to = 0
        for first, last in KEPT:
            rows = 2 * (last - first)
            copies.append(
                pltpu.make_async_copy(
                    kept_ref.at[:, pl.ds(to, rows)],
                    main_ref.at[:, pl.ds(2 * first + 2, rows)],
                    sems.at[len(copies)],
                )
            )
            to += rows
        for copy in copies:
            copy.start()
        unload(plan_ref, ins, late_ref)
        fill_inner(fields_ref, late_ref, INNER[1], main_ref)
        fill_sides(below_in, above_in, below_ref, above_ref, 5, 15)
        for copy in copies:
            copy.wait()

    stream_pair(2 * (PAIRS[1][0] + g), out_ref, main_ref, below_ref, above_ref)


def whole_of(value):
    rank = len(value.shape)
    return pl.BlockSpec(value.shape, lambda g, *_: (0,) * rank)


def scratch_of_lattice():
    side = pltpu.VMEM((9, EDGE + 2, SUB, LANES), jnp.float32)
    return [
        pltpu.VMEM((NQ, 2 * EDGE + 4, SUB, LANES), jnp.float32), side, side,
        pltpu.VMEM((LATE_TILES * SUB * SUB, LANES), jnp.float32),
    ]


def advance(plan, homes, fields, xlo, xhi, below, above):
    pairs = PAIRS[0]
    inputs = [*homes, fields, xlo, xhi, below, above]
    kept = jax.ShapeDtypeStruct(
        (NQ, 2 * sum(last - first for first, last in KEPT), SUB, LANES), jnp.float32
    )
    return pl.pallas_call(
        functools.partial(advance_kernel, len(homes)),
        grid_spec=pltpu.PrefetchScalarGridSpec(
            num_scalar_prefetch=1,
            grid=(len(pairs),),
            in_specs=[whole_of(value) for value in inputs],
            out_specs=[
                pl.BlockSpec(
                    (NQ, SUB, 4 * LANES),
                    lambda g, *_: (0, 0, jnp.where(g == len(pairs) - 1, pairs[-1], g)),
                ),
                whole_of(kept),
            ],
            scratch_shapes=scratch_of_lattice(),
        ),
        out_shape=[jax.ShapeDtypeStruct((NQ, SUB, GROUPS * SUB * LANES), jnp.float32), kept],
        compiler_params=pltpu.CompilerParams(vmem_limit_bytes=VMEM_LIMIT),
        cost_estimate=pl.CostEstimate(flops=10**7, bytes_accessed=5 * 10**6, transcendentals=0),
        name="advance",
    )(plan, *inputs)


def finish(plan, homes, fields, kept, below, above, out):
    pairs = PAIRS[1]
    anywhere = pl.BlockSpec(memory_space=pl.ANY)
    return pl.pallas_call(
        functools.partial(finish_kernel, len(homes)),
        grid_spec=pltpu.PrefetchScalarGridSpec(
            num_scalar_prefetch=1,
            grid=(len(pairs),),
            in_specs=[whole_of(value) for value in (*homes, fields)]
            + [anywhere, whole_of(below), whole_of(above), anywhere],
            out_specs=pl.BlockSpec((NQ, SUB, 4 * LANES), lambda g, *_: (0, 0, pairs[0] + g)),
            scratch_shapes=scratch_of_lattice() + [pltpu.SemaphoreType.DMA((len(KEPT),))],
        ),
        out_shape=jax.ShapeDtypeStruct(out.shape, jnp.float32),
        input_output_aliases={len(homes) + 5: 0},
        compiler_params=pltpu.CompilerParams(vmem_limit_bytes=VMEM_LIMIT),
        cost_estimate=pl.CostEstimate(flops=10**7, bytes_accessed=5 * 10**6, transcendentals=0),
        name="finish",
    )(plan, *homes, fields, kept, below, above, out)


def shifted(value, axis, step):
    count = lax.axis_size(axis)
    return lax.ppermute(value, axis, [(i, (i + step) % count) for i in range(count)])


def after(value, *earlier):
    return lax.optimization_barrier((value, *earlier))[0]


def on_device(populations, destination, refinement):
    blocks = populations.shape[0]
    row_count = lax.axis_size("row")
    col_count = lax.axis_size("col")
    cap_row = 2 * ((blocks + row_count - 1) // row_count)
    cap_col = 2 * ((blocks + col_count - 1) // col_count)
    ordered = jnp.transpose(populations, (1, 0, 2))

    def prepared(part, *earlier):
        first = after(destination, *earlier)
        return pre(ordered, first, refinement, part, row_count, cap_row, blocks * col_count)

    def to_rows(sent):
        return lax.all_to_all(sent, "row", split_axis=0, concat_axis=0, tiled=True)

    def to_columns(packed):
        return [exchanged(packed[d], "col", d) for d in range(col_count - 1, 0, -1)] + [packed[0]]

    sent = prepared(0)
    early_row = to_rows(sent)
    late_row = to_rows(prepared(1, sent))
    packed, plan = repack(early_row, None, 0, col_count, cap_col, blocks)
    ylo, yhi, xlo, xhi, picked, fields = faces(to_columns(packed))
    below, above = shifted(yhi, "col", 1), shifted(ylo, "col", -1)
    late_row, below, above = lax.optimization_barrier((late_row, below, above))
    up = jnp.concatenate([xhi.reshape(18, SUB, LANES), below[6:, 1], above[6:, 1]])
    down = jnp.concatenate([xlo.reshape(18, SUB, LANES), below[:3, 0], above[:3, 0]])
    xlo, xhi = shifted(up, "row", 1), shifted(down, "row", -1)
    packed = repack(late_row, plan, 1, col_count, cap_col, blocks)
    middle, last = to_columns(packed[:col_count]), to_columns(packed[col_count:])
    out, kept = advance(picked, middle, fields, xlo, xhi, below, above)
    return jnp.transpose(finish(picked, last, fields, kept, below, above, out), (1, 0, 2))


def solution(mesh):
    return jax.shard_map(
        on_device,
        mesh=mesh,
        in_specs=(P(("row", "col"), None, None), P(("row", "col")), P(("row", "col"))),
        out_specs=P(("row", "col"), None, None),
        check_vma=False,
    )
```

```python
import functools

import jax
import jax.numpy as jnp
from jax import lax
from jax.experimental import pallas as pl
from jax.experimental.pallas import tpu as pltpu
from jax.sharding import PartitionSpec as P

EDGE = 16
VISCOSITY = 0.01
LANES = 128
SUB = 8
NQ = 27
NFIELD = 9
GROUPS = 4
WIDTH = EDGE // GROUPS
CHUNKS = ((0, 3), (1, 2))
INNER = CHUNKS[1]
SIDE_TILES = 3
LATE_TILES = -(-NFIELD * (SUB - 1) // SUB)
VMEM_LIMIT = 20 * 1024 * 1024
LARGE_VMEM_LIMIT = 60 * 1024 * 1024


def velocity(q):
    return (q // 9 - 1, (q // 3) % 3 - 1, q % 3 - 1)


def tiles_of(part):
    return len(INNER) * LATE_TILES if part else len(CHUNKS[0]) * NFIELD + SIDE_TILES


def free_place(c):
    return (c % 2) * (SUB - 1)


def step_to(target, here, count):
    if count & (count - 1) == 0:
        return target ^ here
    return lax.rem(target - here + count, count)


def exchanged(value, axis, step):
    count = lax.axis_size(axis)
    if count & (count - 1) == 0:
        pairs = [(i, i ^ step) for i in range(count)]
    else:
        pairs = [(i, (i + step) % count) for i in range(count)]
    return lax.ppermute(value, axis, pairs)


def raw_moments(f):
    whole, slope, outer = {}, {}, {}
    for i in range(3):
        for j in range(3):
            low, rest, high = (f[i * 9 + j * 3 + k] for k in range(3))
            outer[i, j] = low + high
            whole[i, j] = outer[i, j] + rest
            slope[i, j] = high - low
    column = [whole[i, 0] + whole[i, 1] + whole[i, 2] for i in range(3)]
    tilt = [slope[i, 0] + slope[i, 1] + slope[i, 2] for i in range(3)]
    low_y = whole[0, 0] + whole[1, 0] + whole[2, 0]
    high_y = whole[0, 2] + whole[1, 2] + whole[2, 2]
    ends = column[0] + column[2]
    mzz = sum(outer[i, j] for i in range(3) for j in range(3))
    mxy = (whole[2, 2] - whole[2, 0]) - (whole[0, 2] - whole[0, 0])
    myz = (slope[0, 2] + slope[1, 2] + slope[2, 2]) - (slope[0, 0] + slope[1, 0] + slope[2, 0])
    return (
        ends + column[1],
        column[2] - column[0],
        high_y - low_y,
        tilt[0] + tilt[1] + tilt[2],
        ends,
        low_y + high_y,
        mzz,
        mxy,
        tilt[2] - tilt[0],
        myz,
    )


def collided(f, keep):
    rho, jx, jy, jz, mxx, myy, mzz, mxy, mxz, myz = raw_moments(f)
    inverse = 1.0 / rho
    ux, uy, uz = jx * inverse, jy * inverse, jz * inverse
    kxx = mxx - jx * ux
    return (
        rho, ux, uy, uz,
        keep * (mxy - jx * uy),
        keep * (mxz - jx * uz),
        keep * (myz - jy * uz),
        keep * (kxx - (myy - jy * uy)),
        keep * (kxx - (mzz - jz * uz)),
    )


def pre_kernel(cap, row_count, per_row, part, dest_hbm, level_hbm, x_hbm, out_ref, *refs):
    x_ref, swap_ref, packed_ref, side_ref, dest_ref, level_ref, sems = refs
    order = CHUNKS[part] if part else CHUNKS[0] + INNER
    steps = len(CHUNKS[part])
    blocks = x_ref.shape[2]
    cells = x_ref.shape[3]
    chunks = cells // LANES
    small = [
        pltpu.make_async_copy(dest_hbm, dest_ref, sems.at[0]),
        pltpu.make_async_copy(level_hbm, level_ref, sems.at[1]),
    ]
    large = [
        pltpu.make_async_copy(
            x_hbm.at[:, :, pl.ds(group * cells, cells)], x_ref.at[step], sems.at[2 + step]
        )
        for step, group in enumerate(order)
    ]
    for copy in small + large:
        copy.start()
    for copy in small:
        copy.wait()

    which = lax.broadcasted_iota(jnp.int32, (SUB, LANES), 0)
    spot = lax.broadcasted_iota(jnp.int32, (SUB, LANES), 1) // EDGE
    scale = jnp.zeros((SUB, LANES), jnp.int32)
    tag = jnp.zeros((SUB, LANES), jnp.int32)
    for t in range(blocks):
        scale = jnp.where(which == t, jnp.left_shift(1, level_ref[t]), scale)
        tag = jnp.where(which == t, dest_ref[t], tag)
    rate = 1.0 / (3.0 * VISCOSITY * scale.astype(jnp.float32) + 0.5)
    keep = 1.0 - rate

    rows = [dest_ref[t] // per_row for t in range(blocks)]
    slots = []
    for t in range(blocks):
        slot = rows[t] * cap
        for other in range(t):
            slot = slot + jnp.where(rows[other] == rows[t], 1, 0)
        slots.append(slot)

    def spread(ref, first, count):
        for t in range(blocks):
            for n in range(count):
                moved = ref[pl.ds(n * SUB * SUB + t, SUB, stride=SUB), :]
                out_ref[slots[t], first + n] = moved

    def fields_at(step, c):
        return collided([x_ref[step, q, :, c * LANES : (c + 1) * LANES] for q in range(NQ)], keep)

    for step, group in enumerate(order):
        large[step].wait()
        if part:
            last = fields_at(step, chunks - 1)
            for c in range(chunks - 1):
                place = free_place(c)
                turn = (place - c) * EDGE % LANES
                for n, field in enumerate(fields_at(step, c)):
                    other = pltpu.roll(last[n], turn, axis=1) if turn else last[n]
                    base = (step * LATE_TILES * SUB + n * (chunks - 1) + c) * SUB
                    swap_ref[base : base + SUB, :] = jnp.where(spot == place, other, field)
            continue
        if step < steps:
            for c in range(chunks):
                for n, field in enumerate(fields_at(step, c)):
                    base = (n * chunks + c) * SUB
                    swap_ref[base : base + SUB, :] = field
            spread(swap_ref, SIDE_TILES + step * NFIELD, NFIELD)
            continue
        for q in range(NQ):
            for half in range(2):
                value = packed_ref[half * NQ + q] if step > steps else None
                for x in range(WIDTH):
                    c = x * 2 + half
                    at = (group * WIDTH + x) % SUB
                    moved = x_ref[step, q, :, c * LANES : (c + 1) * LANES]
                    turn = (at + half) * EDGE % LANES
                    if turn:
                        moved = pltpu.roll(moved, turn, axis=1)
                    value = moved if value is None else jnp.where(spot == at, moved, value)
                packed_ref[half * NQ + q] = value

    if part:
        for step in range(steps):
            for row in range(NFIELD * (chunks - 1), LATE_TILES * SUB):
                base = (step * LATE_TILES * SUB + row) * SUB
                swap_ref[base : base + SUB, :] = tag.astype(jnp.float32)
        spread(swap_ref, 0, steps * LATE_TILES)
        return
    for row in range(SIDE_TILES * SUB):
        if not 1 <= row <= 2 * NFIELD:
            side_ref[row * SUB : (row + 1) * SUB, :] = tag.astype(jnp.float32)
    for half in range(2):
        fields = collided([packed_ref[half * NQ + q] for q in range(NQ)], keep)
        for n, field in enumerate(fields):
            base = (1 + half * NFIELD + n) * SUB
            side_ref[base : base + SUB, :] = field
    for slot in range(row_count * cap):
        out_ref[slot, 0] = jnp.full((SUB, LANES), -1.0, jnp.float32)
    spread(side_ref, 0, SIDE_TILES)


def pre(populations, destination, refinement, part, row_count, cap, per_row):
    blocks = populations.shape[1]
    cells = populations.shape[2] // GROUPS
    loaded = len(CHUNKS[part]) + (0 if part else len(INNER))
    rows = tiles_of(1) * SUB if part else NFIELD * cells // LANES
    return pl.pallas_call(
        functools.partial(pre_kernel, cap, row_count, per_row, part),
        in_specs=[pl.BlockSpec(memory_space=pltpu.HBM)] * 3,
        out_specs=pl.BlockSpec(memory_space=pltpu.VMEM),
        out_shape=jax.ShapeDtypeStruct((row_count * cap, tiles_of(part), SUB, LANES), jnp.float32),
        scratch_shapes=[
            pltpu.VMEM((loaded, NQ, blocks, cells), jnp.float32),
            pltpu.VMEM((rows * SUB, LANES), jnp.float32),
            pltpu.VMEM((2 * NQ, SUB, LANES), jnp.float32),
            pltpu.VMEM((SIDE_TILES * SUB * SUB, LANES), jnp.float32),
            pltpu.SMEM((blocks,), jnp.int32),
            pltpu.SMEM((blocks,), jnp.int32),
            pltpu.SemaphoreType.DMA((2 + loaded,)),
        ],
        compiler_params=pltpu.CompilerParams(vmem_limit_bytes=LARGE_VMEM_LIMIT),
        cost_estimate=pl.CostEstimate(flops=10**7, bytes_accessed=4 * 10**6, transcendentals=0),
        name="pre_%d" % part,
    )(destination, refinement, populations)


def read_tags(ins, tag_ref, sems):
    cap = ins[0].shape[0]
    copies = [
        pltpu.make_async_copy(in_ref.at[:, 0, pl.ds(0, 1)], tag_ref.at[pl.ds(d * cap, cap)], sems.at[d])
        for d, in_ref in enumerate(ins)
    ]
    for copy in copies:
        copy.start()
    for copy in copies:
        copy.wait()
    return lambda e: tag_ref[e, 0, 0].astype(jnp.int32)


def tag_scratch(arrays, slots):
    return [pltpu.SMEM((slots, 1, LANES), jnp.float32), pltpu.SemaphoreType.DMA((arrays,))]


def repack_kernel(cap, col_count, blocks, part, *refs):
    if part:
        plan_ref, in_ref, *outs = refs
    else:
        in_ref, *outs, plan_ref, tag_ref, sems, count_ref = refs
        tag_at = read_tags([in_ref], tag_ref, sems)
        here = lax.axis_index("col")
        for d in range(col_count):
            count_ref[d] = 0
        for e in range(col_count * cap):
            plan_ref[e] = -1
        for e in range(in_ref.shape[0]):
            tag = tag_at(e)

            @pl.when(tag >= 0)
            def _():
                d = step_to(lax.rem(tag // blocks, col_count), here, col_count)
                k = count_ref[d]
                count_ref[d] = k + 1
                plan_ref[d * cap + k] = e

    tiles = outs[0].shape[1]
    for place, out in enumerate(outs):
        quarter, d = divmod(place, col_count)
        for k in range(cap):
            e = plan_ref[d * cap + k]

            @pl.when(e >= 0)
            def _():
                out[k] = in_ref[e, quarter * tiles : (quarter + 1) * tiles]

            if part == 0:

                @pl.when(e < 0)
                def _():
                    out[k, 0] = jnp.full((SUB, LANES), -1.0, jnp.float32)


def repack(landed, plan, part, col_count, cap, blocks):
    whole = pl.BlockSpec(memory_space=pltpu.VMEM)
    scalars = pl.BlockSpec(memory_space=pltpu.SMEM)
    scratch = []
    if part == 0:
        scratch = tag_scratch(1, landed.shape[0]) + [pltpu.SMEM((col_count,), jnp.int32)]
    quarters = len(INNER) if part else 1
    shape = (cap, landed.shape[1] // quarters) + landed.shape[2:]
    packed = pl.pallas_call(
        functools.partial(repack_kernel, cap, col_count, blocks, part),
        in_specs=([scalars] if part else []) + [whole],
        out_specs=[whole] * (quarters * col_count) + ([] if part else [scalars]),
        scratch_shapes=scratch,
        out_shape=[jax.ShapeDtypeStruct(shape, jnp.float32)] * (quarters * col_count)
        + ([] if part else [jax.ShapeDtypeStruct((col_count * cap,), jnp.int32)]),
        compiler_params=pltpu.CompilerParams(vmem_limit_bytes=VMEM_LIMIT),
        cost_estimate=pl.CostEstimate(flops=0, bytes_accessed=3 * 10**6, transcendentals=0),
        name="repack_%d" % part,
    )(*([plan] if part else []), landed)
    return packed if part else (packed[:-1], packed[-1])


def backward(zeroth, first, second, u):
    raw_one, raw_two = first, second
    if zeroth is not None:
        moved = u * zeroth
        raw_one = moved if raw_one is None else raw_one + moved
        square = u * moved
        raw_two = square if raw_two is None else raw_two + square
    if first is not None:
        cross = (u + u) * first
        raw_two = cross if raw_two is None else raw_two + cross
    rest = -raw_two if zeroth is None else zeroth - raw_two
    return 0.5 * (raw_two - raw_one), rest, 0.5 * (raw_one + raw_two)


def post_populations(rho, ux, uy, uz, pxy, pxz, pyz, dev_one, dev_two):
    inverse = 1.0 / rho
    pxx = (rho + dev_one + dev_two) * (1.0 / 3.0)
    pyy = pxx - dev_one
    pzz = pxx - dev_two
    sxy, sxz, syz = pxy * inverse, pxz * inverse, pyz * inverse
    syy, szz = pyy * inverse, pzz * inverse
    central = {
        (0, 0, 0): rho, (2, 0, 0): pxx, (0, 2, 0): pyy, (0, 0, 2): pzz,
        (1, 1, 0): pxy, (1, 0, 1): pxz, (0, 1, 1): pyz,
        (2, 2, 0): pxx * syy + 2.0 * pxy * sxy,
        (2, 0, 2): pxx * szz + 2.0 * pxz * sxz,
        (0, 2, 2): pyy * szz + 2.0 * pyz * syz,
        (2, 1, 1): pxx * syz + 2.0 * pxy * sxz,
        (1, 2, 1): pyy * sxz + 2.0 * pxy * syz,
        (1, 1, 2): pzz * sxy + 2.0 * pxz * syz,
        (2, 2, 2): pxx * syy * szz
        + 2.0 * (pxx * syz * syz + pyy * sxz * sxz + pzz * sxy * sxy)
        + 8.0 * pxy * sxz * syz,
    }
    along_z = {}
    for a in range(3):
        for b in range(3):
            parts = backward(*(central.get((a, b, c)) for c in range(3)), uz)
            for k in range(3):
                along_z[a, b, k] = parts[k]
    along_y = {}
    for a in range(3):
        for k in range(3):
            parts = backward(*(along_z[a, b, k] for b in range(3)), uy)
            for j in range(3):
                along_y[a, j, k] = parts[j]
    result = [None] * NQ
    for j in range(3):
        for k in range(3):
            parts = backward(*(along_y[a, j, k] for a in range(3)), ux)
            for i in range(3):
                result[i * 9 + j * 3 + k] = parts[i]
    return result


def unload(plan_ref, ins, fields_ref):
    cap, tiles = ins[0].shape[:2]
    for e in range(len(ins) * cap):
        t = plan_ref[e]

        @pl.when(t >= 0)
        def _():
            for tile in range(tiles):
                fields_ref[pl.ds(tile * SUB * SUB + t, SUB, stride=SUB), :] = ins[e // cap][e % cap, tile]


def row_of(ref, row):
    return ref[row * SUB : (row + 1) * SUB, :]


def turned(value, places):
    turn = places * EDGE % LANES
    return pltpu.roll(value, turn, axis=1) if turn else value


def places_y():
    return lax.broadcasted_iota(jnp.int32, (SUB, LANES), 1) // EDGE


def outer_fields(fields_ref, step, c):
    first = (SIDE_TILES + step * NFIELD) * SUB
    return [row_of(fields_ref, first + n * SUB + c) for n in range(NFIELD)]


def side_fields(fields_ref, half):
    return [row_of(fields_ref, 1 + half * NFIELD + n) for n in range(NFIELD)]


def fill_outer(fields_ref, main_ref):
    for step, group in enumerate(CHUNKS[0]):
        for c in range(SUB):
            for q, value in enumerate(post_populations(*outer_fields(fields_ref, step, c))):
                main_ref[q, 2 + group * SUB + c] = value


def fill_inner(fields_ref, late_ref, group, main_ref):
    spot = places_y()
    last = [None] * NFIELD
    for c in range(SUB):
        at = (group * WIDTH + c // 2) % SUB
        place = free_place(c)
        side = side_fields(fields_ref, c % 2)
        fields = []
        for n in range(NFIELD):
            if c < SUB - 1:
                row = row_of(late_ref, n * (SUB - 1) + c)
                part = turned(row, c - place)
                last[n] = part if c == 0 else jnp.where(spot == c, part, last[n])
            else:
                row = last[n]
            fields.append(jnp.where(spot == place, turned(side[n], place - at), row))
        for q, value in enumerate(post_populations(*fields)):
            main_ref[q, 2 + group * SUB + c] = value


def fill_sides(below_in, above_in, below_ref, above_ref, first, last):
    for x in range(first, last):
        at = x % SUB
        for k in range(9):
            below_ref[k, x + 1] = turned(below_in[k, x // SUB], SUB - 1 - at)
            above_ref[k, x + 1] = turned(above_in[k, x // SUB], -at)


def stream_pair(first_x, out_ref, main_ref, below_ref, above_ref):
    lane = lax.broadcasted_iota(jnp.int32, (SUB, LANES), 1)
    block = lax.broadcasted_iota(jnp.int32, (SUB, LANES), 0)
    along = lane % EDGE
    first_z, last_z = along == 0, along == EDGE - 1
    floor = first_z & (block == 0)
    ceiling = last_z & (block == SUB - 1)
    low_y, high_y = lane < EDGE, lane >= LANES - EDGE
    for i in range(2):
        for half in range(2):
            c = i * 2 + half
            for q in range(NQ):
                cx, cy, cz = velocity(q)
                x = first_x + i - cx + 1
                a = main_ref[q, x * 2 + half]
                k = (cx + 1) * 3 + cz + 1
                if cy == 1:
                    a = jnp.where(high_y, main_ref[q, x * 2] if half else below_ref[k, x], a)
                elif cy == -1:
                    a = jnp.where(low_y, above_ref[k, x] if half else main_ref[q, x * 2 + 1], a)
                shift = EDGE * cy + cz
                value = a if shift == 0 else pltpu.roll(a, shift % LANES, axis=1)
                if cz:
                    bounced = main_ref[26 - q, (first_x + i + 1) * 2 + half]
                    turn = (1 if cz == 1 else SUB - 1)
                    fill = pltpu.roll(pltpu.roll(a, turn, axis=0), (shift - cz * EDGE) % LANES, axis=1)
                    value = jnp.where(first_z if cz == 1 else last_z, fill, value)
                    value = jnp.where(floor if cz == 1 else ceiling, bounced, value)
                out_ref[q, :, c * LANES : (c + 1) * LANES] = value


def stream_pairs(pairs, out_hbm, pair_ref, sems, *lattice):
    span = pair_ref.shape[3]

    def copy(i):
        return pltpu.make_async_copy(
            pair_ref.at[i], out_hbm.at[:, :, pl.ds(pairs[i] * span, span)], sems.at[i]
        )

    for i, pair in enumerate(pairs):
        stream_pair(2 * pair, pair_ref.at[i], *lattice)
        copy(i).start()
    for i in range(len(pairs)):
        copy(i).wait()


def faces_kernel(count, *refs):
    ins = refs[:count]
    ylo_ref, yhi_ref, xlo_ref, xhi_ref, plan_ref, fields_ref, tag_ref, sems = refs[count:]
    tag_at = read_tags(ins, tag_ref, sems)
    for e in range(count * ins[0].shape[0]):
        tag = tag_at(e)
        plan_ref[e] = jnp.where(tag >= 0, lax.rem(tag, SUB), -1)
    unload(plan_ref, ins, fields_ref)
    spot = places_y()
    for half in range(2):
        packed = [side_fields(fields_ref, half)] * 2
        place = half * (SUB - 1)
        for step, group in enumerate(CHUNKS[0]):
            tile = group * WIDTH // SUB
            for x in range(group * WIDTH, (group + 1) * WIDTH):
                c = (x - group * WIDTH) * 2 + half
                packed[tile] = [
                    jnp.where(spot == x % SUB, turned(value, x % SUB - place), old)
                    for value, old in zip(outer_fields(fields_ref, step, c), packed[tile])
                ]
        for tile in range(2):
            result = post_populations(*packed[tile])
            for i in range(3):
                for k in range(3):
                    (yhi_ref if half else ylo_ref)[i * 3 + k, tile] = result[i * 9 + half * 6 + k]
        low = post_populations(*outer_fields(fields_ref, CHUNKS[0].index(0), half))
        high = post_populations(*outer_fields(fields_ref, CHUNKS[0].index(GROUPS - 1), SUB - 2 + half))
        for q in range(9):
            xlo_ref[q, half] = low[q]
            xhi_ref[q, half] = high[18 + q]


def faces(homes):
    shape = jax.ShapeDtypeStruct
    face = shape((9, 2, SUB, LANES), jnp.float32)
    slots = len(homes) * homes[0].shape[0]
    whole = pl.BlockSpec(memory_space=pltpu.VMEM)
    return pl.pallas_call(
        functools.partial(faces_kernel, len(homes)),
        in_specs=[whole] * len(homes),
        out_specs=[whole] * 4 + [pl.BlockSpec(memory_space=pltpu.SMEM), whole],
        scratch_shapes=tag_scratch(len(homes), slots),
        out_shape=[face] * 4
        + [shape((slots,), jnp.int32), shape((tiles_of(0) * SUB * SUB, LANES), jnp.float32)],
        compiler_params=pltpu.CompilerParams(vmem_limit_bytes=VMEM_LIMIT),
        cost_estimate=pl.CostEstimate(flops=10**7, bytes_accessed=3 * 10**6, transcendentals=0),
        name="faces",
    )(*homes)


PAIRS = ((0, 1, 2, 7), (3, 4, 5, 6))
KEPT = ((5, 8), (12, 15))


def advance_kernel(count, plan_ref, *refs):
    ins = refs[:count]
    (
        fields_ref, xlo_ref, xhi_ref, below_in, above_in, out_ref, kept_ref,
        main_ref, below_ref, above_ref, late_ref, pair_ref, sems,
    ) = refs[count:]
    unload(plan_ref, ins, late_ref)
    fill_outer(fields_ref, main_ref)
    fill_inner(fields_ref, late_ref, INNER[0], main_ref)
    fill_sides(below_in, above_in, below_ref, above_ref, 0, 7)
    fill_sides(below_in, above_in, below_ref, above_ref, 13, EDGE)
    for k in range(3):
        below_ref[6 + k, 0] = xlo_ref[18 + k]
        above_ref[6 + k, 0] = turned(xlo_ref[21 + k], 1)
        below_ref[k, EDGE + 1] = turned(xhi_ref[18 + k], -1)
        above_ref[k, EDGE + 1] = xhi_ref[21 + k]
    for q in range(9):
        for half in range(2):
            main_ref[18 + q, half] = xlo_ref[q * 2 + half]
            main_ref[q, 2 * EDGE + 2 + half] = xhi_ref[q * 2 + half]
    to = 0
    for first, last in KEPT:
        for row in range(2 * first + 2, 2 * last + 2):
            for q in range(NQ):
                kept_ref[q, to] = main_ref[q, row]
            to += 1

    stream_pairs(PAIRS[0], out_ref, pair_ref, sems, main_ref, below_ref, above_ref)


def finish_kernel(count, plan_ref, *refs):
    ins = refs[:count]
    (
        fields_ref, kept_ref, below_in, above_in, _, out_ref,
        main_ref, below_ref, above_ref, late_ref, pair_ref, sems,
    ) = refs[count:]
    copies = []
    to = 0
    for first, last in KEPT:
        rows = 2 * (last - first)
        copies.append(
            pltpu.make_async_copy(
                kept_ref.at[:, pl.ds(to, rows)],
                main_ref.at[:, pl.ds(2 * first + 2, rows)],
                sems.at[len(PAIRS[1]) + len(copies)],
            )
        )
        to += rows
    for copy in copies:
        copy.start()
    unload(plan_ref, ins, late_ref)
    fill_inner(fields_ref, late_ref, INNER[1], main_ref)
    fill_sides(below_in, above_in, below_ref, above_ref, 5, 15)
    for copy in copies:
        copy.wait()

    stream_pairs(PAIRS[1], out_ref, pair_ref, sems, main_ref, below_ref, above_ref)


def scratch_of_lattice():
    side = pltpu.VMEM((9, EDGE + 2, SUB, LANES), jnp.float32)
    return [
        pltpu.VMEM((NQ, 2 * EDGE + 4, SUB, LANES), jnp.float32), side, side,
        pltpu.VMEM((LATE_TILES * SUB * SUB, LANES), jnp.float32),
        pltpu.VMEM((len(PAIRS[0]), NQ, SUB, 4 * LANES), jnp.float32),
        pltpu.SemaphoreType.DMA((len(PAIRS[0]) + len(KEPT),)),
    ]


def advance(plan, homes, fields, xlo, xhi, below, above):
    inputs = [*homes, fields, xlo, xhi, below, above]
    whole = pl.BlockSpec(memory_space=pltpu.VMEM)
    kept = 2 * sum(last - first for first, last in KEPT)
    return pl.pallas_call(
        functools.partial(advance_kernel, len(homes)),
        in_specs=[pl.BlockSpec(memory_space=pltpu.SMEM)] + [whole] * len(inputs),
        out_specs=[pl.BlockSpec(memory_space=pltpu.HBM), whole],
        scratch_shapes=scratch_of_lattice(),
        out_shape=[
            jax.ShapeDtypeStruct((NQ, SUB, GROUPS * SUB * LANES), jnp.float32),
            jax.ShapeDtypeStruct((NQ, kept, SUB, LANES), jnp.float32),
        ],
        compiler_params=pltpu.CompilerParams(vmem_limit_bytes=VMEM_LIMIT),
        cost_estimate=pl.CostEstimate(flops=10**7, bytes_accessed=5 * 10**6, transcendentals=0),
        name="advance",
    )(plan, *inputs)


def finish(plan, homes, fields, kept, below, above, out):
    inputs = [*homes, fields, kept, below, above]
    whole = pl.BlockSpec(memory_space=pltpu.VMEM)
    target = pl.BlockSpec(memory_space=pltpu.HBM)
    return pl.pallas_call(
        functools.partial(finish_kernel, len(homes)),
        in_specs=[pl.BlockSpec(memory_space=pltpu.SMEM)] + [whole] * len(inputs) + [target],
        out_specs=target,
        scratch_shapes=scratch_of_lattice(),
        out_shape=jax.ShapeDtypeStruct(out.shape, jnp.float32),
        input_output_aliases={1 + len(inputs): 0},
        compiler_params=pltpu.CompilerParams(vmem_limit_bytes=VMEM_LIMIT),
        cost_estimate=pl.CostEstimate(flops=10**7, bytes_accessed=5 * 10**6, transcendentals=0),
        name="finish",
    )(plan, *inputs, out)


def shifted(value, axis, step):
    count = lax.axis_size(axis)
    return lax.ppermute(value, axis, [(i, (i + step) % count) for i in range(count)])


def after(value, *earlier):
    return lax.optimization_barrier((value, *earlier))[0]


def on_device(populations, destination, refinement):
    blocks = populations.shape[0]
    row_count = lax.axis_size("row")
    col_count = lax.axis_size("col")
    cap_row = 2 * ((blocks + row_count - 1) // row_count)
    cap_col = 2 * ((blocks + col_count - 1) // col_count)
    ordered = jnp.transpose(populations, (1, 0, 2))

    def prepared(part, *earlier):
        first = after(destination, *earlier)
        return pre(ordered, first, refinement, part, row_count, cap_row, blocks * col_count)

    def to_rows(sent):
        return lax.all_to_all(sent, "row", split_axis=0, concat_axis=0, tiled=True)

    def to_columns(packed):
        return [exchanged(packed[d], "col", d) for d in range(col_count - 1, 0, -1)] + [packed[0]]

    sent = prepared(0)
    early_row = to_rows(sent)
    late_row = to_rows(prepared(1, sent))
    packed, plan = repack(early_row, None, 0, col_count, cap_col, blocks)
    ylo, yhi, xlo, xhi, picked, fields = faces(to_columns(packed))
    below, above = shifted(yhi, "col", 1), shifted(ylo, "col", -1)
    up = jnp.concatenate([xhi.reshape(18, SUB, LANES), below[6:, 1], above[6:, 1]])
    down = jnp.concatenate([xlo.reshape(18, SUB, LANES), below[:3, 0], above[:3, 0]])
    xlo, xhi = shifted(up, "row", 1), shifted(down, "row", -1)
    packed = repack(after(late_row, up, down), plan, 1, col_count, cap_col, blocks)
    middle, last = to_columns(packed[:col_count]), to_columns(packed[col_count:])
    out, kept = advance(picked, middle, fields, xlo, xhi, below, above)
    return jnp.transpose(finish(picked, last, fields, kept, below, above, out), (1, 0, 2))


def solution(mesh):
    return jax.shard_map(
        on_device,
        mesh=mesh,
        in_specs=(P(("row", "col"), None, None), P(("row", "col")), P(("row", "col"))),
        out_specs=P(("row", "col"), None, None),
        check_vma=False,
    )
```

```python
import functools

import jax
import jax.numpy as jnp
from jax import lax
from jax.experimental import pallas as pl
from jax.experimental.pallas import tpu as pltpu
from jax.sharding import PartitionSpec as P

EDGE = 16
VISCOSITY = 0.01
LANES = 128
SUB = 8
NQ = 27
NFIELD = 9
GROUPS = 4
WIDTH = EDGE // GROUPS
CHUNKS = ((0, 3), (1, 2))
INNER = CHUNKS[1]
SIDE_TILES = 3
LATE_TILES = -(-NFIELD * (SUB - 1) // SUB)
VMEM_LIMIT = 20 * 1024 * 1024
LARGE_VMEM_LIMIT = 60 * 1024 * 1024


def velocity(q):
    return (q // 9 - 1, (q // 3) % 3 - 1, q % 3 - 1)


def tiles_of(part):
    return len(INNER) * LATE_TILES if part else len(CHUNKS[0]) * NFIELD + SIDE_TILES


def free_place(c):
    return (c % 2) * (SUB - 1)


def step_to(target, here, count):
    if count & (count - 1) == 0:
        return target ^ here
    return lax.rem(target - here + count, count)


def exchanged(value, axis, step):
    count = lax.axis_size(axis)
    if count & (count - 1) == 0:
        pairs = [(i, i ^ step) for i in range(count)]
    else:
        pairs = [(i, (i + step) % count) for i in range(count)]
    return lax.ppermute(value, axis, pairs)


def raw_moments(f):
    whole, slope, outer = {}, {}, {}
    for i in range(3):
        for j in range(3):
            low, rest, high = (f[i * 9 + j * 3 + k] for k in range(3))
            outer[i, j] = low + high
            whole[i, j] = outer[i, j] + rest
            slope[i, j] = high - low
    column = [whole[i, 0] + whole[i, 1] + whole[i, 2] for i in range(3)]
    tilt = [slope[i, 0] + slope[i, 1] + slope[i, 2] for i in range(3)]
    low_y = whole[0, 0] + whole[1, 0] + whole[2, 0]
    high_y = whole[0, 2] + whole[1, 2] + whole[2, 2]
    ends = column[0] + column[2]
    mzz = sum(outer[i, j] for i in range(3) for j in range(3))
    mxy = (whole[2, 2] - whole[2, 0]) - (whole[0, 2] - whole[0, 0])
    myz = (slope[0, 2] + slope[1, 2] + slope[2, 2]) - (slope[0, 0] + slope[1, 0] + slope[2, 0])
    return (
        ends + column[1],
        column[2] - column[0],
        high_y - low_y,
        tilt[0] + tilt[1] + tilt[2],
        ends,
        low_y + high_y,
        mzz,
        mxy,
        tilt[2] - tilt[0],
        myz,
    )


def collided(f, keep):
    rho, jx, jy, jz, mxx, myy, mzz, mxy, mxz, myz = raw_moments(f)
    inverse = 1.0 / rho
    ux, uy, uz = jx * inverse, jy * inverse, jz * inverse
    kxx = mxx - jx * ux
    return (
        rho, ux, uy, uz,
        keep * (mxy - jx * uy),
        keep * (mxz - jx * uz),
        keep * (myz - jy * uz),
        keep * (kxx - (myy - jy * uy)),
        keep * (kxx - (mzz - jz * uz)),
    )


def pre_kernel(cap, row_count, per_row, part, dest_hbm, level_hbm, x_hbm, out_ref, *refs):
    x_ref, swap_ref, packed_ref, side_ref, dest_ref, level_ref, sems = refs
    order = CHUNKS[part] if part else CHUNKS[0] + INNER
    steps = len(CHUNKS[part])
    blocks = x_ref.shape[2]
    cells = x_ref.shape[3]
    chunks = cells // LANES
    small = [
        pltpu.make_async_copy(dest_hbm, dest_ref, sems.at[0]),
        pltpu.make_async_copy(level_hbm, level_ref, sems.at[1]),
    ]
    large = [
        pltpu.make_async_copy(
            x_hbm.at[:, :, pl.ds(group * cells, cells)], x_ref.at[step], sems.at[2 + step]
        )
        for step, group in enumerate(order)
    ]
    for copy in small + large:
        copy.start()
    for copy in small:
        copy.wait()

    which = lax.broadcasted_iota(jnp.int32, (SUB, LANES), 0)
    spot = lax.broadcasted_iota(jnp.int32, (SUB, LANES), 1) // EDGE
    scale = jnp.zeros((SUB, LANES), jnp.int32)
    tag = jnp.zeros((SUB, LANES), jnp.int32)
    for t in range(blocks):
        scale = jnp.where(which == t, jnp.left_shift(1, level_ref[t]), scale)
        tag = jnp.where(which == t, dest_ref[t], tag)
    rate = 1.0 / (3.0 * VISCOSITY * scale.astype(jnp.float32) + 0.5)
    keep = 1.0 - rate

    rows = [dest_ref[t] // per_row for t in range(blocks)]
    slots = []
    for t in range(blocks):
        slot = rows[t] * cap
        for other in range(t):
            slot = slot + jnp.where(rows[other] == rows[t], 1, 0)
        slots.append(slot)

    def spread(ref, first, count):
        for t in range(blocks):
            for n in range(count):
                moved = ref[pl.ds(n * SUB * SUB + t, SUB, stride=SUB), :]
                out_ref[slots[t], first + n] = moved

    def fields_at(step, c):
        return collided([x_ref[step, q, :, c * LANES : (c + 1) * LANES] for q in range(NQ)], keep)

    for step, group in enumerate(order):
        large[step].wait()
        if part:
            last = fields_at(step, chunks - 1)
            for c in range(chunks - 1):
                place = free_place(c)
                turn = (place - c) * EDGE % LANES
                for n, field in enumerate(fields_at(step, c)):
                    other = pltpu.roll(last[n], turn, axis=1) if turn else last[n]
                    base = (step * LATE_TILES * SUB + n * (chunks - 1) + c) * SUB
                    swap_ref[base : base + SUB, :] = jnp.where(spot == place, other, field)
            continue
        if step < steps:
            for c in range(chunks):
                for n, field in enumerate(fields_at(step, c)):
                    base = (n * chunks + c) * SUB
                    swap_ref[base : base + SUB, :] = field
            spread(swap_ref, SIDE_TILES + step * NFIELD, NFIELD)
            continue
        for q in range(NQ):
            for half in range(2):
                value = packed_ref[half * NQ + q] if step > steps else None
                for x in range(WIDTH):
                    c = x * 2 + half
                    at = (group * WIDTH + x) % SUB
                    moved = x_ref[step, q, :, c * LANES : (c + 1) * LANES]
                    turn = (at + half) * EDGE % LANES
                    if turn:
                        moved = pltpu.roll(moved, turn, axis=1)
                    value = moved if value is None else jnp.where(spot == at, moved, value)
                packed_ref[half * NQ + q] = value

    if part:
        for step in range(steps):
            for row in range(NFIELD * (chunks - 1), LATE_TILES * SUB):
                base = (step * LATE_TILES * SUB + row) * SUB
                swap_ref[base : base + SUB, :] = tag.astype(jnp.float32)
        spread(swap_ref, 0, steps * LATE_TILES)
        return
    for row in range(SIDE_TILES * SUB):
        if not 1 <= row <= 2 * NFIELD:
            side_ref[row * SUB : (row + 1) * SUB, :] = tag.astype(jnp.float32)
    for half in range(2):
        fields = collided([packed_ref[half * NQ + q] for q in range(NQ)], keep)
        for n, field in enumerate(fields):
            base = (1 + half * NFIELD + n) * SUB
            side_ref[base : base + SUB, :] = field
    for slot in range(row_count * cap):
        out_ref[slot, 0] = jnp.full((SUB, LANES), -1.0, jnp.float32)
    spread(side_ref, 0, SIDE_TILES)


def pre(populations, destination, refinement, part, row_count, cap, per_row):
    blocks = populations.shape[1]
    cells = populations.shape[2] // GROUPS
    loaded = len(CHUNKS[part]) + (0 if part else len(INNER))
    rows = tiles_of(1) * SUB if part else NFIELD * cells // LANES
    return pl.pallas_call(
        functools.partial(pre_kernel, cap, row_count, per_row, part),
        in_specs=[pl.BlockSpec(memory_space=pltpu.HBM)] * 3,
        out_specs=pl.BlockSpec(memory_space=pltpu.VMEM),
        out_shape=jax.ShapeDtypeStruct((row_count * cap, tiles_of(part), SUB, LANES), jnp.float32),
        scratch_shapes=[
            pltpu.VMEM((loaded, NQ, blocks, cells), jnp.float32),
            pltpu.VMEM((rows * SUB, LANES), jnp.float32),
            pltpu.VMEM((2 * NQ, SUB, LANES), jnp.float32),
            pltpu.VMEM((SIDE_TILES * SUB * SUB, LANES), jnp.float32),
            pltpu.SMEM((blocks,), jnp.int32),
            pltpu.SMEM((blocks,), jnp.int32),
            pltpu.SemaphoreType.DMA((2 + loaded,)),
        ],
        compiler_params=pltpu.CompilerParams(vmem_limit_bytes=LARGE_VMEM_LIMIT),
        cost_estimate=pl.CostEstimate(flops=10**7, bytes_accessed=4 * 10**6, transcendentals=0),
        name="pre_%d" % part,
    )(destination, refinement, populations)


def read_tags(ins, tag_ref, sems):
    cap = ins[0].shape[0]
    copies = [
        pltpu.make_async_copy(in_ref.at[:, 0, pl.ds(0, 1)], tag_ref.at[pl.ds(d * cap, cap)], sems.at[d])
        for d, in_ref in enumerate(ins)
    ]
    for copy in copies:
        copy.start()
    for copy in copies:
        copy.wait()
    return lambda e: tag_ref[e, 0, 0].astype(jnp.int32)


def tag_scratch(arrays, slots):
    return [pltpu.SMEM((slots, 1, LANES), jnp.float32), pltpu.SemaphoreType.DMA((arrays,))]


def repack_kernel(cap, col_count, blocks, part, *refs):
    if part:
        plan_ref, in_ref, *outs = refs
    else:
        in_ref, *outs, plan_ref, tag_ref, sems, count_ref = refs
        tag_at = read_tags([in_ref], tag_ref, sems)
        here = lax.axis_index("col")
        for d in range(col_count):
            count_ref[d] = 0
        for e in range(col_count * cap):
            plan_ref[e] = -1
        for e in range(in_ref.shape[0]):
            tag = tag_at(e)

            @pl.when(tag >= 0)
            def _():
                d = step_to(lax.rem(tag // blocks, col_count), here, col_count)
                k = count_ref[d]
                count_ref[d] = k + 1
                plan_ref[d * cap + k] = e

    tiles = outs[0].shape[1]
    for place, out in enumerate(outs):
        quarter, d = divmod(place, col_count)
        for k in range(cap):
            e = plan_ref[d * cap + k]

            @pl.when(e >= 0)
            def _():
                out[k] = in_ref[e, quarter * tiles : (quarter + 1) * tiles]

            if part == 0:

                @pl.when(e < 0)
                def _():
                    out[k, 0] = jnp.full((SUB, LANES), -1.0, jnp.float32)


def repack(landed, plan, part, col_count, cap, blocks):
    whole = pl.BlockSpec(memory_space=pltpu.VMEM)
    scalars = pl.BlockSpec(memory_space=pltpu.SMEM)
    scratch = []
    if part == 0:
        scratch = tag_scratch(1, landed.shape[0]) + [pltpu.SMEM((col_count,), jnp.int32)]
    quarters = len(INNER) if part else 1
    shape = (cap, landed.shape[1] // quarters) + landed.shape[2:]
    packed = pl.pallas_call(
        functools.partial(repack_kernel, cap, col_count, blocks, part),
        in_specs=([scalars] if part else []) + [whole],
        out_specs=[whole] * (quarters * col_count) + ([] if part else [scalars]),
        scratch_shapes=scratch,
        out_shape=[jax.ShapeDtypeStruct(shape, jnp.float32)] * (quarters * col_count)
        + ([] if part else [jax.ShapeDtypeStruct((col_count * cap,), jnp.int32)]),
        compiler_params=pltpu.CompilerParams(vmem_limit_bytes=VMEM_LIMIT),
        cost_estimate=pl.CostEstimate(flops=0, bytes_accessed=3 * 10**6, transcendentals=0),
        name="repack_%d" % part,
    )(*([plan] if part else []), landed)
    return packed if part else (packed[:-1], packed[-1])


def backward(zeroth, first, second, u):
    raw_one, raw_two = first, second
    if zeroth is not None:
        moved = u * zeroth
        raw_one = moved if raw_one is None else raw_one + moved
        square = u * moved
        raw_two = square if raw_two is None else raw_two + square
    if first is not None:
        cross = (u + u) * first
        raw_two = cross if raw_two is None else raw_two + cross
    rest = -raw_two if zeroth is None else zeroth - raw_two
    return 0.5 * (raw_two - raw_one), rest, 0.5 * (raw_one + raw_two)


def post_populations(rho, ux, uy, uz, pxy, pxz, pyz, dev_one, dev_two):
    inverse = 1.0 / rho
    pxx = (rho + dev_one + dev_two) * (1.0 / 3.0)
    pyy = pxx - dev_one
    pzz = pxx - dev_two
    sxy, sxz, syz = pxy * inverse, pxz * inverse, pyz * inverse
    syy, szz = pyy * inverse, pzz * inverse
    central = {
        (0, 0, 0): rho, (2, 0, 0): pxx, (0, 2, 0): pyy, (0, 0, 2): pzz,
        (1, 1, 0): pxy, (1, 0, 1): pxz, (0, 1, 1): pyz,
        (2, 2, 0): pxx * syy + 2.0 * pxy * sxy,
        (2, 0, 2): pxx * szz + 2.0 * pxz * sxz,
        (0, 2, 2): pyy * szz + 2.0 * pyz * syz,
        (2, 1, 1): pxx * syz + 2.0 * pxy * sxz,
        (1, 2, 1): pyy * sxz + 2.0 * pxy * syz,
        (1, 1, 2): pzz * sxy + 2.0 * pxz * syz,
        (2, 2, 2): pxx * syy * szz
        + 2.0 * (pxx * syz * syz + pyy * sxz * sxz + pzz * sxy * sxy)
        + 8.0 * pxy * sxz * syz,
    }
    along_z = {}
    for a in range(3):
        for b in range(3):
            parts = backward(*(central.get((a, b, c)) for c in range(3)), uz)
            for k in range(3):
                along_z[a, b, k] = parts[k]
    along_y = {}
    for a in range(3):
        for k in range(3):
            parts = backward(*(along_z[a, b, k] for b in range(3)), uy)
            for j in range(3):
                along_y[a, j, k] = parts[j]
    result = [None] * NQ
    for j in range(3):
        for k in range(3):
            parts = backward(*(along_y[a, j, k] for a in range(3)), ux)
            for i in range(3):
                result[i * 9 + j * 3 + k] = parts[i]
    return result


def unload(plan_ref, ins, fields_ref):
    cap, tiles = ins[0].shape[:2]
    for e in range(len(ins) * cap):
        t = plan_ref[e]

        @pl.when(t >= 0)
        def _():
            for tile in range(tiles):
                fields_ref[pl.ds(tile * SUB * SUB + t, SUB, stride=SUB), :] = ins[e // cap][e % cap, tile]


def row_of(ref, row):
    return ref[row * SUB : (row + 1) * SUB, :]


def turned(value, places):
    turn = places * EDGE % LANES
    return pltpu.roll(value, turn, axis=1) if turn else value


def places_y():
    return lax.broadcasted_iota(jnp.int32, (SUB, LANES), 1) // EDGE


def outer_fields(fields_ref, step, c):
    first = (SIDE_TILES + step * NFIELD) * SUB
    return [row_of(fields_ref, first + n * SUB + c) for n in range(NFIELD)]


def side_fields(fields_ref, half):
    return [row_of(fields_ref, 1 + half * NFIELD + n) for n in range(NFIELD)]


def fill_outer(fields_ref, main_ref):
    for step, group in enumerate(CHUNKS[0]):
        for c in range(SUB):
            for q, value in enumerate(post_populations(*outer_fields(fields_ref, step, c))):
                main_ref[q, group * SUB + c] = value


def fill_inner(fields_ref, late_ref, group, main_ref, first_row):
    spot = places_y()
    last = [None] * NFIELD
    for c in range(SUB):
        at = (group * WIDTH + c // 2) % SUB
        place = free_place(c)
        side = side_fields(fields_ref, c % 2)
        fields = []
        for n in range(NFIELD):
            if c < SUB - 1:
                row = row_of(late_ref, n * (SUB - 1) + c)
                part = turned(row, c - place)
                last[n] = part if c == 0 else jnp.where(spot == c, part, last[n])
            else:
                row = last[n]
            fields.append(jnp.where(spot == place, turned(side[n], place - at), row))
        for q, value in enumerate(post_populations(*fields)):
            main_ref[q, first_row + c] = value


def fill_sides(below_in, above_in, below_ref, above_ref):
    for x in range(EDGE):
        at = x % SUB
        for k in range(9):
            below_ref[k, x] = turned(below_in[k, x // SUB], SUB - 1 - at)
            above_ref[k, x] = turned(above_in[k, x // SUB], -at)


def stream_pair(first_x, out_ref, main, below, above):
    lane = lax.broadcasted_iota(jnp.int32, (SUB, LANES), 1)
    block = lax.broadcasted_iota(jnp.int32, (SUB, LANES), 0)
    along = lane % EDGE
    first_z, last_z = along == 0, along == EDGE - 1
    floor = first_z & (block == 0)
    ceiling = last_z & (block == SUB - 1)
    low_y, high_y = lane < EDGE, lane >= LANES - EDGE
    for i in range(2):
        for half in range(2):
            c = i * 2 + half
            for q in range(NQ):
                cx, cy, cz = velocity(q)
                x = first_x + i - cx
                a = main(q, x, half)
                k = (cx + 1) * 3 + cz + 1
                if cy == 1:
                    a = jnp.where(high_y, main(q, x, 0) if half else below(k, x), a)
                elif cy == -1:
                    a = jnp.where(low_y, above(k, x) if half else main(q, x, 1), a)
                shift = EDGE * cy + cz
                value = a if shift == 0 else pltpu.roll(a, shift % LANES, axis=1)
                if cz:
                    bounced = main(26 - q, first_x + i, half)
                    turn = (1 if cz == 1 else SUB - 1)
                    fill = pltpu.roll(pltpu.roll(a, turn, axis=0), (shift - cz * EDGE) % LANES, axis=1)
                    value = jnp.where(first_z if cz == 1 else last_z, fill, value)
                    value = jnp.where(floor if cz == 1 else ceiling, bounced, value)
                out_ref[q, :, c * LANES : (c + 1) * LANES] = value


def stream_pairs(pairs, out_hbm, pair_ref, sems, *lattice):
    span = pair_ref.shape[3]

    def copy(i):
        return pltpu.make_async_copy(
            pair_ref.at[i], out_hbm.at[:, :, pl.ds(pairs[i] * span, span)], sems.at[i]
        )

    for i, pair in enumerate(pairs):
        stream_pair(2 * pair, pair_ref.at[i], *lattice)
        copy(i).start()
    for i in range(len(pairs)):
        copy(i).wait()


def faces_kernel(count, *refs):
    ins = refs[:count]
    ylo_ref, yhi_ref, xlo_ref, xhi_ref, plan_ref, fields_ref, tag_ref, sems = refs[count:]
    tag_at = read_tags(ins, tag_ref, sems)
    for e in range(count * ins[0].shape[0]):
        tag = tag_at(e)
        plan_ref[e] = jnp.where(tag >= 0, lax.rem(tag, SUB), -1)
    unload(plan_ref, ins, fields_ref)
    spot = places_y()
    for half in range(2):
        packed = [side_fields(fields_ref, half)] * 2
        place = half * (SUB - 1)
        for step, group in enumerate(CHUNKS[0]):
            tile = group * WIDTH // SUB
            for x in range(group * WIDTH, (group + 1) * WIDTH):
                c = (x - group * WIDTH) * 2 + half
                packed[tile] = [
                    jnp.where(spot == x % SUB, turned(value, x % SUB - place), old)
                    for value, old in zip(outer_fields(fields_ref, step, c), packed[tile])
                ]
        for tile in range(2):
            result = post_populations(*packed[tile])
            for i in range(3):
                for k in range(3):
                    (yhi_ref if half else ylo_ref)[i * 3 + k, tile] = result[i * 9 + half * 6 + k]
        low = post_populations(*outer_fields(fields_ref, CHUNKS[0].index(0), half))
        high = post_populations(*outer_fields(fields_ref, CHUNKS[0].index(GROUPS - 1), SUB - 2 + half))
        for q in range(9):
            xlo_ref[q, half] = low[q]
            xhi_ref[q, half] = high[18 + q]


def faces(homes):
    shape = jax.ShapeDtypeStruct
    face = shape((9, 2, SUB, LANES), jnp.float32)
    slots = len(homes) * homes[0].shape[0]
    whole = pl.BlockSpec(memory_space=pltpu.VMEM)
    return pl.pallas_call(
        functools.partial(faces_kernel, len(homes)),
        in_specs=[whole] * len(homes),
        out_specs=[whole] * 4 + [pl.BlockSpec(memory_space=pltpu.SMEM), whole],
        scratch_shapes=tag_scratch(len(homes), slots),
        out_shape=[face] * 4
        + [shape((slots,), jnp.int32), shape((tiles_of(0) * SUB * SUB, LANES), jnp.float32)],
        compiler_params=pltpu.CompilerParams(vmem_limit_bytes=VMEM_LIMIT),
        cost_estimate=pl.CostEstimate(flops=10**7, bytes_accessed=3 * 10**6, transcendentals=0),
        name="faces",
    )(*homes)


PAIRS = ((1, 2), (0, 3, 4, 5, 6, 7))


def advance_kernel(count, plan_ref, *refs):
    ins = refs[:count]
    (
        fields_ref, below_in, above_in, out_ref, main_ref, below_ref, above_ref,
        late_ref, pair_ref, sems,
    ) = refs[count:]
    unload(plan_ref, ins, late_ref)
    fill_outer(fields_ref, main_ref)
    fill_inner(fields_ref, late_ref, INNER[0], main_ref, INNER[0] * SUB)
    fill_sides(below_in, above_in, below_ref, above_ref)
    stream_pairs(
        PAIRS[0], out_ref, pair_ref, sems,
        lambda q, x, half: main_ref[q, x * 2 + half],
        lambda k, x: below_ref[k, x],
        lambda k, x: above_ref[k, x],
    )


def finish_kernel(count, plan_ref, *refs):
    ins = refs[:count]
    (
        fields_ref, main_ref, below_ref, above_ref, xlo_ref, xhi_ref, _, out_ref,
        own_ref, late_ref, pair_ref, sems,
    ) = refs[count:]
    unload(plan_ref, ins, late_ref)
    fill_inner(fields_ref, late_ref, INNER[1], own_ref, 0)
    first = INNER[1] * WIDTH

    def main(q, x, half):
        if x < 0:
            return xlo_ref[(q - 18) * 2 + half]
        if x == EDGE:
            return xhi_ref[q * 2 + half]
        if first <= x < first + WIDTH:
            return own_ref[q, (x - first) * 2 + half]
        return main_ref[q, x * 2 + half]

    def below(k, x):
        if x < 0:
            return xlo_ref[18 + k - 6]
        return turned(xhi_ref[18 + k], -1) if x == EDGE else below_ref[k, x]

    def above(k, x):
        if x < 0:
            return turned(xlo_ref[21 + k - 6], 1)
        return xhi_ref[21 + k] if x == EDGE else above_ref[k, x]

    stream_pairs(PAIRS[1], out_ref, pair_ref, sems, main, below, above)


def scratch_of(pairs):
    return [
        pltpu.VMEM((LATE_TILES * SUB * SUB, LANES), jnp.float32),
        pltpu.VMEM((len(pairs), NQ, SUB, 4 * LANES), jnp.float32),
        pltpu.SemaphoreType.DMA((len(pairs),)),
    ]


def advance(plan, homes, fields, below, above):
    inputs = [*homes, fields, below, above]
    whole = pl.BlockSpec(memory_space=pltpu.VMEM)
    shape = jax.ShapeDtypeStruct
    return pl.pallas_call(
        functools.partial(advance_kernel, len(homes)),
        in_specs=[pl.BlockSpec(memory_space=pltpu.SMEM)] + [whole] * len(inputs),
        out_specs=[pl.BlockSpec(memory_space=pltpu.HBM), whole, whole, whole],
        scratch_shapes=scratch_of(PAIRS[0]),
        out_shape=[
            shape((NQ, SUB, GROUPS * SUB * LANES), jnp.float32),
            shape((NQ, 2 * EDGE, SUB, LANES), jnp.float32),
            shape((9, EDGE, SUB, LANES), jnp.float32),
            shape((9, EDGE, SUB, LANES), jnp.float32),
        ],
        compiler_params=pltpu.CompilerParams(vmem_limit_bytes=VMEM_LIMIT),
        cost_estimate=pl.CostEstimate(flops=10**7, bytes_accessed=5 * 10**6, transcendentals=0),
        name="advance",
    )(plan, *inputs)


def finish(plan, homes, fields, main, below, above, xlo, xhi, out):
    inputs = [*homes, fields, main, below, above, xlo, xhi]
    whole = pl.BlockSpec(memory_space=pltpu.VMEM)
    target = pl.BlockSpec(memory_space=pltpu.HBM)
    return pl.pallas_call(
        functools.partial(finish_kernel, len(homes)),
        in_specs=[pl.BlockSpec(memory_space=pltpu.SMEM)] + [whole] * len(inputs) + [target],
        out_specs=target,
        scratch_shapes=[pltpu.VMEM((NQ, SUB, SUB, LANES), jnp.float32)] + scratch_of(PAIRS[1]),
        out_shape=jax.ShapeDtypeStruct(out.shape, jnp.float32),
        input_output_aliases={1 + len(inputs): 0},
        compiler_params=pltpu.CompilerParams(vmem_limit_bytes=VMEM_LIMIT),
        cost_estimate=pl.CostEstimate(flops=10**7, bytes_accessed=5 * 10**6, transcendentals=0),
        name="finish",
    )(plan, *inputs, out)


def shifted(value, axis, step):
    count = lax.axis_size(axis)
    return lax.ppermute(value, axis, [(i, (i + step) % count) for i in range(count)])


def after(value, *earlier):
    return lax.optimization_barrier((value, *earlier))[0]


def on_device(populations, destination, refinement):
    blocks = populations.shape[0]
    row_count = lax.axis_size("row")
    col_count = lax.axis_size("col")
    cap_row = 2 * ((blocks + row_count - 1) // row_count)
    cap_col = 2 * ((blocks + col_count - 1) // col_count)
    ordered = jnp.transpose(populations, (1, 0, 2))

    def prepared(part, *earlier):
        first = after(destination, *earlier)
        return pre(ordered, first, refinement, part, row_count, cap_row, blocks * col_count)

    def to_rows(sent):
        return lax.all_to_all(sent, "row", split_axis=0, concat_axis=0, tiled=True)

    def to_columns(packed):
        return [exchanged(packed[d], "col", d) for d in range(col_count - 1, 0, -1)] + [packed[0]]

    sent = prepared(0)
    early_row = to_rows(sent)
    late_row = to_rows(prepared(1, sent))
    packed, plan = repack(early_row, None, 0, col_count, cap_col, blocks)
    ylo, yhi, xlo, xhi, picked, fields = faces(to_columns(packed))
    below, above = shifted(yhi, "col", 1), shifted(ylo, "col", -1)
    packed = repack(after(late_row, below, above), plan, 1, col_count, cap_col, blocks)
    middle = to_columns(packed[:col_count])
    last = to_columns([after(value, middle[-2]) for value in packed[col_count:]])
    up = jnp.concatenate([xhi.reshape(18, SUB, LANES), below[6:, 1], above[6:, 1]])
    down = jnp.concatenate([xlo.reshape(18, SUB, LANES), below[:3, 0], above[:3, 0]])
    up, down = after(up, middle[-2]), after(down, middle[-2])
    xlo, xhi = shifted(up, "row", 1), shifted(down, "row", -1)
    out, *lattice = advance(picked, middle, fields, below, above)
    return jnp.transpose(finish(picked, last, fields, *lattice, xlo, xhi, out), (1, 0, 2))


def solution(mesh):
    return jax.shard_map(
        on_device,
        mesh=mesh,
        in_specs=(P(("row", "col"), None, None), P(("row", "col")), P(("row", "col"))),
        out_specs=P(("row", "col"), None, None),
        check_vma=False,
    )
```

```python
import functools

import jax
import jax.numpy as jnp
from jax import lax
from jax.experimental import pallas as pl
from jax.experimental.pallas import tpu as pltpu
from jax.sharding import PartitionSpec as P

EDGE = 16
VISCOSITY = 0.01
LANES = 128
SUB = 8
NQ = 27
NFIELD = 9
GROUPS = 4
WIDTH = EDGE // GROUPS
CHUNKS = ((0, 3), (1, 2))
INNER = CHUNKS[1]
SIDE_TILES = 3
LATE_TILES = -(-NFIELD * (SUB - 1) // SUB)
VMEM_LIMIT = 20 * 1024 * 1024
LARGE_VMEM_LIMIT = 60 * 1024 * 1024


def velocity(q):
    return (q // 9 - 1, (q // 3) % 3 - 1, q % 3 - 1)


def tiles_of(part):
    return len(INNER) * LATE_TILES if part else len(CHUNKS[0]) * NFIELD + SIDE_TILES


def free_place(c):
    return (c % 2) * (SUB - 1)


def step_to(target, here, count):
    if count & (count - 1) == 0:
        return target ^ here
    return lax.rem(target - here + count, count)


def exchanged(value, axis, step):
    count = lax.axis_size(axis)
    if count & (count - 1) == 0:
        pairs = [(i, i ^ step) for i in range(count)]
    else:
        pairs = [(i, (i + step) % count) for i in range(count)]
    return lax.ppermute(value, axis, pairs)


def raw_moments(f):
    whole, slope, outer = {}, {}, {}
    for i in range(3):
        for j in range(3):
            low, rest, high = (f[i * 9 + j * 3 + k] for k in range(3))
            outer[i, j] = low + high
            whole[i, j] = outer[i, j] + rest
            slope[i, j] = high - low
    column = [whole[i, 0] + whole[i, 1] + whole[i, 2] for i in range(3)]
    tilt = [slope[i, 0] + slope[i, 1] + slope[i, 2] for i in range(3)]
    low_y = whole[0, 0] + whole[1, 0] + whole[2, 0]
    high_y = whole[0, 2] + whole[1, 2] + whole[2, 2]
    ends = column[0] + column[2]
    mzz = sum(outer[i, j] for i in range(3) for j in range(3))
    mxy = (whole[2, 2] - whole[2, 0]) - (whole[0, 2] - whole[0, 0])
    myz = (slope[0, 2] + slope[1, 2] + slope[2, 2]) - (slope[0, 0] + slope[1, 0] + slope[2, 0])
    return (
        ends + column[1],
        column[2] - column[0],
        high_y - low_y,
        tilt[0] + tilt[1] + tilt[2],
        ends,
        low_y + high_y,
        mzz,
        mxy,
        tilt[2] - tilt[0],
        myz,
    )


def collided(f, keep):
    rho, jx, jy, jz, mxx, myy, mzz, mxy, mxz, myz = raw_moments(f)
    inverse = 1.0 / rho
    ux, uy, uz = jx * inverse, jy * inverse, jz * inverse
    kxx = mxx - jx * ux
    return (
        rho, ux, uy, uz,
        keep * (mxy - jx * uy),
        keep * (mxz - jx * uz),
        keep * (myz - jy * uz),
        keep * (kxx - (myy - jy * uy)),
        keep * (kxx - (mzz - jz * uz)),
    )


def pre_kernel(cap, row_count, per_row, part, dest_hbm, level_hbm, x_hbm, out_ref, *refs):
    x_ref, swap_ref, packed_ref, side_ref, dest_ref, level_ref, sems = refs
    order = CHUNKS[part] if part else CHUNKS[0] + INNER
    steps = len(CHUNKS[part])
    blocks = x_ref.shape[2]
    cells = x_ref.shape[3]
    chunks = cells // LANES
    small = [
        pltpu.make_async_copy(dest_hbm, dest_ref, sems.at[0]),
        pltpu.make_async_copy(level_hbm, level_ref, sems.at[1]),
    ]
    large = [
        pltpu.make_async_copy(
            x_hbm.at[:, :, pl.ds(group * cells, cells)], x_ref.at[step], sems.at[2 + step]
        )
        for step, group in enumerate(order)
    ]
    for copy in small + large:
        copy.start()
    for copy in small:
        copy.wait()

    which = lax.broadcasted_iota(jnp.int32, (SUB, LANES), 0)
    spot = lax.broadcasted_iota(jnp.int32, (SUB, LANES), 1) // EDGE
    scale = jnp.zeros((SUB, LANES), jnp.int32)
    tag = jnp.zeros((SUB, LANES), jnp.int32)
    for t in range(blocks):
        scale = jnp.where(which == t, jnp.left_shift(1, level_ref[t]), scale)
        tag = jnp.where(which == t, dest_ref[t], tag)
    rate = 1.0 / (3.0 * VISCOSITY * scale.astype(jnp.float32) + 0.5)
    keep = 1.0 - rate

    rows = [dest_ref[t] // per_row for t in range(blocks)]
    slots = []
    for t in range(blocks):
        slot = rows[t] * cap
        for other in range(t):
            slot = slot + jnp.where(rows[other] == rows[t], 1, 0)
        slots.append(slot)

    def spread(ref, first, count):
        for t in range(blocks):
            for n in range(count):
                moved = ref[pl.ds(n * SUB * SUB + t, SUB, stride=SUB), :]
                out_ref[slots[t], first + n] = moved

    def fields_at(step, c):
        return collided([x_ref[step, q, :, c * LANES : (c + 1) * LANES] for q in range(NQ)], keep)

    for step, group in enumerate(order):
        large[step].wait()
        if part:
            last = fields_at(step, chunks - 1)
            for c in range(chunks - 1):
                place = free_place(c)
                turn = (place - c) * EDGE % LANES
                for n, field in enumerate(fields_at(step, c)):
                    other = pltpu.roll(last[n], turn, axis=1) if turn else last[n]
                    base = (step * LATE_TILES * SUB + n * (chunks - 1) + c) * SUB
                    swap_ref[base : base + SUB, :] = jnp.where(spot == place, other, field)
            continue
        if step < steps:
            for c in range(chunks):
                for n, field in enumerate(fields_at(step, c)):
                    base = (n * chunks + c) * SUB
                    swap_ref[base : base + SUB, :] = field
            spread(swap_ref, SIDE_TILES + step * NFIELD, NFIELD)
            continue
        for q in range(NQ):
            for half in range(2):
                value = packed_ref[half * NQ + q] if step > steps else None
                for x in range(WIDTH):
                    c = x * 2 + half
                    at = (group * WIDTH + x) % SUB
                    moved = x_ref[step, q, :, c * LANES : (c + 1) * LANES]
                    turn = (at + half) * EDGE % LANES
                    if turn:
                        moved = pltpu.roll(moved, turn, axis=1)
                    value = moved if value is None else jnp.where(spot == at, moved, value)
                packed_ref[half * NQ + q] = value

    if part:
        for step in range(steps):
            for row in range(NFIELD * (chunks - 1), LATE_TILES * SUB):
                base = (step * LATE_TILES * SUB + row) * SUB
                swap_ref[base : base + SUB, :] = tag.astype(jnp.float32)
        spread(swap_ref, 0, steps * LATE_TILES)
        return
    for row in range(SIDE_TILES * SUB):
        if not 1 <= row <= 2 * NFIELD:
            side_ref[row * SUB : (row + 1) * SUB, :] = tag.astype(jnp.float32)
    for half in range(2):
        fields = collided([packed_ref[half * NQ + q] for q in range(NQ)], keep)
        for n, field in enumerate(fields):
            base = (1 + half * NFIELD + n) * SUB
            side_ref[base : base + SUB, :] = field
    for slot in range(row_count * cap):
        out_ref[slot, 0] = jnp.full((SUB, LANES), -1.0, jnp.float32)
    spread(side_ref, 0, SIDE_TILES)


def pre(populations, destination, refinement, part, row_count, cap, per_row):
    blocks = populations.shape[1]
    cells = populations.shape[2] // GROUPS
    loaded = len(CHUNKS[part]) + (0 if part else len(INNER))
    rows = tiles_of(1) * SUB if part else NFIELD * cells // LANES
    return pl.pallas_call(
        functools.partial(pre_kernel, cap, row_count, per_row, part),
        in_specs=[pl.BlockSpec(memory_space=pltpu.HBM)] * 3,
        out_specs=pl.BlockSpec(memory_space=pltpu.VMEM),
        out_shape=jax.ShapeDtypeStruct((row_count * cap, tiles_of(part), SUB, LANES), jnp.float32),
        scratch_shapes=[
            pltpu.VMEM((loaded, NQ, blocks, cells), jnp.float32),
            pltpu.VMEM((rows * SUB, LANES), jnp.float32),
            pltpu.VMEM((2 * NQ, SUB, LANES), jnp.float32),
            pltpu.VMEM((SIDE_TILES * SUB * SUB, LANES), jnp.float32),
            pltpu.SMEM((blocks,), jnp.int32),
            pltpu.SMEM((blocks,), jnp.int32),
            pltpu.SemaphoreType.DMA((2 + loaded,)),
        ],
        compiler_params=pltpu.CompilerParams(vmem_limit_bytes=LARGE_VMEM_LIMIT),
        cost_estimate=pl.CostEstimate(flops=10**7, bytes_accessed=4 * 10**6, transcendentals=0),
        name="pre_%d" % part,
    )(destination, refinement, populations)


def read_tags(ins, tag_ref, sems):
    cap = ins[0].shape[0]
    copies = [
        pltpu.make_async_copy(in_ref.at[:, 0, pl.ds(0, 1)], tag_ref.at[pl.ds(d * cap, cap)], sems.at[d])
        for d, in_ref in enumerate(ins)
    ]
    for copy in copies:
        copy.start()
    for copy in copies:
        copy.wait()
    return lambda e: tag_ref[e, 0, 0].astype(jnp.int32)


def tag_scratch(arrays, slots):
    return [pltpu.SMEM((slots, 1, LANES), jnp.float32), pltpu.SemaphoreType.DMA((arrays,))]


def repack_kernel(cap, col_count, blocks, part, *refs):
    if part:
        plan_ref, in_ref, *outs = refs
    else:
        in_ref, *outs, plan_ref, tag_ref, sems, count_ref = refs
        tag_at = read_tags([in_ref], tag_ref, sems)
        here = lax.axis_index("col")
        for d in range(col_count):
            count_ref[d] = 0
        for e in range(col_count * cap):
            plan_ref[e] = -1
        for e in range(in_ref.shape[0]):
            tag = tag_at(e)

            @pl.when(tag >= 0)
            def _():
                d = step_to(lax.rem(tag // blocks, col_count), here, col_count)
                k = count_ref[d]
                count_ref[d] = k + 1
                plan_ref[d * cap + k] = e

    tiles = outs[0].shape[1]
    for place, out in enumerate(outs):
        quarter, d = divmod(place, col_count)
        for k in range(cap):
            e = plan_ref[d * cap + k]

            @pl.when(e >= 0)
            def _():
                out[k] = in_ref[e, quarter * tiles : (quarter + 1) * tiles]

            if part == 0:

                @pl.when(e < 0)
                def _():
                    out[k, 0] = jnp.full((SUB, LANES), -1.0, jnp.float32)


def repack(landed, plan, part, col_count, cap, blocks):
    whole = pl.BlockSpec(memory_space=pltpu.VMEM)
    scalars = pl.BlockSpec(memory_space=pltpu.SMEM)
    scratch = []
    if part == 0:
        scratch = tag_scratch(1, landed.shape[0]) + [pltpu.SMEM((col_count,), jnp.int32)]
    quarters = len(INNER) if part else 1
    shape = (cap, landed.shape[1] // quarters) + landed.shape[2:]
    packed = pl.pallas_call(
        functools.partial(repack_kernel, cap, col_count, blocks, part),
        in_specs=([scalars] if part else []) + [whole],
        out_specs=[whole] * (quarters * col_count) + ([] if part else [scalars]),
        scratch_shapes=scratch,
        out_shape=[jax.ShapeDtypeStruct(shape, jnp.float32)] * (quarters * col_count)
        + ([] if part else [jax.ShapeDtypeStruct((col_count * cap,), jnp.int32)]),
        compiler_params=pltpu.CompilerParams(vmem_limit_bytes=VMEM_LIMIT),
        cost_estimate=pl.CostEstimate(flops=0, bytes_accessed=3 * 10**6, transcendentals=0),
        name="repack_%d" % part,
    )(*([plan] if part else []), landed)
    return packed if part else (packed[:-1], packed[-1])


def backward(zeroth, first, second, u):
    raw_one, raw_two = first, second
    if zeroth is not None:
        moved = u * zeroth
        raw_one = moved if raw_one is None else raw_one + moved
        square = u * moved
        raw_two = square if raw_two is None else raw_two + square
    if first is not None:
        cross = (u + u) * first
        raw_two = cross if raw_two is None else raw_two + cross
    rest = -raw_two if zeroth is None else zeroth - raw_two
    return 0.5 * (raw_two - raw_one), rest, 0.5 * (raw_one + raw_two)


def post_populations(rho, ux, uy, uz, pxy, pxz, pyz, dev_one, dev_two):
    inverse = 1.0 / rho
    pxx = (rho + dev_one + dev_two) * (1.0 / 3.0)
    pyy = pxx - dev_one
    pzz = pxx - dev_two
    sxy, sxz, syz = pxy * inverse, pxz * inverse, pyz * inverse
    syy, szz = pyy * inverse, pzz * inverse
    central = {
        (0, 0, 0): rho, (2, 0, 0): pxx, (0, 2, 0): pyy, (0, 0, 2): pzz,
        (1, 1, 0): pxy, (1, 0, 1): pxz, (0, 1, 1): pyz,
        (2, 2, 0): pxx * syy + 2.0 * pxy * sxy,
        (2, 0, 2): pxx * szz + 2.0 * pxz * sxz,
        (0, 2, 2): pyy * szz + 2.0 * pyz * syz,
        (2, 1, 1): pxx * syz + 2.0 * pxy * sxz,
        (1, 2, 1): pyy * sxz + 2.0 * pxy * syz,
        (1, 1, 2): pzz * sxy + 2.0 * pxz * syz,
        (2, 2, 2): pxx * syy * szz
        + 2.0 * (pxx * syz * syz + pyy * sxz * sxz + pzz * sxy * sxy)
        + 8.0 * pxy * sxz * syz,
    }
    along_z = {}
    for a in range(3):
        for b in range(3):
            parts = backward(*(central.get((a, b, c)) for c in range(3)), uz)
            for k in range(3):
                along_z[a, b, k] = parts[k]
    along_y = {}
    for a in range(3):
        for k in range(3):
            parts = backward(*(along_z[a, b, k] for b in range(3)), uy)
            for j in range(3):
                along_y[a, j, k] = parts[j]
    result = [None] * NQ
    for j in range(3):
        for k in range(3):
            parts = backward(*(along_y[a, j, k] for a in range(3)), ux)
            for i in range(3):
                result[i * 9 + j * 3 + k] = parts[i]
    return result


def unload(plan_ref, ins, fields_ref):
    cap, tiles = ins[0].shape[:2]
    for e in range(len(ins) * cap):
        t = plan_ref[e]

        @pl.when(t >= 0)
        def _():
            for tile in range(tiles):
                fields_ref[pl.ds(tile * SUB * SUB + t, SUB, stride=SUB), :] = ins[e // cap][e % cap, tile]


def row_of(ref, row):
    return ref[row * SUB : (row + 1) * SUB, :]


def turned(value, places):
    turn = places * EDGE % LANES
    return pltpu.roll(value, turn, axis=1) if turn else value


def places_y():
    return lax.broadcasted_iota(jnp.int32, (SUB, LANES), 1) // EDGE


def outer_fields(fields_ref, step, c):
    first = (SIDE_TILES + step * NFIELD) * SUB
    return [row_of(fields_ref, first + n * SUB + c) for n in range(NFIELD)]


def side_fields(fields_ref, half):
    return [row_of(fields_ref, 1 + half * NFIELD + n) for n in range(NFIELD)]


def fill_outer(fields_ref, main_ref):
    for step, group in enumerate(CHUNKS[0]):
        for c in range(SUB):
            for q, value in enumerate(post_populations(*outer_fields(fields_ref, step, c))):
                main_ref[q, group * SUB + c] = value


def fill_inner(fields_ref, late_ref, group, main_ref, first_row):
    spot = places_y()
    last = [None] * NFIELD
    for c in range(SUB):
        at = (group * WIDTH + c // 2) % SUB
        place = free_place(c)
        side = side_fields(fields_ref, c % 2)
        fields = []
        for n in range(NFIELD):
            if c < SUB - 1:
                row = row_of(late_ref, n * (SUB - 1) + c)
                part = turned(row, c - place)
                last[n] = part if c == 0 else jnp.where(spot == c, part, last[n])
            else:
                row = last[n]
            fields.append(jnp.where(spot == place, turned(side[n], place - at), row))
        for q, value in enumerate(post_populations(*fields)):
            main_ref[q, first_row + c] = value


def fill_sides(below_in, above_in, below_ref, above_ref):
    for x in range(EDGE):
        at = x % SUB
        for k in range(9):
            below_ref[k, x] = turned(below_in[k, x // SUB], SUB - 1 - at)
            above_ref[k, x] = turned(above_in[k, x // SUB], -at)


def stream_pair(first_x, out_ref, main, below, above):
    lane = lax.broadcasted_iota(jnp.int32, (SUB, LANES), 1)
    block = lax.broadcasted_iota(jnp.int32, (SUB, LANES), 0)
    along = lane % EDGE
    first_z, last_z = along == 0, along == EDGE - 1
    floor = first_z & (block == 0)
    ceiling = last_z & (block == SUB - 1)
    low_y, high_y = lane < EDGE, lane >= LANES - EDGE
    for i in range(2):
        for half in range(2):
            c = i * 2 + half
            for q in range(NQ):
                cx, cy, cz = velocity(q)
                x = first_x + i - cx
                a = main(q, x, half)
                k = (cx + 1) * 3 + cz + 1
                if cy == 1:
                    a = jnp.where(high_y, main(q, x, 0) if half else below(k, x), a)
                elif cy == -1:
                    a = jnp.where(low_y, above(k, x) if half else main(q, x, 1), a)
                shift = EDGE * cy + cz
                value = a if shift == 0 else pltpu.roll(a, shift % LANES, axis=1)
                if cz:
                    bounced = main(26 - q, first_x + i, half)
                    turn = (1 if cz == 1 else SUB - 1)
                    fill = pltpu.roll(pltpu.roll(a, turn, axis=0), (shift - cz * EDGE) % LANES, axis=1)
                    value = jnp.where(first_z if cz == 1 else last_z, fill, value)
                    value = jnp.where(floor if cz == 1 else ceiling, bounced, value)
                out_ref[q, :, c * LANES : (c + 1) * LANES] = value


def stream_pairs(pairs, out_hbm, pair_ref, sems, *lattice):
    span = pair_ref.shape[3]

    def copy(i):
        return pltpu.make_async_copy(
            pair_ref.at[i], out_hbm.at[:, :, pl.ds(pairs[i] * span, span)], sems.at[i]
        )

    for i, pair in enumerate(pairs):
        stream_pair(2 * pair, pair_ref.at[i], *lattice)
        copy(i).start()
    for i in range(len(pairs)):
        copy(i).wait()


def faces_kernel(count, *refs):
    ins = refs[:count]
    ylo_ref, yhi_ref, xlo_ref, xhi_ref, plan_ref, fields_ref, tag_ref, sems = refs[count:]
    tag_at = read_tags(ins, tag_ref, sems)
    for e in range(count * ins[0].shape[0]):
        tag = tag_at(e)
        plan_ref[e] = jnp.where(tag >= 0, lax.rem(tag, SUB), -1)
    unload(plan_ref, ins, fields_ref)
    spot = places_y()
    for half in range(2):
        packed = [side_fields(fields_ref, half)] * 2
        place = half * (SUB - 1)
        for step, group in enumerate(CHUNKS[0]):
            tile = group * WIDTH // SUB
            for x in range(group * WIDTH, (group + 1) * WIDTH):
                c = (x - group * WIDTH) * 2 + half
                packed[tile] = [
                    jnp.where(spot == x % SUB, turned(value, x % SUB - place), old)
                    for value, old in zip(outer_fields(fields_ref, step, c), packed[tile])
                ]
        for tile in range(2):
            result = post_populations(*packed[tile])
            for i in range(3):
                for k in range(3):
                    (yhi_ref if half else ylo_ref)[i * 3 + k, tile] = result[i * 9 + half * 6 + k]
        low = post_populations(*outer_fields(fields_ref, CHUNKS[0].index(0), half))
        high = post_populations(*outer_fields(fields_ref, CHUNKS[0].index(GROUPS - 1), SUB - 2 + half))
        for q in range(9):
            xlo_ref[q, half] = low[q]
            xhi_ref[q, half] = high[18 + q]


def faces(homes):
    shape = jax.ShapeDtypeStruct
    face = shape((9, 2, SUB, LANES), jnp.float32)
    slots = len(homes) * homes[0].shape[0]
    whole = pl.BlockSpec(memory_space=pltpu.VMEM)
    return pl.pallas_call(
        functools.partial(faces_kernel, len(homes)),
        in_specs=[whole] * len(homes),
        out_specs=[whole] * 4 + [pl.BlockSpec(memory_space=pltpu.SMEM), whole],
        scratch_shapes=tag_scratch(len(homes), slots),
        out_shape=[face] * 4
        + [shape((slots,), jnp.int32), shape((tiles_of(0) * SUB * SUB, LANES), jnp.float32)],
        compiler_params=pltpu.CompilerParams(vmem_limit_bytes=VMEM_LIMIT),
        cost_estimate=pl.CostEstimate(flops=10**7, bytes_accessed=3 * 10**6, transcendentals=0),
        name="faces",
    )(*homes)


PAIRS = ((1, 2), (0, 3, 4, 5, 6, 7))


def advance_kernel(count, plan_ref, *refs):
    ins = refs[:count]
    (
        fields_ref, below_in, above_in, out_ref, main_ref, below_ref, above_ref,
        late_ref, pair_ref, sems,
    ) = refs[count:]
    unload(plan_ref, ins, late_ref)
    fill_outer(fields_ref, main_ref)
    fill_inner(fields_ref, late_ref, INNER[0], main_ref, INNER[0] * SUB)
    fill_sides(below_in, above_in, below_ref, above_ref)
    stream_pairs(
        PAIRS[0], out_ref, pair_ref, sems,
        lambda q, x, half: main_ref[q, x * 2 + half],
        lambda k, x: below_ref[k, x],
        lambda k, x: above_ref[k, x],
    )


def finish_kernel(count, plan_ref, *refs):
    ins = refs[:count]
    (
        fields_ref, main_ref, below_ref, above_ref, xlo_ref, xhi_ref, _, out_ref,
        own_ref, late_ref, pair_ref, sems,
    ) = refs[count:]
    unload(plan_ref, ins, late_ref)
    fill_inner(fields_ref, late_ref, INNER[1], own_ref, 0)
    first = INNER[1] * WIDTH

    def main(q, x, half):
        if x < 0:
            return xlo_ref[(q - 18) * 2 + half]
        if x == EDGE:
            return xhi_ref[q * 2 + half]
        if first <= x < first + WIDTH:
            return own_ref[q, (x - first) * 2 + half]
        return main_ref[q, x * 2 + half]

    def below(k, x):
        if x < 0:
            return xlo_ref[18 + k - 6]
        return turned(xhi_ref[18 + k], -1) if x == EDGE else below_ref[k, x]

    def above(k, x):
        if x < 0:
            return turned(xlo_ref[21 + k - 6], 1)
        return xhi_ref[21 + k] if x == EDGE else above_ref[k, x]

    stream_pairs(PAIRS[1], out_ref, pair_ref, sems, main, below, above)


def scratch_of(pairs):
    return [
        pltpu.VMEM((LATE_TILES * SUB * SUB, LANES), jnp.float32),
        pltpu.VMEM((len(pairs), NQ, SUB, 4 * LANES), jnp.float32),
        pltpu.SemaphoreType.DMA((len(pairs),)),
    ]


def advance(plan, homes, fields, below, above):
    inputs = [*homes, fields, below, above]
    whole = pl.BlockSpec(memory_space=pltpu.VMEM)
    shape = jax.ShapeDtypeStruct
    return pl.pallas_call(
        functools.partial(advance_kernel, len(homes)),
        in_specs=[pl.BlockSpec(memory_space=pltpu.SMEM)] + [whole] * len(inputs),
        out_specs=[pl.BlockSpec(memory_space=pltpu.HBM), whole, whole, whole],
        scratch_shapes=scratch_of(PAIRS[0]),
        out_shape=[
            shape((NQ, SUB, GROUPS * SUB * LANES), jnp.float32),
            shape((NQ, 2 * EDGE, SUB, LANES), jnp.float32),
            shape((9, EDGE, SUB, LANES), jnp.float32),
            shape((9, EDGE, SUB, LANES), jnp.float32),
        ],
        compiler_params=pltpu.CompilerParams(vmem_limit_bytes=VMEM_LIMIT),
        cost_estimate=pl.CostEstimate(flops=10**7, bytes_accessed=5 * 10**6, transcendentals=0),
        name="advance",
    )(plan, *inputs)


def finish(plan, homes, fields, main, below, above, xlo, xhi, out):
    inputs = [*homes, fields, main, below, above, xlo, xhi]
    whole = pl.BlockSpec(memory_space=pltpu.VMEM)
    target = pl.BlockSpec(memory_space=pltpu.HBM)
    return pl.pallas_call(
        functools.partial(finish_kernel, len(homes)),
        in_specs=[pl.BlockSpec(memory_space=pltpu.SMEM)] + [whole] * len(inputs) + [target],
        out_specs=target,
        scratch_shapes=[pltpu.VMEM((NQ, SUB, SUB, LANES), jnp.float32)] + scratch_of(PAIRS[1]),
        out_shape=jax.ShapeDtypeStruct(out.shape, jnp.float32),
        input_output_aliases={1 + len(inputs): 0},
        compiler_params=pltpu.CompilerParams(vmem_limit_bytes=VMEM_LIMIT),
        cost_estimate=pl.CostEstimate(flops=10**7, bytes_accessed=5 * 10**6, transcendentals=0),
        name="finish",
    )(plan, *inputs, out)


def shifted(value, axis, step):
    count = lax.axis_size(axis)
    return lax.ppermute(value, axis, [(i, (i + step) % count) for i in range(count)])


def after(value, *earlier):
    return lax.optimization_barrier((value, *earlier))[0]


def on_device(populations, destination, refinement):
    blocks = populations.shape[0]
    row_count = lax.axis_size("row")
    col_count = lax.axis_size("col")
    cap_row = 2 * ((blocks + row_count - 1) // row_count)
    cap_col = 2 * ((blocks + col_count - 1) // col_count)
    ordered = jnp.transpose(populations, (1, 0, 2))

    def prepared(part, *earlier):
        first = after(destination, *earlier)
        return pre(ordered, first, refinement, part, row_count, cap_row, blocks * col_count)

    def to_rows(sent):
        return lax.all_to_all(sent, "row", split_axis=0, concat_axis=0, tiled=True)

    def to_columns(packed):
        return [exchanged(packed[d], "col", d) for d in range(col_count - 1, 0, -1)] + [packed[0]]

    sent = prepared(0)
    early_row = to_rows(sent)
    late_row = to_rows(prepared(1, sent))
    packed, plan = repack(early_row, None, 0, col_count, cap_col, blocks)
    ylo, yhi, xlo, xhi, picked, fields = faces(to_columns(packed))
    below, above = shifted(yhi, "col", 1), shifted(ylo, "col", -1)
    packed = repack(after(late_row, below, above), plan, 1, col_count, cap_col, blocks)
    middle = to_columns(packed[:col_count])
    last = to_columns([after(value, middle[-2]) for value in packed[col_count:]])
    out, *lattice = advance(picked, middle, fields, below, above)
    up = jnp.concatenate([xhi.reshape(18, SUB, LANES), below[6:, 1], above[6:, 1]])
    down = jnp.concatenate([xlo.reshape(18, SUB, LANES), below[:3, 0], above[:3, 0]])
    up, down = after(up, lattice[1]), after(down, lattice[1])
    xlo, xhi = shifted(up, "row", 1), shifted(down, "row", -1)
    return jnp.transpose(finish(picked, last, fields, *lattice, xlo, xhi, out), (1, 0, 2))


def solution(mesh):
    return jax.shard_map(
        on_device,
        mesh=mesh,
        in_specs=(P(("row", "col"), None, None), P(("row", "col")), P(("row", "col"))),
        out_specs=P(("row", "col"), None, None),
        check_vma=False,
    )
```

```python
import functools

import jax
import jax.numpy as jnp
from jax import lax
from jax.experimental import pallas as pl
from jax.experimental.pallas import tpu as pltpu
from jax.sharding import PartitionSpec as P

EDGE = 16
VISCOSITY = 0.01
LANES = 128
SUB = 8
NQ = 27
NFIELD = 9
GROUPS = 4
WIDTH = EDGE // GROUPS
CHUNKS = ((0, 3), (1, 2))
INNER = CHUNKS[1]
SIDE_TILES = 3
LATE_TILES = -(-NFIELD * (SUB - 1) // SUB)
VMEM_LIMIT = 20 * 1024 * 1024
LARGE_VMEM_LIMIT = 60 * 1024 * 1024


def velocity(q):
    return (q // 9 - 1, (q // 3) % 3 - 1, q % 3 - 1)


def tiles_of(part):
    return len(INNER) * LATE_TILES if part else len(CHUNKS[0]) * NFIELD + SIDE_TILES


def free_place(c):
    return (c % 2) * (SUB - 1)


def step_to(target, here, count):
    if count & (count - 1) == 0:
        return target ^ here
    return lax.rem(target - here + count, count)


def exchanged(value, axis, step):
    count = lax.axis_size(axis)
    if count & (count - 1) == 0:
        pairs = [(i, i ^ step) for i in range(count)]
    else:
        pairs = [(i, (i + step) % count) for i in range(count)]
    return lax.ppermute(value, axis, pairs)


def raw_moments(f):
    whole, slope, outer = {}, {}, {}
    for i in range(3):
        for j in range(3):
            low, rest, high = (f[i * 9 + j * 3 + k] for k in range(3))
            outer[i, j] = low + high
            whole[i, j] = outer[i, j] + rest
            slope[i, j] = high - low
    column = [whole[i, 0] + whole[i, 1] + whole[i, 2] for i in range(3)]
    tilt = [slope[i, 0] + slope[i, 1] + slope[i, 2] for i in range(3)]
    low_y = whole[0, 0] + whole[1, 0] + whole[2, 0]
    high_y = whole[0, 2] + whole[1, 2] + whole[2, 2]
    ends = column[0] + column[2]
    mzz = sum(outer[i, j] for i in range(3) for j in range(3))
    mxy = (whole[2, 2] - whole[2, 0]) - (whole[0, 2] - whole[0, 0])
    myz = (slope[0, 2] + slope[1, 2] + slope[2, 2]) - (slope[0, 0] + slope[1, 0] + slope[2, 0])
    return (
        ends + column[1],
        column[2] - column[0],
        high_y - low_y,
        tilt[0] + tilt[1] + tilt[2],
        ends,
        low_y + high_y,
        mzz,
        mxy,
        tilt[2] - tilt[0],
        myz,
    )


def collided(f, keep):
    rho, jx, jy, jz, mxx, myy, mzz, mxy, mxz, myz = raw_moments(f)
    inverse = 1.0 / rho
    ux, uy, uz = jx * inverse, jy * inverse, jz * inverse
    kxx = mxx - jx * ux
    return (
        rho, ux, uy, uz,
        keep * (mxy - jx * uy),
        keep * (mxz - jx * uz),
        keep * (myz - jy * uz),
        keep * (kxx - (myy - jy * uy)),
        keep * (kxx - (mzz - jz * uz)),
    )


def pre_kernel(cap, row_count, per_row, part, dest_hbm, level_hbm, x_hbm, out_ref, *refs):
    x_ref, swap_ref, packed_ref, side_ref, dest_ref, level_ref, sems = refs
    order = CHUNKS[part] if part else CHUNKS[0] + INNER
    steps = len(CHUNKS[part])
    blocks = x_ref.shape[2]
    cells = x_ref.shape[3]
    chunks = cells // LANES
    small = [
        pltpu.make_async_copy(dest_hbm, dest_ref, sems.at[0]),
        pltpu.make_async_copy(level_hbm, level_ref, sems.at[1]),
    ]
    large = [
        pltpu.make_async_copy(
            x_hbm.at[:, :, pl.ds(group * cells, cells)], x_ref.at[step], sems.at[2 + step]
        )
        for step, group in enumerate(order)
    ]
    for copy in small + large:
        copy.start()
    for copy in small:
        copy.wait()

    which = lax.broadcasted_iota(jnp.int32, (SUB, LANES), 0)
    spot = lax.broadcasted_iota(jnp.int32, (SUB, LANES), 1) // EDGE
    scale = jnp.zeros((SUB, LANES), jnp.int32)
    tag = jnp.zeros((SUB, LANES), jnp.int32)
    for t in range(blocks):
        scale = jnp.where(which == t, jnp.left_shift(1, level_ref[t]), scale)
        tag = jnp.where(which == t, dest_ref[t], tag)
    rate = 1.0 / (3.0 * VISCOSITY * scale.astype(jnp.float32) + 0.5)
    keep = 1.0 - rate

    rows = [dest_ref[t] // per_row for t in range(blocks)]
    slots = []
    for t in range(blocks):
        slot = rows[t] * cap
        for other in range(t):
            slot = slot + jnp.where(rows[other] == rows[t], 1, 0)
        slots.append(slot)

    def spread(ref, first, count):
        for t in range(blocks):
            for n in range(count):
                moved = ref[pl.ds(n * SUB * SUB + t, SUB, stride=SUB), :]
                out_ref[slots[t], first + n] = moved

    def fields_at(step, c):
        return collided([x_ref[step, q, :, c * LANES : (c + 1) * LANES] for q in range(NQ)], keep)

    for step, group in enumerate(order):
        large[step].wait()
        if part:
            last = fields_at(step, chunks - 1)
            for c in range(chunks - 1):
                place = free_place(c)
                turn = (place - c) * EDGE % LANES
                for n, field in enumerate(fields_at(step, c)):
                    other = pltpu.roll(last[n], turn, axis=1) if turn else last[n]
                    base = (step * LATE_TILES * SUB + n * (chunks - 1) + c) * SUB
                    swap_ref[base : base + SUB, :] = jnp.where(spot == place, other, field)
            continue
        if step < steps:
            for c in range(chunks):
                for n, field in enumerate(fields_at(step, c)):
                    base = (n * chunks + c) * SUB
                    swap_ref[base : base + SUB, :] = field
            spread(swap_ref, SIDE_TILES + step * NFIELD, NFIELD)
            continue
        for q in range(NQ):
            for half in range(2):
                value = packed_ref[half * NQ + q] if step > steps else None
                for x in range(WIDTH):
                    c = x * 2 + half
                    at = (group * WIDTH + x) % SUB
                    moved = x_ref[step, q, :, c * LANES : (c + 1) * LANES]
                    turn = (at + half) * EDGE % LANES
                    if turn:
                        moved = pltpu.roll(moved, turn, axis=1)
                    value = moved if value is None else jnp.where(spot == at, moved, value)
                packed_ref[half * NQ + q] = value

    if part:
        for step in range(steps):
            for row in range(NFIELD * (chunks - 1), LATE_TILES * SUB):
                base = (step * LATE_TILES * SUB + row) * SUB
                swap_ref[base : base + SUB, :] = tag.astype(jnp.float32)
        spread(swap_ref, 0, steps * LATE_TILES)
        return
    for row in range(SIDE_TILES * SUB):
        if not 1 <= row <= 2 * NFIELD:
            side_ref[row * SUB : (row + 1) * SUB, :] = tag.astype(jnp.float32)
    for half in range(2):
        fields = collided([packed_ref[half * NQ + q] for q in range(NQ)], keep)
        for n, field in enumerate(fields):
            base = (1 + half * NFIELD + n) * SUB
            side_ref[base : base + SUB, :] = field
    for slot in range(row_count * cap):
        out_ref[slot, 0] = jnp.full((SUB, LANES), -1.0, jnp.float32)
    spread(side_ref, 0, SIDE_TILES)


def pre(populations, destination, refinement, part, row_count, cap, per_row):
    blocks = populations.shape[1]
    cells = populations.shape[2] // GROUPS
    loaded = len(CHUNKS[part]) + (0 if part else len(INNER))
    rows = tiles_of(1) * SUB if part else NFIELD * cells // LANES
    return pl.pallas_call(
        functools.partial(pre_kernel, cap, row_count, per_row, part),
        in_specs=[pl.BlockSpec(memory_space=pltpu.HBM)] * 3,
        out_specs=pl.BlockSpec(memory_space=pltpu.VMEM),
        out_shape=jax.ShapeDtypeStruct((row_count * cap, tiles_of(part), SUB, LANES), jnp.float32),
        scratch_shapes=[
            pltpu.VMEM((loaded, NQ, blocks, cells), jnp.float32),
            pltpu.VMEM((rows * SUB, LANES), jnp.float32),
            pltpu.VMEM((2 * NQ, SUB, LANES), jnp.float32),
            pltpu.VMEM((SIDE_TILES * SUB * SUB, LANES), jnp.float32),
            pltpu.SMEM((blocks,), jnp.int32),
            pltpu.SMEM((blocks,), jnp.int32),
            pltpu.SemaphoreType.DMA((2 + loaded,)),
        ],
        compiler_params=pltpu.CompilerParams(vmem_limit_bytes=LARGE_VMEM_LIMIT),
        cost_estimate=pl.CostEstimate(flops=10**7, bytes_accessed=4 * 10**6, transcendentals=0),
        name="pre_%d" % part,
    )(destination, refinement, populations)


def read_tags(ins, tag_ref, sems):
    cap = ins[0].shape[0]
    copies = [
        pltpu.make_async_copy(in_ref.at[:, 0, pl.ds(0, 1)], tag_ref.at[pl.ds(d * cap, cap)], sems.at[d])
        for d, in_ref in enumerate(ins)
    ]
    for copy in copies:
        copy.start()
    for copy in copies:
        copy.wait()
    return lambda e: tag_ref[e, 0, 0].astype(jnp.int32)


def tag_scratch(arrays, slots):
    return [pltpu.SMEM((slots, 1, LANES), jnp.float32), pltpu.SemaphoreType.DMA((arrays,))]


def repack_kernel(cap, col_count, blocks, part, *refs):
    if part:
        plan_ref, in_ref, *outs = refs
    else:
        in_ref, *outs, plan_ref, tag_ref, sems, count_ref = refs
        tag_at = read_tags([in_ref], tag_ref, sems)
        here = lax.axis_index("col")
        for d in range(col_count):
            count_ref[d] = 0
        for e in range(col_count * cap):
            plan_ref[e] = -1
        for e in range(in_ref.shape[0]):
            tag = tag_at(e)

            @pl.when(tag >= 0)
            def _():
                d = step_to(lax.rem(tag // blocks, col_count), here, col_count)
                k = count_ref[d]
                count_ref[d] = k + 1
                plan_ref[d * cap + k] = e

    for place, out in enumerate(outs):
        tiles = out.shape[1]
        quarter, d = divmod(place - 1, col_count - 1) if part else (0, place)
        if part and place == 0:
            quarter, d = 0, col_count - 1
        for k in range(cap):
            e = plan_ref[d * cap + k]

            @pl.when(e >= 0)
            def _():
                out[k] = in_ref[e, quarter * tiles : (quarter + 1) * tiles]

            if part == 0:

                @pl.when(e < 0)
                def _():
                    out[k, 0] = jnp.full((SUB, LANES), -1.0, jnp.float32)


def repack(landed, plan, part, col_count, cap, blocks):
    whole = pl.BlockSpec(memory_space=pltpu.VMEM)
    scalars = pl.BlockSpec(memory_space=pltpu.SMEM)
    scratch = []
    if part == 0:
        scratch = tag_scratch(1, landed.shape[0]) + [pltpu.SMEM((col_count,), jnp.int32)]
    tiles = landed.shape[1]
    sizes = [tiles] * col_count
    if part:
        sizes = [tiles] + [tiles // len(INNER)] * (len(INNER) * (col_count - 1))
    packed = pl.pallas_call(
        functools.partial(repack_kernel, cap, col_count, blocks, part),
        in_specs=([scalars] if part else []) + [whole],
        out_specs=[whole] * len(sizes) + ([] if part else [scalars]),
        scratch_shapes=scratch,
        out_shape=[jax.ShapeDtypeStruct((cap, size) + landed.shape[2:], jnp.float32) for size in sizes]
        + ([] if part else [jax.ShapeDtypeStruct((col_count * cap,), jnp.int32)]),
        compiler_params=pltpu.CompilerParams(vmem_limit_bytes=VMEM_LIMIT),
        cost_estimate=pl.CostEstimate(flops=0, bytes_accessed=3 * 10**6, transcendentals=0),
        name="repack_%d" % part,
    )(*([plan] if part else []), landed)
    return packed if part else (packed[:-1], packed[-1])


def backward(zeroth, first, second, u):
    raw_one, raw_two = first, second
    if zeroth is not None:
        moved = u * zeroth
        raw_one = moved if raw_one is None else raw_one + moved
        square = u * moved
        raw_two = square if raw_two is None else raw_two + square
    if first is not None:
        cross = (u + u) * first
        raw_two = cross if raw_two is None else raw_two + cross
    rest = -raw_two if zeroth is None else zeroth - raw_two
    return 0.5 * (raw_two - raw_one), rest, 0.5 * (raw_one + raw_two)


def post_populations(rho, ux, uy, uz, pxy, pxz, pyz, dev_one, dev_two):
    inverse = 1.0 / rho
    pxx = (rho + dev_one + dev_two) * (1.0 / 3.0)
    pyy = pxx - dev_one
    pzz = pxx - dev_two
    sxy, sxz, syz = pxy * inverse, pxz * inverse, pyz * inverse
    syy, szz = pyy * inverse, pzz * inverse
    central = {
        (0, 0, 0): rho, (2, 0, 0): pxx, (0, 2, 0): pyy, (0, 0, 2): pzz,
        (1, 1, 0): pxy, (1, 0, 1): pxz, (0, 1, 1): pyz,
        (2, 2, 0): pxx * syy + 2.0 * pxy * sxy,
        (2, 0, 2): pxx * szz + 2.0 * pxz * sxz,
        (0, 2, 2): pyy * szz + 2.0 * pyz * syz,
        (2, 1, 1): pxx * syz + 2.0 * pxy * sxz,
        (1, 2, 1): pyy * sxz + 2.0 * pxy * syz,
        (1, 1, 2): pzz * sxy + 2.0 * pxz * syz,
        (2, 2, 2): pxx * syy * szz
        + 2.0 * (pxx * syz * syz + pyy * sxz * sxz + pzz * sxy * sxy)
        + 8.0 * pxy * sxz * syz,
    }
    along_z = {}
    for a in range(3):
        for b in range(3):
            parts = backward(*(central.get((a, b, c)) for c in range(3)), uz)
            for k in range(3):
                along_z[a, b, k] = parts[k]
    along_y = {}
    for a in range(3):
        for k in range(3):
            parts = backward(*(along_z[a, b, k] for b in range(3)), uy)
            for j in range(3):
                along_y[a, j, k] = parts[j]
    result = [None] * NQ
    for j in range(3):
        for k in range(3):
            parts = backward(*(along_y[a, j, k] for a in range(3)), ux)
            for i in range(3):
                result[i * 9 + j * 3 + k] = parts[i]
    return result


def unload(plan_ref, ins, fields_ref, index=0):
    cap = ins[0].shape[0]
    tiles = ins[-1].shape[1]
    for e in range(len(ins) * cap):
        t = plan_ref[e]
        in_ref = ins[e // cap]
        first = index * tiles if in_ref.shape[1] > tiles else 0

        @pl.when(t >= 0)
        def _():
            for tile in range(tiles):
                fields_ref[pl.ds(tile * SUB * SUB + t, SUB, stride=SUB), :] = in_ref[e % cap, first + tile]


def row_of(ref, row):
    return ref[row * SUB : (row + 1) * SUB, :]


def turned(value, places):
    turn = places * EDGE % LANES
    return pltpu.roll(value, turn, axis=1) if turn else value


def places_y():
    return lax.broadcasted_iota(jnp.int32, (SUB, LANES), 1) // EDGE


def outer_fields(fields_ref, step, c):
    first = (SIDE_TILES + step * NFIELD) * SUB
    return [row_of(fields_ref, first + n * SUB + c) for n in range(NFIELD)]


def side_fields(fields_ref, half):
    return [row_of(fields_ref, 1 + half * NFIELD + n) for n in range(NFIELD)]


def fill_outer(fields_ref, main_ref):
    for step, group in enumerate(CHUNKS[0]):
        for c in range(SUB):
            for q, value in enumerate(post_populations(*outer_fields(fields_ref, step, c))):
                main_ref[q, 2 + group * SUB + c] = value


def fill_inner(fields_ref, late_ref, group, main_ref):
    spot = places_y()
    last = [None] * NFIELD
    for c in range(SUB):
        at = (group * WIDTH + c // 2) % SUB
        place = free_place(c)
        side = side_fields(fields_ref, c % 2)
        fields = []
        for n in range(NFIELD):
            if c < SUB - 1:
                row = row_of(late_ref, n * (SUB - 1) + c)
                part = turned(row, c - place)
                last[n] = part if c == 0 else jnp.where(spot == c, part, last[n])
            else:
                row = last[n]
            fields.append(jnp.where(spot == place, turned(side[n], place - at), row))
        for q, value in enumerate(post_populations(*fields)):
            main_ref[q, 2 + group * SUB + c] = value


def fill_sides(below_in, above_in, below_ref, above_ref, first, last):
    for x in range(first, last):
        at = x % SUB
        for k in range(9):
            below_ref[k, x + 1] = turned(below_in[k, x // SUB], SUB - 1 - at)
            above_ref[k, x + 1] = turned(above_in[k, x // SUB], -at)


def stream_pair(first_x, out_ref, main_ref, below_ref, above_ref):
    lane = lax.broadcasted_iota(jnp.int32, (SUB, LANES), 1)
    block = lax.broadcasted_iota(jnp.int32, (SUB, LANES), 0)
    along = lane % EDGE
    first_z, last_z = along == 0, along == EDGE - 1
    floor = first_z & (block == 0)
    ceiling = last_z & (block == SUB - 1)
    low_y, high_y = lane < EDGE, lane >= LANES - EDGE
    for i in range(2):
        for half in range(2):
            c = i * 2 + half
            for q in range(NQ):
                cx, cy, cz = velocity(q)
                x = first_x + i - cx + 1
                a = main_ref[q, x * 2 + half]
                k = (cx + 1) * 3 + cz + 1
                if cy == 1:
                    a = jnp.where(high_y, main_ref[q, x * 2] if half else below_ref[k, x], a)
                elif cy == -1:
                    a = jnp.where(low_y, above_ref[k, x] if half else main_ref[q, x * 2 + 1], a)
                shift = EDGE * cy + cz
                value = a if shift == 0 else pltpu.roll(a, shift % LANES, axis=1)
                if cz:
                    bounced = main_ref[26 - q, (first_x + i + 1) * 2 + half]
                    turn = (1 if cz == 1 else SUB - 1)
                    fill = pltpu.roll(pltpu.roll(a, turn, axis=0), (shift - cz * EDGE) % LANES, axis=1)
                    value = jnp.where(first_z if cz == 1 else last_z, fill, value)
                    value = jnp.where(floor if cz == 1 else ceiling, bounced, value)
                out_ref[q, :, c * LANES : (c + 1) * LANES] = value


def stream_pairs(pairs, out_hbm, pair_ref, sems, *lattice):
    span = pair_ref.shape[3]

    def copy(i):
        return pltpu.make_async_copy(
            pair_ref.at[i], out_hbm.at[:, :, pl.ds(pairs[i] * span, span)], sems.at[i]
        )

    for i, pair in enumerate(pairs):
        stream_pair(2 * pair, pair_ref.at[i], *lattice)
        copy(i).start()
    for i in range(len(pairs)):
        copy(i).wait()


def faces_kernel(count, *refs):
    ins = refs[:count]
    ylo_ref, yhi_ref, xlo_ref, xhi_ref, plan_ref, fields_ref, tag_ref, sems = refs[count:]
    tag_at = read_tags(ins, tag_ref, sems)
    for e in range(count * ins[0].shape[0]):
        tag = tag_at(e)
        plan_ref[e] = jnp.where(tag >= 0, lax.rem(tag, SUB), -1)
    unload(plan_ref, ins, fields_ref)
    spot = places_y()
    for half in range(2):
        packed = [side_fields(fields_ref, half)] * 2
        place = half * (SUB - 1)
        for step, group in enumerate(CHUNKS[0]):
            tile = group * WIDTH // SUB
            for x in range(group * WIDTH, (group + 1) * WIDTH):
                c = (x - group * WIDTH) * 2 + half
                packed[tile] = [
                    jnp.where(spot == x % SUB, turned(value, x % SUB - place), old)
                    for value, old in zip(outer_fields(fields_ref, step, c), packed[tile])
                ]
        for tile in range(2):
            result = post_populations(*packed[tile])
            for i in range(3):
                for k in range(3):
                    (yhi_ref if half else ylo_ref)[i * 3 + k, tile] = result[i * 9 + half * 6 + k]
        low = post_populations(*outer_fields(fields_ref, CHUNKS[0].index(0), half))
        high = post_populations(*outer_fields(fields_ref, CHUNKS[0].index(GROUPS - 1), SUB - 2 + half))
        for q in range(9):
            xlo_ref[q, half] = low[q]
            xhi_ref[q, half] = high[18 + q]


def faces(homes):
    shape = jax.ShapeDtypeStruct
    face = shape((9, 2, SUB, LANES), jnp.float32)
    slots = len(homes) * homes[0].shape[0]
    whole = pl.BlockSpec(memory_space=pltpu.VMEM)
    return pl.pallas_call(
        functools.partial(faces_kernel, len(homes)),
        in_specs=[whole] * len(homes),
        out_specs=[whole] * 4 + [pl.BlockSpec(memory_space=pltpu.SMEM), whole],
        scratch_shapes=tag_scratch(len(homes), slots),
        out_shape=[face] * 4
        + [shape((slots,), jnp.int32), shape((tiles_of(0) * SUB * SUB, LANES), jnp.float32)],
        compiler_params=pltpu.CompilerParams(vmem_limit_bytes=VMEM_LIMIT),
        cost_estimate=pl.CostEstimate(flops=10**7, bytes_accessed=3 * 10**6, transcendentals=0),
        name="faces",
    )(*homes)


PAIRS = ((0, 1, 2, 7), (3, 4, 5, 6))
KEPT = ((5, 8), (12, 15))


def advance_kernel(count, plan_ref, *refs):
    ins = refs[:count]
    (
        fields_ref, xlo_ref, xhi_ref, below_in, above_in, out_ref, kept_ref,
        main_ref, below_ref, above_ref, late_ref, pair_ref, sems,
    ) = refs[count:]
    unload(plan_ref, ins, late_ref)
    fill_outer(fields_ref, main_ref)
    fill_inner(fields_ref, late_ref, INNER[0], main_ref)
    fill_sides(below_in, above_in, below_ref, above_ref, 0, 7)
    fill_sides(below_in, above_in, below_ref, above_ref, 13, EDGE)
    for k in range(3):
        below_ref[6 + k, 0] = xlo_ref[18 + k]
        above_ref[6 + k, 0] = turned(xlo_ref[21 + k], 1)
        below_ref[k, EDGE + 1] = turned(xhi_ref[18 + k], -1)
        above_ref[k, EDGE + 1] = xhi_ref[21 + k]
    for q in range(9):
        for half in range(2):
            main_ref[18 + q, half] = xlo_ref[q * 2 + half]
            main_ref[q, 2 * EDGE + 2 + half] = xhi_ref[q * 2 + half]
    to = 0
    for first, last in KEPT:
        for row in range(2 * first + 2, 2 * last + 2):
            for q in range(NQ):
                kept_ref[q, to] = main_ref[q, row]
            to += 1

    stream_pairs(PAIRS[0], out_ref, pair_ref, sems, main_ref, below_ref, above_ref)


def finish_kernel(count, plan_ref, *refs):
    ins = refs[:count]
    (
        fields_ref, kept_ref, below_in, above_in, _, out_ref,
        main_ref, below_ref, above_ref, late_ref, pair_ref, sems,
    ) = refs[count:]
    copies = []
    to = 0
    for first, last in KEPT:
        rows = 2 * (last - first)
        copies.append(
            pltpu.make_async_copy(
                kept_ref.at[:, pl.ds(to, rows)],
                main_ref.at[:, pl.ds(2 * first + 2, rows)],
                sems.at[len(PAIRS[1]) + len(copies)],
            )
        )
        to += rows
    for copy in copies:
        copy.start()
    unload(plan_ref, ins, late_ref, 1)
    fill_inner(fields_ref, late_ref, INNER[1], main_ref)
    fill_sides(below_in, above_in, below_ref, above_ref, 5, 15)
    for copy in copies:
        copy.wait()

    stream_pairs(PAIRS[1], out_ref, pair_ref, sems, main_ref, below_ref, above_ref)


def scratch_of_lattice():
    side = pltpu.VMEM((9, EDGE + 2, SUB, LANES), jnp.float32)
    return [
        pltpu.VMEM((NQ, 2 * EDGE + 4, SUB, LANES), jnp.float32), side, side,
        pltpu.VMEM((LATE_TILES * SUB * SUB, LANES), jnp.float32),
        pltpu.VMEM((len(PAIRS[0]), NQ, SUB, 4 * LANES), jnp.float32),
        pltpu.SemaphoreType.DMA((len(PAIRS[0]) + len(KEPT),)),
    ]


def advance(plan, homes, fields, xlo, xhi, below, above):
    inputs = [*homes, fields, xlo, xhi, below, above]
    whole = pl.BlockSpec(memory_space=pltpu.VMEM)
    kept = 2 * sum(last - first for first, last in KEPT)
    return pl.pallas_call(
        functools.partial(advance_kernel, len(homes)),
        in_specs=[pl.BlockSpec(memory_space=pltpu.SMEM)] + [whole] * len(inputs),
        out_specs=[pl.BlockSpec(memory_space=pltpu.HBM), whole],
        scratch_shapes=scratch_of_lattice(),
        out_shape=[
            jax.ShapeDtypeStruct((NQ, SUB, GROUPS * SUB * LANES), jnp.float32),
            jax.ShapeDtypeStruct((NQ, kept, SUB, LANES), jnp.float32),
        ],
        compiler_params=pltpu.CompilerParams(vmem_limit_bytes=VMEM_LIMIT),
        cost_estimate=pl.CostEstimate(flops=10**7, bytes_accessed=5 * 10**6, transcendentals=0),
        name="advance",
    )(plan, *inputs)


def finish(plan, homes, fields, kept, below, above, out):
    inputs = [*homes, fields, kept, below, above]
    whole = pl.BlockSpec(memory_space=pltpu.VMEM)
    target = pl.BlockSpec(memory_space=pltpu.HBM)
    return pl.pallas_call(
        functools.partial(finish_kernel, len(homes)),
        in_specs=[pl.BlockSpec(memory_space=pltpu.SMEM)] + [whole] * len(inputs) + [target],
        out_specs=target,
        scratch_shapes=scratch_of_lattice(),
        out_shape=jax.ShapeDtypeStruct(out.shape, jnp.float32),
        input_output_aliases={1 + len(inputs): 0},
        compiler_params=pltpu.CompilerParams(vmem_limit_bytes=VMEM_LIMIT),
        cost_estimate=pl.CostEstimate(flops=10**7, bytes_accessed=5 * 10**6, transcendentals=0),
        name="finish",
    )(plan, *inputs, out)


def shifted(value, axis, step):
    count = lax.axis_size(axis)
    return lax.ppermute(value, axis, [(i, (i + step) % count) for i in range(count)])


def after(value, *earlier):
    return lax.optimization_barrier((value, *earlier))[0]


def on_device(populations, destination, refinement):
    blocks = populations.shape[0]
    row_count = lax.axis_size("row")
    col_count = lax.axis_size("col")
    cap_row = 2 * ((blocks + row_count - 1) // row_count)
    cap_col = 2 * ((blocks + col_count - 1) // col_count)
    ordered = jnp.transpose(populations, (1, 0, 2))

    def prepared(part, *earlier):
        first = after(destination, *earlier)
        return pre(ordered, first, refinement, part, row_count, cap_row, blocks * col_count)

    def to_rows(sent):
        return lax.all_to_all(sent, "row", split_axis=0, concat_axis=0, tiled=True)

    def to_columns(packed):
        return [exchanged(packed[d], "col", d) for d in range(len(packed) - 1, 0, -1)] + [packed[0]]

    sent = prepared(0)
    early_row = to_rows(sent)
    late_row = to_rows(prepared(1, sent))
    packed, plan = repack(early_row, None, 0, col_count, cap_col, blocks)
    ylo, yhi, xlo, xhi, picked, fields = faces(to_columns(packed))
    below, above = shifted(yhi, "col", 1), shifted(ylo, "col", -1)
    up = jnp.concatenate([xhi.reshape(18, SUB, LANES), below[6:, 1], above[6:, 1]])
    down = jnp.concatenate([xlo.reshape(18, SUB, LANES), below[:3, 0], above[:3, 0]])
    xlo, xhi = shifted(up, "row", 1), shifted(down, "row", -1)
    packed = repack(after(late_row, up, down), plan, 1, col_count, cap_col, blocks)
    far, *packed = packed
    far = exchanged(far, "col", col_count - 1)
    middle = [far] + to_columns(packed[: col_count - 1])
    last = [far] + to_columns(packed[col_count - 1 :])
    out, kept = advance(picked, middle, fields, xlo, xhi, below, above)
    return jnp.transpose(finish(picked, last, fields, kept, below, above, out), (1, 0, 2))


def solution(mesh):
    return jax.shard_map(
        on_device,
        mesh=mesh,
        in_specs=(P(("row", "col"), None, None), P(("row", "col")), P(("row", "col"))),
        out_specs=P(("row", "col"), None, None),
        check_vma=False,
    )
```

```python
import functools

import jax
import jax.numpy as jnp
from jax import lax
from jax.experimental import pallas as pl
from jax.experimental.pallas import tpu as pltpu
from jax.sharding import PartitionSpec as P

EDGE = 16
VISCOSITY = 0.01
LANES = 128
SUB = 8
NQ = 27
NFIELD = 9
GROUPS = 4
WIDTH = EDGE // GROUPS
CHUNKS = ((0, 3), (1, 2))
INNER = CHUNKS[1]
SIDE_TILES = 3
LATE_TILES = -(-NFIELD * (SUB - 1) // SUB)
VMEM_LIMIT = 20 * 1024 * 1024
LARGE_VMEM_LIMIT = 60 * 1024 * 1024


def velocity(q):
    return (q // 9 - 1, (q // 3) % 3 - 1, q % 3 - 1)


def tiles_of(part):
    return len(INNER) * LATE_TILES if part else len(CHUNKS[0]) * NFIELD + SIDE_TILES


def free_place(c):
    return (c % 2) * (SUB - 1)


def step_to(target, here, count):
    if count & (count - 1) == 0:
        return target ^ here
    return lax.rem(target - here + count, count)


def exchanged(value, axis, step):
    count = lax.axis_size(axis)
    if count & (count - 1) == 0:
        pairs = [(i, i ^ step) for i in range(count)]
    else:
        pairs = [(i, (i + step) % count) for i in range(count)]
    return lax.ppermute(value, axis, pairs)


def raw_moments(f):
    whole, slope, outer = {}, {}, {}
    for i in range(3):
        for j in range(3):
            low, rest, high = (f[i * 9 + j * 3 + k] for k in range(3))
            outer[i, j] = low + high
            whole[i, j] = outer[i, j] + rest
            slope[i, j] = high - low
    column = [whole[i, 0] + whole[i, 1] + whole[i, 2] for i in range(3)]
    tilt = [slope[i, 0] + slope[i, 1] + slope[i, 2] for i in range(3)]
    low_y = whole[0, 0] + whole[1, 0] + whole[2, 0]
    high_y = whole[0, 2] + whole[1, 2] + whole[2, 2]
    ends = column[0] + column[2]
    mzz = sum(outer[i, j] for i in range(3) for j in range(3))
    mxy = (whole[2, 2] - whole[2, 0]) - (whole[0, 2] - whole[0, 0])
    myz = (slope[0, 2] + slope[1, 2] + slope[2, 2]) - (slope[0, 0] + slope[1, 0] + slope[2, 0])
    return (
        ends + column[1],
        column[2] - column[0],
        high_y - low_y,
        tilt[0] + tilt[1] + tilt[2],
        ends,
        low_y + high_y,
        mzz,
        mxy,
        tilt[2] - tilt[0],
        myz,
    )


def collided(f, keep):
    rho, jx, jy, jz, mxx, myy, mzz, mxy, mxz, myz = raw_moments(f)
    inverse = 1.0 / rho
    ux, uy, uz = jx * inverse, jy * inverse, jz * inverse
    kxx = mxx - jx * ux
    return (
        rho, ux, uy, uz,
        keep * (mxy - jx * uy),
        keep * (mxz - jx * uz),
        keep * (myz - jy * uz),
        keep * (kxx - (myy - jy * uy)),
        keep * (kxx - (mzz - jz * uz)),
    )


def pre_kernel(cap, row_count, per_row, part, dest_hbm, level_hbm, x_hbm, out_ref, *refs):
    x_ref, swap_ref, packed_ref, side_ref, dest_ref, level_ref, sems = refs
    order = CHUNKS[part] if part else CHUNKS[0] + INNER
    steps = len(CHUNKS[part])
    blocks = x_ref.shape[2]
    cells = x_ref.shape[3]
    chunks = cells // LANES
    small = [
        pltpu.make_async_copy(dest_hbm, dest_ref, sems.at[0]),
        pltpu.make_async_copy(level_hbm, level_ref, sems.at[1]),
    ]
    large = [
        pltpu.make_async_copy(
            x_hbm.at[:, :, pl.ds(group * cells, cells)], x_ref.at[step], sems.at[2 + step]
        )
        for step, group in enumerate(order)
    ]
    for copy in small + large:
        copy.start()
    for copy in small:
        copy.wait()

    which = lax.broadcasted_iota(jnp.int32, (SUB, LANES), 0)
    spot = lax.broadcasted_iota(jnp.int32, (SUB, LANES), 1) // EDGE
    scale = jnp.zeros((SUB, LANES), jnp.int32)
    tag = jnp.zeros((SUB, LANES), jnp.int32)
    for t in range(blocks):
        scale = jnp.where(which == t, jnp.left_shift(1, level_ref[t]), scale)
        tag = jnp.where(which == t, dest_ref[t], tag)
    rate = 1.0 / (3.0 * VISCOSITY * scale.astype(jnp.float32) + 0.5)
    keep = 1.0 - rate

    rows = [dest_ref[t] // per_row for t in range(blocks)]
    slots = []
    for t in range(blocks):
        slot = rows[t] * cap
        for other in range(t):
            slot = slot + jnp.where(rows[other] == rows[t], 1, 0)
        slots.append(slot)

    def spread(ref, first, count):
        for t in range(blocks):
            for n in range(count):
                moved = ref[pl.ds(n * SUB * SUB + t, SUB, stride=SUB), :]
                out_ref[slots[t], first + n] = moved

    def fields_at(step, c):
        return collided([x_ref[step, q, :, c * LANES : (c + 1) * LANES] for q in range(NQ)], keep)

    for step, group in enumerate(order):
        large[step].wait()
        if part:
            last = fields_at(step, chunks - 1)
            for c in range(chunks - 1):
                place = free_place(c)
                turn = (place - c) * EDGE % LANES
                for n, field in enumerate(fields_at(step, c)):
                    other = pltpu.roll(last[n], turn, axis=1) if turn else last[n]
                    base = (step * LATE_TILES * SUB + n * (chunks - 1) + c) * SUB
                    swap_ref[base : base + SUB, :] = jnp.where(spot == place, other, field)
            continue
        if step < steps:
            for c in range(chunks):
                for n, field in enumerate(fields_at(step, c)):
                    base = (n * chunks + c) * SUB
                    swap_ref[base : base + SUB, :] = field
            spread(swap_ref, SIDE_TILES + step * NFIELD, NFIELD)
            continue
        for q in range(NQ):
            for half in range(2):
                value = packed_ref[half * NQ + q] if step > steps else None
                for x in range(WIDTH):
                    c = x * 2 + half
                    at = (group * WIDTH + x) % SUB
                    moved = x_ref[step, q, :, c * LANES : (c + 1) * LANES]
                    turn = (at + half) * EDGE % LANES
                    if turn:
                        moved = pltpu.roll(moved, turn, axis=1)
                    value = moved if value is None else jnp.where(spot == at, moved, value)
                packed_ref[half * NQ + q] = value

    if part:
        for step in range(steps):
            for row in range(NFIELD * (chunks - 1), LATE_TILES * SUB):
                base = (step * LATE_TILES * SUB + row) * SUB
                swap_ref[base : base + SUB, :] = tag.astype(jnp.float32)
        spread(swap_ref, 0, steps * LATE_TILES)
        return
    for row in range(SIDE_TILES * SUB):
        if not 1 <= row <= 2 * NFIELD:
            side_ref[row * SUB : (row + 1) * SUB, :] = tag.astype(jnp.float32)
    for half in range(2):
        fields = collided([packed_ref[half * NQ + q] for q in range(NQ)], keep)
        for n, field in enumerate(fields):
            base = (1 + half * NFIELD + n) * SUB
            side_ref[base : base + SUB, :] = field
    for slot in range(row_count * cap):
        out_ref[slot, 0] = jnp.full((SUB, LANES), -1.0, jnp.float32)
    spread(side_ref, 0, SIDE_TILES)


def pre(populations, destination, refinement, part, row_count, cap, per_row):
    blocks = populations.shape[1]
    cells = populations.shape[2] // GROUPS
    loaded = len(CHUNKS[part]) + (0 if part else len(INNER))
    rows = tiles_of(1) * SUB if part else NFIELD * cells // LANES
    return pl.pallas_call(
        functools.partial(pre_kernel, cap, row_count, per_row, part),
        in_specs=[pl.BlockSpec(memory_space=pltpu.HBM)] * 3,
        out_specs=pl.BlockSpec(memory_space=pltpu.VMEM),
        out_shape=jax.ShapeDtypeStruct((row_count * cap, tiles_of(part), SUB, LANES), jnp.float32),
        scratch_shapes=[
            pltpu.VMEM((loaded, NQ, blocks, cells), jnp.float32),
            pltpu.VMEM((rows * SUB, LANES), jnp.float32),
            pltpu.VMEM((2 * NQ, SUB, LANES), jnp.float32),
            pltpu.VMEM((SIDE_TILES * SUB * SUB, LANES), jnp.float32),
            pltpu.SMEM((blocks,), jnp.int32),
            pltpu.SMEM((blocks,), jnp.int32),
            pltpu.SemaphoreType.DMA((2 + loaded,)),
        ],
        compiler_params=pltpu.CompilerParams(vmem_limit_bytes=LARGE_VMEM_LIMIT),
        cost_estimate=pl.CostEstimate(flops=10**7, bytes_accessed=4 * 10**6, transcendentals=0),
        name="pre_%d" % part,
    )(destination, refinement, populations)


def read_tags(ins, tag_ref, sems):
    cap = ins[0].shape[0]
    copies = [
        pltpu.make_async_copy(in_ref.at[:, 0, pl.ds(0, 1)], tag_ref.at[pl.ds(d * cap, cap)], sems.at[d])
        for d, in_ref in enumerate(ins)
    ]
    for copy in copies:
        copy.start()
    for copy in copies:
        copy.wait()
    return lambda e: tag_ref[e, 0, 0].astype(jnp.int32)


def tag_scratch(arrays, slots):
    return [pltpu.SMEM((slots, 1, LANES), jnp.float32), pltpu.SemaphoreType.DMA((arrays,))]


def repack_kernel(cap, col_count, blocks, part, *refs):
    if part:
        plan_ref, in_ref, *outs = refs
    else:
        in_ref, *outs, plan_ref, tag_ref, sems, count_ref = refs
        tag_at = read_tags([in_ref], tag_ref, sems)
        here = lax.axis_index("col")
        for d in range(col_count):
            count_ref[d] = 0
        for e in range(col_count * cap):
            plan_ref[e] = -1
        for e in range(in_ref.shape[0]):
            tag = tag_at(e)

            @pl.when(tag >= 0)
            def _():
                d = step_to(lax.rem(tag // blocks, col_count), here, col_count)
                k = count_ref[d]
                count_ref[d] = k + 1
                plan_ref[d * cap + k] = e

    for place, out in enumerate(outs):
        tiles = out.shape[1]
        quarter, d = divmod(place - 1, col_count - 1) if part else (0, place)
        if part and place == 0:
            quarter, d = 0, col_count - 1
        for k in range(cap):
            e = plan_ref[d * cap + k]

            @pl.when(e >= 0)
            def _():
                out[k] = in_ref[e, quarter * tiles : (quarter + 1) * tiles]

            if part == 0:

                @pl.when(e < 0)
                def _():
                    out[k, 0] = jnp.full((SUB, LANES), -1.0, jnp.float32)


def repack(landed, plan, part, col_count, cap, blocks):
    whole = pl.BlockSpec(memory_space=pltpu.VMEM)
    scalars = pl.BlockSpec(memory_space=pltpu.SMEM)
    scratch = []
    if part == 0:
        scratch = tag_scratch(1, landed.shape[0]) + [pltpu.SMEM((col_count,), jnp.int32)]
    tiles = landed.shape[1]
    sizes = [tiles] * col_count
    if part:
        sizes = [tiles] + [tiles // len(INNER)] * (len(INNER) * (col_count - 1))
    packed = pl.pallas_call(
        functools.partial(repack_kernel, cap, col_count, blocks, part),
        in_specs=([scalars] if part else []) + [whole],
        out_specs=[whole] * len(sizes) + ([] if part else [scalars]),
        scratch_shapes=scratch,
        out_shape=[jax.ShapeDtypeStruct((cap, size) + landed.shape[2:], jnp.float32) for size in sizes]
        + ([] if part else [jax.ShapeDtypeStruct((col_count * cap,), jnp.int32)]),
        compiler_params=pltpu.CompilerParams(vmem_limit_bytes=VMEM_LIMIT),
        cost_estimate=pl.CostEstimate(flops=0, bytes_accessed=3 * 10**6, transcendentals=0),
        name="repack_%d" % part,
    )(*([plan] if part else []), landed)
    return packed if part else (packed[:-1], packed[-1])


def backward(zeroth, first, second, u):
    raw_one, raw_two = first, second
    if zeroth is not None:
        moved = u * zeroth
        raw_one = moved if raw_one is None else raw_one + moved
        square = u * moved
        raw_two = square if raw_two is None else raw_two + square
    if first is not None:
        cross = (u + u) * first
        raw_two = cross if raw_two is None else raw_two + cross
    rest = -raw_two if zeroth is None else zeroth - raw_two
    return 0.5 * (raw_two - raw_one), rest, 0.5 * (raw_one + raw_two)


def post_populations(rho, ux, uy, uz, pxy, pxz, pyz, dev_one, dev_two):
    inverse = 1.0 / rho
    pxx = (rho + dev_one + dev_two) * (1.0 / 3.0)
    pyy = pxx - dev_one
    pzz = pxx - dev_two
    sxy, sxz, syz = pxy * inverse, pxz * inverse, pyz * inverse
    syy, szz = pyy * inverse, pzz * inverse
    central = {
        (0, 0, 0): rho, (2, 0, 0): pxx, (0, 2, 0): pyy, (0, 0, 2): pzz,
        (1, 1, 0): pxy, (1, 0, 1): pxz, (0, 1, 1): pyz,
        (2, 2, 0): pxx * syy + 2.0 * pxy * sxy,
        (2, 0, 2): pxx * szz + 2.0 * pxz * sxz,
        (0, 2, 2): pyy * szz + 2.0 * pyz * syz,
        (2, 1, 1): pxx * syz + 2.0 * pxy * sxz,
        (1, 2, 1): pyy * sxz + 2.0 * pxy * syz,
        (1, 1, 2): pzz * sxy + 2.0 * pxz * syz,
        (2, 2, 2): pxx * syy * szz
        + 2.0 * (pxx * syz * syz + pyy * sxz * sxz + pzz * sxy * sxy)
        + 8.0 * pxy * sxz * syz,
    }
    along_z = {}
    for a in range(3):
        for b in range(3):
            parts = backward(*(central.get((a, b, c)) for c in range(3)), uz)
            for k in range(3):
                along_z[a, b, k] = parts[k]
    along_y = {}
    for a in range(3):
        for k in range(3):
            parts = backward(*(along_z[a, b, k] for b in range(3)), uy)
            for j in range(3):
                along_y[a, j, k] = parts[j]
    result = [None] * NQ
    for j in range(3):
        for k in range(3):
            parts = backward(*(along_y[a, j, k] for a in range(3)), ux)
            for i in range(3):
                result[i * 9 + j * 3 + k] = parts[i]
    return result


def unload(plan_ref, ins, fields_ref, index=0):
    cap = ins[0].shape[0]
    tiles = ins[-1].shape[1]
    for e in range(len(ins) * cap):
        t = plan_ref[e]
        in_ref = ins[e // cap]
        first = index * tiles if in_ref.shape[1] > tiles else 0

        @pl.when(t >= 0)
        def _():
            for tile in range(tiles):
                fields_ref[pl.ds(tile * SUB * SUB + t, SUB, stride=SUB), :] = in_ref[e % cap, first + tile]


def row_of(ref, row):
    return ref[row * SUB : (row + 1) * SUB, :]


def turned(value, places):
    turn = places * EDGE % LANES
    return pltpu.roll(value, turn, axis=1) if turn else value


def places_y():
    return lax.broadcasted_iota(jnp.int32, (SUB, LANES), 1) // EDGE


def outer_fields(fields_ref, step, c):
    first = (SIDE_TILES + step * NFIELD) * SUB
    return [row_of(fields_ref, first + n * SUB + c) for n in range(NFIELD)]


def side_fields(fields_ref, half):
    return [row_of(fields_ref, 1 + half * NFIELD + n) for n in range(NFIELD)]


def fill_outer(fields_ref, main_ref):
    for step, group in enumerate(CHUNKS[0]):
        for c in range(SUB):
            for q, value in enumerate(post_populations(*outer_fields(fields_ref, step, c))):
                main_ref[q, 2 + group * SUB + c] = value


def fill_inner(fields_ref, late_ref, group, main_ref):
    spot = places_y()
    last = [None] * NFIELD
    for c in range(SUB):
        at = (group * WIDTH + c // 2) % SUB
        place = free_place(c)
        side = side_fields(fields_ref, c % 2)
        fields = []
        for n in range(NFIELD):
            if c < SUB - 1:
                row = row_of(late_ref, n * (SUB - 1) + c)
                part = turned(row, c - place)
                last[n] = part if c == 0 else jnp.where(spot == c, part, last[n])
            else:
                row = last[n]
            fields.append(jnp.where(spot == place, turned(side[n], place - at), row))
        for q, value in enumerate(post_populations(*fields)):
            main_ref[q, 2 + group * SUB + c] = value


def fill_sides(below_in, above_in, below_ref, above_ref, first, last):
    for x in range(first, last):
        at = x % SUB
        for k in range(9):
            below_ref[k, x + 1] = turned(below_in[k, x // SUB], SUB - 1 - at)
            above_ref[k, x + 1] = turned(above_in[k, x // SUB], -at)


def stream_pair(first_x, out_ref, main_ref, below_ref, above_ref):
    lane = lax.broadcasted_iota(jnp.int32, (SUB, LANES), 1)
    block = lax.broadcasted_iota(jnp.int32, (SUB, LANES), 0)
    along = lane % EDGE
    first_z, last_z = along == 0, along == EDGE - 1
    floor = first_z & (block == 0)
    ceiling = last_z & (block == SUB - 1)
    low_y, high_y = lane < EDGE, lane >= LANES - EDGE
    for i in range(2):
        for half in range(2):
            c = i * 2 + half
            for q in range(NQ):
                cx, cy, cz = velocity(q)
                x = first_x + i - cx + 1
                a = main_ref[q, x * 2 + half]
                k = (cx + 1) * 3 + cz + 1
                if cy == 1:
                    a = jnp.where(high_y, main_ref[q, x * 2] if half else below_ref[k, x], a)
                elif cy == -1:
                    a = jnp.where(low_y, above_ref[k, x] if half else main_ref[q, x * 2 + 1], a)
                shift = EDGE * cy + cz
                value = a if shift == 0 else pltpu.roll(a, shift % LANES, axis=1)
                if cz:
                    bounced = main_ref[26 - q, (first_x + i + 1) * 2 + half]
                    turn = (1 if cz == 1 else SUB - 1)
                    fill = pltpu.roll(pltpu.roll(a, turn, axis=0), (shift - cz * EDGE) % LANES, axis=1)
                    value = jnp.where(first_z if cz == 1 else last_z, fill, value)
                    value = jnp.where(floor if cz == 1 else ceiling, bounced, value)
                out_ref[q, :, c * LANES : (c + 1) * LANES] = value


def stream_pairs(pairs, out_hbm, pair_ref, sems, *lattice, meanwhile=lambda: None):
    span = pair_ref.shape[3]

    def copy(i):
        return pltpu.make_async_copy(
            pair_ref.at[i], out_hbm.at[:, :, pl.ds(pairs[i] * span, span)], sems.at[i]
        )

    for i, pair in enumerate(pairs):
        stream_pair(2 * pair, pair_ref.at[i], *lattice)
        copy(i).start()
    meanwhile()
    for i in range(len(pairs)):
        copy(i).wait()


def faces_kernel(count, *refs):
    ins = refs[:count]
    ylo_ref, yhi_ref, xlo_ref, xhi_ref, plan_ref, fields_ref, tag_ref, sems = refs[count:]
    tag_at = read_tags(ins, tag_ref, sems)
    for e in range(count * ins[0].shape[0]):
        tag = tag_at(e)
        plan_ref[e] = jnp.where(tag >= 0, lax.rem(tag, SUB), -1)
    unload(plan_ref, ins, fields_ref)
    spot = places_y()
    for half in range(2):
        packed = [side_fields(fields_ref, half)] * 2
        place = half * (SUB - 1)
        for step, group in enumerate(CHUNKS[0]):
            tile = group * WIDTH // SUB
            for x in range(group * WIDTH, (group + 1) * WIDTH):
                c = (x - group * WIDTH) * 2 + half
                packed[tile] = [
                    jnp.where(spot == x % SUB, turned(value, x % SUB - place), old)
                    for value, old in zip(outer_fields(fields_ref, step, c), packed[tile])
                ]
        for tile in range(2):
            result = post_populations(*packed[tile])
            for i in range(3):
                for k in range(3):
                    (yhi_ref if half else ylo_ref)[i * 3 + k, tile] = result[i * 9 + half * 6 + k]
        low = post_populations(*outer_fields(fields_ref, CHUNKS[0].index(0), half))
        high = post_populations(*outer_fields(fields_ref, CHUNKS[0].index(GROUPS - 1), SUB - 2 + half))
        for q in range(9):
            xlo_ref[q, half] = low[q]
            xhi_ref[q, half] = high[18 + q]


def faces(homes):
    shape = jax.ShapeDtypeStruct
    face = shape((9, 2, SUB, LANES), jnp.float32)
    slots = len(homes) * homes[0].shape[0]
    whole = pl.BlockSpec(memory_space=pltpu.VMEM)
    return pl.pallas_call(
        functools.partial(faces_kernel, len(homes)),
        in_specs=[whole] * len(homes),
        out_specs=[whole] * 4 + [pl.BlockSpec(memory_space=pltpu.SMEM), whole],
        scratch_shapes=tag_scratch(len(homes), slots),
        out_shape=[face] * 4
        + [shape((slots,), jnp.int32), shape((tiles_of(0) * SUB * SUB, LANES), jnp.float32)],
        compiler_params=pltpu.CompilerParams(vmem_limit_bytes=VMEM_LIMIT),
        cost_estimate=pl.CostEstimate(flops=10**7, bytes_accessed=3 * 10**6, transcendentals=0),
        name="faces",
    )(*homes)


PAIRS = ((0, 1, 2, 7), (3, 4, 5, 6))
KEPT = ((5, 8), (12, 15))


def advance_kernel(count, plan_ref, *refs):
    ins = refs[:count]
    (
        fields_ref, xlo_ref, xhi_ref, below_in, above_in, out_ref, kept_ref,
        main_ref, below_ref, above_ref, late_ref, pair_ref, sems,
    ) = refs[count:]
    unload(plan_ref, ins, late_ref)
    fill_outer(fields_ref, main_ref)
    fill_inner(fields_ref, late_ref, INNER[0], main_ref)
    fill_sides(below_in, above_in, below_ref, above_ref, 0, 7)
    fill_sides(below_in, above_in, below_ref, above_ref, 13, EDGE)
    for k in range(3):
        below_ref[6 + k, 0] = xlo_ref[18 + k]
        above_ref[6 + k, 0] = turned(xlo_ref[21 + k], 1)
        below_ref[k, EDGE + 1] = turned(xhi_ref[18 + k], -1)
        above_ref[k, EDGE + 1] = xhi_ref[21 + k]
    for q in range(9):
        for half in range(2):
            main_ref[18 + q, half] = xlo_ref[q * 2 + half]
            main_ref[q, 2 * EDGE + 2 + half] = xhi_ref[q * 2 + half]
    def keep_rows():
        to = 0
        for first, last in KEPT:
            for row in range(2 * first + 2, 2 * last + 2):
                for q in range(NQ):
                    kept_ref[q, to] = main_ref[q, row]
                to += 1

    stream_pairs(PAIRS[0], out_ref, pair_ref, sems, main_ref, below_ref, above_ref, meanwhile=keep_rows)


def finish_kernel(count, plan_ref, *refs):
    ins = refs[:count]
    (
        fields_ref, kept_ref, below_in, above_in, _, out_ref,
        main_ref, below_ref, above_ref, late_ref, pair_ref, sems,
    ) = refs[count:]
    copies = []
    to = 0
    for first, last in KEPT:
        rows = 2 * (last - first)
        copies.append(
            pltpu.make_async_copy(
                kept_ref.at[:, pl.ds(to, rows)],
                main_ref.at[:, pl.ds(2 * first + 2, rows)],
                sems.at[len(PAIRS[1]) + len(copies)],
            )
        )
        to += rows
    for copy in copies:
        copy.start()
    unload(plan_ref, ins, late_ref, 1)
    fill_inner(fields_ref, late_ref, INNER[1], main_ref)
    fill_sides(below_in, above_in, below_ref, above_ref, 5, 15)
    for copy in copies:
        copy.wait()

    stream_pairs(PAIRS[1], out_ref, pair_ref, sems, main_ref, below_ref, above_ref)


def scratch_of_lattice():
    side = pltpu.VMEM((9, EDGE + 2, SUB, LANES), jnp.float32)
    return [
        pltpu.VMEM((NQ, 2 * EDGE + 4, SUB, LANES), jnp.float32), side, side,
        pltpu.VMEM((LATE_TILES * SUB * SUB, LANES), jnp.float32),
        pltpu.VMEM((len(PAIRS[0]), NQ, SUB, 4 * LANES), jnp.float32),
        pltpu.SemaphoreType.DMA((len(PAIRS[0]) + len(KEPT),)),
    ]


def advance(plan, homes, fields, xlo, xhi, below, above):
    inputs = [*homes, fields, xlo, xhi, below, above]
    whole = pl.BlockSpec(memory_space=pltpu.VMEM)
    kept = 2 * sum(last - first for first, last in KEPT)
    return pl.pallas_call(
        functools.partial(advance_kernel, len(homes)),
        in_specs=[pl.BlockSpec(memory_space=pltpu.SMEM)] + [whole] * len(inputs),
        out_specs=[pl.BlockSpec(memory_space=pltpu.HBM), whole],
        scratch_shapes=scratch_of_lattice(),
        out_shape=[
            jax.ShapeDtypeStruct((NQ, SUB, GROUPS * SUB * LANES), jnp.float32),
            jax.ShapeDtypeStruct((NQ, kept, SUB, LANES), jnp.float32),
        ],
        compiler_params=pltpu.CompilerParams(vmem_limit_bytes=VMEM_LIMIT),
        cost_estimate=pl.CostEstimate(flops=10**7, bytes_accessed=5 * 10**6, transcendentals=0),
        name="advance",
    )(plan, *inputs)


def finish(plan, homes, fields, kept, below, above, out):
    inputs = [*homes, fields, kept, below, above]
    whole = pl.BlockSpec(memory_space=pltpu.VMEM)
    target = pl.BlockSpec(memory_space=pltpu.HBM)
    return pl.pallas_call(
        functools.partial(finish_kernel, len(homes)),
        in_specs=[pl.BlockSpec(memory_space=pltpu.SMEM)] + [whole] * len(inputs) + [target],
        out_specs=target,
        scratch_shapes=scratch_of_lattice(),
        out_shape=jax.ShapeDtypeStruct(out.shape, jnp.float32),
        input_output_aliases={1 + len(inputs): 0},
        compiler_params=pltpu.CompilerParams(vmem_limit_bytes=VMEM_LIMIT),
        cost_estimate=pl.CostEstimate(flops=10**7, bytes_accessed=5 * 10**6, transcendentals=0),
        name="finish",
    )(plan, *inputs, out)


def shifted(value, axis, step):
    count = lax.axis_size(axis)
    return lax.ppermute(value, axis, [(i, (i + step) % count) for i in range(count)])


def after(value, *earlier):
    return lax.optimization_barrier((value, *earlier))[0]


def on_device(populations, destination, refinement):
    blocks = populations.shape[0]
    row_count = lax.axis_size("row")
    col_count = lax.axis_size("col")
    cap_row = 2 * ((blocks + row_count - 1) // row_count)
    cap_col = 2 * ((blocks + col_count - 1) // col_count)
    ordered = jnp.transpose(populations, (1, 0, 2))

    def prepared(part, *earlier):
        first = after(destination, *earlier)
        return pre(ordered, first, refinement, part, row_count, cap_row, blocks * col_count)

    def to_rows(sent):
        return lax.all_to_all(sent, "row", split_axis=0, concat_axis=0, tiled=True)

    def to_columns(packed):
        return [exchanged(packed[d], "col", d) for d in range(len(packed) - 1, 0, -1)] + [packed[0]]

    sent = prepared(0)
    early_row = to_rows(sent)
    late_row = to_rows(prepared(1, sent))
    packed, plan = repack(early_row, None, 0, col_count, cap_col, blocks)
    ylo, yhi, xlo, xhi, picked, fields = faces(to_columns(packed))
    below, above = shifted(yhi, "col", 1), shifted(ylo, "col", -1)
    up = jnp.concatenate([xhi.reshape(18, SUB, LANES), below[6:, 1], above[6:, 1]])
    down = jnp.concatenate([xlo.reshape(18, SUB, LANES), below[:3, 0], above[:3, 0]])
    xlo, xhi = shifted(up, "row", 1), shifted(down, "row", -1)
    packed = repack(after(late_row, up, down), plan, 1, col_count, cap_col, blocks)
    far, *packed = packed
    far = exchanged(far, "col", col_count - 1)
    middle = [far] + to_columns(packed[: col_count - 1])
    last = [far] + to_columns(packed[col_count - 1 :])
    out, kept = advance(picked, middle, fields, xlo, xhi, below, above)
    return jnp.transpose(finish(picked, last, fields, kept, below, above, out), (1, 0, 2))


def solution(mesh):
    return jax.shard_map(
        on_device,
        mesh=mesh,
        in_specs=(P(("row", "col"), None, None), P(("row", "col")), P(("row", "col"))),
        out_specs=P(("row", "col"), None, None),
        check_vma=False,
    )
```
